32 devices in a mesh: row: 8 (over z, y), col: 4 (over x, core).
Axes of the slice: x: 2, y: 2, z: 4, core: 2. Of those that a mesh axis runs over, the one named last changes fastest.
Arguments:
- rhs: float32 [2, 8, 1024, 128], P(None, 'row'), may hold values from -6 to 6
- diag_inv: bfloat16 [4, 1024, 1024], P(None, 'row'), as said below
- blocks: bfloat16 [1, 4, 8, 1, 1024, 1024], P(None, 'col', 'row'), may hold values from -0.09375 to 0.09375
- block_rows: int32 [1, 4, 8, 1], P(None, 'col', 'row'), may hold values from 0 to 1, as said below
- counts: int32 [1, 4, 8], P(None, 'col', 'row'), may hold values from 0 to 1, as said below
Outputs:
- solved: float32 [1, 4, 1024, 128], P(None, 'col')
- remainder: float32 [2, 8, 1024, 128], P(None, 'row')
The draws below stay inside these ranges and needn't reach their ends.
Inputs may be any that keep to these rules, and one draw needn't show every extreme that they name: `diag_inv`: lower triangular. `block_rows`: the 1 entries of one list are different; for row indices r below 4, slot 0 lists local block row 0. `counts`: 1 is reached in every draw; for row indices r below 4 the count is 1.
All inputs are finite; a program needn't handle non-finite values.
Results may differ from the reference program's by a relative error of at most 0.0041.
Values may be sent and summed in bfloat16 or wider, within the bound.
No kernel may reach another device: no remote copies, remote signals or barrier semaphores. Data moves between devices by JAX's collectives and lax.ppermute only.
A program may use at most 64 MiB of HBM per device.

```python
import jax
import jax.numpy as jnp
from jax import lax

BS = 1024
RHS = 128
RB_DEV = 2
NZ_DEV = 1
KC = 4
KJ = 1
N_ROW = 8
N_COL = 4


def draw_diag_inv(key, part):
    key = jax.random.fold_in(key, 3)
    first, second = jax.random.split(key)
    off = jax.random.normal(first, (KC, BS, BS), jnp.float32) / jnp.sqrt(jnp.float32(BS))
    scales = jnp.exp(jax.random.uniform(second, (KC, BS), jnp.float32, jnp.log(0.5), jnp.log(1.5)))
    lower = jnp.tril(off, -1)
    eye = jnp.eye(BS, dtype=jnp.float32)
    return (lower + eye[None] * scales[:, :, None]).astype(jnp.bfloat16)


def draw_block_rows(key, part):
    key = jax.random.fold_in(key, 1)
    scores = jax.random.randint(key, (KJ, N_COL, N_ROW, RB_DEV), 0, 1 << 20) * RB_DEV
    scores = scores + jnp.arange(RB_DEV, dtype=jnp.int32)
    ranks = jnp.arange(N_ROW, dtype=jnp.int32)[:, None]
    locals_ids = jnp.arange(RB_DEV, dtype=jnp.int32)[None, :]
    forced = ((ranks < KC) & (locals_ids == 0)).astype(jnp.int32)
    scores = scores - forced * (1 << 23)
    order = jnp.argsort(scores, axis=-1, stable=True)
    return order[..., :NZ_DEV].astype(jnp.int32)


def draw_counts(key, part):
    key = jax.random.fold_in(key, 2)
    first, second = jax.random.split(key)
    base = jax.random.randint(first, (KJ * N_COL * N_ROW,), 0, NZ_DEV + 1)
    pick = jax.random.randint(second, (), 0, KJ * N_COL * N_ROW)
    spots = jnp.arange(KJ * N_COL * N_ROW, dtype=jnp.int32)
    base = jnp.where(spots == pick, NZ_DEV, base)
    ranks = spots % N_ROW
    base = jnp.where(ranks < KC, NZ_DEV, base)
    return base.reshape(KJ, N_COL, N_ROW).astype(jnp.int32)


def shard_levels(rng, shape, pieces, smallest, largest):
    def one(dim, shards_of):
        heights = jax.random.uniform(jax.random.fold_in(jax.random.fold_in(rng, 6), dim), (shards_of,), jnp.float32, smallest / len(pieces), largest / len(pieces))
        return jnp.repeat(jnp.exp(heights), shape[dim] // shards_of).reshape((-1,) + (1,) * (len(shape) - dim - 1))

    gain = one(*pieces[0])
    for cut in pieces[1:]:
        gain = gain * one(*cut)
    return gain


def bell_draw(key, extent, deviation, reach, cuts=(), kind=jnp.bfloat16):
    drawn = deviation * jax.random.normal(key, extent, jnp.float32)
    if cuts:
        drawn = drawn * shard_levels(key, extent, cuts, -0.22, 0.18)
    return jnp.clip(drawn, -reach, reach).astype(kind)


def setup_inputs(seed: int = 0) -> dict:
    arg_keys = jax.random.split(jax.random.key(seed), 6)
    rhs = bell_draw(arg_keys[0], (RB_DEV, N_ROW, BS, RHS), 1.0, 6.0, ((1, 8),), jnp.float32)
    diag_inv = draw_diag_inv(jax.random.fold_in(arg_keys[5], 71), 0)
    blocks = bell_draw(arg_keys[2], (KJ, N_COL, N_ROW, NZ_DEV, BS, BS), (4 * BS) ** -0.5, 0.09375, ((1, 4), (2, 8)))
    block_rows = draw_block_rows(jax.random.fold_in(arg_keys[5], 71), 0)
    counts = draw_counts(jax.random.fold_in(arg_keys[5], 71), 0)
    return dict(rhs=rhs, diag_inv=diag_inv, blocks=blocks, block_rows=block_rows, counts=counts)


def reference(rhs, diag_inv, blocks, block_rows, counts):
    acc = rhs.reshape(RB_DEV * N_ROW, BS, RHS)
    results = []
    ranks = jnp.arange(N_ROW, dtype=jnp.int32)
    slots = jnp.arange(NZ_DEV, dtype=jnp.int32)
    for k in range(KC):
        j = k // N_COL
        c = k % N_COL
        pivot = acc[k].astype(jnp.bfloat16)
        sol = jnp.dot(diag_inv[k], pivot, preferred_element_type=jnp.float32)
        results.append(sol)
        quant = sol.astype(jnp.bfloat16).astype(jnp.float32)
        rows = block_rows[j, c]
        glob = rows * N_ROW + ranks[:, None]
        valid = (slots[None, :] < counts[j, c][:, None]) & (glob > k)
        contrib = jnp.einsum("rsab,bn->rsan", blocks[j, c].astype(jnp.float32), quant, precision=lax.Precision.HIGHEST)
        contrib = jnp.where(valid[:, :, None, None], contrib, jnp.float32(0.0))
        acc = acc.at[glob.reshape(-1)].add(-contrib.reshape(N_ROW * NZ_DEV, BS, RHS))
    solved = jnp.stack(results).reshape(KJ, N_COL, BS, RHS)
    return solved, acc.reshape(RB_DEV, N_ROW, BS, RHS)
```

```python
import functools

import jax
import jax.numpy as jnp
from jax import lax
from jax.experimental import pallas as pl
from jax.experimental.pallas import tpu as pltpu
from jax.sharding import PartitionSpec as P

VMEM = pl.BlockSpec(memory_space=pltpu.VMEM)
ANY = pl.BlockSpec(memory_space=pl.ANY)
SMEM = pl.BlockSpec(memory_space=pltpu.SMEM)
TAIL = 16


def broadcast(value, axis, root):
    mine = lax.axis_index(axis) == root
    return lax.psum(jnp.where(mine, value, jnp.zeros_like(value)), axis)


def on_device_any(rhs, diag_inv, blocks, block_rows, counts):
    nrow = lax.axis_size("row")
    ncol = lax.axis_size("col")
    my_row = lax.axis_index("row")
    my_col = lax.axis_index("col")
    kc = diag_inv.shape[0]
    rb_local = rhs.shape[0]
    nz_local = blocks.shape[3]
    local_rhs = rhs[:, 0]
    partial_value = jnp.zeros(local_rhs.shape, jnp.float32)
    solved_list = [jnp.zeros(local_rhs.shape[1:], jnp.float32)]
    slot_ids = jnp.arange(nz_local, dtype=jnp.int32)
    local_ids = jnp.arange(rb_local, dtype=jnp.int32)
    for k in range(kc):
        j = k // ncol
        owner_row = k % nrow
        local_pivot = k // nrow
        mine_row = my_row == owner_row
        mine_col = my_col == k % ncol
        pivot_part = jnp.where(mine_row, partial_value[local_pivot], jnp.float32(0.0))
        summed = lax.psum(pivot_part, "col")
        updated = (local_rhs[local_pivot] - summed).astype(jnp.bfloat16)
        pivot_bf = broadcast(updated, "row", owner_row)
        row_part = jnp.dot(diag_inv[k], pivot_bf, preferred_element_type=jnp.float32)
        sol = lax.all_gather(row_part, "row", axis=0, tiled=True)
        sol_bf = sol.astype(jnp.bfloat16)
        rows = block_rows[j, 0, 0]
        glob = rows * nrow + my_row
        valid = (slot_ids < counts[j, 0, 0]) & (glob > k) & mine_col
        weights = (valid[:, None] & (rows[:, None] == local_ids[None, :])).astype(jnp.float32)
        contrib = jnp.einsum(
            "sab,bn->san", blocks[j, 0, 0], sol_bf, preferred_element_type=jnp.float32
        )
        partial_value = partial_value + jnp.einsum(
            "sl,san->lan", weights, contrib, precision=lax.Precision.HIGHEST
        )
        solved_list[j] = jnp.where(mine_col, sol, solved_list[j])
    total = lax.psum(partial_value, "col")
    remainder = (local_rhs - total)[:, None]
    solved = jnp.stack(solved_list)[:, None]
    return (solved, remainder)


NR, NC = 8, 4
SOLVER = {1: (1, 0), 2: (2, 1), 3: (3, 2)}
SOURCE = {0: (2, 0), 1: (3, 1), 2: (2, 2), 3: (3, 2)}
ORDER = (5, 7, 4, 6, 3, 2, 1, 0)


def send(value, pairs):
    return lax.ppermute(value, ("row", "col"), [(a * NC + b, c * NC + d) for (a, b), (c, d) in pairs])


def dot(a, b):
    return jnp.dot(a, b, preferred_element_type=jnp.float32)


def first_kernel(rhs_ref, hi_ref, lo_ref, out_ref):
    n = hi_ref.shape[0]
    p = rhs_ref[...].astype(jnp.bfloat16)
    out_ref[:n] = dot(hi_ref[...], p).astype(jnp.bfloat16)
    out_ref[n:] = dot(lo_ref[...], p[: lo_ref.shape[1]]).astype(jnp.bfloat16)


def at(device):
    return (lax.axis_index("row") == device[0]) & (lax.axis_index("col") == device[1])


def any_of(devices):
    flag = at(devices[0])
    for d in devices[1:]:
        flag = flag | at(d)
    return flag


def step_kernel(k, *refs):
    n_in = 4 if k == 1 else 1
    q_in = refs[:n_in]
    if k == 1:
        s_in = s_prev = q_prev = None
        rest = refs[n_in:]
    else:
        s_in, s_prev, q_prev = refs[n_in : n_in + 3]
        rest = refs[n_in + 3 :]
    rhs_ref, l_hbm = rest[:2]
    d_hbm = rest[2 : 2 + NR]
    s_out, q_out = rest[2 + NR : 4 + NR]
    l_v, p_v, q_v = rest[4 + NR : 7 + NR]
    d_v = rest[7 + NR : 7 + 2 * NR]
    l_sem, d_sem = rest[7 + 2 * NR :]
    size = l_hbm.shape[0]
    part = size // NR
    quarter = size // 4

    solver = at(SOLVER[k])
    updates = [SOLVER[k]]
    if k == 1:
        updates += [(2, 0), (3, 0)]
    elif k == 2:
        updates += [(3, 1)]
    update = any_of(updates)

    l_copy = [
        pltpu.make_async_copy(l_hbm.at[pl.ds(i * quarter, quarter)], l_v.at[pl.ds(i * quarter, quarter)], l_sem.at[i])
        for i in range(4)
    ]
    d_copy = [pltpu.make_async_copy(d_hbm[i], d_v[i], d_sem.at[i]) for i in range(NR)]

    @pl.when(update)
    def _():
        for c in l_copy:
            c.start()

    @pl.when(solver)
    def _():
        for c in d_copy:
            c.start()

    if k == 1:
        row = lax.axis_index("row")
        for j in range(4):
            src = lax.rem(row + 7 - j, 4)
            hi = pl.multiple_of((4 + src) * part, part)
            lo = pl.multiple_of(lax.rem(src + 1, 4) * part, part)
            q_v[pl.ds(hi, part)] = q_in[j][:part]
            q_v[pl.ds(lo, part)] = q_in[j][part:]
    else:
        q_v[...] = q_in[0][...]

    @pl.when(update)
    def _():
        q = q_v[...]
        for i in range(4):
            l_copy[i].wait()
            rows = pl.ds(i * quarter, quarter)
            s = dot(l_v[rows], q)
            if s_in is not None:
                s = s + s_in[rows].astype(jnp.float32)
            s_out[rows] = s.astype(jnp.bfloat16)
            p_v[rows] = (rhs_ref[rows] - s).astype(jnp.bfloat16)

    @pl.when(jnp.logical_not(update))
    def _():
        if s_prev is None:
            s_out[...] = jnp.zeros_like(s_out)
        else:
            s_out[...] = s_prev[...]

    @pl.when(solver)
    def _():
        for i in range(NR):
            d_copy[i].wait()
            width = (i + 1) * part
            q_out[pl.ds(i * part, part)] = dot(d_v[i][...], p_v[:width]).astype(jnp.bfloat16)

    @pl.when(jnp.logical_not(solver))
    def _():
        if k == 1:
            q_out[...] = q_v[...]
        elif k == 2:
            keep = at(SOURCE[1])
            q_out[...] = jnp.where(keep, q_v[...], q_prev[...])
        else:
            q_out[...] = q_prev[...]


def step(k, q_in, s_in, s_prev, q_prev, rhs0, block, d_parts):
    shape = rhs0.shape
    args = list(q_in)
    if k > 1:
        args += [s_in, s_prev, q_prev]
    args += [rhs0, block]
    n_vmem = len(args) - 1
    args += list(d_parts)
    return pl.pallas_call(
        functools.partial(step_kernel, k),
        out_shape=[jax.ShapeDtypeStruct(shape, jnp.bfloat16)] * 2,
        in_specs=[VMEM] * n_vmem + [ANY] * (1 + NR),
        out_specs=[VMEM] * 2,
        scratch_shapes=[
            pltpu.VMEM(block.shape, jnp.bfloat16),
            pltpu.VMEM(shape, jnp.bfloat16),
            pltpu.VMEM(shape, jnp.bfloat16),
        ]
        + [pltpu.VMEM(d.shape, jnp.bfloat16) for d in d_parts]
        + [pltpu.SemaphoreType.DMA((4,)), pltpu.SemaphoreType.DMA((NR,))],
        compiler_params=pltpu.CompilerParams(vmem_limit_bytes=24 << 20),
        name=f"step{k}",
    )(*args)


def update_kernel(*refs):
    rows_ref, counts_ref = refs[:2]
    got = refs[2 : 2 + NR]
    s_ref, l_hbm = refs[2 + NR : 4 + NR]
    solved_ref, out_ref = refs[4 + NR : 6 + NR]
    l_v, q_v, l_sem, q_sem = refs[6 + NR :]
    size = l_hbm.shape[0]
    quarter = size // 4
    row = lax.axis_index("row")
    col = lax.axis_index("col")
    below = row >= NC
    l_copy = [
        pltpu.make_async_copy(l_hbm.at[pl.ds(i * quarter, quarter)], l_v.at[pl.ds(i * quarter, quarter)], l_sem.at[i])
        for i in range(4)
    ]

    @pl.when(below)
    def _():
        for c in l_copy:
            c.start()

    for j in range(NR):

        @pl.when(row == ORDER[j])
        def _():
            copy = pltpu.make_async_copy(got[j], q_v, q_sem)
            copy.start()
            copy.wait()

    q = q_v[...]
    solved_ref[...] = q.astype(jnp.float32)

    @pl.when(below)
    def _():
        for i in range(4):
            l_copy[i].wait()
            rows = pl.ds(i * quarter, quarter)
            out_ref[rows] = dot(l_v[rows], q).astype(jnp.bfloat16)

    @pl.when(jnp.logical_not(below))
    def _():
        out_ref[pl.ds(0, size)] = s_ref[...]

    listed = rows_ref[0, 0, 0, 0]
    there = below & (counts_ref[0, 0, 0] > 0)
    first = (there & (listed == 0)) | (jnp.logical_not(below) & (row >= 1) & (col == row - 1))
    second = there & (listed == 1)
    ids = lax.broadcasted_iota(jnp.int32, (TAIL, out_ref.shape[1]), 0)
    flag = ((ids == 0) & first) | ((ids == 1) & second)
    out_ref[pl.ds(size, TAIL)] = jnp.where(flag, 1.0, 0.0).astype(jnp.bfloat16)


def final_kernel(rhs_ref, *refs):
    sums, out_ref = refs[:-1], refs[-1]
    size = out_ref.shape[1]
    for i in range(out_ref.shape[0]):
        acc = rhs_ref[i]
        for s in sums:
            keep = s[pl.ds(size, TAIL)].astype(jnp.float32)[i : i + 1] > 0.5
            acc = acc - jnp.where(keep, s[pl.ds(0, size)].astype(jnp.float32), 0.0)
        out_ref[i] = acc


def on_device_8x4(rhs, diag_inv, blocks, block_rows, counts):
    col = lax.axis_index("col")
    size, width = rhs.shape[2:]
    part = size // NR
    rhs0 = rhs[0, 0]
    block = blocks[0, 0, 0, 0]

    hi = send(diag_inv[0], [((4 + c, c), (0, c)) for c in range(4)])
    lo = send(diag_inv[0, :, : 4 * part], [(((c + 1) % 4, c), (0, c)) for c in range(4)])

    mine = lax.rem(col + 1, NC)
    d_parts = []
    for r in range(NR):
        cut = lax.dynamic_slice(diag_inv, (mine, 0, 0), (1, part, (r + 1) * part))[0]
        d_parts.append(send(cut, [((r, SOLVER[k][1]), SOLVER[k]) for k in (1, 2, 3)]))

    q0 = pl.pallas_call(
        first_kernel,
        out_shape=jax.ShapeDtypeStruct((2 * part, width), jnp.bfloat16),
        in_specs=[VMEM] * 3,
        out_specs=VMEM,
        name="first",
    )(rhs0, hi, lo)
    takers = ((1, 0), (2, 0), (3, 0), (0, 0))
    got = [send(q0, [((0, c), takers[(c + j) % 4]) for c in range(4)]) for j in range(4)]

    s1, q1 = step(1, got, None, None, None, rhs0, block, d_parts)
    s_in = send(s1, [((2, 0), (2, 1)), ((3, 0), (3, 1))])
    q_in_a = send(q1, [((1, 0), (2, 1))])
    q_in_b = send(q1, [((1, 0), (3, 1))])
    q_in = jnp.where(lax.axis_index("row") == 2, q_in_a, q_in_b)
    s2, q2 = step(2, [q_in], s_in, s1, q1, rhs0, block, d_parts)
    s_in = send(s2, [((3, 1), (3, 2))])
    q_in = send(q2, [((2, 1), (3, 2))])
    q2_far = send(q2, [((2, 1), (2, 2))])
    s3, q3 = step(3, [q_in], s_in, s2, q2, rhs0, block, d_parts)
    q_all = jnp.where((lax.axis_index("row") == 2) & (col == 2), q2_far, q3)
    got = [send(q_all, [(SOURCE[k], (r, k)) for k in range(NC)]) for r in ORDER]

    solved, mine_sum = pl.pallas_call(
        update_kernel,
        out_shape=[
            jax.ShapeDtypeStruct((size, width), jnp.float32),
            jax.ShapeDtypeStruct((size + TAIL, width), jnp.bfloat16),
        ],
        in_specs=[SMEM, SMEM] + [ANY] * NR + [VMEM, ANY],
        out_specs=[VMEM, VMEM],
        scratch_shapes=[
            pltpu.VMEM(block.shape, jnp.bfloat16),
            pltpu.VMEM((size, width), jnp.bfloat16),
            pltpu.SemaphoreType.DMA((4,)),
            pltpu.SemaphoreType.DMA,
        ],
        compiler_params=pltpu.CompilerParams(vmem_limit_bytes=16 << 20),
        name="update",
    )(block_rows, counts, *got, s3, block)

    others = [
        send(mine_sum, [((r, c), (r, (c + s) % NC)) for r in range(NR) for c in range(NC)])
        for s in range(1, NC)
    ]
    remainder = pl.pallas_call(
        final_kernel,
        out_shape=jax.ShapeDtypeStruct((rhs.shape[0], size, width), jnp.float32),
        in_specs=[VMEM] * (1 + NC),
        out_specs=VMEM,
        compiler_params=pltpu.CompilerParams(vmem_limit_bytes=16 << 20),
        name="final",
    )(rhs[:, 0], mine_sum, *others)
    return solved[None, None], remainder[:, None]


def solution(mesh):
    in_specs = (
        P(None, "row", None, None),
        P(None, "row", None),
        P(None, "col", "row", None, None, None),
        P(None, "col", "row", None),
        P(None, "col", "row"),
    )
    out_specs = (P(None, "col", None, None), P(None, "row", None, None))
    small = mesh.shape["row"] == NR and mesh.shape["col"] == NC
    return jax.shard_map(
        on_device_8x4 if small else on_device_any,
        mesh=mesh,
        in_specs=in_specs,
        out_specs=out_specs,
        check_vma=False,
    )
```

```python
import functools

import jax
import jax.numpy as jnp
from jax import lax
from jax.experimental import pallas as pl
from jax.experimental.pallas import tpu as pltpu
from jax.sharding import PartitionSpec as P

VMEM = pl.BlockSpec(memory_space=pltpu.VMEM)
ANY = pl.BlockSpec(memory_space=pl.ANY)
SMEM = pl.BlockSpec(memory_space=pltpu.SMEM)
TAIL = 16


def broadcast(value, axis, root):
    mine = lax.axis_index(axis) == root
    return lax.psum(jnp.where(mine, value, jnp.zeros_like(value)), axis)


def on_device_any(rhs, diag_inv, blocks, block_rows, counts):
    nrow = lax.axis_size("row")
    ncol = lax.axis_size("col")
    my_row = lax.axis_index("row")
    my_col = lax.axis_index("col")
    kc = diag_inv.shape[0]
    rb_local = rhs.shape[0]
    nz_local = blocks.shape[3]
    local_rhs = rhs[:, 0]
    partial_value = jnp.zeros(local_rhs.shape, jnp.float32)
    solved_list = [jnp.zeros(local_rhs.shape[1:], jnp.float32)]
    slot_ids = jnp.arange(nz_local, dtype=jnp.int32)
    local_ids = jnp.arange(rb_local, dtype=jnp.int32)
    for k in range(kc):
        j = k // ncol
        owner_row = k % nrow
        local_pivot = k // nrow
        mine_row = my_row == owner_row
        mine_col = my_col == k % ncol
        pivot_part = jnp.where(mine_row, partial_value[local_pivot], jnp.float32(0.0))
        summed = lax.psum(pivot_part, "col")
        updated = (local_rhs[local_pivot] - summed).astype(jnp.bfloat16)
        pivot_bf = broadcast(updated, "row", owner_row)
        row_part = jnp.dot(diag_inv[k], pivot_bf, preferred_element_type=jnp.float32)
        sol = lax.all_gather(row_part, "row", axis=0, tiled=True)
        sol_bf = sol.astype(jnp.bfloat16)
        rows = block_rows[j, 0, 0]
        glob = rows * nrow + my_row
        valid = (slot_ids < counts[j, 0, 0]) & (glob > k) & mine_col
        weights = (valid[:, None] & (rows[:, None] == local_ids[None, :])).astype(jnp.float32)
        contrib = jnp.einsum(
            "sab,bn->san", blocks[j, 0, 0], sol_bf, preferred_element_type=jnp.float32
        )
        partial_value = partial_value + jnp.einsum(
            "sl,san->lan", weights, contrib, precision=lax.Precision.HIGHEST
        )
        solved_list[j] = jnp.where(mine_col, sol, solved_list[j])
    total = lax.psum(partial_value, "col")
    remainder = (local_rhs - total)[:, None]
    solved = jnp.stack(solved_list)[:, None]
    return (solved, remainder)


NR, NC = 8, 4
SOLVER = {1: (1, 0), 2: (2, 1), 3: (3, 2)}
SOURCE = {0: (2, 0), 1: (3, 1), 2: (2, 2), 3: (3, 2)}
ORDER = (5, 7, 4, 6, 3, 2, 1, 0)


def send(value, pairs):
    to = {a * NC + b: c * NC + d for (a, b), (c, d) in pairs}
    back = {d: s for s, d in to.items()}
    for last in [d for d in to.values() if d not in to]:
        first = last
        while first in back:
            first = back[first]
        to[last] = first
    for i in range(NR * NC):
        to.setdefault(i, i)
    return lax.ppermute(value, ("row", "col"), sorted(to.items()))


def dot(a, b):
    return jnp.dot(a, b, preferred_element_type=jnp.float32)


def first_kernel(rhs_ref, hi_ref, lo_ref, out_ref):
    n = hi_ref.shape[0]
    p = rhs_ref[...].astype(jnp.bfloat16)
    out_ref[:n] = dot(hi_ref[...], p).astype(jnp.bfloat16)
    out_ref[n:] = dot(lo_ref[...], p[: lo_ref.shape[1]]).astype(jnp.bfloat16)


def at(device):
    return (lax.axis_index("row") == device[0]) & (lax.axis_index("col") == device[1])


def any_of(devices):
    flag = at(devices[0])
    for d in devices[1:]:
        flag = flag | at(d)
    return flag


def whole_kernel(*refs):
    parts, out_ref, sem = refs[:NR], refs[NR], refs[NR + 1]
    part = out_ref.shape[0] // NR
    half = out_ref.shape[0] // 2

    @pl.when(any_of(list(SOLVER.values())))
    def _():
        copies = []
        for i in range(NR):
            wide = parts[i].shape[1]
            copies.append(
                pltpu.make_async_copy(parts[i], out_ref.at[pl.ds(i * part, part), pl.ds(0, wide)], sem.at[i])
            )
            copies[-1].start()
        out_ref[:half, half:] = jnp.zeros((half, half), out_ref.dtype)
        for c in copies:
            c.wait()


def step_kernel(k, *refs):
    n_in = {1: 4, 2: 2, 3: 1}[k]
    q_in = refs[:n_in]
    if k == 1:
        s_in = s_prev = q_prev = None
        rest = refs[n_in:]
    else:
        s_in, s_prev, q_prev = refs[n_in : n_in + 3]
        rest = refs[n_in + 3 :]
    rhs_ref, l_ref, d_ref, s_out, q_out, p_v, q_v = rest
    size = l_ref.shape[0]
    part = size // NR
    half = size // 2
    row = lax.axis_index("row")

    solver = at(SOLVER[k])
    updates = [SOLVER[k]]
    if k == 1:
        updates += [(2, 0), (3, 0)]
    elif k == 2:
        updates += [(3, 1)]
    update = any_of(updates)

    if k == 1:
        for j in range(4):
            src = lax.rem(row + 7 - j, 4)
            hi = pl.multiple_of((4 + src) * part, part)
            lo = pl.multiple_of(lax.rem(src + 1, 4) * part, part)
            q_v[pl.ds(hi, part)] = q_in[j][:part]
            q_v[pl.ds(lo, part)] = q_in[j][part:]
    elif k == 2:

        @pl.when(row == 2)
        def _():
            q_v[...] = q_in[0][...]

        @pl.when(row != 2)
        def _():
            q_v[...] = q_in[1][...]

    @pl.when(update)
    def _():
        s = dot(l_ref[...], q_in[0][...] if k == 3 else q_v[...])
        if s_in is not None:
            s = s + s_in[...].astype(jnp.float32)
        s_out[...] = s.astype(jnp.bfloat16)
        p_v[...] = (rhs_ref[...] - s).astype(jnp.bfloat16)

    @pl.when(jnp.logical_not(update))
    def _():
        if s_prev is None:
            s_out[...] = jnp.zeros_like(s_out)
        else:
            s_out[...] = s_prev[...]

    @pl.when(solver)
    def _():
        q_out[:half] = dot(d_ref[:half, :half], p_v[:half]).astype(jnp.bfloat16)
        q_out[half:] = dot(d_ref[half:], p_v[...]).astype(jnp.bfloat16)

    @pl.when(jnp.logical_not(solver))
    def _():
        if k == 1:
            q_out[...] = q_v[...]
        elif k == 2:
            keep = at(SOURCE[1])
            q_out[...] = jnp.where(keep, q_v[...], q_prev[...])
        else:
            q_out[...] = q_prev[...]


def step(k, q_in, s_in, s_prev, q_prev, rhs0, block, diag):
    shape = rhs0.shape
    args = list(q_in)
    if k > 1:
        args += [s_in, s_prev, q_prev]
    args += [rhs0, block, diag]
    return pl.pallas_call(
        functools.partial(step_kernel, k),
        out_shape=[jax.ShapeDtypeStruct(shape, jnp.bfloat16)] * 2,
        in_specs=[VMEM] * len(args),
        out_specs=[VMEM] * 2,
        scratch_shapes=[pltpu.VMEM(shape, jnp.bfloat16)] * 2,
        compiler_params=pltpu.CompilerParams(vmem_limit_bytes=16 << 20),
        name=f"step{k}",
    )(*args)


def update_kernel(*refs):
    rows_ref, counts_ref = refs[:2]
    got = refs[2 : 2 + NR]
    s_ref, l_ref = refs[2 + NR : 4 + NR]
    solved_ref, out_ref = refs[4 + NR : 6 + NR]
    q_v, q_sem = refs[6 + NR :]
    size = l_ref.shape[0]
    row = lax.axis_index("row")
    col = lax.axis_index("col")
    below = row >= NC

    for j in range(NR):

        @pl.when(row == ORDER[j])
        def _():
            copy = pltpu.make_async_copy(got[j], q_v, q_sem)
            copy.start()
            copy.wait()

    @pl.when(below)
    def _():
        out_ref[pl.ds(0, size)] = dot(l_ref[...], q_v[...]).astype(jnp.bfloat16)

    @pl.when(jnp.logical_not(below))
    def _():
        out_ref[pl.ds(0, size)] = s_ref[...]

    solved_ref[...] = q_v[...].astype(jnp.float32)

    listed = rows_ref[0, 0, 0, 0]
    there = below & (counts_ref[0, 0, 0] > 0)
    first = (there & (listed == 0)) | (jnp.logical_not(below) & (row >= 1) & (col == row - 1))
    second = there & (listed == 1)
    ids = lax.broadcasted_iota(jnp.int32, (TAIL, out_ref.shape[1]), 0)
    flag = ((ids == 0) & first) | ((ids == 1) & second)
    out_ref[pl.ds(size, TAIL)] = jnp.where(flag, 1.0, 0.0).astype(jnp.bfloat16)


def final_kernel(rhs_ref, *refs):
    sums, out_ref = refs[:-1], refs[-1]
    size = out_ref.shape[1]
    for i in range(out_ref.shape[0]):
        acc = rhs_ref[i]
        for s in sums:
            keep = s[pl.ds(size, TAIL)].astype(jnp.float32)[i : i + 1] > 0.5
            acc = acc - jnp.where(keep, s[pl.ds(0, size)].astype(jnp.float32), 0.0)
        out_ref[i] = acc


def on_device_8x4(rhs, diag_inv, blocks, block_rows, counts):
    col = lax.axis_index("col")
    size, width = rhs.shape[2:]
    part = size // NR
    rhs0 = rhs[0, 0]
    block = blocks[0, 0, 0, 0]

    hi = send(diag_inv[0], [((4 + c, c), (0, c)) for c in range(4)])
    lo = send(diag_inv[0, :, : 4 * part], [(((c + 1) % 4, c), (0, c)) for c in range(4)])

    mine = lax.rem(col + 1, NC)
    wide = lax.dynamic_index_in_dim(diag_inv, mine, 0, keepdims=False)
    narrow = wide[:, : 4 * part]
    d_parts = [
        send(narrow if r < 4 else wide, [((r, SOLVER[k][1]), SOLVER[k]) for k in (1, 2, 3)]) for r in range(NR)
    ]
    diag = pl.pallas_call(
        whole_kernel,
        out_shape=jax.ShapeDtypeStruct((size, size), jnp.bfloat16),
        in_specs=[ANY] * NR,
        out_specs=VMEM,
        scratch_shapes=[pltpu.SemaphoreType.DMA((NR,))],
        compiler_params=pltpu.CompilerParams(vmem_limit_bytes=8 << 20),
        name="whole",
    )(*d_parts)

    q0 = pl.pallas_call(
        first_kernel,
        out_shape=jax.ShapeDtypeStruct((2 * part, width), jnp.bfloat16),
        in_specs=[VMEM] * 3,
        out_specs=VMEM,
        name="first",
    )(rhs0, hi, lo)
    takers = ((1, 0), (2, 0), (3, 0), (0, 0))
    got = [send(q0, [((0, c), takers[(c + j) % 4]) for c in range(4)]) for j in range(4)]

    s1, q1 = step(1, got, None, None, None, rhs0, block, diag)
    s_in = send(s1, [((2, 0), (2, 1)), ((3, 0), (3, 1))])
    q_in_a = send(q1, [((1, 0), (2, 1))])
    q_in_b = send(q1, [((1, 0), (3, 1))])
    s2, q2 = step(2, [q_in_a, q_in_b], s_in, s1, q1, rhs0, block, diag)
    s_in = send(s2, [((3, 1), (3, 2))])
    q_in = send(q2, [((2, 1), (3, 2))])
    q2_far = send(q2, [((2, 1), (2, 2))])
    s3, q3 = step(3, [q_in], s_in, s2, q2, rhs0, block, diag)
    q_all = jnp.where((lax.axis_index("row") == 2) & (col == 2), q2_far, q3)
    got = [send(q_all, [(SOURCE[k], (r, k)) for k in range(NC)]) for r in ORDER]

    solved, mine_sum = pl.pallas_call(
        update_kernel,
        out_shape=[
            jax.ShapeDtypeStruct((size, width), jnp.float32),
            jax.ShapeDtypeStruct((size + TAIL, width), jnp.bfloat16),
        ],
        in_specs=[SMEM, SMEM] + [ANY] * NR + [VMEM, VMEM],
        out_specs=[VMEM, VMEM],
        scratch_shapes=[
            pltpu.VMEM((size, width), jnp.bfloat16),
            pltpu.SemaphoreType.DMA,
        ],
        compiler_params=pltpu.CompilerParams(vmem_limit_bytes=16 << 20),
        name="update",
    )(block_rows, counts, *got, s3, block)

    others = [
        send(mine_sum, [((r, c), (r, (c + s) % NC)) for r in range(NR) for c in range(NC)])
        for s in range(1, NC)
    ]
    remainder = pl.pallas_call(
        final_kernel,
        out_shape=jax.ShapeDtypeStruct((rhs.shape[0], size, width), jnp.float32),
        in_specs=[VMEM] * (1 + NC),
        out_specs=VMEM,
        compiler_params=pltpu.CompilerParams(vmem_limit_bytes=16 << 20),
        name="final",
    )(rhs[:, 0], mine_sum, *others)
    return solved[None, None], remainder[:, None]


def solution(mesh):
    in_specs = (
        P(None, "row", None, None),
        P(None, "row", None),
        P(None, "col", "row", None, None, None),
        P(None, "col", "row", None),
        P(None, "col", "row"),
    )
    out_specs = (P(None, "col", None, None), P(None, "row", None, None))
    small = mesh.shape["row"] == NR and mesh.shape["col"] == NC
    return jax.shard_map(
        on_device_8x4 if small else on_device_any,
        mesh=mesh,
        in_specs=in_specs,
        out_specs=out_specs,
        check_vma=False,
    )
```

```python
import functools

import jax
import jax.numpy as jnp
from jax import lax
from jax.experimental import pallas as pl
from jax.experimental.pallas import tpu as pltpu
from jax.sharding import PartitionSpec as P

VMEM = pl.BlockSpec(memory_space=pltpu.VMEM)
ANY = pl.BlockSpec(memory_space=pl.ANY)
SMEM = pl.BlockSpec(memory_space=pltpu.SMEM)
TAIL = 16


def broadcast(value, axis, root):
    mine = lax.axis_index(axis) == root
    return lax.psum(jnp.where(mine, value, jnp.zeros_like(value)), axis)


def on_device_any(rhs, diag_inv, blocks, block_rows, counts):
    nrow = lax.axis_size("row")
    ncol = lax.axis_size("col")
    my_row = lax.axis_index("row")
    my_col = lax.axis_index("col")
    kc = diag_inv.shape[0]
    rb_local = rhs.shape[0]
    nz_local = blocks.shape[3]
    local_rhs = rhs[:, 0]
    partial_value = jnp.zeros(local_rhs.shape, jnp.float32)
    solved_list = [jnp.zeros(local_rhs.shape[1:], jnp.float32)]
    slot_ids = jnp.arange(nz_local, dtype=jnp.int32)
    local_ids = jnp.arange(rb_local, dtype=jnp.int32)
    for k in range(kc):
        j = k // ncol
        owner_row = k % nrow
        local_pivot = k // nrow
        mine_row = my_row == owner_row
        mine_col = my_col == k % ncol
        pivot_part = jnp.where(mine_row, partial_value[local_pivot], jnp.float32(0.0))
        summed = lax.psum(pivot_part, "col")
        updated = (local_rhs[local_pivot] - summed).astype(jnp.bfloat16)
        pivot_bf = broadcast(updated, "row", owner_row)
        row_part = jnp.dot(diag_inv[k], pivot_bf, preferred_element_type=jnp.float32)
        sol = lax.all_gather(row_part, "row", axis=0, tiled=True)
        sol_bf = sol.astype(jnp.bfloat16)
        rows = block_rows[j, 0, 0]
        glob = rows * nrow + my_row
        valid = (slot_ids < counts[j, 0, 0]) & (glob > k) & mine_col
        weights = (valid[:, None] & (rows[:, None] == local_ids[None, :])).astype(jnp.float32)
        contrib = jnp.einsum(
            "sab,bn->san", blocks[j, 0, 0], sol_bf, preferred_element_type=jnp.float32
        )
        partial_value = partial_value + jnp.einsum(
            "sl,san->lan", weights, contrib, precision=lax.Precision.HIGHEST
        )
        solved_list[j] = jnp.where(mine_col, sol, solved_list[j])
    total = lax.psum(partial_value, "col")
    remainder = (local_rhs - total)[:, None]
    solved = jnp.stack(solved_list)[:, None]
    return (solved, remainder)


NR, NC = 8, 4
MAKER = ((1, 0), (2, 1), (3, 2), (5, 3))
SIDE = (3, 0)


def send(value, pairs):
    return lax.ppermute(value, ("row", "col"), [(a * NC + b, c * NC + d) for (a, b), (c, d) in pairs])


def dot(a, b):
    return jnp.dot(a, b, preferred_element_type=jnp.float32)


def low(a):
    return a.astype(jnp.bfloat16)


def at(device):
    return (lax.axis_index("row") == device[0]) & (lax.axis_index("col") == device[1])


def any_of(devices):
    flag = at(devices[0])
    for d in devices[1:]:
        flag = flag | at(d)
    return flag


def call(kernel, outs, ins, in_specs, out_specs, scratch=(), limit=16):
    return pl.pallas_call(
        kernel,
        out_shape=outs,
        in_specs=in_specs,
        out_specs=out_specs,
        scratch_shapes=list(scratch),
        compiler_params=pltpu.CompilerParams(vmem_limit_bytes=limit << 20),
        name=kernel.func.__name__ if isinstance(kernel, functools.partial) else kernel.__name__,
    )(*ins)


def cut_kernel(rhs_ref, diag_ref, p_ref, *refs):
    cuts, (rhs_v, rhs_sem, sem) = refs[:NR], refs[NR:]
    row, col = lax.axis_index("row"), lax.axis_index("col")
    part = diag_ref.shape[1]

    for r in range(NR):

        @pl.when(row == r)
        def _():
            pltpu.make_async_copy(diag_ref.at[col, :, pl.ds(0, (r + 1) * part)], cuts[r], sem).start()

    @pl.when(row == 0)
    def _():
        copy = pltpu.make_async_copy(rhs_ref.at[0], rhs_v, rhs_sem)
        copy.start()
        copy.wait()
        p_ref[...] = low(rhs_v[...])

    for r in range(NR):

        @pl.when(row == r)
        def _():
            pltpu.make_async_copy(diag_ref.at[col, :, pl.ds(0, (r + 1) * part)], cuts[r], sem).wait()


def whole_kernel(*refs):
    parts, own, out_ref, sem = refs[:NR], refs[NR : 2 * NR], refs[2 * NR], refs[2 * NR + 1]
    size = out_ref.shape[0]
    part = size // NR
    row = lax.axis_index("row")

    @pl.when(any_of(MAKER))
    def _():
        def copy(i, source):
            return pltpu.make_async_copy(
                source, out_ref.at[pl.ds(i * part, part), pl.ds(0, (i + 1) * part)], sem.at[i]
            )

        for i in range(NR):

            @pl.when(row == i)
            def _():
                copy(i, own[i]).start()

            @pl.when(row != i)
            def _():
                copy(i, parts[i]).start()

        for i in range(NR - 1):
            right = (i + 1) * part
            out_ref[pl.ds(i * part, part), pl.ds(right, size - right)] = jnp.zeros((part, size - right), out_ref.dtype)
        for i in range(NR):
            copy(i, parts[i]).wait()


def lower_dot(d_ref, p):
    half = d_ref.shape[0] // 2
    return low(dot(d_ref[:half, :half], p[:half])), low(dot(d_ref[half:], p))


def step0_kernel(p_ref, rhs_ref, d_ref, l_ref, msg_ref, q_ref, s_ref):
    size = l_ref.shape[0]
    half = size // 2
    active = at(MAKER[0])

    @pl.when(active)
    def _():
        q_ref[:half], q_ref[half:] = lower_dot(d_ref, p_ref[...])
        q = q_ref[...]
        s = dot(l_ref[...], q)
        s_ref[...] = low(s)
        msg_ref[:size] = low(rhs_ref[0] - s)
        msg_ref[size:] = q

    @pl.when(jnp.logical_not(active))
    def _():
        q_ref[...] = jnp.zeros_like(q_ref)


def step1_kernel(in_ref, side_ref, rhs_ref, d_ref, l_ref, l2_ref, q_prev, s_prev, msg_ref, q_ref, s_ref):
    size = l_ref.shape[0]
    half = size // 2
    active = at(MAKER[1])
    side = at(SIDE)

    @pl.when(active)
    def _():
        q_ref[:half], q_ref[half:] = lower_dot(d_ref, in_ref[:size])
        q = q_ref[...]
        s = dot(l_ref[...], q) + dot(l2_ref[...], in_ref[size:])
        s_ref[...] = low(s)
        msg_ref[:size] = low(rhs_ref[0] - s)
        msg_ref[size:] = q

    @pl.when(side)
    def _():
        q = side_ref[...]
        q_ref[...] = q
        s_ref[...] = low(dot(l_ref[...], q))

    @pl.when(jnp.logical_not(active | side))
    def _():
        q_ref[...] = q_prev[...]
        s_ref[...] = s_prev[...]


def step2_kernel(in_ref, sum_ref, rhs_ref, d_ref, l_ref, l2_ref, q_prev, s_prev, p_ref, q_ref, s_ref):
    size = l_ref.shape[0]
    half = size // 2
    active = at(MAKER[2])

    @pl.when(active)
    def _():
        q_ref[:half], q_ref[half:] = lower_dot(d_ref, in_ref[:size])
        s = dot(l_ref[...], q_ref[...]) + dot(l2_ref[...], in_ref[size:]) + sum_ref[...].astype(jnp.float32)
        s_ref[...] = low(s)
        p_ref[...] = low(rhs_ref[0] - s)

    @pl.when(jnp.logical_not(active))
    def _():
        q_ref[...] = q_prev[...]
        s_ref[...] = s_prev[...]


def step3_kernel(p_ref, d_ref, q_ref):
    half = d_ref.shape[0] // 2
    active = at(MAKER[3])

    @pl.when(active)
    def _():
        q_ref[:half], q_ref[half:] = lower_dot(d_ref, p_ref[...])

    @pl.when(jnp.logical_not(active))
    def _():
        q_ref[...] = jnp.zeros_like(q_ref)


def update_kernel(rows_ref, counts_ref, s_ref, l_ref, *refs):
    firsts, lasts, out_ref = refs[:2], refs[2:6], refs[6]
    size = l_ref.shape[0]
    row, col = lax.axis_index("row"), lax.axis_index("col")
    below = row >= NC

    def product(parts):
        q = parts[0][...]
        for p in parts[1:]:
            q = q + p[...]
        out_ref[pl.ds(0, size)] = low(dot(l_ref[...], q))

    @pl.when(below & (col < NC - 1))
    def _():
        product(firsts)

    @pl.when(below & (col == NC - 1))
    def _():
        product(lasts)

    @pl.when(jnp.logical_not(below))
    def _():
        out_ref[pl.ds(0, size)] = s_ref[...]

    listed = rows_ref[0, 0, 0, 0]
    there = below & (counts_ref[0, 0, 0] > 0)
    first = (there & (listed == 0)) | (jnp.logical_not(below) & (row >= 1) & (col == row - 1))
    second = there & (listed == 1)
    ids = lax.broadcasted_iota(jnp.int32, (TAIL, out_ref.shape[1]), 0)
    flag = ((ids == 0) & first) | ((ids == 1) & second)
    out_ref[pl.ds(size, TAIL)] = low(jnp.where(flag, 1.0, 0.0))


def final_kernel(rhs_ref, *refs):
    sums, parts, (solved_ref, out_ref) = refs[:NC], refs[NC:-2], refs[-2:]
    size = out_ref.shape[1]
    firsts, lasts = parts[:2], parts[2:]
    col = lax.axis_index("col")

    def keep_sum(values):
        q = values[0][...]
        for p in values[1:]:
            q = q + p[...]
        solved_ref[...] = q.astype(jnp.float32)

    @pl.when(col < NC - 1)
    def _():
        keep_sum(firsts)

    @pl.when(col == NC - 1)
    def _():
        keep_sum(lasts)

    for i in range(out_ref.shape[0]):
        acc = rhs_ref[i]
        for s in sums:
            keep = s[pl.ds(size, TAIL)].astype(jnp.float32)[i : i + 1] > 0.5
            acc = acc - jnp.where(keep, s[pl.ds(0, size)].astype(jnp.float32), 0.0)
        out_ref[i] = acc


def on_device_8x4(rhs, diag_inv, blocks, block_rows, counts):
    size, width = rhs.shape[2:]
    part = size // NR
    rhs = rhs[:, 0]
    block = blocks[0, 0, 0, 0]
    vec = jax.ShapeDtypeStruct((size, width), jnp.bfloat16)
    two = jax.ShapeDtypeStruct((2 * size, width), jnp.bfloat16)

    p0, *cuts = call(
        cut_kernel,
        [vec] + [jax.ShapeDtypeStruct((part, (r + 1) * part), jnp.bfloat16) for r in range(NR)],
        [rhs, diag_inv],
        [ANY, ANY],
        [VMEM] + [ANY] * NR,
        [pltpu.VMEM((size, width), jnp.float32), pltpu.SemaphoreType.DMA, pltpu.SemaphoreType.DMA],
    )
    parts = {}
    for r in (7, 6, 5, 4, 3, 2, 1, 0):
        parts[r] = send(cuts[r], [((r, c), MAKER[c]) for c in range(NC) if MAKER[c][0] != r])
    p0 = send(p0, [((0, 0), MAKER[0])])
    block2 = send(block, [((2, 0), MAKER[1]), ((3, 1), MAKER[2])])
    diag = call(
        whole_kernel,
        jax.ShapeDtypeStruct((size, size), jnp.bfloat16),
        [parts[r] for r in range(NR)] + cuts,
        [ANY] * (2 * NR),
        VMEM,
        [pltpu.SemaphoreType.DMA((NR,))],
    )

    msg, q, s = call(step0_kernel, [two, vec, vec], [p0, rhs, diag, block], [VMEM] * 4, [VMEM] * 3)
    side = send(q, [(MAKER[0], SIDE)])
    msg = send(msg, [(MAKER[0], MAKER[1])])
    msg, q, s = call(
        step1_kernel, [two, vec, vec], [msg, side, rhs, diag, block, block2, q, s], [VMEM] * 8, [VMEM] * 3
    )
    msg = send(msg, [(MAKER[1], MAKER[2])])
    side = send(s, [(SIDE, MAKER[2])])
    p3, q, s = call(
        step2_kernel, [vec, vec, vec], [msg, side, rhs, diag, block, block2, q, s], [VMEM] * 8, [VMEM] * 3
    )
    p3 = send(p3, [(MAKER[2], MAKER[3])])

    def tree(value, *columns):
        return send(value, [((a, k), (b, k)) for k, edges in enumerate(columns) for a, b in edges])

    got = tree(q, [(3, 5), (1, 0)], [(2, 4)], [(3, 5)])
    q = q + got
    got = tree(q, [(5, 4), (3, 2)], [(4, 5), (2, 3)], [(5, 4), (3, 2)])
    q = q + got
    q, p3 = lax.optimization_barrier((q, p3))
    got = tree(q, [(5, 7), (4, 6)], [(4, 6), (5, 7), (2, 0), (3, 1)], [(5, 7), (4, 6), (3, 1), (2, 0)])

    q3 = call(step3_kernel, vec, [p3, diag], [VMEM] * 2, VMEM)
    last = [send(q3, [(MAKER[3], (r, 3))]) for r in (4, 7, 6)]

    mine = call(
        update_kernel,
        jax.ShapeDtypeStruct((size + TAIL, width), jnp.bfloat16),
        [block_rows, counts, s, block, q, got, q3, *last],
        [SMEM] * 2 + [VMEM] * 8,
        VMEM,
    )

    def swap(value, step):
        return send(value, [((r, c), (r, c ^ step)) for r in range(NR) for c in range(NC)])

    near = swap(mine, 1)
    far = swap(mine, 2)
    farther = swap(far, 1)
    q3 = q3 + last[0] + last[1] + last[2]
    rest = send(q3, [((a, 3), (b, 3)) for a, b in ((5, 1), (7, 3), (4, 2), (6, 0))])
    solved, remainder = call(
        final_kernel,
        [jax.ShapeDtypeStruct((size, width), jnp.float32), jax.ShapeDtypeStruct(rhs.shape, jnp.float32)],
        [rhs, mine, near, far, farther, q, got, q3, rest],
        [VMEM] * 9,
        [VMEM] * 2,
    )
    return solved[None, None], remainder[:, None]


def solution(mesh):
    in_specs = (
        P(None, "row", None, None),
        P(None, "row", None),
        P(None, "col", "row", None, None, None),
        P(None, "col", "row", None),
        P(None, "col", "row"),
    )
    out_specs = (P(None, "col", None, None), P(None, "row", None, None))
    small = mesh.shape["row"] == NR and mesh.shape["col"] == NC
    return jax.shard_map(
        on_device_8x4 if small else on_device_any,
        mesh=mesh,
        in_specs=in_specs,
        out_specs=out_specs,
        check_vma=False,
    )
```

```python
import functools

import jax
import jax.numpy as jnp
from jax import lax
from jax.experimental import pallas as pl
from jax.experimental.pallas import tpu as pltpu
from jax.sharding import PartitionSpec as P

VMEM = pl.BlockSpec(memory_space=pltpu.VMEM)
ANY = pl.BlockSpec(memory_space=pl.ANY)
SMEM = pl.BlockSpec(memory_space=pltpu.SMEM)
TAIL = 16


def broadcast(value, axis, root):
    mine = lax.axis_index(axis) == root
    return lax.psum(jnp.where(mine, value, jnp.zeros_like(value)), axis)


def on_device_any(rhs, diag_inv, blocks, block_rows, counts):
    nrow = lax.axis_size("row")
    ncol = lax.axis_size("col")
    my_row = lax.axis_index("row")
    my_col = lax.axis_index("col")
    kc = diag_inv.shape[0]
    rb_local = rhs.shape[0]
    nz_local = blocks.shape[3]
    local_rhs = rhs[:, 0]
    partial_value = jnp.zeros(local_rhs.shape, jnp.float32)
    solved_list = [jnp.zeros(local_rhs.shape[1:], jnp.float32)]
    slot_ids = jnp.arange(nz_local, dtype=jnp.int32)
    local_ids = jnp.arange(rb_local, dtype=jnp.int32)
    for k in range(kc):
        j = k // ncol
        owner_row = k % nrow
        local_pivot = k // nrow
        mine_row = my_row == owner_row
        mine_col = my_col == k % ncol
        pivot_part = jnp.where(mine_row, partial_value[local_pivot], jnp.float32(0.0))
        summed = lax.psum(pivot_part, "col")
        updated = (local_rhs[local_pivot] - summed).astype(jnp.bfloat16)
        pivot_bf = broadcast(updated, "row", owner_row)
        row_part = jnp.dot(diag_inv[k], pivot_bf, preferred_element_type=jnp.float32)
        sol = lax.all_gather(row_part, "row", axis=0, tiled=True)
        sol_bf = sol.astype(jnp.bfloat16)
        rows = block_rows[j, 0, 0]
        glob = rows * nrow + my_row
        valid = (slot_ids < counts[j, 0, 0]) & (glob > k) & mine_col
        weights = (valid[:, None] & (rows[:, None] == local_ids[None, :])).astype(jnp.float32)
        contrib = jnp.einsum(
            "sab,bn->san", blocks[j, 0, 0], sol_bf, preferred_element_type=jnp.float32
        )
        partial_value = partial_value + jnp.einsum(
            "sl,san->lan", weights, contrib, precision=lax.Precision.HIGHEST
        )
        solved_list[j] = jnp.where(mine_col, sol, solved_list[j])
    total = lax.psum(partial_value, "col")
    remainder = (local_rhs - total)[:, None]
    solved = jnp.stack(solved_list)[:, None]
    return (solved, remainder)


NR, NC = 8, 4
MAKER = (None, (2, 1), (3, 2), (5, 3))
FIRST = (1, 0)
NEAR = (5, 2)


def send(value, pairs):
    return lax.ppermute(value, ("row", "col"), [(a * NC + b, c * NC + d) for (a, b), (c, d) in pairs])


def hops(a, b):
    d = a ^ b
    return 4 * (abs((a >> 3) - (b >> 3)) + ((d >> 2) & 1) + ((d >> 1) & 1)) + (d & 1) if d else 1000


def complete(pairs):
    to = {a * NC + b: c * NC + d for (a, b), (c, d) in pairs}
    free_from = [i for i in range(NR * NC) if i not in to]
    free_to = [i for i in range(NR * NC) if i not in to.values()]
    n = len(free_from)
    u, v, match = [0] * (n + 1), [0] * (n + 1), [0] * (n + 1)
    for i in range(1, n + 1):
        match[0], j0 = i, 0
        least, way, used = [10**9] * (n + 1), [0] * (n + 1), [False] * (n + 1)
        while True:
            used[j0] = True
            i0, delta, j1 = match[j0], 10**9, 0
            for j in range(1, n + 1):
                if not used[j]:
                    cur = hops(free_from[i0 - 1], free_to[j - 1]) - u[i0] - v[j]
                    if cur < least[j]:
                        least[j], way[j] = cur, j0
                    if least[j] < delta:
                        delta, j1 = least[j], j
            for j in range(n + 1):
                if used[j]:
                    u[match[j]] += delta
                    v[j] -= delta
                else:
                    least[j] -= delta
            j0 = j1
            if match[j0] == 0:
                break
        while j0:
            j1 = way[j0]
            match[j0] = match[j1]
            j0 = j1
    for j in range(1, n + 1):
        to[free_from[match[j] - 1]] = free_to[j - 1]
    return [(divmod(a, NC), divmod(b, NC)) for a, b in sorted(to.items())]


def dot(a, b):
    return jnp.dot(a, b, preferred_element_type=jnp.float32)


def low(a):
    return a.astype(jnp.bfloat16)


def at(device):
    return (lax.axis_index("row") == device[0]) & (lax.axis_index("col") == device[1])


def any_of(devices):
    flag = at(devices[0])
    for d in devices[1:]:
        flag = flag | at(d)
    return flag


def call(kernel, outs, ins, in_specs, out_specs, scratch=(), limit=16):
    return pl.pallas_call(
        kernel,
        out_shape=outs,
        in_specs=in_specs,
        out_specs=out_specs,
        scratch_shapes=list(scratch),
        compiler_params=pltpu.CompilerParams(vmem_limit_bytes=limit << 20),
        name=kernel.func.__name__ if isinstance(kernel, functools.partial) else kernel.__name__,
    )(*ins)


def cut0_kernel(diag_ref, hi_ref, lo_ref, sem):
    row = lax.axis_index("row")
    half = lo_ref.shape[1]

    @pl.when(row >= 4)
    def _():
        copy = pltpu.make_async_copy(diag_ref.at[0], hi_ref, sem)
        copy.start()
        copy.wait()

    @pl.when(row < 4)
    def _():
        copy = pltpu.make_async_copy(diag_ref.at[0, :, pl.ds(0, half)], lo_ref, sem)
        copy.start()
        copy.wait()


def first_kernel(rhs_ref, hi_ref, lo_ref, out_ref, rhs_v, sem):
    n = hi_ref.shape[0]

    @pl.when(lax.axis_index("row") == 0)
    def _():
        copy = pltpu.make_async_copy(rhs_ref.at[0], rhs_v, sem)
        copy.start()
        copy.wait()
        p = low(rhs_v[...])
        out_ref[:n] = low(dot(hi_ref[...], p))
        out_ref[n:] = low(dot(lo_ref[...], p[: lo_ref.shape[1]]))


def step0_kernel(g0, g1, g2, g3, rhs_ref, l_ref, p_ref, q_ref, s_ref):
    size = l_ref.shape[0]
    part = size // NR
    row = lax.axis_index("row")
    active = (row < 4) & (lax.axis_index("col") == 0)

    @pl.when(active)
    def _():
        for j, got in enumerate((g0, g1, g2, g3)):
            src = lax.rem(row + 7 - j, 4)
            hi = pl.multiple_of((4 + src) * part, part)
            lo = pl.multiple_of(lax.rem(src + 1, 4) * part, part)
            q_ref[pl.ds(hi, part)] = got[:part]
            q_ref[pl.ds(lo, part)] = got[part:]

    @pl.when(active & (row > 0))
    def _():
        s = dot(l_ref[...], q_ref[...])
        s_ref[...] = low(s)
        p_ref[...] = low(rhs_ref[0] - s)

    @pl.when(jnp.logical_not(active))
    def _():
        q_ref[...] = jnp.zeros_like(q_ref)


def cut_kernel(diag_ref, after_ref, *refs):
    cuts, sem = refs[:NR], refs[NR]
    row, col = lax.axis_index("row"), lax.axis_index("col")
    part = diag_ref.shape[1]
    for r in range(NR):

        @pl.when(row == r)
        def _():
            copy = pltpu.make_async_copy(diag_ref.at[col, :, pl.ds(0, (r + 1) * part)], cuts[r], sem)
            copy.start()
            copy.wait()


def join_kernel(rows, *refs):
    n = len(rows)
    parts, own = refs[:n], refs[n : 2 * n]
    out_ref, sem = refs[-2:]
    part = parts[0].shape[0]
    row = lax.axis_index("row")

    @pl.when(any_of(MAKER[1:]))
    def _():
        def copy(i, source):
            width = (rows[i] + 1) * part
            return pltpu.make_async_copy(source, out_ref.at[pl.ds(i * part, part), pl.ds(0, width)], sem.at[i])

        for i in range(n):

            @pl.when(row == rows[i])
            def _():
                copy(i, own[i]).start()

            @pl.when(row != rows[i])
            def _():
                copy(i, parts[i]).start()

        for i in range(n):
            right = (rows[i] + 1) * part
            rest = out_ref.shape[1] - right
            if rest:
                out_ref[pl.ds(i * part, part), pl.ds(right, rest)] = jnp.zeros((part, rest), out_ref.dtype)
        for i in range(n):
            copy(i, parts[i]).wait()


def lower_dot(q_ref, d_refs, p):
    top = 0
    for d in d_refs:
        bottom = top + d.shape[0]
        q_ref[top:bottom] = low(dot(d[:, :bottom], p[:bottom]))
        top = bottom


def step1_kernel(p_ref, sum_ref, rhs_ref, d0, d1, d2, l_ref, q_prev, s_prev, msg_ref, q_ref, s_ref):
    size = l_ref.shape[0]
    active = at(MAKER[1])

    @pl.when(active)
    def _():
        lower_dot(q_ref, (d0, d1, d2), p_ref[...])
        q = q_ref[...]
        s = dot(l_ref[...], q) + sum_ref[...].astype(jnp.float32)
        s_ref[...] = low(s)
        msg_ref[:size] = low(rhs_ref[0] - s)
        msg_ref[size:] = q

    @pl.when(jnp.logical_not(active))
    def _():
        q_ref[...] = q_prev[...]
        s_ref[...] = s_prev[...]


def step2_kernel(in_ref, sum_ref, rhs_ref, d0, d1, d2, l_ref, l2_ref, q_prev, s_prev, p_ref, q_ref, s_ref):
    size = l_ref.shape[0]
    active = at(MAKER[2])

    @pl.when(active)
    def _():
        lower_dot(q_ref, (d0, d1, d2), in_ref[:size])
        s = dot(l_ref[...], q_ref[...]) + dot(l2_ref[...], in_ref[size:]) + sum_ref[...].astype(jnp.float32)
        s_ref[...] = low(s)
        p_ref[...] = low(rhs_ref[0] - s)

    @pl.when(jnp.logical_not(active))
    def _():
        q_ref[...] = q_prev[...]
        s_ref[...] = s_prev[...]


def step3_kernel(p_ref, near_ref, d0, d1, d2, q_ref):
    active = at(MAKER[3])

    @pl.when(active)
    def _():
        lower_dot(q_ref, (d0, d1, d2), p_ref[...])

    @pl.when(jnp.logical_not(active))
    def _():
        q_ref[...] = near_ref[...]


def update_kernel(rows_ref, counts_ref, s_ref, l_ref, *refs):
    parts, q_ref, out_ref = refs[:-2], refs[-2], refs[-1]
    size = l_ref.shape[0]
    row, col = lax.axis_index("row"), lax.axis_index("col")
    below = row >= NC
    q = parts[0][...]
    for p in parts[1:]:
        q = q + p[...]
    q_ref[...] = q

    @pl.when(below)
    def _():
        out_ref[pl.ds(0, size)] = low(dot(l_ref[...], q_ref[...]))

    @pl.when(jnp.logical_not(below))
    def _():
        out_ref[pl.ds(0, size)] = s_ref[...]

    listed = rows_ref[0, 0, 0, 0]
    there = below & (counts_ref[0, 0, 0] > 0)
    first = (there & (listed == 0)) | (jnp.logical_not(below) & (row >= 1) & (col == row - 1))
    second = there & (listed == 1)
    ids = lax.broadcasted_iota(jnp.int32, (TAIL, out_ref.shape[1]), 0)
    flag = ((ids == 0) & first) | ((ids == 1) & second)
    out_ref[pl.ds(size, TAIL)] = low(jnp.where(flag, 1.0, 0.0))


def final_kernel(rhs_ref, q_ref, rest_ref, *refs):
    sums, (solved_ref, out_ref) = refs[:NC], refs[NC:]
    size = out_ref.shape[1]
    solved_ref[...] = (q_ref[...] + rest_ref[...]).astype(jnp.float32)
    for i in range(out_ref.shape[0]):
        acc = rhs_ref[i]
        for s in sums:
            keep = s[pl.ds(size, TAIL)].astype(jnp.float32)[i : i + 1] > 0.5
            acc = acc - jnp.where(keep, s[pl.ds(0, size)].astype(jnp.float32), 0.0)
        out_ref[i] = acc


def on_device_8x4(rhs, diag_inv, blocks, block_rows, counts):
    size, width = rhs.shape[2:]
    part = size // NR
    rhs = rhs[:, 0]
    block = blocks[0, 0, 0, 0]
    bf16 = jnp.bfloat16
    vec = jax.ShapeDtypeStruct((size, width), bf16)
    two = jax.ShapeDtypeStruct((2 * size, width), bf16)
    dma = pltpu.SemaphoreType.DMA

    hi, lo = call(
        cut0_kernel,
        [jax.ShapeDtypeStruct((part, size), bf16), jax.ShapeDtypeStruct((part, size // 2), bf16)],
        [diag_inv],
        [ANY],
        [ANY, ANY],
        [dma],
    )
    hi = send(hi, [((4 + c, c), (0, c)) for c in range(4)])
    lo = send(lo, [(((c + 1) % 4, c), (0, c)) for c in range(4)])
    q = call(
        first_kernel,
        jax.ShapeDtypeStruct((2 * part, width), bf16),
        [rhs, hi, lo],
        [ANY, VMEM, VMEM],
        VMEM,
        [pltpu.VMEM((size, width), jnp.float32), dma],
    )
    takers = ((1, 0), (2, 0), (3, 0), (0, 0))
    got = [send(q, [((0, c), takers[(c + j) % 4]) for c in range(4)]) for j in range(4)]
    p, q, s = call(step0_kernel, [vec] * 3, [*got, rhs, block], [VMEM] * 6, [VMEM] * 3)
    p_in = send(p, complete([(FIRST, MAKER[1])]))
    side = send(s, complete([((2, 0), MAKER[1]), ((3, 0), MAKER[2])]))

    cuts = call(
        cut_kernel,
        [jax.ShapeDtypeStruct((part, (r + 1) * part), bf16) for r in range(NR)],
        [diag_inv, p],
        [ANY, ANY],
        [ANY] * NR,
        [dma],
    )
    parts = {
        r: send(cuts[r], [((r, c), MAKER[c]) for c in range(1, NC) if MAKER[c][0] != r]) for r in (7, 6, 5, 4, 3, 2, 1, 0)
    }
    block2 = send(block, [((3, 1), MAKER[2])])
    diag = []
    for rows in ((6, 7), (4, 5), (0, 1, 2, 3)):
        take = [parts[r] for r in rows]
        if diag:
            take[0], diag[-1] = lax.optimization_barrier((take[0], diag[-1]))
        diag.append(
            call(
                functools.partial(join_kernel, rows),
                jax.ShapeDtypeStruct((len(rows) * part, (rows[-1] + 1) * part), bf16),
                take + [cuts[r] for r in rows],
                [ANY] * (2 * len(rows)),
                VMEM,
                [pltpu.SemaphoreType.DMA((len(rows),))],
            )
        )
    diag = diag[::-1]

    msg, q, s = call(
        step1_kernel, [two, vec, vec], [p_in, side, rhs, *diag, block, q, s], [VMEM] * 9, [VMEM] * 3
    )
    msg = send(msg, complete([(MAKER[1], MAKER[2])]))

    def tree(value, *columns):
        return send(value, [((a, k), (b, k)) for k, edges in enumerate(columns) for a, b in edges])

    q = q + tree(q, [(0, 4), (1, 5), (2, 6), (3, 7)], [(2, 4)])
    q = q + tree(q, [], [(4, 5), (2, 3)])
    msg, q = lax.optimization_barrier((msg, q))
    got = tree(q, [], [(4, 6), (5, 7), (2, 0), (3, 1)])

    p, q, s = call(
        step2_kernel,
        [vec, vec, vec],
        [msg, side, rhs, *diag, block, block2, q, s],
        [VMEM] * 10,
        [VMEM] * 3,
    )
    p = send(p, [(MAKER[2], MAKER[3])])
    near = send(q, [(MAKER[2], NEAR)])
    hub = call(step3_kernel, vec, [p, near, *diag], [VMEM] * 5, VMEM)
    last = [send(hub, [((5, c), (r, c)) for c in (2, 3)]) for r in (4, 7, 6)]
    q, mine = call(
        update_kernel,
        [vec, jax.ShapeDtypeStruct((size + TAIL, width), bf16)],
        [block_rows, counts, s, block, q, got, hub, *last],
        [SMEM] * 2 + [VMEM] * 8,
        [VMEM] * 2,
    )

    def swap(value, step):
        return send(value, [((r, c), (r, c ^ step)) for r in range(NR) for c in range(NC)])

    beside = swap(mine, 1)
    across = swap(mine, 2)
    corner = swap(across, 1)
    rest = send(
        q, [((a, 3), (b, 3)) for a, b in ((5, 1), (7, 3), (4, 2), (6, 0))] + [((a, 2), (a - 4, 2)) for a in (4, 5, 6)]
    )
    solved, remainder = call(
        final_kernel,
        [jax.ShapeDtypeStruct((size, width), jnp.float32), jax.ShapeDtypeStruct(rhs.shape, jnp.float32)],
        [rhs, q, rest, mine, beside, across, corner],
        [VMEM] * 7,
        [VMEM] * 2,
    )
    return solved[None, None], remainder[:, None]


def solution(mesh):
    in_specs = (
        P(None, "row", None, None),
        P(None, "row", None),
        P(None, "col", "row", None, None, None),
        P(None, "col", "row", None),
        P(None, "col", "row"),
    )
    out_specs = (P(None, "col", None, None), P(None, "row", None, None))
    small = mesh.shape["row"] == NR and mesh.shape["col"] == NC
    return jax.shard_map(
        on_device_8x4 if small else on_device_any,
        mesh=mesh,
        in_specs=in_specs,
        out_specs=out_specs,
        check_vma=False,
    )
```

```python
import functools

import jax
import jax.numpy as jnp
from jax import lax
from jax.experimental import pallas as pl
from jax.experimental.pallas import tpu as pltpu
from jax.sharding import PartitionSpec as P

VMEM = pl.BlockSpec(memory_space=pltpu.VMEM)
ANY = pl.BlockSpec(memory_space=pl.ANY)
HBM = pl.BlockSpec(memory_space=pltpu.HBM)
SMEM = pl.BlockSpec(memory_space=pltpu.SMEM)
TAIL = 16


def broadcast(value, axis, root):
    mine = lax.axis_index(axis) == root
    return lax.psum(jnp.where(mine, value, jnp.zeros_like(value)), axis)


def on_device_any(rhs, diag_inv, blocks, block_rows, counts):
    nrow = lax.axis_size("row")
    ncol = lax.axis_size("col")
    my_row = lax.axis_index("row")
    my_col = lax.axis_index("col")
    kc = diag_inv.shape[0]
    rb_local = rhs.shape[0]
    nz_local = blocks.shape[3]
    local_rhs = rhs[:, 0]
    partial_value = jnp.zeros(local_rhs.shape, jnp.float32)
    solved_list = [jnp.zeros(local_rhs.shape[1:], jnp.float32)]
    slot_ids = jnp.arange(nz_local, dtype=jnp.int32)
    local_ids = jnp.arange(rb_local, dtype=jnp.int32)
    for k in range(kc):
        j = k // ncol
        owner_row = k % nrow
        local_pivot = k // nrow
        mine_row = my_row == owner_row
        mine_col = my_col == k % ncol
        pivot_part = jnp.where(mine_row, partial_value[local_pivot], jnp.float32(0.0))
        summed = lax.psum(pivot_part, "col")
        updated = (local_rhs[local_pivot] - summed).astype(jnp.bfloat16)
        pivot_bf = broadcast(updated, "row", owner_row)
        row_part = jnp.dot(diag_inv[k], pivot_bf, preferred_element_type=jnp.float32)
        sol = lax.all_gather(row_part, "row", axis=0, tiled=True)
        sol_bf = sol.astype(jnp.bfloat16)
        rows = block_rows[j, 0, 0]
        glob = rows * nrow + my_row
        valid = (slot_ids < counts[j, 0, 0]) & (glob > k) & mine_col
        weights = (valid[:, None] & (rows[:, None] == local_ids[None, :])).astype(jnp.float32)
        contrib = jnp.einsum(
            "sab,bn->san", blocks[j, 0, 0], sol_bf, preferred_element_type=jnp.float32
        )
        partial_value = partial_value + jnp.einsum(
            "sl,san->lan", weights, contrib, precision=lax.Precision.HIGHEST
        )
        solved_list[j] = jnp.where(mine_col, sol, solved_list[j])
    total = lax.psum(partial_value, "col")
    remainder = (local_rhs - total)[:, None]
    solved = jnp.stack(solved_list)[:, None]
    return (solved, remainder)


NR, NC = 8, 4
MAKER = (None, (2, 1), (3, 2), (5, 3))
FIRST = (1, 0)
BESIDE = (3, 1)
NEAR = (5, 2)


def hops(a, b):
    d = a ^ b
    return 4 * (abs((a >> 3) - (b >> 3)) + ((d >> 2) & 1) + ((d >> 1) & 1)) + (d & 1) if d else 1000


def complete(pairs):
    to = {a * NC + b: c * NC + d for (a, b), (c, d) in pairs}
    free_from = [i for i in range(NR * NC) if i not in to]
    free_to = [i for i in range(NR * NC) if i not in to.values()]
    n = len(free_from)
    u, v, match = [0] * (n + 1), [0] * (n + 1), [0] * (n + 1)
    for i in range(1, n + 1):
        match[0], j0 = i, 0
        least, way, used = [10**9] * (n + 1), [0] * (n + 1), [False] * (n + 1)
        while True:
            used[j0] = True
            i0, delta, j1 = match[j0], 10**9, 0
            for j in range(1, n + 1):
                if not used[j]:
                    cur = hops(free_from[i0 - 1], free_to[j - 1]) - u[i0] - v[j]
                    if cur < least[j]:
                        least[j], way[j] = cur, j0
                    if least[j] < delta:
                        delta, j1 = least[j], j
            for j in range(n + 1):
                if used[j]:
                    u[match[j]] += delta
                    v[j] -= delta
                else:
                    least[j] -= delta
            j0 = j1
            if match[j0] == 0:
                break
        while j0:
            j1 = way[j0]
            match[j0] = match[j1]
            j0 = j1
    for j in range(1, n + 1):
        to[free_from[match[j] - 1]] = free_to[j - 1]
    return [(divmod(a, NC), divmod(b, NC)) for a, b in sorted(to.items())]


def send(value, pairs):
    moves = [(a * NC + b, c * NC + d) for (a, b), (c, d) in complete(pairs)]
    return lax.ppermute(value, ("row", "col"), moves)


def dot(a, b):
    return jnp.dot(a, b, preferred_element_type=jnp.float32)


def low(a):
    return a.astype(jnp.bfloat16)


def at(device):
    return (lax.axis_index("row") == device[0]) & (lax.axis_index("col") == device[1])


def any_of(devices):
    flag = at(devices[0])
    for d in devices[1:]:
        flag = flag | at(d)
    return flag


def call(kernel, outs, ins, in_specs, out_specs, scratch=(), limit=16):
    return pl.pallas_call(
        kernel,
        out_shape=outs,
        in_specs=in_specs,
        out_specs=out_specs,
        scratch_shapes=list(scratch),
        compiler_params=pltpu.CompilerParams(vmem_limit_bytes=limit << 20),
        name=kernel.func.__name__ if isinstance(kernel, functools.partial) else kernel.__name__,
    )(*ins)


def cut_kernel(diag_ref, *refs):
    cuts, sem = refs[:NR], refs[NR]
    row, col = lax.axis_index("row"), lax.axis_index("col")
    part = diag_ref.shape[1]
    for r in range(NR):

        @pl.when(row == r)
        def _():
            copy = pltpu.make_async_copy(diag_ref.at[col, :, pl.ds(0, (r + 1) * part)], cuts[r], sem)
            copy.start()
            copy.wait()


def first_kernel(rhs_ref, own_ref, *refs):
    parts, out_ref = refs[:NR], refs[NR]
    rhs_v, lo_v, hi_v, rhs_sem, lo_sem, hi_sem = refs[NR + 1 :]
    n = out_ref.shape[0] // 2
    col = lax.axis_index("col")

    @pl.when(lax.axis_index("row") == 0)
    def _():
        rhs_copy = pltpu.make_async_copy(rhs_ref.at[0], rhs_v, rhs_sem)
        rhs_copy.start()

        def piece(c):
            lo = own_ref if c == 0 else parts[c]
            wide = (4 + c + 1) * n
            return (
                pltpu.make_async_copy(lo, lo_v.at[:, pl.ds(0, (c + 1) * n)], lo_sem),
                pltpu.make_async_copy(parts[4 + c], hi_v.at[:, pl.ds(0, wide)], hi_sem),
            )

        for c in range(NC):

            @pl.when(col == c)
            def _():
                for copy in piece(c):
                    copy.start()

        rhs_copy.wait()
        p = low(rhs_v[...])
        for c in range(NC):

            @pl.when(col == c)
            def _():
                for copy in piece(c):
                    copy.wait()
                wide = (4 + c + 1) * n
                out_ref[:n] = low(dot(hi_v[:, :wide], p[:wide]))
                out_ref[n:] = low(dot(lo_v[:, : (c + 1) * n], p[: (c + 1) * n]))


def whole_kernel(*refs):
    parts, own, out_ref, sem = refs[:NR], refs[NR : 2 * NR], refs[2 * NR], refs[2 * NR + 1]
    size = out_ref.shape[0]
    part = size // NR
    row = lax.axis_index("row")

    @pl.when(any_of(MAKER[1:]))
    def _():
        def copy(i, source):
            return pltpu.make_async_copy(
                source, out_ref.at[pl.ds(i * part, part), pl.ds(0, (i + 1) * part)], sem.at[i]
            )

        for i in range(NR):

            @pl.when(row == i)
            def _():
                copy(i, own[i]).start()

            @pl.when(row != i)
            def _():
                copy(i, parts[i]).start()

        for i in range(NR - 1):
            right = (i + 1) * part
            out_ref[pl.ds(i * part, part), pl.ds(right, size - right)] = jnp.zeros((part, size - right), out_ref.dtype)
        for i in range(NR):
            copy(i, parts[i]).wait()


def lower_dot(q_ref, d_ref, p_ref):
    half = d_ref.shape[0] // 2
    q_ref[:half] = low(dot(d_ref[:half, :half], p_ref[:half]))
    q_ref[half:] = low(dot(d_ref[half:], p_ref[...]))


def step0_kernel(g0, g1, g2, g3, rhs_ref, l_ref, p_ref, q_ref, s_ref):
    part = l_ref.shape[0] // NR
    row = lax.axis_index("row")

    @pl.when((row >= 1) & (row < 4) & (lax.axis_index("col") == 0))
    def _():
        for j, got in enumerate((g0, g1, g2, g3)):
            src = lax.rem(row + 7 - j, 4)
            hi = pl.multiple_of((4 + src) * part, part)
            lo = pl.multiple_of(src * part, part)
            q_ref[pl.ds(hi, part)] = got[:part]
            q_ref[pl.ds(lo, part)] = got[part:]
        s = dot(l_ref[...], q_ref[...])
        s_ref[...] = low(s)
        p_ref[...] = low(rhs_ref[0] - s)


def step1_kernel(p_in, sum_ref, rhs_ref, d_ref, l_ref, q_prev, s_prev, p_ref, q_ref, s_ref):
    active = at(MAKER[1])

    @pl.when(active)
    def _():
        lower_dot(q_ref, d_ref, p_in)
        s = dot(l_ref[...], q_ref[...]) + sum_ref[...].astype(jnp.float32)
        s_ref[...] = low(s)
        p_ref[...] = low(rhs_ref[0] - s)

    @pl.when(jnp.logical_not(active))
    def _():
        q_ref[...] = q_prev[...]
        s_ref[...] = s_prev[...]


def step2_kernel(p_in, q_in, sum_ref, d_ref, l_ref, q_prev, s_prev, q_ref, s_ref):
    active, beside = at(MAKER[2]), at(BESIDE)

    @pl.when(active)
    def _():
        lower_dot(q_ref, d_ref, p_in)
        s_ref[...] = low(dot(l_ref[...], q_ref[...]))

    @pl.when(beside)
    def _():
        q_ref[...] = q_in[...]
        s_ref[...] = low(dot(l_ref[...], q_in[...]) + sum_ref[...].astype(jnp.float32))

    @pl.when(jnp.logical_not(active | beside))
    def _():
        q_ref[...] = q_prev[...]
        s_ref[...] = s_prev[...]


def step3_kernel(sum_ref, rhs_ref, s_prev, p_ref, s_ref):
    active = at(MAKER[2])

    @pl.when(active)
    def _():
        s = s_prev[...].astype(jnp.float32) + sum_ref[...].astype(jnp.float32)
        s_ref[...] = low(s)
        p_ref[...] = low(rhs_ref[0] - s)

    @pl.when(jnp.logical_not(active))
    def _():
        s_ref[...] = s_prev[...]


def step4_kernel(p_in, near_ref, d_ref, q_ref):
    @pl.when(at(MAKER[3]))
    def _():
        lower_dot(q_ref, d_ref, p_in)

    @pl.when(at(NEAR))
    def _():
        q_ref[...] = near_ref[...]


def relay_kernel(q_ref, got_ref, out_ref):
    row = lax.axis_index("row")
    taken = (row == 4) | (row == 5) | at((0, 0))

    @pl.when(taken)
    def _():
        out_ref[...] = got_ref[...]

    @pl.when(jnp.logical_not(taken))
    def _():
        out_ref[...] = q_ref[...]


def update_kernel(rows_ref, counts_ref, s_ref, l_ref, q0, q1, hub, h4, h7, h6, q_ref, out_ref):
    size = l_ref.shape[0]
    row, col = lax.axis_index("row"), lax.axis_index("col")
    below = row >= NC
    right = col >= 2
    late = jnp.logical_not(right) & ((row >= 6) | ((row < 2) & (col == 1)))

    def take(flag, source):
        @pl.when(flag)
        def _():
            q_ref[...] = source[...]

    take(late, q1)
    take(jnp.logical_not(late) & jnp.logical_not(right & below), q0)
    for r, source in ((5, hub), (4, h4), (7, h7), (6, h6)):
        take(right & (row == r), source)

    @pl.when(below)
    def _():
        out_ref[pl.ds(0, size)] = low(dot(l_ref[...], q_ref[...]))

    @pl.when(jnp.logical_not(below))
    def _():
        out_ref[pl.ds(0, size)] = s_ref[...]

    listed = rows_ref[0, 0, 0, 0]
    there = below & (counts_ref[0, 0, 0] > 0)
    first = (there & (listed == 0)) | (jnp.logical_not(below) & (row >= 1) & (col == row - 1))
    second = there & (listed == 1)
    ids = lax.broadcasted_iota(jnp.int32, (TAIL, out_ref.shape[1]), 0)
    flag = ((ids == 0) & first) | ((ids == 1) & second)
    out_ref[pl.ds(size, TAIL)] = low(jnp.where(flag, 1.0, 0.0))


def final_kernel(rhs_ref, q_ref, rest_ref, *refs):
    sums, (solved_ref, out_ref) = refs[:NC], refs[NC:]
    size = out_ref.shape[1]
    row, col = lax.axis_index("row"), lax.axis_index("col")
    came = (row < NC) & (col >= 2) & jnp.logical_not(at(MAKER[2]))

    @pl.when(came)
    def _():
        solved_ref[...] = rest_ref[...].astype(jnp.float32)

    @pl.when(jnp.logical_not(came))
    def _():
        solved_ref[...] = q_ref[...].astype(jnp.float32)

    for i in range(out_ref.shape[0]):
        acc = rhs_ref[i]
        for s in sums:
            keep = s[pl.ds(size, TAIL)].astype(jnp.float32)[i : i + 1] > 0.5
            acc = acc - jnp.where(keep, s[pl.ds(0, size)].astype(jnp.float32), 0.0)
        out_ref[i] = acc


def on_device_8x4(rhs, diag_inv, blocks, block_rows, counts):
    size, width = rhs.shape[2:]
    part = size // NR
    rhs = rhs[:, 0]
    block = blocks[0, 0, 0, 0]
    bf16 = jnp.bfloat16
    vec = jax.ShapeDtypeStruct((size, width), bf16)
    dma = pltpu.SemaphoreType.DMA

    cuts = call(
        cut_kernel,
        [jax.ShapeDtypeStruct((part, (r + 1) * part), bf16) for r in range(NR)],
        [diag_inv],
        [HBM],
        [ANY] * NR,
        [dma],
    )
    parts = []
    for r in range(NR):
        pairs = [((r, 0), (0, r % 4))] if r else []
        pairs += [((r, c), MAKER[c]) for c in range(1, NC) if MAKER[c][0] != r]
        parts.append(send(cuts[r], pairs))
    q = call(
        first_kernel,
        jax.ShapeDtypeStruct((2 * part, width), bf16),
        [rhs, cuts[0], *parts],
        [HBM] + [ANY] * (1 + NR),
        VMEM,
        [
            pltpu.VMEM((size, width), jnp.float32),
            pltpu.VMEM((part, 4 * part), bf16),
            pltpu.VMEM((part, size), bf16),
            dma,
            dma,
            dma,
        ],
    )
    takers = (FIRST, (2, 0), (3, 0))
    got = [send(q, [((0, c), takers[(c + j) % 4]) for c in range(4) if (c + j) % 4 < 3]) for j in range(4)]
    diag = call(
        whole_kernel,
        jax.ShapeDtypeStruct((size, size), bf16),
        [*parts, *cuts],
        [ANY] * (2 * NR),
        VMEM,
        [pltpu.SemaphoreType.DMA((NR,))],
    )

    p, q, s = call(step0_kernel, [vec] * 3, [*got, rhs, block], [VMEM] * 6, [VMEM] * 3)
    p_in = send(p, [(FIRST, MAKER[1])])
    sums = send(s, [((2, 0), MAKER[1]), ((3, 0), BESIDE)])
    p, q, s = call(step1_kernel, [vec] * 3, [p_in, sums, rhs, diag, block, q, s], [VMEM] * 7, [VMEM] * 3)
    p_in = send(p, [(MAKER[1], MAKER[2])])
    q_in = send(q, [(MAKER[1], BESIDE)])
    q, s = call(step2_kernel, [vec] * 2, [p_in, q_in, sums, diag, block, q, s], [VMEM] * 7, [VMEM] * 2)
    sums = send(s, [(BESIDE, MAKER[2])])
    near = send(q, [(MAKER[2], NEAR)])
    p, s = call(step3_kernel, [vec] * 2, [sums, rhs, s], [VMEM] * 3, [VMEM] * 2)
    p_in = send(p, [(MAKER[2], MAKER[3])])

    got = send(
        q, [((2, 0), (4, 0)), ((3, 0), (5, 0)), ((1, 0), (0, 0)), ((2, 1), (4, 1)), ((3, 1), (5, 1))]
    )
    q = call(relay_kernel, vec, [q, got], [VMEM] * 2, VMEM)
    got = send(
        q,
        [((4, c), (6, c)) for c in (0, 1)] + [((5, c), (7, c)) for c in (0, 1)] + [((2, 1), (0, 1)), ((3, 1), (1, 1))],
    )

    hub = call(step4_kernel, vec, [p_in, near, diag], [VMEM] * 3, VMEM)
    last = [send(hub, [((5, c), (r, c)) for c in (2, 3)]) for r in (4, 7, 6)]
    q, mine = call(
        update_kernel,
        [vec, jax.ShapeDtypeStruct((size + TAIL, width), bf16)],
        [block_rows, counts, s, block, q, got, hub, *last],
        [SMEM] * 2 + [VMEM] * 8,
        [VMEM] * 2,
    )

    def swap(value, step):
        return send(value, [((r, c), (r, c ^ step)) for r in range(NR) for c in range(NC)])

    beside = swap(mine, 1)
    across = swap(mine, 2)
    corner = swap(across, 1)
    rest = send(
        q, [((a, 3), (b, 3)) for a, b in ((5, 1), (7, 3), (4, 2), (6, 0))] + [((a, 2), (a - 4, 2)) for a in (4, 5, 6)]
    )
    solved, remainder = call(
        final_kernel,
        [jax.ShapeDtypeStruct((size, width), jnp.float32), jax.ShapeDtypeStruct(rhs.shape, jnp.float32)],
        [rhs, q, rest, mine, beside, across, corner],
        [VMEM] * 7,
        [VMEM] * 2,
    )
    return solved[None, None], remainder[:, None]


def solution(mesh):
    in_specs = (
        P(None, "row", None, None),
        P(None, "row", None),
        P(None, "col", "row", None, None, None),
        P(None, "col", "row", None),
        P(None, "col", "row"),
    )
    out_specs = (P(None, "col", None, None), P(None, "row", None, None))
    small = mesh.shape["row"] == NR and mesh.shape["col"] == NC
    return jax.shard_map(
        on_device_8x4 if small else on_device_any,
        mesh=mesh,
        in_specs=in_specs,
        out_specs=out_specs,
        check_vma=False,
    )
```

```python
import functools

import jax
import jax.numpy as jnp
from jax import lax
from jax.experimental import pallas as pl
from jax.experimental.pallas import tpu as pltpu
from jax.sharding import PartitionSpec as P

VMEM = pl.BlockSpec(memory_space=pltpu.VMEM)
ANY = pl.BlockSpec(memory_space=pl.ANY)
HBM = pl.BlockSpec(memory_space=pltpu.HBM)
SMEM = pl.BlockSpec(memory_space=pltpu.SMEM)
TAIL = 16


def broadcast(value, axis, root):
    mine = lax.axis_index(axis) == root
    return lax.psum(jnp.where(mine, value, jnp.zeros_like(value)), axis)


def on_device_any(rhs, diag_inv, blocks, block_rows, counts):
    nrow = lax.axis_size("row")
    ncol = lax.axis_size("col")
    my_row = lax.axis_index("row")
    my_col = lax.axis_index("col")
    kc = diag_inv.shape[0]
    rb_local = rhs.shape[0]
    nz_local = blocks.shape[3]
    local_rhs = rhs[:, 0]
    partial_value = jnp.zeros(local_rhs.shape, jnp.float32)
    solved_list = [jnp.zeros(local_rhs.shape[1:], jnp.float32)]
    slot_ids = jnp.arange(nz_local, dtype=jnp.int32)
    local_ids = jnp.arange(rb_local, dtype=jnp.int32)
    for k in range(kc):
        j = k // ncol
        owner_row = k % nrow
        local_pivot = k // nrow
        mine_row = my_row == owner_row
        mine_col = my_col == k % ncol
        pivot_part = jnp.where(mine_row, partial_value[local_pivot], jnp.float32(0.0))
        summed = lax.psum(pivot_part, "col")
        updated = (local_rhs[local_pivot] - summed).astype(jnp.bfloat16)
        pivot_bf = broadcast(updated, "row", owner_row)
        row_part = jnp.dot(diag_inv[k], pivot_bf, preferred_element_type=jnp.float32)
        sol = lax.all_gather(row_part, "row", axis=0, tiled=True)
        sol_bf = sol.astype(jnp.bfloat16)
        rows = block_rows[j, 0, 0]
        glob = rows * nrow + my_row
        valid = (slot_ids < counts[j, 0, 0]) & (glob > k) & mine_col
        weights = (valid[:, None] & (rows[:, None] == local_ids[None, :])).astype(jnp.float32)
        contrib = jnp.einsum(
            "sab,bn->san", blocks[j, 0, 0], sol_bf, preferred_element_type=jnp.float32
        )
        partial_value = partial_value + jnp.einsum(
            "sl,san->lan", weights, contrib, precision=lax.Precision.HIGHEST
        )
        solved_list[j] = jnp.where(mine_col, sol, solved_list[j])
    total = lax.psum(partial_value, "col")
    remainder = (local_rhs - total)[:, None]
    solved = jnp.stack(solved_list)[:, None]
    return (solved, remainder)


NR, NC = 8, 4
MAKER = (None, (2, 1), (3, 2), (5, 3))
FIRST = (1, 0)
BESIDE = (3, 1)
PARTNER = (None, (2, 0), (3, 3), (5, 2))


def hops(a, b):
    d = a ^ b
    return 4 * (abs((a >> 3) - (b >> 3)) + ((d >> 2) & 1) + ((d >> 1) & 1)) + (d & 1) if d else 1000


def complete(pairs):
    to = {a * NC + b: c * NC + d for (a, b), (c, d) in pairs}
    free_from = [i for i in range(NR * NC) if i not in to]
    free_to = [i for i in range(NR * NC) if i not in to.values()]
    n = len(free_from)
    u, v, match = [0] * (n + 1), [0] * (n + 1), [0] * (n + 1)
    for i in range(1, n + 1):
        match[0], j0 = i, 0
        least, way, used = [10**9] * (n + 1), [0] * (n + 1), [False] * (n + 1)
        while True:
            used[j0] = True
            i0, delta, j1 = match[j0], 10**9, 0
            for j in range(1, n + 1):
                if not used[j]:
                    cur = hops(free_from[i0 - 1], free_to[j - 1]) - u[i0] - v[j]
                    if cur < least[j]:
                        least[j], way[j] = cur, j0
                    if least[j] < delta:
                        delta, j1 = least[j], j
            for j in range(n + 1):
                if used[j]:
                    u[match[j]] += delta
                    v[j] -= delta
                else:
                    least[j] -= delta
            j0 = j1
            if match[j0] == 0:
                break
        while j0:
            j1 = way[j0]
            match[j0] = match[j1]
            j0 = j1
    for j in range(1, n + 1):
        to[free_from[match[j] - 1]] = free_to[j - 1]
    return [(divmod(a, NC), divmod(b, NC)) for a, b in sorted(to.items())]


def send(value, pairs):
    return lax.ppermute(value, ("row", "col"), [(a * NC + b, c * NC + d) for (a, b), (c, d) in complete(pairs)])


def send_only(value, pairs):
    return lax.ppermute(value, ("row", "col"), [(a * NC + b, c * NC + d) for (a, b), (c, d) in pairs])


def dot(a, b):
    return jnp.dot(a, b, preferred_element_type=jnp.float32)


def low(a):
    return a.astype(jnp.bfloat16)


def at(device):
    return (lax.axis_index("row") == device[0]) & (lax.axis_index("col") == device[1])


def any_of(devices):
    flag = at(devices[0])
    for d in devices[1:]:
        flag = flag | at(d)
    return flag


def call(kernel, outs, ins, in_specs, out_specs, scratch=(), limit=16):
    return pl.pallas_call(
        kernel,
        out_shape=outs,
        in_specs=in_specs,
        out_specs=out_specs,
        scratch_shapes=list(scratch),
        compiler_params=pltpu.CompilerParams(vmem_limit_bytes=limit << 20),
        name=kernel.func.__name__ if isinstance(kernel, functools.partial) else kernel.__name__,
    )(*ins)


def pair_width(m, part):
    return 2 * (m + 1) * part


def cut_kernel(diag_ref, *refs):
    cuts, sem = refs[:-1], refs[-1]
    row, col = lax.axis_index("row"), lax.axis_index("col")
    part = diag_ref.shape[1]
    k = jnp.where(lax.rem(row, 2) == 1, col, col + 1 - 2 * lax.rem(col, 2))
    for m in range(NR // 2):

        @pl.when(row // 2 == m)
        def _():
            copy = pltpu.make_async_copy(diag_ref.at[k, :, pl.ds(0, pair_width(m, part))], cuts[m], sem)
            copy.start()
            copy.wait()


def first_kernel(rhs_ref, diag_ref, *refs):
    parts, out_ref = refs[: NR // 2], refs[NR // 2]
    rhs_v, lo_v, hi_v, rhs_sem, lo_sem, hi_sem = refs[NR // 2 + 1 :]
    n = out_ref.shape[0] // 2
    col = lax.axis_index("col")

    @pl.when(lax.axis_index("row") == 0)
    def _():
        rhs_copy = pltpu.make_async_copy(rhs_ref.at[0], rhs_v, rhs_sem)
        rhs_copy.start()

        def piece(c):
            lo_wide, hi_wide = pair_width(c // 2, n), pair_width(2 + c // 2, n)
            lo = parts[c // 2] if c else diag_ref.at[0, :, pl.ds(0, lo_wide)]
            return (
                pltpu.make_async_copy(lo, lo_v.at[:, pl.ds(0, lo_wide)], lo_sem),
                pltpu.make_async_copy(parts[2 + c // 2], hi_v.at[:, pl.ds(0, hi_wide)], hi_sem),
            )

        for c in range(NC):

            @pl.when(col == c)
            def _():
                for copy in piece(c):
                    copy.start()

        rhs_copy.wait()
        p = low(rhs_v[...])
        for c in range(NC):

            @pl.when(col == c)
            def _():
                for copy in piece(c):
                    copy.wait()
                lo_wide, hi_wide = pair_width(c // 2, n), pair_width(2 + c // 2, n)
                out_ref[:n] = low(dot(hi_v[:, :hi_wide], p[:hi_wide]))
                out_ref[n:] = low(dot(lo_v[:, :lo_wide], p[:lo_wide]))


def pack_kernel(*refs):
    parts, out_ref, sem = refs[:-2], refs[-2], refs[-1]

    @pl.when(any_of(PARTNER[1:]))
    def _():
        copies, left = [], 0
        for m, source in enumerate(parts):
            wide = source.shape[1]
            copies.append(pltpu.make_async_copy(source, out_ref.at[:, pl.ds(left, wide)], sem.at[m]))
            left += wide
        for copy in copies:
            copy.start()
        for copy in copies:
            copy.wait()


def whole_kernel(diag_ref, even_ref, *refs):
    odd, out_ref, sem = refs[:-2], refs[-2], refs[-1]
    size = out_ref.shape[0]
    part = size // NR
    row, col = lax.axis_index("row"), lax.axis_index("col")

    @pl.when(any_of(MAKER[1:]))
    def _():
        def copy(i, source):
            wide = pair_width(i // 2, part)
            return pltpu.make_async_copy(source, out_ref.at[pl.ds(i * part, part), pl.ds(0, wide)], sem.at[i])

        left = 0
        for i in range(NR):
            wide = pair_width(i // 2, part)
            if i % 2:
                source = odd[i // 2]
            else:
                source = even_ref.at[:, pl.ds(left, wide)]
                left += wide

            @pl.when(row == i)
            def _():
                copy(i, diag_ref.at[col, :, pl.ds(0, wide)]).start()

            @pl.when(row != i)
            def _():
                copy(i, source).start()

        for m in range(NR // 2 - 1):
            right = pair_width(m, part)
            out_ref[pl.ds(2 * m * part, 2 * part), pl.ds(right, size - right)] = jnp.zeros(
                (2 * part, size - right), out_ref.dtype
            )
        for i in range(NR):
            copy(i, odd[i // 2]).wait()


def lower_dot(q_ref, d_ref, p_ref):
    half = d_ref.shape[0] // 2
    q_ref[:half] = low(dot(d_ref[:half, :half], p_ref[:half]))
    q_ref[half:] = low(dot(d_ref[half:], p_ref[...]))


def step0_kernel(g0, g1, g2, g3, rhs_ref, l_ref, p_ref, q_ref, s_ref):
    part = l_ref.shape[0] // NR
    row = lax.axis_index("row")

    @pl.when((row >= 1) & (row < 4) & (lax.axis_index("col") == 0))
    def _():
        for j, got in enumerate((g0, g1, g2, g3)):
            src = lax.rem(row + 7 - j, 4)
            hi = pl.multiple_of((4 + src) * part, part)
            lo = pl.multiple_of(src * part, part)
            q_ref[pl.ds(hi, part)] = got[:part]
            q_ref[pl.ds(lo, part)] = got[part:]
        s = dot(l_ref[...], q_ref[...])
        s_ref[...] = low(s)
        p_ref[...] = low(rhs_ref[0] - s)


def step1_kernel(p_in, sum_ref, rhs_ref, d_ref, l_ref, q_prev, s_prev, p_ref, q_ref, s_ref):
    active = at(MAKER[1])

    @pl.when(active)
    def _():
        lower_dot(q_ref, d_ref, p_in)
        s = dot(l_ref[...], q_ref[...]) + sum_ref[...].astype(jnp.float32)
        s_ref[...] = low(s)
        p_ref[...] = low(rhs_ref[0] - s)

    @pl.when(jnp.logical_not(active))
    def _():
        q_ref[...] = q_prev[...]
        s_ref[...] = s_prev[...]


def step2_kernel(p_in, q_in, sum_ref, rhs_ref, d_ref, l_ref, q_prev, s_prev, a_ref, q_ref, s_ref):
    active, beside = at(MAKER[2]), at(BESIDE)

    @pl.when(active)
    def _():
        lower_dot(q_ref, d_ref, p_in)
        s_ref[...] = low(dot(l_ref[...], q_ref[...]))

    @pl.when(beside)
    def _():
        q_ref[...] = q_in[...]
        s = dot(l_ref[...], q_in[...]) + sum_ref[...].astype(jnp.float32)
        s_ref[...] = low(s)
        a_ref[...] = low(rhs_ref[0] - s)

    @pl.when(jnp.logical_not(active | beside))
    def _():
        q_ref[...] = q_prev[...]
        s_ref[...] = s_prev[...]


def step3_kernel(a_ref, sum_ref, d_ref, q_ref, p_v):
    @pl.when(at(MAKER[3]))
    def _():
        p_v[...] = low(a_ref[...].astype(jnp.float32) - sum_ref[...].astype(jnp.float32))
        lower_dot(q_ref, d_ref, p_v)


def relay_kernel(q_ref, got_ref, out_ref):
    row = lax.axis_index("row")
    taken = (row == 4) | (row == 5) | at((0, 0)) | at((2, 2))

    @pl.when(taken)
    def _():
        out_ref[...] = got_ref[...]

    @pl.when(jnp.logical_not(taken))
    def _():
        out_ref[...] = q_ref[...]


def update_kernel(rows_ref, counts_ref, s_ref, l_ref, q0, r2, r3, r4, hub, h4, h7, h6, h3, h1, q_ref, out_ref):
    size = l_ref.shape[0]
    row, col = lax.axis_index("row"), lax.axis_index("col")
    below = row >= NC

    def take(flag, source):
        @pl.when(flag)
        def _():
            q_ref[...] = source[...]

    from_r2 = ((col < 2) & ((row >= 6) | ((row < 2) & (col == 1)))) | at((4, 2)) | at((5, 2))
    from_r3 = (col == 2) & (row >= 6)
    from_r4 = (col == 2) & (row < 2)
    take(from_r2, r2)
    take(from_r3, r3)
    take(from_r4, r4)
    take((col < 3) & jnp.logical_not(from_r2 | from_r3 | from_r4), q0)
    for r, source in ((5, hub), (4, h4), (7, h7), (6, h6), (3, h3), (1, h1)):
        take((col == 3) & (row == r), source)

    @pl.when(below)
    def _():
        out_ref[pl.ds(0, size)] = low(dot(l_ref[...], q_ref[...]))

    @pl.when(jnp.logical_not(below))
    def _():
        out_ref[pl.ds(0, size)] = s_ref[...]

    listed = rows_ref[0, 0, 0, 0]
    there = below & (counts_ref[0, 0, 0] > 0)
    done = at(FIRST) | at(MAKER[1]) | at(BESIDE) | at(MAKER[2])
    first = (there & (listed == 0)) | done
    second = there & (listed == 1)
    ids = lax.broadcasted_iota(jnp.int32, (TAIL, out_ref.shape[1]), 0)
    flag = ((ids == 0) & first) | ((ids == 1) & second)
    out_ref[pl.ds(size, TAIL)] = low(jnp.where(flag, 1.0, 0.0))


def final_kernel(rhs_ref, q_ref, rest_ref, *refs):
    sums, (solved_ref, out_ref) = refs[:NC], refs[NC:]
    size = out_ref.shape[1]
    came = at((2, 3)) | at((0, 3))

    @pl.when(came)
    def _():
        solved_ref[...] = rest_ref[...].astype(jnp.float32)

    @pl.when(jnp.logical_not(came))
    def _():
        solved_ref[...] = q_ref[...].astype(jnp.float32)

    for i in range(out_ref.shape[0]):
        acc = rhs_ref[i]
        for s in sums:
            keep = s[pl.ds(size, TAIL)].astype(jnp.float32)[i : i + 1] > 0.5
            acc = acc - jnp.where(keep, s[pl.ds(0, size)].astype(jnp.float32), 0.0)
        out_ref[i] = acc


def on_device_8x4(rhs, diag_inv, blocks, block_rows, counts):
    size, width = rhs.shape[2:]
    part = size // NR
    rhs = rhs[:, 0]
    block = blocks[0, 0, 0, 0]
    bf16 = jnp.bfloat16
    vec = jax.ShapeDtypeStruct((size, width), bf16)
    dma = pltpu.SemaphoreType.DMA

    wides = [pair_width(m, part) for m in range(NR // 2)]
    cuts = call(
        cut_kernel, [jax.ShapeDtypeStruct((part, w), bf16) for w in wides], [diag_inv], [HBM], [ANY] * len(wides), [dma]
    )
    parts = []
    for m, cut in enumerate(cuts):
        even, odd = 2 * m, 2 * m + 1
        pairs = [((odd, 0), (0, odd % 4))] + ([((even, 1), (0, even % 4))] if even else [])
        for k in range(1, NC):
            maker, partner = MAKER[k], PARTNER[k]
            if maker[0] != odd:
                pairs.append(((odd, maker[1]), maker))
            if partner[0] != even:
                pairs.append(((even, partner[1]), partner))
        parts.append(send(cut, pairs))
    q = call(
        first_kernel,
        jax.ShapeDtypeStruct((2 * part, width), bf16),
        [rhs, diag_inv, *parts],
        [HBM, HBM] + [ANY] * len(wides),
        VMEM,
        [
            pltpu.VMEM((size, width), jnp.float32),
            pltpu.VMEM((part, size // 2), bf16),
            pltpu.VMEM((part, size), bf16),
            dma,
            dma,
            dma,
        ],
    )
    takers = (FIRST, (2, 0), (3, 0))
    got = [send(q, [((0, c), takers[(c + j) % 4]) for c in range(4) if (c + j) % 4 < 3]) for j in range(4)]
    even = call(
        pack_kernel,
        jax.ShapeDtypeStruct((part, sum(wides)), bf16),
        parts,
        [ANY] * len(wides),
        VMEM,
        [pltpu.SemaphoreType.DMA((len(wides),))],
    )
    even = send(even, [(PARTNER[k], MAKER[k]) for k in range(1, NC)])
    diag = call(
        whole_kernel,
        jax.ShapeDtypeStruct((size, size), bf16),
        [diag_inv, even, *parts],
        [HBM] + [ANY] * (1 + len(wides)),
        VMEM,
        [pltpu.SemaphoreType.DMA((NR,))],
    )

    p, q, s = call(step0_kernel, [vec] * 3, [*got, rhs, block], [VMEM] * 6, [VMEM] * 3)
    p_in = send(p, [(FIRST, MAKER[1])])
    sums = send(s, [((2, 0), MAKER[1]), ((3, 0), BESIDE)])
    p, q, s = call(step1_kernel, [vec] * 3, [p_in, sums, rhs, diag, block, q, s], [VMEM] * 7, [VMEM] * 3)
    p_in = send(p, [(MAKER[1], MAKER[2])])
    q_in = send(q, [(MAKER[1], BESIDE)])
    a, q, s = call(step2_kernel, [vec] * 3, [p_in, q_in, sums, rhs, diag, block, q, s], [VMEM] * 8, [VMEM] * 3)
    sums = send(s, [(MAKER[2], MAKER[3])])
    a = send(a, [(BESIDE, MAKER[3])])
    hub = call(step3_kernel, vec, [a, sums, diag], [VMEM] * 3, VMEM, [pltpu.VMEM((size, width), bf16)])

    h4, h7, h6 = [send(hub, [(MAKER[3], (r, 3))]) for r in (4, 7, 6)]
    h3, h1 = [send(hub, [(MAKER[3], (r, 3))]) for r in (3, 1)]

    def tree(value, *columns):
        return send_only(value, [((a, k), (b, k)) for k, edges in enumerate(columns) for a, b in edges])

    r1 = tree(q, [(2, 4), (3, 5), (1, 0)], [(2, 4), (3, 5)], [(3, 2)])
    q = call(relay_kernel, vec, [q, r1], [VMEM] * 2, VMEM)
    r2 = tree(q, [(4, 6), (5, 7)], [(4, 6), (5, 7), (2, 0), (3, 1)], [(2, 4), (3, 5)])
    r3 = tree(q, [], [], [(2, 6), (3, 7)])
    r4 = tree(q, [], [], [(2, 0), (3, 1)])

    q, mine = call(
        update_kernel,
        [vec, jax.ShapeDtypeStruct((size + TAIL, width), bf16)],
        [block_rows, counts, s, block, q, r2, r3, r4, hub, h4, h7, h6, h3, h1],
        [SMEM] * 2 + [VMEM] * 12,
        [VMEM] * 2,
    )

    def swap(value, step):
        return send(value, [((r, c), (r, c ^ step)) for r in range(NR) for c in range(NC)])

    rest = send_only(q, [((3, 3), (2, 3)), ((1, 3), (0, 3))])
    across = swap(mine, 2)
    mine_after, across = lax.optimization_barrier((mine, across))
    beside = swap(mine_after, 1)
    corner = swap(across, 1)
    solved, remainder = call(
        final_kernel,
        [jax.ShapeDtypeStruct((size, width), jnp.float32), jax.ShapeDtypeStruct(rhs.shape, jnp.float32)],
        [rhs, q, rest, mine, beside, across, corner],
        [VMEM] * 7,
        [VMEM] * 2,
    )
    return solved[None, None], remainder[:, None]


def solution(mesh):
    in_specs = (
        P(None, "row", None, None),
        P(None, "row", None),
        P(None, "col", "row", None, None, None),
        P(None, "col", "row", None),
        P(None, "col", "row"),
    )
    out_specs = (P(None, "col", None, None), P(None, "row", None, None))
    small = mesh.shape["row"] == NR and mesh.shape["col"] == NC
    return jax.shard_map(
        on_device_8x4 if small else on_device_any,
        mesh=mesh,
        in_specs=in_specs,
        out_specs=out_specs,
        check_vma=False,
    )
```

```python
import functools

import jax
import jax.numpy as jnp
from jax import lax
from jax.experimental import pallas as pl
from jax.experimental.pallas import tpu as pltpu
from jax.sharding import PartitionSpec as P

VMEM = pl.BlockSpec(memory_space=pltpu.VMEM)
ANY = pl.BlockSpec(memory_space=pl.ANY)
HBM = pl.BlockSpec(memory_space=pltpu.HBM)
SMEM = pl.BlockSpec(memory_space=pltpu.SMEM)
TAIL = 16


def broadcast(value, axis, root):
    mine = lax.axis_index(axis) == root
    return lax.psum(jnp.where(mine, value, jnp.zeros_like(value)), axis)


def on_device_any(rhs, diag_inv, blocks, block_rows, counts):
    nrow = lax.axis_size("row")
    ncol = lax.axis_size("col")
    my_row = lax.axis_index("row")
    my_col = lax.axis_index("col")
    kc = diag_inv.shape[0]
    rb_local = rhs.shape[0]
    nz_local = blocks.shape[3]
    local_rhs = rhs[:, 0]
    partial_value = jnp.zeros(local_rhs.shape, jnp.float32)
    solved_list = [jnp.zeros(local_rhs.shape[1:], jnp.float32)]
    slot_ids = jnp.arange(nz_local, dtype=jnp.int32)
    local_ids = jnp.arange(rb_local, dtype=jnp.int32)
    for k in range(kc):
        j = k // ncol
        owner_row = k % nrow
        local_pivot = k // nrow
        mine_row = my_row == owner_row
        mine_col = my_col == k % ncol
        pivot_part = jnp.where(mine_row, partial_value[local_pivot], jnp.float32(0.0))
        summed = lax.psum(pivot_part, "col")
        updated = (local_rhs[local_pivot] - summed).astype(jnp.bfloat16)
        pivot_bf = broadcast(updated, "row", owner_row)
        row_part = jnp.dot(diag_inv[k], pivot_bf, preferred_element_type=jnp.float32)
        sol = lax.all_gather(row_part, "row", axis=0, tiled=True)
        sol_bf = sol.astype(jnp.bfloat16)
        rows = block_rows[j, 0, 0]
        glob = rows * nrow + my_row
        valid = (slot_ids < counts[j, 0, 0]) & (glob > k) & mine_col
        weights = (valid[:, None] & (rows[:, None] == local_ids[None, :])).astype(jnp.float32)
        contrib = jnp.einsum(
            "sab,bn->san", blocks[j, 0, 0], sol_bf, preferred_element_type=jnp.float32
        )
        partial_value = partial_value + jnp.einsum(
            "sl,san->lan", weights, contrib, precision=lax.Precision.HIGHEST
        )
        solved_list[j] = jnp.where(mine_col, sol, solved_list[j])
    total = lax.psum(partial_value, "col")
    remainder = (local_rhs - total)[:, None]
    solved = jnp.stack(solved_list)[:, None]
    return (solved, remainder)


NR, NC = 8, 4
MAKER = (None, (2, 1), (3, 2), (5, 3))
FIRST = (1, 0)
BESIDE = (3, 1)
PARTNER = (None, (3, 1), (3, 3), (5, 2))
PIECES = ((4, 0), (2, 1), (6, 5), (7, 3))
REST = ((2, 3), (0, 3), (0, 2), (1, 2))


def hops(a, b):
    d = a ^ b
    return 4 * (abs((a >> 3) - (b >> 3)) + ((d >> 2) & 1) + ((d >> 1) & 1)) + (d & 1) if d else 1000


def complete(pairs):
    to = {a * NC + b: c * NC + d for (a, b), (c, d) in pairs}
    free_from = [i for i in range(NR * NC) if i not in to]
    free_to = [i for i in range(NR * NC) if i not in to.values()]
    n = len(free_from)
    u, v, match = [0] * (n + 1), [0] * (n + 1), [0] * (n + 1)
    for i in range(1, n + 1):
        match[0], j0 = i, 0
        least, way, used = [10**9] * (n + 1), [0] * (n + 1), [False] * (n + 1)
        while True:
            used[j0] = True
            i0, delta, j1 = match[j0], 10**9, 0
            for j in range(1, n + 1):
                if not used[j]:
                    cur = hops(free_from[i0 - 1], free_to[j - 1]) - u[i0] - v[j]
                    if cur < least[j]:
                        least[j], way[j] = cur, j0
                    if least[j] < delta:
                        delta, j1 = least[j], j
            for j in range(n + 1):
                if used[j]:
                    u[match[j]] += delta
                    v[j] -= delta
                else:
                    least[j] -= delta
            j0 = j1
            if match[j0] == 0:
                break
        while j0:
            j1 = way[j0]
            match[j0] = match[j1]
            j0 = j1
    for j in range(1, n + 1):
        to[free_from[match[j] - 1]] = free_to[j - 1]
    return [(divmod(a, NC), divmod(b, NC)) for a, b in sorted(to.items())]


def send(value, pairs):
    return lax.ppermute(value, ("row", "col"), [(a * NC + b, c * NC + d) for (a, b), (c, d) in complete(pairs)])


def send_only(value, pairs):
    return lax.ppermute(value, ("row", "col"), [(a * NC + b, c * NC + d) for (a, b), (c, d) in pairs])


def dot(a, b):
    return jnp.dot(a, b, preferred_element_type=jnp.float32)


def low(a):
    return a.astype(jnp.bfloat16)


def at(device):
    return (lax.axis_index("row") == device[0]) & (lax.axis_index("col") == device[1])


def any_of(devices):
    flag = at(devices[0])
    for d in devices[1:]:
        flag = flag | at(d)
    return flag


def call(kernel, outs, ins, in_specs, out_specs, scratch=(), limit=16):
    return pl.pallas_call(
        kernel,
        out_shape=outs,
        in_specs=in_specs,
        out_specs=out_specs,
        scratch_shapes=list(scratch),
        compiler_params=pltpu.CompilerParams(vmem_limit_bytes=limit << 20),
        name=kernel.func.__name__ if isinstance(kernel, functools.partial) else kernel.__name__,
    )(*ins)


def pair_width(m, part):
    return 2 * (m + 1) * part


def cut_kernel(diag_ref, *refs):
    cuts, sem = refs[:-1], refs[-1]
    row, col = lax.axis_index("row"), lax.axis_index("col")
    part = diag_ref.shape[1]
    k = jnp.where(lax.rem(row, 2) == 1, col, col + 1 - 2 * lax.rem(col, 2))
    for m in range(NR // 2):

        @pl.when(row // 2 == m)
        def _():
            copy = pltpu.make_async_copy(diag_ref.at[k, :, pl.ds(0, pair_width(m, part))], cuts[m], sem)
            copy.start()
            copy.wait()


def first_kernel(rhs_ref, diag_ref, *refs):
    parts, out_ref = refs[: NR // 2], refs[NR // 2]
    rhs_v, d_v, rhs_sem, d_sem = refs[NR // 2 + 1 :]
    n = out_ref.shape[0] // 2
    col = lax.axis_index("col")

    @pl.when(lax.axis_index("row") == 0)
    def _():
        rhs_copy = pltpu.make_async_copy(rhs_ref.at[0], rhs_v, rhs_sem)
        rhs_copy.start()

        def pieces(c):
            copies = []
            for i, r in enumerate(PIECES[c]):
                wide = pair_width(r // 2, n)
                source = parts[r // 2] if r else diag_ref.at[0, :, pl.ds(0, wide)]
                copies.append(pltpu.make_async_copy(source, d_v.at[i, :, pl.ds(0, wide)], d_sem.at[i]))
            return copies

        for c in range(NC):

            @pl.when(col == c)
            def _():
                for copy in pieces(c):
                    copy.start()

        rhs_copy.wait()
        p = low(rhs_v[...])
        for c in range(NC):

            @pl.when(col == c)
            def _():
                for i, copy in enumerate(pieces(c)):
                    copy.wait()
                    wide = pair_width(PIECES[c][i] // 2, n)
                    out_ref[i * n : (i + 1) * n] = low(dot(d_v[i, :, :wide], p[:wide]))


def pack_kernel(*refs):
    parts, out_ref, sem = refs[:-2], refs[-2], refs[-1]

    @pl.when(any_of(PARTNER[1:]))
    def _():
        copies, left = [], 0
        for m, source in enumerate(parts):
            wide = source.shape[1]
            copies.append(pltpu.make_async_copy(source, out_ref.at[:, pl.ds(left, wide)], sem.at[m]))
            left += wide
        for copy in copies:
            copy.start()
        for copy in copies:
            copy.wait()


def whole_kernel(diag_ref, even_ref, *refs):
    odd, out_ref, sem = refs[:-2], refs[-2], refs[-1]
    size = out_ref.shape[0]
    part = size // NR
    row, col = lax.axis_index("row"), lax.axis_index("col")

    @pl.when(any_of(MAKER[1:]))
    def _():
        def copy(i, source):
            wide = pair_width(i // 2, part)
            return pltpu.make_async_copy(source, out_ref.at[pl.ds(i * part, part), pl.ds(0, wide)], sem.at[i])

        left = 0
        for i in range(NR):
            wide = pair_width(i // 2, part)
            if i % 2:
                source = odd[i // 2]
            else:
                source = even_ref.at[:, pl.ds(left, wide)]
                left += wide

            @pl.when(row == i)
            def _():
                copy(i, diag_ref.at[col, :, pl.ds(0, wide)]).start()

            @pl.when(row != i)
            def _():
                copy(i, source).start()

        for m in range(NR // 2 - 1):
            right = pair_width(m, part)
            out_ref[pl.ds(2 * m * part, 2 * part), pl.ds(right, size - right)] = jnp.zeros(
                (2 * part, size - right), out_ref.dtype
            )
        for i in range(NR):
            copy(i, odd[i // 2]).wait()


def lower_dot(q_ref, d_ref, p_ref):
    half = d_ref.shape[0] // 2
    q_ref[:half] = low(dot(d_ref[:half, :half], p_ref[:half]))
    q_ref[half:] = low(dot(d_ref[half:], p_ref[...]))


def step0_kernel(g0, g1, g2, g3, rhs_ref, l_ref, p_ref, q_ref, s_ref):
    part = l_ref.shape[0] // NR
    row = lax.axis_index("row")

    def lookup(c, i):
        r = jnp.int32(PIECES[0][i])
        for n in range(1, NC):
            r = jnp.where(c == n, PIECES[n][i], r)
        return pl.multiple_of(r * part, part)

    @pl.when((row >= 1) & (row < 4) & (lax.axis_index("col") == 0))
    def _():
        for j, got in enumerate((g0, g1, g2, g3)):
            src = lax.rem(row + 7 - j, 4)
            q_ref[pl.ds(lookup(src, 0), part)] = got[:part]
            q_ref[pl.ds(lookup(src, 1), part)] = got[part:]
        s = dot(l_ref[...], q_ref[...])
        s_ref[...] = low(s)
        p_ref[...] = low(rhs_ref[0] - s)


def step1_kernel(p_in, sum_ref, rhs_ref, d_ref, l_ref, q_prev, s_prev, p_ref, q_ref, s_ref):
    active = at(MAKER[1])

    @pl.when(active)
    def _():
        lower_dot(q_ref, d_ref, p_in)
        s = dot(l_ref[...], q_ref[...]) + sum_ref[...].astype(jnp.float32)
        s_ref[...] = low(s)
        p_ref[...] = low(rhs_ref[0] - s)

    @pl.when(jnp.logical_not(active))
    def _():
        q_ref[...] = q_prev[...]
        s_ref[...] = s_prev[...]


def step2_kernel(p_in, q_in, sum_ref, rhs_ref, d_ref, l_ref, q_prev, s_prev, a_ref, q_ref, s_ref):
    active, beside = at(MAKER[2]), at(BESIDE)

    @pl.when(active)
    def _():
        lower_dot(q_ref, d_ref, p_in)
        s_ref[...] = low(dot(l_ref[...], q_ref[...]))

    @pl.when(beside)
    def _():
        q_ref[...] = q_in[...]
        s = dot(l_ref[...], q_in[...]) + sum_ref[...].astype(jnp.float32)
        s_ref[...] = low(s)
        a_ref[...] = low(rhs_ref[0] - s)

    @pl.when(jnp.logical_not(active | beside))
    def _():
        q_ref[...] = q_prev[...]
        s_ref[...] = s_prev[...]


def step3_kernel(took, a_ref, sum_ref, d_ref, q_prev, came_ref, q_ref, p_v):
    active, taken = at(MAKER[3]), any_of(took)

    @pl.when(active)
    def _():
        p_v[...] = low(a_ref[...].astype(jnp.float32) - sum_ref[...].astype(jnp.float32))
        lower_dot(q_ref, d_ref, p_v)

    @pl.when(taken)
    def _():
        q_ref[...] = came_ref[...]

    @pl.when(jnp.logical_not(active | taken))
    def _():
        q_ref[...] = q_prev[...]


def update_kernel(takers, rows_ref, counts_ref, s_ref, l_ref, q_prev, *refs):
    got, q_ref, out_ref = refs[:-2], refs[-2], refs[-1]
    size = l_ref.shape[0]
    row, col = lax.axis_index("row"), lax.axis_index("col")
    below = row >= NC

    def take(flag, source):
        @pl.when(flag)
        def _():
            q_ref[...] = source[...]

    kept = jnp.logical_not(any_of([d for devices in takers for d in devices]))
    take(kept, q_prev)
    for devices, source in zip(takers, got):
        take(any_of(devices), source)

    @pl.when(below)
    def _():
        out_ref[pl.ds(0, size)] = low(dot(l_ref[...], q_ref[...]))

    @pl.when(jnp.logical_not(below))
    def _():
        out_ref[pl.ds(0, size)] = s_ref[...]

    listed = rows_ref[0, 0, 0, 0]
    there = below & (counts_ref[0, 0, 0] > 0)
    done = at(FIRST) | at(MAKER[1]) | at(BESIDE) | at(MAKER[2])
    first = (there & (listed == 0)) | done
    second = there & (listed == 1)
    ids = lax.broadcasted_iota(jnp.int32, (TAIL, out_ref.shape[1]), 0)
    flag = ((ids == 0) & first) | ((ids == 1) & second)
    out_ref[pl.ds(size, TAIL)] = low(jnp.where(flag, 1.0, 0.0))


def final_kernel(rhs_ref, q_ref, rest_ref, *refs):
    sums, (solved_ref, out_ref) = refs[:NC], refs[NC:]
    size = out_ref.shape[1]
    came = any_of(REST)

    @pl.when(came)
    def _():
        solved_ref[...] = rest_ref[...].astype(jnp.float32)

    @pl.when(jnp.logical_not(came))
    def _():
        solved_ref[...] = q_ref[...].astype(jnp.float32)

    for i in range(out_ref.shape[0]):
        acc = rhs_ref[i]
        for s in sums:
            keep = s[pl.ds(size, TAIL)].astype(jnp.float32)[i : i + 1] > 0.5
            acc = acc - jnp.where(keep, s[pl.ds(0, size)].astype(jnp.float32), 0.0)
        out_ref[i] = acc


def on_device_8x4(rhs, diag_inv, blocks, block_rows, counts):
    size, width = rhs.shape[2:]
    part = size // NR
    rhs = rhs[:, 0]
    block = blocks[0, 0, 0, 0]
    bf16 = jnp.bfloat16
    vec = jax.ShapeDtypeStruct((size, width), bf16)
    dma = pltpu.SemaphoreType.DMA

    wides = [pair_width(m, part) for m in range(NR // 2)]
    cuts = call(
        cut_kernel, [jax.ShapeDtypeStruct((part, w), bf16) for w in wides], [diag_inv], [HBM], [ANY] * len(wides), [dma]
    )
    parts = []
    for m, cut in enumerate(cuts):
        even, odd = 2 * m, 2 * m + 1
        at_piece = {r: (0, c) for c, rows in enumerate(PIECES) for r in rows}
        pairs = [((odd, 0), at_piece[odd])] + ([((even, 1), at_piece[even])] if even else [])
        for k in range(1, NC):
            maker = MAKER[k]
            if maker[0] != odd:
                pairs.append(((odd, k), maker))
            if maker[0] != even:
                pairs.append(((even, k ^ 1), PARTNER[k]))
        parts.append(send(cut, pairs))
    q = call(
        first_kernel,
        jax.ShapeDtypeStruct((2 * part, width), bf16),
        [rhs, diag_inv, *parts],
        [HBM, HBM] + [ANY] * len(wides),
        VMEM,
        [
            pltpu.VMEM((size, width), jnp.float32),
            pltpu.VMEM((2, part, size), bf16),
            dma,
            pltpu.SemaphoreType.DMA((2,)),
        ],
    )
    takers = (FIRST, (2, 0), (3, 0))
    got = [send(q, [((0, c), takers[(c + j) % 4]) for c in range(4) if (c + j) % 4 < 3]) for j in range(4)]
    even = call(
        pack_kernel,
        jax.ShapeDtypeStruct((part, sum(wides)), bf16),
        parts,
        [ANY] * len(wides),
        VMEM,
        [pltpu.SemaphoreType.DMA((len(wides),))],
    )
    even = send(even, [(PARTNER[k], MAKER[k]) for k in range(1, NC)])
    diag = call(
        whole_kernel,
        jax.ShapeDtypeStruct((size, size), bf16),
        [diag_inv, even, *parts],
        [HBM] + [ANY] * (1 + len(wides)),
        VMEM,
        [pltpu.SemaphoreType.DMA((NR,))],
    )

    p, q, s = call(step0_kernel, [vec] * 3, [*got, rhs, block], [VMEM] * 6, [VMEM] * 3)
    p_in = send(p, [(FIRST, MAKER[1])])
    sums = send(s, [((2, 0), MAKER[1]), ((3, 0), BESIDE)])
    p, q, s = call(step1_kernel, [vec] * 3, [p_in, sums, rhs, diag, block, q, s], [VMEM] * 7, [VMEM] * 3)
    p_in = send(p, [(MAKER[1], MAKER[2])])
    q_in = send(q, [(MAKER[1], BESIDE)])

    p_in, spread = lax.optimization_barrier((p_in, q))
    came = send(spread, [((2, 0), (4, 0)), ((3, 0), (5, 0)), ((1, 0), (0, 0)), ((2, 1), (4, 1))])
    took = [(4, 0), (5, 0), (0, 0), (4, 1)]

    a, q, s = call(step2_kernel, [vec] * 3, [p_in, q_in, sums, rhs, diag, block, q, s], [VMEM] * 8, [VMEM] * 3)
    sums = send(s, [(MAKER[2], MAKER[3])])
    a = send(a, [(BESIDE, MAKER[3])])
    q = call(
        functools.partial(step3_kernel, took),
        vec,
        [a, sums, diag, q, came],
        [VMEM] * 5,
        VMEM,
        [pltpu.VMEM((size, width), bf16)],
    )

    makers = [(MAKER[3], (r, 3)) for r in (4, 7, 6, 3, 1)]
    second = [(MAKER[2], (r, 2)) for r in (4, 5, 6, 7, 2)]
    others = [
        [((4, 0), (6, 0)), ((5, 0), (7, 0)), ((4, 1), (6, 1)), ((3, 1), (5, 1)), ((2, 1), (0, 1))],
        [((4, 1), (7, 1)), ((3, 1), (1, 1))],
    ]
    sends = [[makers[i], second[i], *(others[i] if i < 2 else [])] for i in range(5)]
    got = [send(q, pairs) for pairs in sends]
    q, mine = call(
        functools.partial(update_kernel, [[b for _, b in pairs] for pairs in sends]),
        [vec, jax.ShapeDtypeStruct((size + TAIL, width), bf16)],
        [block_rows, counts, s, block, q, *got],
        [SMEM] * 2 + [VMEM] * (3 + len(got)),
        [VMEM] * 2,
    )

    def swap(value, step):
        return send(value, [((r, c), (r, c ^ step)) for r in range(NR) for c in range(NC)])

    rest = send_only(q, [(a, b) for a, b in zip(((3, 3), (1, 3), (2, 2), MAKER[2]), REST)])
    across = swap(mine, 2)
    mine_after, across = lax.optimization_barrier((mine, across))
    beside = swap(mine_after, 1)
    corner = swap(across, 1)
    solved, remainder = call(
        final_kernel,
        [jax.ShapeDtypeStruct((size, width), jnp.float32), jax.ShapeDtypeStruct(rhs.shape, jnp.float32)],
        [rhs, q, rest, mine, beside, across, corner],
        [VMEM] * 7,
        [VMEM] * 2,
    )
    return solved[None, None], remainder[:, None]


def solution(mesh):
    in_specs = (
        P(None, "row", None, None),
        P(None, "row", None),
        P(None, "col", "row", None, None, None),
        P(None, "col", "row", None),
        P(None, "col", "row"),
    )
    out_specs = (P(None, "col", None, None), P(None, "row", None, None))
    small = mesh.shape["row"] == NR and mesh.shape["col"] == NC
    return jax.shard_map(
        on_device_8x4 if small else on_device_any,
        mesh=mesh,
        in_specs=in_specs,
        out_specs=out_specs,
        check_vma=False,
    )
```

```python
import functools

import jax
import jax.numpy as jnp
from jax import lax
from jax.experimental import pallas as pl
from jax.experimental.pallas import tpu as pltpu
from jax.sharding import PartitionSpec as P

VMEM = pl.BlockSpec(memory_space=pltpu.VMEM)
ANY = pl.BlockSpec(memory_space=pl.ANY)
HBM = pl.BlockSpec(memory_space=pltpu.HBM)
SMEM = pl.BlockSpec(memory_space=pltpu.SMEM)
TAIL = 16


def broadcast(value, axis, root):
    mine = lax.axis_index(axis) == root
    return lax.psum(jnp.where(mine, value, jnp.zeros_like(value)), axis)


def on_device_any(rhs, diag_inv, blocks, block_rows, counts):
    nrow = lax.axis_size("row")
    ncol = lax.axis_size("col")
    my_row = lax.axis_index("row")
    my_col = lax.axis_index("col")
    kc = diag_inv.shape[0]
    rb_local = rhs.shape[0]
    nz_local = blocks.shape[3]
    local_rhs = rhs[:, 0]
    partial_value = jnp.zeros(local_rhs.shape, jnp.float32)
    solved_list = [jnp.zeros(local_rhs.shape[1:], jnp.float32)]
    slot_ids = jnp.arange(nz_local, dtype=jnp.int32)
    local_ids = jnp.arange(rb_local, dtype=jnp.int32)
    for k in range(kc):
        j = k // ncol
        owner_row = k % nrow
        local_pivot = k // nrow
        mine_row = my_row == owner_row
        mine_col = my_col == k % ncol
        pivot_part = jnp.where(mine_row, partial_value[local_pivot], jnp.float32(0.0))
        summed = lax.psum(pivot_part, "col")
        updated = (local_rhs[local_pivot] - summed).astype(jnp.bfloat16)
        pivot_bf = broadcast(updated, "row", owner_row)
        row_part = jnp.dot(diag_inv[k], pivot_bf, preferred_element_type=jnp.float32)
        sol = lax.all_gather(row_part, "row", axis=0, tiled=True)
        sol_bf = sol.astype(jnp.bfloat16)
        rows = block_rows[j, 0, 0]
        glob = rows * nrow + my_row
        valid = (slot_ids < counts[j, 0, 0]) & (glob > k) & mine_col
        weights = (valid[:, None] & (rows[:, None] == local_ids[None, :])).astype(jnp.float32)
        contrib = jnp.einsum(
            "sab,bn->san", blocks[j, 0, 0], sol_bf, preferred_element_type=jnp.float32
        )
        partial_value = partial_value + jnp.einsum(
            "sl,san->lan", weights, contrib, precision=lax.Precision.HIGHEST
        )
        solved_list[j] = jnp.where(mine_col, sol, solved_list[j])
    total = lax.psum(partial_value, "col")
    remainder = (local_rhs - total)[:, None]
    solved = jnp.stack(solved_list)[:, None]
    return (solved, remainder)


NR, NC = 8, 4
MAKER = (None, (2, 1), (3, 2), (5, 3))
FIRST = (1, 0)
BESIDE = (3, 1)
PARTNER = (None, (3, 1), (3, 3), (5, 2))
PIECES = ((4, 0), (2, 1), (6, 5), (7, 3))
REST = ((2, 3), (0, 3), (0, 2), (1, 2))


def hops(a, b):
    d = a ^ b
    if d < 2:
        return 1 if d else 10000
    return 100 + abs((a >> 3) - (b >> 3)) + ((d >> 2) & 1) + ((d >> 1) & 1)


def complete(pairs):
    to = {a * NC + b: c * NC + d for (a, b), (c, d) in pairs}
    free_from = [i for i in range(NR * NC) if i not in to]
    free_to = [i for i in range(NR * NC) if i not in to.values()]
    n = len(free_from)
    u, v, match = [0] * (n + 1), [0] * (n + 1), [0] * (n + 1)
    for i in range(1, n + 1):
        match[0], j0 = i, 0
        least, way, used = [10**9] * (n + 1), [0] * (n + 1), [False] * (n + 1)
        while True:
            used[j0] = True
            i0, delta, j1 = match[j0], 10**9, 0
            for j in range(1, n + 1):
                if not used[j]:
                    cur = hops(free_from[i0 - 1], free_to[j - 1]) - u[i0] - v[j]
                    if cur < least[j]:
                        least[j], way[j] = cur, j0
                    if least[j] < delta:
                        delta, j1 = least[j], j
            for j in range(n + 1):
                if used[j]:
                    u[match[j]] += delta
                    v[j] -= delta
                else:
                    least[j] -= delta
            j0 = j1
            if match[j0] == 0:
                break
        while j0:
            j1 = way[j0]
            match[j0] = match[j1]
            j0 = j1
    for j in range(1, n + 1):
        to[free_from[match[j] - 1]] = free_to[j - 1]
    return [(divmod(a, NC), divmod(b, NC)) for a, b in sorted(to.items())]


def send(value, pairs):
    return lax.ppermute(value, ("row", "col"), [(a * NC + b, c * NC + d) for (a, b), (c, d) in complete(pairs)])


def send_only(value, pairs):
    return lax.ppermute(value, ("row", "col"), [(a * NC + b, c * NC + d) for (a, b), (c, d) in pairs])


def dot(a, b):
    return jnp.dot(a, b, preferred_element_type=jnp.float32)


def low(a):
    return a.astype(jnp.bfloat16)


def at(device):
    return (lax.axis_index("row") == device[0]) & (lax.axis_index("col") == device[1])


def any_of(devices):
    flag = at(devices[0])
    for d in devices[1:]:
        flag = flag | at(d)
    return flag


def call(kernel, outs, ins, in_specs, out_specs, scratch=(), limit=16):
    return pl.pallas_call(
        kernel,
        out_shape=outs,
        in_specs=in_specs,
        out_specs=out_specs,
        scratch_shapes=list(scratch),
        compiler_params=pltpu.CompilerParams(vmem_limit_bytes=limit << 20),
        name=kernel.func.__name__ if isinstance(kernel, functools.partial) else kernel.__name__,
    )(*ins)


def pair_width(m, part):
    return 2 * (m + 1) * part


def cut_kernel(diag_ref, *refs):
    cuts, sem = refs[:-1], refs[-1]
    row, col = lax.axis_index("row"), lax.axis_index("col")
    part = diag_ref.shape[1]
    k = jnp.where(lax.rem(row, 2) == 1, col, col + 1 - 2 * lax.rem(col, 2))
    for m in range(NR // 2):

        @pl.when(row // 2 == m)
        def _():
            copy = pltpu.make_async_copy(diag_ref.at[k, :, pl.ds(0, pair_width(m, part))], cuts[m], sem)
            copy.start()
            copy.wait()


def first_kernel(rhs_ref, diag_ref, *refs):
    parts, out_ref = refs[: NR // 2], refs[NR // 2]
    rhs_v, d_v, rhs_sem, d_sem = refs[NR // 2 + 1 :]
    n = out_ref.shape[0] // 2
    col = lax.axis_index("col")

    @pl.when(lax.axis_index("row") == 0)
    def _():
        rhs_copy = pltpu.make_async_copy(rhs_ref.at[0], rhs_v, rhs_sem)
        rhs_copy.start()

        def pieces(c):
            copies = []
            for i, r in enumerate(PIECES[c]):
                wide = pair_width(r // 2, n)
                source = parts[r // 2] if r else diag_ref.at[0, :, pl.ds(0, wide)]
                copies.append(pltpu.make_async_copy(source, d_v.at[i, :, pl.ds(0, wide)], d_sem.at[i]))
            return copies

        for c in range(NC):

            @pl.when(col == c)
            def _():
                for copy in pieces(c):
                    copy.start()

        rhs_copy.wait()
        p = low(rhs_v[...])
        for c in range(NC):

            @pl.when(col == c)
            def _():
                for i, copy in enumerate(pieces(c)):
                    copy.wait()
                    wide = pair_width(PIECES[c][i] // 2, n)
                    out_ref[i * n : (i + 1) * n] = low(dot(d_v[i, :, :wide], p[:wide]))


def pack_kernel(*refs):
    parts, out_ref, sem = refs[:-2], refs[-2], refs[-1]

    @pl.when(any_of(PARTNER[1:]))
    def _():
        copies, left = [], 0
        for m, source in enumerate(parts):
            wide = source.shape[1]
            copies.append(pltpu.make_async_copy(source, out_ref.at[:, pl.ds(left, wide)], sem.at[m]))
            left += wide
        for copy in copies:
            copy.start()
        for copy in copies:
            copy.wait()


def whole_kernel(diag_ref, even_ref, *refs):
    odd, out_ref, sem = refs[:-2], refs[-2], refs[-1]
    size = out_ref.shape[0]
    part = size // NR
    row, col = lax.axis_index("row"), lax.axis_index("col")

    @pl.when(any_of(MAKER[1:]))
    def _():
        def copy(i, source):
            wide = pair_width(i // 2, part)
            return pltpu.make_async_copy(source, out_ref.at[pl.ds(i * part, part), pl.ds(0, wide)], sem.at[i])

        left = 0
        for i in range(NR):
            wide = pair_width(i // 2, part)
            if i % 2:
                source = odd[i // 2]
            else:
                source = even_ref.at[:, pl.ds(left, wide)]
                left += wide

            @pl.when(row == i)
            def _():
                copy(i, diag_ref.at[col, :, pl.ds(0, wide)]).start()

            @pl.when(row != i)
            def _():
                copy(i, source).start()

        for m in range(NR // 2 - 1):
            right = pair_width(m, part)
            out_ref[pl.ds(2 * m * part, 2 * part), pl.ds(right, size - right)] = jnp.zeros(
                (2 * part, size - right), out_ref.dtype
            )
        for i in range(NR):
            copy(i, odd[i // 2]).wait()


def lower_dot(q_ref, d_ref, p_ref):
    half = d_ref.shape[0] // 2
    q_ref[:half] = low(dot(d_ref[:half, :half], p_ref[:half]))
    q_ref[half:] = low(dot(d_ref[half:], p_ref[...]))


def step0_kernel(g0, g1, g2, g3, rhs_ref, l_ref, p_ref, q_ref, s_ref):
    part = l_ref.shape[0] // NR
    row = lax.axis_index("row")

    def lookup(c, i):
        r = jnp.int32(PIECES[0][i])
        for n in range(1, NC):
            r = jnp.where(c == n, PIECES[n][i], r)
        return pl.multiple_of(r * part, part)

    @pl.when((row >= 1) & (row < 4) & (lax.axis_index("col") == 0))
    def _():
        for j, got in enumerate((g0, g1, g2, g3)):
            src = lax.rem(row + 7 - j, 4)
            q_ref[pl.ds(lookup(src, 0), part)] = got[:part]
            q_ref[pl.ds(lookup(src, 1), part)] = got[part:]
        s = dot(l_ref[...], q_ref[...])
        s_ref[...] = low(s)
        p_ref[...] = low(rhs_ref[0] - s)


def step1_kernel(p_in, sum_ref, rhs_ref, d_ref, l_ref, q_prev, s_prev, p_ref, q_ref, s_ref):
    active = at(MAKER[1])

    @pl.when(active)
    def _():
        lower_dot(q_ref, d_ref, p_in)
        s = dot(l_ref[...], q_ref[...]) + sum_ref[...].astype(jnp.float32)
        s_ref[...] = low(s)
        p_ref[...] = low(rhs_ref[0] - s)

    @pl.when(jnp.logical_not(active))
    def _():
        q_ref[...] = q_prev[...]
        s_ref[...] = s_prev[...]


def step2_kernel(p_in, q_in, sum_ref, rhs_ref, d_ref, l_ref, q_prev, s_prev, a_ref, q_ref, s_ref):
    active, beside = at(MAKER[2]), at(BESIDE)

    @pl.when(active)
    def _():
        lower_dot(q_ref, d_ref, p_in)
        s_ref[...] = low(dot(l_ref[...], q_ref[...]))

    @pl.when(beside)
    def _():
        q_ref[...] = q_in[...]
        s = dot(l_ref[...], q_in[...]) + sum_ref[...].astype(jnp.float32)
        s_ref[...] = low(s)
        a_ref[...] = low(rhs_ref[0] - s)

    @pl.when(jnp.logical_not(active | beside))
    def _():
        q_ref[...] = q_prev[...]
        s_ref[...] = s_prev[...]


def step3_kernel(took, a_ref, sum_ref, d_ref, q_prev, came_ref, q_ref, p_v):
    active, taken = at(MAKER[3]), any_of(took)

    @pl.when(active)
    def _():
        p_v[...] = low(a_ref[...].astype(jnp.float32) - sum_ref[...].astype(jnp.float32))
        lower_dot(q_ref, d_ref, p_v)

    @pl.when(taken)
    def _():
        q_ref[...] = came_ref[...]

    @pl.when(jnp.logical_not(active | taken))
    def _():
        q_ref[...] = q_prev[...]


def update_kernel(takers, rows_ref, counts_ref, s_ref, l_ref, q_prev, *refs):
    got, q_ref, out_ref = refs[:-2], refs[-2], refs[-1]
    size = l_ref.shape[0]
    row, col = lax.axis_index("row"), lax.axis_index("col")
    below = row >= NC

    def take(flag, source):
        @pl.when(flag)
        def _():
            q_ref[...] = source[...]

    kept = jnp.logical_not(any_of([d for devices in takers for d in devices]))
    take(kept, q_prev)
    for devices, source in zip(takers, got):
        take(any_of(devices), source)

    @pl.when(below)
    def _():
        out_ref[pl.ds(0, size)] = low(dot(l_ref[...], q_ref[...]))

    @pl.when(jnp.logical_not(below))
    def _():
        out_ref[pl.ds(0, size)] = s_ref[...]

    listed = rows_ref[0, 0, 0, 0]
    there = below & (counts_ref[0, 0, 0] > 0)
    done = at(FIRST) | at(MAKER[1]) | at(BESIDE) | at(MAKER[2])
    first = (there & (listed == 0)) | done
    second = there & (listed == 1)
    ids = lax.broadcasted_iota(jnp.int32, (TAIL, out_ref.shape[1]), 0)
    flag = ((ids == 0) & first) | ((ids == 1) & second)
    out_ref[pl.ds(size, TAIL)] = low(jnp.where(flag, 1.0, 0.0))


def final_kernel(rhs_ref, q_ref, rest_ref, *refs):
    sums, (solved_ref, out_ref) = refs[:NC], refs[NC:]
    size = out_ref.shape[1]
    came = any_of(REST)

    @pl.when(came)
    def _():
        solved_ref[...] = rest_ref[...].astype(jnp.float32)

    @pl.when(jnp.logical_not(came))
    def _():
        solved_ref[...] = q_ref[...].astype(jnp.float32)

    for i in range(out_ref.shape[0]):
        acc = rhs_ref[i]
        for s in sums:
            keep = s[pl.ds(size, TAIL)].astype(jnp.float32)[i : i + 1] > 0.5
            acc = acc - jnp.where(keep, s[pl.ds(0, size)].astype(jnp.float32), 0.0)
        out_ref[i] = acc


def on_device_8x4(rhs, diag_inv, blocks, block_rows, counts):
    size, width = rhs.shape[2:]
    part = size // NR
    rhs = rhs[:, 0]
    block = blocks[0, 0, 0, 0]
    bf16 = jnp.bfloat16
    vec = jax.ShapeDtypeStruct((size, width), bf16)
    dma = pltpu.SemaphoreType.DMA

    wides = [pair_width(m, part) for m in range(NR // 2)]
    cuts = call(
        cut_kernel, [jax.ShapeDtypeStruct((part, w), bf16) for w in wides], [diag_inv], [HBM], [ANY] * len(wides), [dma]
    )
    parts = []
    for m, cut in enumerate(cuts):
        even, odd = 2 * m, 2 * m + 1
        at_piece = {r: (0, c) for c, rows in enumerate(PIECES) for r in rows}
        pairs = [((odd, 0), at_piece[odd])] + ([((even, 1), at_piece[even])] if even else [])
        for k in range(1, NC):
            maker = MAKER[k]
            if maker[0] != odd:
                pairs.append(((odd, k), maker))
            if maker[0] != even:
                pairs.append(((even, k ^ 1), PARTNER[k]))
        parts.append(send_only(cut, pairs))
    q = call(
        first_kernel,
        jax.ShapeDtypeStruct((2 * part, width), bf16),
        [rhs, diag_inv, *parts],
        [HBM, HBM] + [ANY] * len(wides),
        VMEM,
        [
            pltpu.VMEM((size, width), jnp.float32),
            pltpu.VMEM((2, part, size), bf16),
            dma,
            pltpu.SemaphoreType.DMA((2,)),
        ],
    )
    takers = (FIRST, (2, 0), (3, 0))
    got = [send(q, [((0, c), takers[(c + j) % 4]) for c in range(4) if (c + j) % 4 < 3]) for j in range(4)]
    even = call(
        pack_kernel,
        jax.ShapeDtypeStruct((part, sum(wides)), bf16),
        parts,
        [ANY] * len(wides),
        VMEM,
        [pltpu.SemaphoreType.DMA((len(wides),))],
    )
    even = send(even, [(PARTNER[k], MAKER[k]) for k in range(1, NC)])
    diag = call(
        whole_kernel,
        jax.ShapeDtypeStruct((size, size), bf16),
        [diag_inv, even, *parts],
        [HBM] + [ANY] * (1 + len(wides)),
        VMEM,
        [pltpu.SemaphoreType.DMA((NR,))],
    )

    p, q, s = call(step0_kernel, [vec] * 3, [*got, rhs, block], [VMEM] * 6, [VMEM] * 3)
    p_in = send(p, [(FIRST, MAKER[1])])
    sums = send(s, [((2, 0), MAKER[1]), ((3, 0), BESIDE)])
    p, q, s = call(step1_kernel, [vec] * 3, [p_in, sums, rhs, diag, block, q, s], [VMEM] * 7, [VMEM] * 3)
    p_in = send(p, [(MAKER[1], MAKER[2])])
    q_in = send(q, [(MAKER[1], BESIDE)])

    p_in, spread = lax.optimization_barrier((p_in, q))
    came = send(spread, [((2, 0), (4, 0)), ((3, 0), (5, 0)), ((1, 0), (0, 0)), ((2, 1), (4, 1))])
    took = [(4, 0), (5, 0), (0, 0), (4, 1)]

    a, q, s = call(step2_kernel, [vec] * 3, [p_in, q_in, sums, rhs, diag, block, q, s], [VMEM] * 8, [VMEM] * 3)
    sums = send(s, [(MAKER[2], MAKER[3])])
    a = send(a, [(BESIDE, MAKER[3])])

    q = call(
        functools.partial(step3_kernel, took),
        vec,
        [a, sums, diag, q, came],
        [VMEM] * 5,
        VMEM,
        [pltpu.VMEM((size, width), bf16)],
    )

    sends = [
        [(MAKER[3], (4, 3)), ((4, 0), (6, 0)), ((5, 0), (7, 0)), ((4, 1), (6, 1)), ((3, 1), (5, 1)), ((2, 1), (0, 1))],
        [(MAKER[3], (7, 3)), ((4, 1), (7, 1)), ((3, 1), (1, 1))],
        [(MAKER[3], (6, 3))],
        [(MAKER[3], (3, 3))],
        [(MAKER[3], (1, 3))],
    ]
    for pairs, r in zip(sends, (4, 5, 6, 7, 2)):
        pairs.append((MAKER[2], (r, 2)))
    got = [send_only(q, pairs) for pairs in sends]
    takers = [[b for _, b in pairs] for pairs in sends]
    q, mine = call(
        functools.partial(update_kernel, takers),
        [vec, jax.ShapeDtypeStruct((size + TAIL, width), bf16)],
        [block_rows, counts, s, block, q, *got],
        [SMEM] * 2 + [VMEM] * (3 + len(got)),
        [VMEM] * 2,
    )

    def swap(value, step):
        return send(value, [((r, c), (r, c ^ step)) for r in range(NR) for c in range(NC)])

    rest = send_only(q, list(zip(((3, 3), (1, 3), (2, 2), MAKER[2]), REST)))
    across = swap(mine, 2)
    mine_after, across = lax.optimization_barrier((mine, across))
    beside = swap(mine_after, 1)
    corner = swap(across, 1)
    solved, remainder = call(
        final_kernel,
        [jax.ShapeDtypeStruct((size, width), jnp.float32), jax.ShapeDtypeStruct(rhs.shape, jnp.float32)],
        [rhs, q, rest, mine, beside, across, corner],
        [VMEM] * 7,
        [VMEM] * 2,
    )
    return solved[None, None], remainder[:, None]


def solution(mesh):
    in_specs = (
        P(None, "row", None, None),
        P(None, "row", None),
        P(None, "col", "row", None, None, None),
        P(None, "col", "row", None),
        P(None, "col", "row"),
    )
    out_specs = (P(None, "col", None, None), P(None, "row", None, None))
    small = mesh.shape["row"] == NR and mesh.shape["col"] == NC
    return jax.shard_map(
        on_device_8x4 if small else on_device_any,
        mesh=mesh,
        in_specs=in_specs,
        out_specs=out_specs,
        check_vma=False,
    )
```

```python
import functools

import jax
import jax.numpy as jnp
from jax import lax
from jax.experimental import pallas as pl
from jax.experimental.pallas import tpu as pltpu
from jax.sharding import PartitionSpec as P

VMEM = pl.BlockSpec(memory_space=pltpu.VMEM)
ANY = pl.BlockSpec(memory_space=pl.ANY)
HBM = pl.BlockSpec(memory_space=pltpu.HBM)
SMEM = pl.BlockSpec(memory_space=pltpu.SMEM)
TAIL = 16


def broadcast(value, axis, root):
    mine = lax.axis_index(axis) == root
    return lax.psum(jnp.where(mine, value, jnp.zeros_like(value)), axis)


def on_device_any(rhs, diag_inv, blocks, block_rows, counts):
    nrow = lax.axis_size("row")
    ncol = lax.axis_size("col")
    my_row = lax.axis_index("row")
    my_col = lax.axis_index("col")
    kc = diag_inv.shape[0]
    rb_local = rhs.shape[0]
    nz_local = blocks.shape[3]
    local_rhs = rhs[:, 0]
    partial_value = jnp.zeros(local_rhs.shape, jnp.float32)
    solved_list = [jnp.zeros(local_rhs.shape[1:], jnp.float32)]
    slot_ids = jnp.arange(nz_local, dtype=jnp.int32)
    local_ids = jnp.arange(rb_local, dtype=jnp.int32)
    for k in range(kc):
        j = k // ncol
        owner_row = k % nrow
        local_pivot = k // nrow
        mine_row = my_row == owner_row
        mine_col = my_col == k % ncol
        pivot_part = jnp.where(mine_row, partial_value[local_pivot], jnp.float32(0.0))
        summed = lax.psum(pivot_part, "col")
        updated = (local_rhs[local_pivot] - summed).astype(jnp.bfloat16)
        pivot_bf = broadcast(updated, "row", owner_row)
        row_part = jnp.dot(diag_inv[k], pivot_bf, preferred_element_type=jnp.float32)
        sol = lax.all_gather(row_part, "row", axis=0, tiled=True)
        sol_bf = sol.astype(jnp.bfloat16)
        rows = block_rows[j, 0, 0]
        glob = rows * nrow + my_row
        valid = (slot_ids < counts[j, 0, 0]) & (glob > k) & mine_col
        weights = (valid[:, None] & (rows[:, None] == local_ids[None, :])).astype(jnp.float32)
        contrib = jnp.einsum(
            "sab,bn->san", blocks[j, 0, 0], sol_bf, preferred_element_type=jnp.float32
        )
        partial_value = partial_value + jnp.einsum(
            "sl,san->lan", weights, contrib, precision=lax.Precision.HIGHEST
        )
        solved_list[j] = jnp.where(mine_col, sol, solved_list[j])
    total = lax.psum(partial_value, "col")
    remainder = (local_rhs - total)[:, None]
    solved = jnp.stack(solved_list)[:, None]
    return (solved, remainder)


NR, NC = 8, 4
MAKER = (None, (2, 1), (3, 2), (5, 3))
FIRST = (1, 0)
BESIDE = (3, 1)
PARTNER = (None, (3, 1), (3, 3), (5, 2))
PIECES = ((4, 0), (6, 2), (5, 1), (7, 3))
SENDS = (
    (1, 0, 3, 2),
    (3, 1, 0, 2),
    (0, 1, 3, 2),
    (2, 1, 0, 3),
    (0, 1, 3, 2),
    (2, 3, 0, 1),
    (0, 3, 1, 2),
    (1, 2, 0, 3),
)
REST = ((2, 3), (3, 3), (0, 3), (1, 3), (0, 2), (1, 2))


def hops(a, b):
    d = a ^ b
    if d < 2:
        return 1 if d else 10000
    return 100 + abs((a >> 3) - (b >> 3)) + ((d >> 2) & 1) + ((d >> 1) & 1)


def complete(pairs):
    to = {a * NC + b: c * NC + d for (a, b), (c, d) in pairs}
    free_from = [i for i in range(NR * NC) if i not in to]
    free_to = [i for i in range(NR * NC) if i not in to.values()]
    n = len(free_from)
    u, v, match = [0] * (n + 1), [0] * (n + 1), [0] * (n + 1)
    for i in range(1, n + 1):
        match[0], j0 = i, 0
        least, way, used = [10**9] * (n + 1), [0] * (n + 1), [False] * (n + 1)
        while True:
            used[j0] = True
            i0, delta, j1 = match[j0], 10**9, 0
            for j in range(1, n + 1):
                if not used[j]:
                    cur = hops(free_from[i0 - 1], free_to[j - 1]) - u[i0] - v[j]
                    if cur < least[j]:
                        least[j], way[j] = cur, j0
                    if least[j] < delta:
                        delta, j1 = least[j], j
            for j in range(n + 1):
                if used[j]:
                    u[match[j]] += delta
                    v[j] -= delta
                else:
                    least[j] -= delta
            j0 = j1
            if match[j0] == 0:
                break
        while j0:
            j1 = way[j0]
            match[j0] = match[j1]
            j0 = j1
    for j in range(1, n + 1):
        to[free_from[match[j] - 1]] = free_to[j - 1]
    return [(divmod(a, NC), divmod(b, NC)) for a, b in sorted(to.items())]


def send(value, pairs):
    return lax.ppermute(value, ("row", "col"), [(a * NC + b, c * NC + d) for (a, b), (c, d) in complete(pairs)])


def send_only(value, pairs):
    return lax.ppermute(value, ("row", "col"), [(a * NC + b, c * NC + d) for (a, b), (c, d) in pairs])


def dot(a, b):
    return jnp.dot(a, b, preferred_element_type=jnp.float32)


def low(a):
    return a.astype(jnp.bfloat16)


def at(device):
    return (lax.axis_index("row") == device[0]) & (lax.axis_index("col") == device[1])


def any_of(devices):
    flag = at(devices[0])
    for d in devices[1:]:
        flag = flag | at(d)
    return flag


def call(kernel, outs, ins, in_specs, out_specs, scratch=(), limit=16):
    return pl.pallas_call(
        kernel,
        out_shape=outs,
        in_specs=in_specs,
        out_specs=out_specs,
        scratch_shapes=list(scratch),
        compiler_params=pltpu.CompilerParams(vmem_limit_bytes=limit << 20),
        name=kernel.func.__name__ if isinstance(kernel, functools.partial) else kernel.__name__,
    )(*ins)


def pair_width(m, part):
    return 2 * (m + 1) * part


def cut_kernel(diag_ref, *refs):
    cuts, sem = refs[:-1], refs[-1]
    row, col = lax.axis_index("row"), lax.axis_index("col")
    part = diag_ref.shape[1]
    k = jnp.int32(0)
    for r in range(NR):
        for c in range(NC):
            k = jnp.where((row == r) & (col == c), SENDS[r][c], k)
    for m in range(NR // 2):

        @pl.when(row // 2 == m)
        def _():
            copy = pltpu.make_async_copy(diag_ref.at[k, :, pl.ds(0, pair_width(m, part))], cuts[m], sem)
            copy.start()
            copy.wait()


def first_kernel(rhs_ref, diag_ref, *refs):
    parts, out_ref = refs[: NR // 2], refs[NR // 2]
    rhs_v, d_v, rhs_sem, d_sem = refs[NR // 2 + 1 :]
    n = out_ref.shape[0] // 2
    col = lax.axis_index("col")

    @pl.when(lax.axis_index("row") == 0)
    def _():
        rhs_copy = pltpu.make_async_copy(rhs_ref.at[0], rhs_v, rhs_sem)
        rhs_copy.start()

        def pieces(c):
            copies = []
            for i, r in enumerate(PIECES[c]):
                wide = pair_width(r // 2, n)
                source = parts[r // 2] if r else diag_ref.at[0, :, pl.ds(0, wide)]
                copies.append(pltpu.make_async_copy(source, d_v.at[i, :, pl.ds(0, wide)], d_sem.at[i]))
            return copies

        for c in range(NC):

            @pl.when(col == c)
            def _():
                for copy in pieces(c):
                    copy.start()

        rhs_copy.wait()
        p = low(rhs_v[...])
        for c in range(NC):

            @pl.when(col == c)
            def _():
                for i, copy in enumerate(pieces(c)):
                    copy.wait()
                    wide = pair_width(PIECES[c][i] // 2, n)
                    out_ref[i * n : (i + 1) * n] = low(dot(d_v[i, :, :wide], p[:wide]))


def pack_kernel(*refs):
    parts, out_ref, sem = refs[:-2], refs[-2], refs[-1]

    @pl.when(any_of(PARTNER[1:]))
    def _():
        copies, left = [], 0
        for m, source in enumerate(parts):
            wide = source.shape[1]
            copies.append(pltpu.make_async_copy(source, out_ref.at[:, pl.ds(left, wide)], sem.at[m]))
            left += wide
        for copy in copies:
            copy.start()
        for copy in copies:
            copy.wait()


def whole_kernel(diag_ref, even_ref, *refs):
    odd, out_ref, sem = refs[:-2], refs[-2], refs[-1]
    size = out_ref.shape[0]
    part = size // NR
    row, col = lax.axis_index("row"), lax.axis_index("col")

    @pl.when(any_of(MAKER[1:]))
    def _():
        def copy(i, source):
            wide = pair_width(i // 2, part)
            return pltpu.make_async_copy(source, out_ref.at[pl.ds(i * part, part), pl.ds(0, wide)], sem.at[i])

        left = 0
        for i in range(NR):
            wide = pair_width(i // 2, part)
            if i % 2:
                source = odd[i // 2]
            else:
                source = even_ref.at[:, pl.ds(left, wide)]
                left += wide

            @pl.when(row == i)
            def _():
                copy(i, diag_ref.at[col, :, pl.ds(0, wide)]).start()

            @pl.when(row != i)
            def _():
                copy(i, source).start()

        for m in range(NR // 2 - 1):
            right = pair_width(m, part)
            out_ref[pl.ds(2 * m * part, 2 * part), pl.ds(right, size - right)] = jnp.zeros(
                (2 * part, size - right), out_ref.dtype
            )
        for i in range(NR):
            copy(i, odd[i // 2]).wait()


def lower_dot(q_ref, d_ref, p_ref):
    half = d_ref.shape[0] // 2
    q_ref[:half] = low(dot(d_ref[:half, :half], p_ref[:half]))
    q_ref[half:] = low(dot(d_ref[half:], p_ref[...]))


def step0_kernel(g0, g1, g2, g3, rhs_ref, l_ref, p_ref, q_ref, s_ref):
    part = l_ref.shape[0] // NR
    row = lax.axis_index("row")

    def lookup(c, i):
        r = jnp.int32(PIECES[0][i])
        for n in range(1, NC):
            r = jnp.where(c == n, PIECES[n][i], r)
        return pl.multiple_of(r * part, part)

    @pl.when((row >= 1) & (row < 4) & (lax.axis_index("col") == 0))
    def _():
        for j, got in enumerate((g0, g1, g2, g3)):
            src = lax.rem(row + 7 - j, 4)
            q_ref[pl.ds(lookup(src, 0), part)] = got[:part]
            q_ref[pl.ds(lookup(src, 1), part)] = got[part:]
        s = dot(l_ref[...], q_ref[...])
        s_ref[...] = low(s)
        p_ref[...] = low(rhs_ref[0] - s)


def step1_kernel(p_in, sum_ref, rhs_ref, d_ref, l_ref, q_prev, s_prev, p_ref, q_ref, s_ref):
    active = at(MAKER[1])

    @pl.when(active)
    def _():
        lower_dot(q_ref, d_ref, p_in)
        s = dot(l_ref[...], q_ref[...]) + sum_ref[...].astype(jnp.float32)
        s_ref[...] = low(s)
        p_ref[...] = low(rhs_ref[0] - s)

    @pl.when(jnp.logical_not(active))
    def _():
        q_ref[...] = q_prev[...]
        s_ref[...] = s_prev[...]


def step2_kernel(p_in, q_in, sum_ref, rhs_ref, d_ref, l_ref, q_prev, s_prev, a_ref, q_ref, s_ref):
    active, beside = at(MAKER[2]), at(BESIDE)

    @pl.when(active)
    def _():
        lower_dot(q_ref, d_ref, p_in)
        s_ref[...] = low(dot(l_ref[...], q_ref[...]))

    @pl.when(beside)
    def _():
        q_ref[...] = q_in[...]
        s = dot(l_ref[...], q_in[...]) + sum_ref[...].astype(jnp.float32)
        s_ref[...] = low(s)
        a_ref[...] = low(rhs_ref[0] - s)

    @pl.when(jnp.logical_not(active | beside))
    def _():
        q_ref[...] = q_prev[...]
        s_ref[...] = s_prev[...]


def step3_kernel(took, a_ref, sum_ref, d_ref, q_prev, came_ref, q_ref, p_v):
    active, taken = at(MAKER[3]), any_of(took)

    @pl.when(active)
    def _():
        p_v[...] = low(a_ref[...].astype(jnp.float32) - sum_ref[...].astype(jnp.float32))
        lower_dot(q_ref, d_ref, p_v)

    @pl.when(taken)
    def _():
        q_ref[...] = came_ref[...]

    @pl.when(jnp.logical_not(active | taken))
    def _():
        q_ref[...] = q_prev[...]


def update_kernel(takers, rows_ref, counts_ref, s_ref, l_ref, q_prev, *refs):
    got, q_ref, out_ref = refs[:-2], refs[-2], refs[-1]
    size = l_ref.shape[0]
    row, col = lax.axis_index("row"), lax.axis_index("col")
    below = row >= NC

    def take(flag, source):
        @pl.when(flag)
        def _():
            q_ref[...] = source[...]

    kept = jnp.logical_not(any_of([d for devices in takers for d in devices]))
    take(kept, q_prev)
    for devices, source in zip(takers, got):
        take(any_of(devices), source)

    @pl.when(below)
    def _():
        out_ref[pl.ds(0, size)] = low(dot(l_ref[...], q_ref[...]))

    @pl.when(jnp.logical_not(below))
    def _():
        out_ref[pl.ds(0, size)] = s_ref[...]

    listed = rows_ref[0, 0, 0, 0]
    there = below & (counts_ref[0, 0, 0] > 0)
    done = at(FIRST) | at(MAKER[1]) | at(BESIDE) | at(MAKER[2])
    first = (there & (listed == 0)) | done
    second = there & (listed == 1)
    ids = lax.broadcasted_iota(jnp.int32, (TAIL, out_ref.shape[1]), 0)
    flag = ((ids == 0) & first) | ((ids == 1) & second)
    out_ref[pl.ds(size, TAIL)] = low(jnp.where(flag, 1.0, 0.0))


def solved_kernel(q_ref, rest_ref, solved_ref):
    came = any_of(REST)

    @pl.when(came)
    def _():
        solved_ref[...] = rest_ref[...].astype(jnp.float32)

    @pl.when(jnp.logical_not(came))
    def _():
        solved_ref[...] = q_ref[...].astype(jnp.float32)


def final_kernel(rhs_ref, *refs):
    sums, out_ref = refs[:NC], refs[NC]
    size = out_ref.shape[1]
    for i in range(out_ref.shape[0]):
        acc = rhs_ref[i]
        for s in sums:
            keep = s[pl.ds(size, TAIL)].astype(jnp.float32)[i : i + 1] > 0.5
            acc = acc - jnp.where(keep, s[pl.ds(0, size)].astype(jnp.float32), 0.0)
        out_ref[i] = acc


def on_device_8x4(rhs, diag_inv, blocks, block_rows, counts):
    size, width = rhs.shape[2:]
    part = size // NR
    rhs = rhs[:, 0]
    block = blocks[0, 0, 0, 0]
    bf16 = jnp.bfloat16
    vec = jax.ShapeDtypeStruct((size, width), bf16)
    dma = pltpu.SemaphoreType.DMA

    wides = [pair_width(m, part) for m in range(NR // 2)]
    cuts = call(
        cut_kernel, [jax.ShapeDtypeStruct((part, w), bf16) for w in wides], [diag_inv], [HBM], [ANY] * len(wides), [dma]
    )
    at_piece = {r: (0, c) for c, rows in enumerate(PIECES) for r in rows}
    parts = []
    for m, cut in enumerate(cuts):
        pairs = []
        for r in (2 * m, 2 * m + 1):
            for c, k in enumerate(SENDS[r]):
                if k == 0 and r:
                    pairs.append(((r, c), at_piece[r]))
                if k and MAKER[k][0] != r:
                    pairs.append(((r, c), MAKER[k] if r % 2 else PARTNER[k]))
        parts.append(send_only(cut, pairs))
    q = call(
        first_kernel,
        jax.ShapeDtypeStruct((2 * part, width), bf16),
        [rhs, diag_inv, *parts],
        [HBM, HBM] + [ANY] * len(wides),
        VMEM,
        [
            pltpu.VMEM((size, width), jnp.float32),
            pltpu.VMEM((2, part, size), bf16),
            dma,
            pltpu.SemaphoreType.DMA((2,)),
        ],
    )
    takers = (FIRST, (2, 0), (3, 0))
    got = [send(q, [((0, c), takers[(c + j) % 4]) for c in range(4) if (c + j) % 4 < 3]) for j in range(4)]
    even = call(
        pack_kernel,
        jax.ShapeDtypeStruct((part, sum(wides)), bf16),
        parts,
        [ANY] * len(wides),
        VMEM,
        [pltpu.SemaphoreType.DMA((len(wides),))],
    )
    even = send(even, [(PARTNER[k], MAKER[k]) for k in range(1, NC)])
    diag = call(
        whole_kernel,
        jax.ShapeDtypeStruct((size, size), bf16),
        [diag_inv, even, *parts],
        [HBM] + [ANY] * (1 + len(wides)),
        VMEM,
        [pltpu.SemaphoreType.DMA((NR,))],
    )

    p, q, s = call(step0_kernel, [vec] * 3, [*got, rhs, block], [VMEM] * 6, [VMEM] * 3)
    p_in = send(p, [(FIRST, MAKER[1])])
    sums = send(s, [((2, 0), MAKER[1]), ((3, 0), BESIDE)])
    p, q, s = call(step1_kernel, [vec] * 3, [p_in, sums, rhs, diag, block, q, s], [VMEM] * 7, [VMEM] * 3)
    p_in = send(p, [(MAKER[1], MAKER[2])])
    q_in = send(q, [(MAKER[1], BESIDE)])

    p_in, spread = lax.optimization_barrier((p_in, q))
    came = send(spread, [((2, 0), (4, 0)), ((3, 0), (5, 0)), ((1, 0), (0, 0)), ((2, 1), (4, 1))])
    took = [(4, 0), (5, 0), (0, 0), (4, 1)]

    a, q, s = call(step2_kernel, [vec] * 3, [p_in, q_in, sums, rhs, diag, block, q, s], [VMEM] * 8, [VMEM] * 3)
    sums = send_only(s, [(MAKER[2], MAKER[3])])
    a = send_only(a, [(BESIDE, MAKER[3])])

    q = call(
        functools.partial(step3_kernel, took),
        vec,
        [a, sums, diag, q, came],
        [VMEM] * 5,
        VMEM,
        [pltpu.VMEM((size, width), bf16)],
    )

    sends = [
        [(MAKER[3], (6, 3)), ((4, 0), (6, 0)), ((5, 0), (7, 0)), ((4, 1), (6, 1)), ((3, 1), (5, 1)), ((2, 1), (0, 1))],
        [(MAKER[3], (7, 3)), ((4, 1), (7, 1)), ((3, 1), (1, 1))],
        [(MAKER[3], (4, 3))],
        [],
        [],
    ]
    for pairs, r in zip(sends, (4, 6, 7, 5, 2)):
        pairs.append((MAKER[2], (r, 2)))
    got = [send_only(q, pairs) for pairs in sends]
    takers = [[b for _, b in pairs] for pairs in sends]
    q, mine = call(
        functools.partial(update_kernel, takers),
        [vec, jax.ShapeDtypeStruct((size + TAIL, width), bf16)],
        [block_rows, counts, s, block, q, *got],
        [SMEM] * 2 + [VMEM] * (3 + len(got)),
        [VMEM] * 2,
    )

    def swap(value, step):
        return send(value, [((r, c), (r, c ^ step)) for r in range(NR) for c in range(NC)])

    across = swap(mine, 2)
    rest = send_only(q, list(zip(((4, 3), (5, 3), (6, 3), (7, 3), (2, 2), MAKER[2]), REST)))
    solved = call(solved_kernel, jax.ShapeDtypeStruct((size, width), jnp.float32), [q, rest], [VMEM] * 2, VMEM)
    beside, across, solved = lax.optimization_barrier((mine, across, solved))
    beside = swap(beside, 1)
    corner = swap(across, 1)
    remainder = call(
        final_kernel,
        jax.ShapeDtypeStruct(rhs.shape, jnp.float32),
        [rhs, mine, beside, across, corner],
        [VMEM] * 5,
        VMEM,
    )
    return solved[None, None], remainder[:, None]


def solution(mesh):
    in_specs = (
        P(None, "row", None, None),
        P(None, "row", None),
        P(None, "col", "row", None, None, None),
        P(None, "col", "row", None),
        P(None, "col", "row"),
    )
    out_specs = (P(None, "col", None, None), P(None, "row", None, None))
    small = mesh.shape["row"] == NR and mesh.shape["col"] == NC
    return jax.shard_map(
        on_device_8x4 if small else on_device_any,
        mesh=mesh,
        in_specs=in_specs,
        out_specs=out_specs,
        check_vma=False,
    )
```

```python
import functools

import jax
import jax.numpy as jnp
from jax import lax
from jax.experimental import pallas as pl
from jax.experimental.pallas import tpu as pltpu
from jax.sharding import PartitionSpec as P

VMEM = pl.BlockSpec(memory_space=pltpu.VMEM)
ANY = pl.BlockSpec(memory_space=pl.ANY)
HBM = pl.BlockSpec(memory_space=pltpu.HBM)
SMEM = pl.BlockSpec(memory_space=pltpu.SMEM)
TAIL = 16


def broadcast(value, axis, root):
    mine = lax.axis_index(axis) == root
    return lax.psum(jnp.where(mine, value, jnp.zeros_like(value)), axis)


def on_device_any(rhs, diag_inv, blocks, block_rows, counts):
    nrow = lax.axis_size("row")
    ncol = lax.axis_size("col")
    my_row = lax.axis_index("row")
    my_col = lax.axis_index("col")
    kc = diag_inv.shape[0]
    rb_local = rhs.shape[0]
    nz_local = blocks.shape[3]
    local_rhs = rhs[:, 0]
    partial_value = jnp.zeros(local_rhs.shape, jnp.float32)
    solved_list = [jnp.zeros(local_rhs.shape[1:], jnp.float32)]
    slot_ids = jnp.arange(nz_local, dtype=jnp.int32)
    local_ids = jnp.arange(rb_local, dtype=jnp.int32)
    for k in range(kc):
        j = k // ncol
        owner_row = k % nrow
        local_pivot = k // nrow
        mine_row = my_row == owner_row
        mine_col = my_col == k % ncol
        pivot_part = jnp.where(mine_row, partial_value[local_pivot], jnp.float32(0.0))
        summed = lax.psum(pivot_part, "col")
        updated = (local_rhs[local_pivot] - summed).astype(jnp.bfloat16)
        pivot_bf = broadcast(updated, "row", owner_row)
        row_part = jnp.dot(diag_inv[k], pivot_bf, preferred_element_type=jnp.float32)
        sol = lax.all_gather(row_part, "row", axis=0, tiled=True)
        sol_bf = sol.astype(jnp.bfloat16)
        rows = block_rows[j, 0, 0]
        glob = rows * nrow + my_row
        valid = (slot_ids < counts[j, 0, 0]) & (glob > k) & mine_col
        weights = (valid[:, None] & (rows[:, None] == local_ids[None, :])).astype(jnp.float32)
        contrib = jnp.einsum(
            "sab,bn->san", blocks[j, 0, 0], sol_bf, preferred_element_type=jnp.float32
        )
        partial_value = partial_value + jnp.einsum(
            "sl,san->lan", weights, contrib, precision=lax.Precision.HIGHEST
        )
        solved_list[j] = jnp.where(mine_col, sol, solved_list[j])
    total = lax.psum(partial_value, "col")
    remainder = (local_rhs - total)[:, None]
    solved = jnp.stack(solved_list)[:, None]
    return (solved, remainder)


NR, NC = 8, 4
MAKER = (None, (2, 1), (3, 2), (5, 3))
FIRST = (1, 0)
BESIDE = (3, 1)
PARTNER = (None, (2, 0), (3, 3), (5, 2))
PIECES = ((6, 0), (7, 1), (4, 2), (5, 3))
SENDS = (
    (1, None, 2, 3),
    (2, 0, 1, 3),
    (None, 3, 0, 2),
    (3, None, 1, 0),
    (1, 3, 0, 2),
    (1, None, 2, 0),
    (0, 1, 2, 3),
    (1, 0, 2, 3),
)
REST = ((2, 3), (0, 3), (1, 3), (0, 2))


def hops(a, b):
    d = a ^ b
    if d < 2:
        return 1 if d else 10000
    return 100 + abs((a >> 3) - (b >> 3)) + ((d >> 2) & 1) + ((d >> 1) & 1)


def complete(pairs):
    to = {a * NC + b: c * NC + d for (a, b), (c, d) in pairs}
    free_from = [i for i in range(NR * NC) if i not in to]
    free_to = [i for i in range(NR * NC) if i not in to.values()]
    n = len(free_from)
    u, v, match = [0] * (n + 1), [0] * (n + 1), [0] * (n + 1)
    for i in range(1, n + 1):
        match[0], j0 = i, 0
        least, way, used = [10**9] * (n + 1), [0] * (n + 1), [False] * (n + 1)
        while True:
            used[j0] = True
            i0, delta, j1 = match[j0], 10**9, 0
            for j in range(1, n + 1):
                if not used[j]:
                    cur = hops(free_from[i0 - 1], free_to[j - 1]) - u[i0] - v[j]
                    if cur < least[j]:
                        least[j], way[j] = cur, j0
                    if least[j] < delta:
                        delta, j1 = least[j], j
            for j in range(n + 1):
                if used[j]:
                    u[match[j]] += delta
                    v[j] -= delta
                else:
                    least[j] -= delta
            j0 = j1
            if match[j0] == 0:
                break
        while j0:
            j1 = way[j0]
            match[j0] = match[j1]
            j0 = j1
    for j in range(1, n + 1):
        to[free_from[match[j] - 1]] = free_to[j - 1]
    return [(divmod(a, NC), divmod(b, NC)) for a, b in sorted(to.items())]


def send(value, pairs):
    return lax.ppermute(value, ("row", "col"), [(a * NC + b, c * NC + d) for (a, b), (c, d) in complete(pairs)])


def send_only(value, pairs):
    return lax.ppermute(value, ("row", "col"), [(a * NC + b, c * NC + d) for (a, b), (c, d) in pairs])


def dot(a, b):
    return jnp.dot(a, b, preferred_element_type=jnp.float32)


def low(a):
    return a.astype(jnp.bfloat16)


def at(device):
    return (lax.axis_index("row") == device[0]) & (lax.axis_index("col") == device[1])


def any_of(devices):
    flag = at(devices[0])
    for d in devices[1:]:
        flag = flag | at(d)
    return flag


def call(kernel, outs, ins, in_specs, out_specs, scratch=(), limit=16):
    return pl.pallas_call(
        kernel,
        out_shape=outs,
        in_specs=in_specs,
        out_specs=out_specs,
        scratch_shapes=list(scratch),
        compiler_params=pltpu.CompilerParams(vmem_limit_bytes=limit << 20),
        name=kernel.func.__name__ if isinstance(kernel, functools.partial) else kernel.__name__,
    )(*ins)


def pair_width(m, part):
    return 2 * (m + 1) * part


def sent_here():
    row, col = lax.axis_index("row"), lax.axis_index("col")
    k = jnp.int32(-1)
    for r in range(NR):
        for c in range(NC):
            if SENDS[r][c] is not None:
                k = jnp.where((row == r) & (col == c), SENDS[r][c], k)
    return k


def cut(diag_ref, flag, k, out, sem):
    @pl.when(flag)
    def _():
        copy = pltpu.make_async_copy(diag_ref.at[k, :, pl.ds(0, out.shape[1])], out, sem)
        copy.start()
        copy.wait()


def cut_first_kernel(diag_ref, hi_ref, lo_ref, sem):
    row, k = lax.axis_index("row"), sent_here()
    cut(diag_ref, (k == 0) & (row >= 4), 0, hi_ref, sem)
    cut(diag_ref, ((k == 0) & (row < 4)) | ((k > 0) & (row == 0)), k, lo_ref, sem)


def cut_rest_kernel(diag_ref, after_ref, *refs):
    cuts, sem = refs[:-1], refs[-1]
    row, k = lax.axis_index("row"), sent_here()
    for m, out in enumerate(cuts):
        cut(diag_ref, (k > 0) & (row > 0) & (row // 2 == m), k, out, sem)


def first_kernel(rhs_ref, diag_ref, hi_ref, lo_ref, out_ref, rhs_v, lo_v, rhs_sem, lo_sem):
    n, half = lo_ref.shape
    col = lax.axis_index("col")

    @pl.when(lax.axis_index("row") == 0)
    def _():
        copy = pltpu.make_async_copy(rhs_ref.at[0], rhs_v, rhs_sem)
        copy.start()
        own = pltpu.make_async_copy(diag_ref.at[0, :, pl.ds(0, half)], lo_v, lo_sem)

        @pl.when(col == 0)
        def _():
            own.start()

        @pl.when(col != 0)
        def _():
            lo_v[...] = lo_ref[...]

        copy.wait()
        p = low(rhs_v[...])
        out_ref[:n] = low(dot(hi_ref[...], p))

        @pl.when(col == 0)
        def _():
            own.wait()

        out_ref[n:] = low(dot(lo_v[...], p[:half]))


def pack_kernel(*refs):
    parts, out_ref, sem = refs[:-2], refs[-2], refs[-1]
    part = out_ref.shape[0]

    @pl.when(any_of(PARTNER[1:]))
    def _():
        copies, left = [], 0
        for m, source in enumerate(parts):
            wide = pair_width(m, part)
            copies.append(
                pltpu.make_async_copy(source.at[:, pl.ds(0, wide)], out_ref.at[:, pl.ds(left, wide)], sem.at[m])
            )
            left += wide
        for copy in copies:
            copy.start()
        for copy in copies:
            copy.wait()


def whole_kernel(diag_ref, even_ref, *refs):
    odd, out_ref, sem = refs[:-2], refs[-2], refs[-1]
    size = out_ref.shape[0]
    part = size // NR
    row, col = lax.axis_index("row"), lax.axis_index("col")

    @pl.when(any_of(MAKER[1:]))
    def _():
        def copy(i, source):
            wide = pair_width(i // 2, part)
            return pltpu.make_async_copy(source, out_ref.at[pl.ds(i * part, part), pl.ds(0, wide)], sem.at[i])

        left = 0
        for i in range(NR):
            wide = pair_width(i // 2, part)
            if i % 2:
                source = odd[i // 2]
            else:
                source = even_ref.at[:, pl.ds(left, wide)]
                left += wide

            @pl.when(row == i)
            def _():
                copy(i, diag_ref.at[col, :, pl.ds(0, wide)]).start()

            @pl.when(row != i)
            def _():
                copy(i, source).start()

        for m in range(NR // 2 - 1):
            right = pair_width(m, part)
            out_ref[pl.ds(2 * m * part, 2 * part), pl.ds(right, size - right)] = jnp.zeros(
                (2 * part, size - right), out_ref.dtype
            )
        for i in range(NR):
            copy(i, odd[i // 2]).wait()


def lower_dot(q_ref, d_ref, p_ref):
    half = d_ref.shape[0] // 2
    q_ref[:half] = low(dot(d_ref[:half, :half], p_ref[:half]))
    q_ref[half:] = low(dot(d_ref[half:], p_ref[...]))


def collect(got, first, q_ref):
    part = q_ref.shape[0] // NR
    for j, pieces in enumerate(got):
        src = lax.rem(first + j, NC)
        for i in range(2):
            r = jnp.int32(PIECES[0][i])
            for n in range(1, NC):
                r = jnp.where(src == n, PIECES[n][i], r)
            q_ref[pl.ds(pl.multiple_of(r * part, part), part)] = pieces[i * part : (i + 1) * part]


def step0_kernel(g0, g1, g2, g3, rhs_ref, l_ref, p_ref, q_ref, s_ref):
    row = lax.axis_index("row")

    @pl.when(at(FIRST) | at((3, 0)))
    def _():
        collect((g0, g1, g2, g3), jnp.where(row == 3, 1, 0), q_ref)
        s = dot(l_ref[...], q_ref[...])
        p_ref[...] = low(rhs_ref[0] - s)
        s_ref[...] = low(s)


def step0_again_kernel(g0, g1, g2, g3, l_ref, q_prev, s_prev, q_ref, s_ref):
    active = at((2, 0))

    @pl.when(active)
    def _():
        collect((g0, g1, g2, g3), 0, q_ref)
        s_ref[...] = low(dot(l_ref[...], q_ref[...]))

    @pl.when(jnp.logical_not(active))
    def _():
        q_ref[...] = q_prev[...]
        s_ref[...] = s_prev[...]


def step1_kernel(p_in, sum_ref, rhs_ref, d_ref, l_ref, q_prev, s_prev, p_ref, q_ref, s_ref):
    active = at(MAKER[1])

    @pl.when(active)
    def _():
        lower_dot(q_ref, d_ref, p_in)
        s = dot(l_ref[...], q_ref[...]) + sum_ref[...].astype(jnp.float32)
        s_ref[...] = low(s)
        p_ref[...] = low(rhs_ref[0] - s)

    @pl.when(jnp.logical_not(active))
    def _():
        q_ref[...] = q_prev[...]
        s_ref[...] = s_prev[...]


def step2_kernel(p_in, q_in, sum_ref, rhs_ref, d_ref, l_ref, q_prev, s_prev, a_ref, q_ref, s_ref):
    active, beside = at(MAKER[2]), at(BESIDE)

    @pl.when(active)
    def _():
        lower_dot(q_ref, d_ref, p_in)
        a_ref[...] = q_ref[...]
        s_ref[...] = low(dot(l_ref[...], q_ref[...]))

    @pl.when(beside)
    def _():
        q_ref[...] = q_in[...]
        s = dot(l_ref[...], q_in[...]) + sum_ref[...].astype(jnp.float32)
        s_ref[...] = low(s)
        a_ref[...] = low(rhs_ref[0] - s)

    @pl.when(jnp.logical_not(active | beside))
    def _():
        q_ref[...] = q_prev[...]
        s_ref[...] = s_prev[...]


def step3_kernel(takers, sum_ref, a_ref, *refs):
    came, (d_ref, q_prev, q_ref, p_v) = refs[:-4], refs[-4:]
    active = at(MAKER[3])

    @pl.when(active)
    def _():
        p_v[...] = low(a_ref[...].astype(jnp.float32) - sum_ref[...].astype(jnp.float32))
        lower_dot(q_ref, d_ref, p_v)

    for devices, source in zip(takers, (a_ref, *came)):

        @pl.when(any_of(devices))
        def _():
            q_ref[...] = source[...]

    @pl.when(jnp.logical_not(active | any_of([d for devices in takers for d in devices])))
    def _():
        q_ref[...] = q_prev[...]


def update_kernel(takers, rows_ref, counts_ref, s_ref, l_ref, q_prev, *refs):
    got, q_ref, out_ref = refs[:-2], refs[-2], refs[-1]
    size = l_ref.shape[0]
    row, col = lax.axis_index("row"), lax.axis_index("col")
    below = row >= NC

    def take(flag, source):
        @pl.when(flag)
        def _():
            q_ref[...] = source[...]

    kept = jnp.logical_not(any_of([d for devices in takers for d in devices]))
    take(kept, q_prev)
    for devices, source in zip(takers, got):
        take(any_of(devices), source)

    @pl.when(below)
    def _():
        out_ref[pl.ds(0, size)] = low(dot(l_ref[...], q_ref[...]))

    @pl.when(jnp.logical_not(below))
    def _():
        out_ref[pl.ds(0, size)] = s_ref[...]

    listed = rows_ref[0, 0, 0, 0]
    there = below & (counts_ref[0, 0, 0] > 0)
    done = at(FIRST) | at(MAKER[1]) | at(BESIDE) | at(MAKER[2])
    first = (there & (listed == 0)) | done
    second = there & (listed == 1)
    ids = lax.broadcasted_iota(jnp.int32, (TAIL, out_ref.shape[1]), 0)
    flag = ((ids == 0) & first) | ((ids == 1) & second)
    out_ref[pl.ds(size, TAIL)] = low(jnp.where(flag, 1.0, 0.0))


def solved_kernel(q_ref, rest_ref, solved_ref):
    came = any_of(REST)

    @pl.when(came)
    def _():
        solved_ref[...] = rest_ref[...].astype(jnp.float32)

    @pl.when(jnp.logical_not(came))
    def _():
        solved_ref[...] = q_ref[...].astype(jnp.float32)


def final_kernel(rhs_ref, *refs):
    sums, out_ref = refs[:NC], refs[NC]
    size = out_ref.shape[1]
    for i in range(out_ref.shape[0]):
        acc = rhs_ref[i]
        for s in sums:
            keep = s[pl.ds(size, TAIL)].astype(jnp.float32)[i : i + 1] > 0.5
            acc = acc - jnp.where(keep, s[pl.ds(0, size)].astype(jnp.float32), 0.0)
        out_ref[i] = acc


def on_device_8x4(rhs, diag_inv, blocks, block_rows, counts):
    size, width = rhs.shape[2:]
    part = size // NR
    rhs = rhs[:, 0]
    block = blocks[0, 0, 0, 0]
    bf16 = jnp.bfloat16
    vec = jax.ShapeDtypeStruct((size, width), bf16)
    dma = pltpu.SemaphoreType.DMA

    wides = [pair_width(m, part) for m in range(NR // 2)]
    hi, lo = call(
        cut_first_kernel,
        [jax.ShapeDtypeStruct((part, w), bf16) for w in (size, size // 2)],
        [diag_inv],
        [HBM],
        [ANY, ANY],
        [dma],
    )
    source = {(r, k): (r, c) for r in range(NR) for c, k in enumerate(SENDS[r]) if k is not None}
    hi = send_only(hi, [(source[rows[0], 0], (0, c)) for c, rows in enumerate(PIECES)])
    lo = send_only(
        lo,
        [(source[rows[1], 0], (0, c)) for c, rows in enumerate(PIECES) if rows[1]]
        + [(source[0, k], PARTNER[k]) for k in range(1, NC)],
    )
    q = call(
        first_kernel,
        jax.ShapeDtypeStruct((2 * part, width), bf16),
        [rhs, diag_inv, hi, lo],
        [HBM, HBM, VMEM, VMEM],
        VMEM,
        [pltpu.VMEM((size, width), jnp.float32), pltpu.VMEM((part, size // 2), bf16), dma, dma],
    )
    cuts = call(
        cut_rest_kernel,
        [jax.ShapeDtypeStruct((part, w), bf16) for w in wides],
        [diag_inv, q],
        [HBM, ANY],
        [ANY] * len(wides),
        [dma],
    )
    parts = [
        send_only(
            cut,
            [
                (source[r, k], MAKER[k] if r % 2 else PARTNER[k])
                for r in (2 * m, 2 * m + 1)
                for k in range(1, NC)
                if r and MAKER[k][0] != r
            ],
        )
        for m, cut in enumerate(cuts)
    ]
    got = [send(q, [((0, j), FIRST), ((0, (j + 1) % NC), (3, 0))]) for j in range(NC)]
    got_again = [send(q, [((0, j), (2, 0))]) for j in range(NC)]
    even = call(
        pack_kernel,
        jax.ShapeDtypeStruct((part, sum(wides)), bf16),
        [lo, *parts[1:]],
        [ANY] * len(wides),
        VMEM,
        [pltpu.SemaphoreType.DMA((len(wides),))],
    )
    even = send(even, [(PARTNER[k], MAKER[k]) for k in range(1, NC)])
    diag = call(
        whole_kernel,
        jax.ShapeDtypeStruct((size, size), bf16),
        [diag_inv, even, *parts],
        [HBM] + [ANY] * (1 + len(wides)),
        VMEM,
        [pltpu.SemaphoreType.DMA((NR,))],
    )

    p, q, s = call(step0_kernel, [vec] * 3, [*got, rhs, block], [VMEM] * 6, [VMEM] * 3)
    p_in = send(p, [(FIRST, MAKER[1])])
    q, s = call(step0_again_kernel, [vec] * 2, [*got_again, block, q, s], [VMEM] * 7, [VMEM] * 2)
    sums = send(s, [((2, 0), MAKER[1]), ((3, 0), BESIDE)])
    p, q, s = call(step1_kernel, [vec] * 3, [p_in, sums, rhs, diag, block, q, s], [VMEM] * 7, [VMEM] * 3)
    p_in = send(p, [(MAKER[1], MAKER[2])])
    q_in = send(q, [(MAKER[1], BESIDE)])

    p_in, spread = lax.optimization_barrier((p_in, q))
    came = send(spread, [((2, 0), (4, 0)), ((3, 0), (5, 0)), ((1, 0), (0, 0)), ((2, 1), (4, 1))])
    took = [(4, 0), (5, 0), (0, 0), (4, 1)]

    a, q, s = call(step2_kernel, [vec] * 3, [p_in, q_in, sums, rhs, diag, block, q, s], [VMEM] * 8, [VMEM] * 3)
    sums = send(s, [(MAKER[2], MAKER[3])])
    q_2 = a
    a = send_only(a, [(BESIDE, MAKER[3]), (MAKER[2], (2, 2))])
    q_2 = send_only(q_2, [(MAKER[2], (7, 2))])
    q = call(
        functools.partial(step3_kernel, [[(2, 2)], [(7, 2)], took]),
        vec,
        [sums, a, q_2, came, diag, q],
        [VMEM] * 6,
        VMEM,
        [pltpu.VMEM((size, width), bf16)],
    )

    sends = [
        [
            (MAKER[3], (7, 3)), ((2, 2), (6, 2)), (MAKER[2], (5, 2)),
            ((4, 0), (6, 0)), ((5, 0), (7, 0)), ((4, 1), (6, 1)), ((3, 1), (5, 1)), ((2, 1), (0, 1)),
        ],
        [(MAKER[3], (6, 3)), ((2, 2), (4, 2)), (MAKER[2], (1, 2)), ((4, 1), (7, 1)), ((3, 1), (1, 1))],
        [(MAKER[3], (4, 3))],
        [(MAKER[3], (3, 3))],
    ]
    got = [send_only(q, pairs) for pairs in sends]
    takers = [[b for _, b in pairs] for pairs in sends]
    q, mine = call(
        functools.partial(update_kernel, takers),
        [vec, jax.ShapeDtypeStruct((size + TAIL, width), bf16)],
        [block_rows, counts, s, block, q, *got],
        [SMEM] * 2 + [VMEM] * (3 + len(got)),
        [VMEM] * 2,
    )

    def swap(value, step):
        return send(value, [((r, c), (r, c ^ step)) for r in range(NR) for c in range(NC)])

    across = swap(mine, 2)
    rest = send_only(q, list(zip(((3, 3), (6, 3), (7, 3), (2, 2)), REST)))
    solved = call(solved_kernel, jax.ShapeDtypeStruct((size, width), jnp.float32), [q, rest], [VMEM] * 2, VMEM)
    beside, across, solved = lax.optimization_barrier((mine, across, solved))
    beside = swap(beside, 1)
    corner = swap(across, 1)
    remainder = call(
        final_kernel,
        jax.ShapeDtypeStruct(rhs.shape, jnp.float32),
        [rhs, mine, beside, across, corner],
        [VMEM] * 5,
        VMEM,
    )
    return solved[None, None], remainder[:, None]


def solution(mesh):
    in_specs = (
        P(None, "row", None, None),
        P(None, "row", None),
        P(None, "col", "row", None, None, None),
        P(None, "col", "row", None),
        P(None, "col", "row"),
    )
    out_specs = (P(None, "col", None, None), P(None, "row", None, None))
    small = mesh.shape["row"] == NR and mesh.shape["col"] == NC
    return jax.shard_map(
        on_device_8x4 if small else on_device_any,
        mesh=mesh,
        in_specs=in_specs,
        out_specs=out_specs,
        check_vma=False,
    )
```

```python
import functools

import jax
import jax.numpy as jnp
from jax import lax
from jax.experimental import pallas as pl
from jax.experimental.pallas import tpu as pltpu
from jax.sharding import PartitionSpec as P

VMEM = pl.BlockSpec(memory_space=pltpu.VMEM)
ANY = pl.BlockSpec(memory_space=pl.ANY)
HBM = pl.BlockSpec(memory_space=pltpu.HBM)
SMEM = pl.BlockSpec(memory_space=pltpu.SMEM)
TAIL = 16


def broadcast(value, axis, root):
    mine = lax.axis_index(axis) == root
    return lax.psum(jnp.where(mine, value, jnp.zeros_like(value)), axis)


def on_device_any(rhs, diag_inv, blocks, block_rows, counts):
    nrow = lax.axis_size("row")
    ncol = lax.axis_size("col")
    my_row = lax.axis_index("row")
    my_col = lax.axis_index("col")
    kc = diag_inv.shape[0]
    rb_local = rhs.shape[0]
    nz_local = blocks.shape[3]
    local_rhs = rhs[:, 0]
    partial_value = jnp.zeros(local_rhs.shape, jnp.float32)
    solved_list = [jnp.zeros(local_rhs.shape[1:], jnp.float32)]
    slot_ids = jnp.arange(nz_local, dtype=jnp.int32)
    local_ids = jnp.arange(rb_local, dtype=jnp.int32)
    for k in range(kc):
        j = k // ncol
        owner_row = k % nrow
        local_pivot = k // nrow
        mine_row = my_row == owner_row
        mine_col = my_col == k % ncol
        pivot_part = jnp.where(mine_row, partial_value[local_pivot], jnp.float32(0.0))
        summed = lax.psum(pivot_part, "col")
        updated = (local_rhs[local_pivot] - summed).astype(jnp.bfloat16)
        pivot_bf = broadcast(updated, "row", owner_row)
        row_part = jnp.dot(diag_inv[k], pivot_bf, preferred_element_type=jnp.float32)
        sol = lax.all_gather(row_part, "row", axis=0, tiled=True)
        sol_bf = sol.astype(jnp.bfloat16)
        rows = block_rows[j, 0, 0]
        glob = rows * nrow + my_row
        valid = (slot_ids < counts[j, 0, 0]) & (glob > k) & mine_col
        weights = (valid[:, None] & (rows[:, None] == local_ids[None, :])).astype(jnp.float32)
        contrib = jnp.einsum(
            "sab,bn->san", blocks[j, 0, 0], sol_bf, preferred_element_type=jnp.float32
        )
        partial_value = partial_value + jnp.einsum(
            "sl,san->lan", weights, contrib, precision=lax.Precision.HIGHEST
        )
        solved_list[j] = jnp.where(mine_col, sol, solved_list[j])
    total = lax.psum(partial_value, "col")
    remainder = (local_rhs - total)[:, None]
    solved = jnp.stack(solved_list)[:, None]
    return (solved, remainder)


NR, NC = 8, 4
MAKER = (None, (2, 1), (3, 2), (5, 3))
FIRST = (1, 0)
BESIDE = (3, 1)
PARTNER = (None, (3, 1), (3, 3), (5, 2))
PIECES = ((4, 0), (6, 2), (5, 1), (7, 3))
SENDS = (
    (0, 1, 2, 3),
    (3, 1, 0, 2),
    (0, 1, 3, 2),
    (3, 1, 0, 2),
    (0, 1, 3, 2),
    (2, 0, 3, 1),
    (0, 3, 1, 2),
    (1, 3, 0, 2),
)
REST = ((2, 3), (0, 3), (1, 3), (0, 2))


def hops(a, b):
    d = a ^ b
    if d < 2:
        return 1 if d else 10000
    return 100 + abs((a >> 3) - (b >> 3)) + ((d >> 2) & 1) + ((d >> 1) & 1)


def complete(pairs):
    to = {a * NC + b: c * NC + d for (a, b), (c, d) in pairs}
    free_from = [i for i in range(NR * NC) if i not in to]
    free_to = [i for i in range(NR * NC) if i not in to.values()]
    n = len(free_from)
    u, v, match = [0] * (n + 1), [0] * (n + 1), [0] * (n + 1)
    for i in range(1, n + 1):
        match[0], j0 = i, 0
        least, way, used = [10**9] * (n + 1), [0] * (n + 1), [False] * (n + 1)
        while True:
            used[j0] = True
            i0, delta, j1 = match[j0], 10**9, 0
            for j in range(1, n + 1):
                if not used[j]:
                    cur = hops(free_from[i0 - 1], free_to[j - 1]) - u[i0] - v[j]
                    if cur < least[j]:
                        least[j], way[j] = cur, j0
                    if least[j] < delta:
                        delta, j1 = least[j], j
            for j in range(n + 1):
                if used[j]:
                    u[match[j]] += delta
                    v[j] -= delta
                else:
                    least[j] -= delta
            j0 = j1
            if match[j0] == 0:
                break
        while j0:
            j1 = way[j0]
            match[j0] = match[j1]
            j0 = j1
    for j in range(1, n + 1):
        to[free_from[match[j] - 1]] = free_to[j - 1]
    return [(divmod(a, NC), divmod(b, NC)) for a, b in sorted(to.items())]


def send(value, pairs):
    return lax.ppermute(value, ("row", "col"), [(a * NC + b, c * NC + d) for (a, b), (c, d) in complete(pairs)])


def send_only(value, pairs):
    return lax.ppermute(value, ("row", "col"), [(a * NC + b, c * NC + d) for (a, b), (c, d) in pairs])


def dot(a, b):
    return jnp.dot(a, b, preferred_element_type=jnp.float32)


def low(a):
    return a.astype(jnp.bfloat16)


def at(device):
    return (lax.axis_index("row") == device[0]) & (lax.axis_index("col") == device[1])


def any_of(devices):
    flag = at(devices[0])
    for d in devices[1:]:
        flag = flag | at(d)
    return flag


def call(kernel, outs, ins, in_specs, out_specs, scratch=(), limit=16):
    return pl.pallas_call(
        kernel,
        out_shape=outs,
        in_specs=in_specs,
        out_specs=out_specs,
        scratch_shapes=list(scratch),
        compiler_params=pltpu.CompilerParams(vmem_limit_bytes=limit << 20),
        name=kernel.func.__name__ if isinstance(kernel, functools.partial) else kernel.__name__,
    )(*ins)


def pair_width(m, part):
    return 2 * (m + 1) * part


def cut_kernel(diag_ref, *refs):
    cuts, sem = refs[:-1], refs[-1]
    row, col = lax.axis_index("row"), lax.axis_index("col")
    part = diag_ref.shape[1]
    k = jnp.int32(0)
    for r in range(NR):
        for c in range(NC):
            k = jnp.where((row == r) & (col == c), SENDS[r][c], k)
    for m in range(NR // 2):

        @pl.when(jnp.where((row == 1) & (k == 0), 1, row // 2) == m)
        def _():
            copy = pltpu.make_async_copy(diag_ref.at[k, :, pl.ds(0, pair_width(m, part))], cuts[m], sem)
            copy.start()
            copy.wait()


def first_kernel(rhs_ref, diag_ref, *refs):
    parts, (out_ref, rhs_v, d_v, rhs_sem, d_sem) = refs[:-5], refs[-5:]
    n = out_ref.shape[0] // 2
    col = lax.axis_index("col")

    @pl.when(lax.axis_index("row") == 0)
    def _():
        rhs_copy = pltpu.make_async_copy(rhs_ref.at[0], rhs_v, rhs_sem)
        rhs_copy.start()

        def pieces(c):
            copies = []
            for i, r in enumerate(PIECES[c]):
                m = max(r // 2, 1)
                wide = pair_width(m, n)
                source = parts[m - 1] if r else diag_ref.at[0, :, pl.ds(0, wide)]
                copies.append(pltpu.make_async_copy(source, d_v.at[i, :, pl.ds(0, wide)], d_sem.at[i]))
            return copies

        for c in range(NC):

            @pl.when(col == c)
            def _():
                for copy in pieces(c):
                    copy.start()

        rhs_copy.wait()
        p = low(rhs_v[...])
        for c in range(NC):

            @pl.when(col == c)
            def _():
                for i, copy in enumerate(pieces(c)):
                    copy.wait()
                    wide = pair_width(max(PIECES[c][i] // 2, 1), n)
                    out_ref[i * n : (i + 1) * n] = low(dot(d_v[i, :, :wide], p[:wide]))


def pack_kernel(*refs):
    parts, out_ref, sem = refs[:-2], refs[-2], refs[-1]

    @pl.when(any_of(PARTNER[1:]))
    def _():
        copies, left = [], 0
        for m, source in enumerate(parts):
            wide = source.shape[1]
            copies.append(pltpu.make_async_copy(source, out_ref.at[:, pl.ds(left, wide)], sem.at[m]))
            left += wide
        for copy in copies:
            copy.start()
        for copy in copies:
            copy.wait()


def whole_kernel(diag_ref, top_ref, even_ref, *refs):
    odd, out_ref, sem = refs[:-2], refs[-2], refs[-1]
    size = out_ref.shape[0]
    part = size // NR
    row, col = lax.axis_index("row"), lax.axis_index("col")

    @pl.when(any_of(MAKER[1:]))
    def _():
        def copy(i, source):
            wide = pair_width(i // 2, part)
            return pltpu.make_async_copy(source, out_ref.at[pl.ds(i * part, part), pl.ds(0, wide)], sem.at[i])

        left = 0
        for i in range(NR):
            wide = pair_width(i // 2, part)
            if i % 2:
                source = odd[i // 2]
            elif i:
                source = even_ref.at[:, pl.ds(left, wide)]
                left += wide
            else:
                source = top_ref

            @pl.when(row == i)
            def _():
                copy(i, diag_ref.at[col, :, pl.ds(0, wide)]).start()

            @pl.when(row != i)
            def _():
                copy(i, source).start()

        for m in range(NR // 2 - 1):
            right = pair_width(m, part)
            out_ref[pl.ds(2 * m * part, 2 * part), pl.ds(right, size - right)] = jnp.zeros(
                (2 * part, size - right), out_ref.dtype
            )
        for i in range(NR):
            copy(i, odd[i // 2]).wait()


def lower_dot(q_ref, d_ref, p_ref):
    half = d_ref.shape[0] // 2
    q_ref[:half] = low(dot(d_ref[:half, :half], p_ref[:half]))
    q_ref[half:] = low(dot(d_ref[half:], p_ref[...]))


def step0_kernel(g0, g1, g2, g3, rhs_ref, l_ref, p_ref, q_ref, s_ref):
    part = l_ref.shape[0] // NR
    row = lax.axis_index("row")

    def lookup(c, i):
        r = jnp.int32(PIECES[0][i])
        for n in range(1, NC):
            r = jnp.where(c == n, PIECES[n][i], r)
        return pl.multiple_of(r * part, part)

    @pl.when((row >= 1) & (row < 4) & (lax.axis_index("col") == 0))
    def _():
        for j, got in enumerate((g0, g1, g2, g3)):
            src = lax.rem(row + 7 - j, 4)
            q_ref[pl.ds(lookup(src, 0), part)] = got[:part]
            q_ref[pl.ds(lookup(src, 1), part)] = got[part:]
        s = dot(l_ref[...], q_ref[...])
        s_ref[...] = low(s)
        p_ref[...] = low(rhs_ref[0] - s)


def step1_kernel(p_in, sum_ref, rhs_ref, d_ref, l_ref, q_prev, s_prev, p_ref, q_ref, s_ref):
    active = at(MAKER[1])

    @pl.when(active)
    def _():
        lower_dot(q_ref, d_ref, p_in)
        s = dot(l_ref[...], q_ref[...]) + sum_ref[...].astype(jnp.float32)
        s_ref[...] = low(s)
        p_ref[...] = low(rhs_ref[0] - s)

    @pl.when(jnp.logical_not(active))
    def _():
        q_ref[...] = q_prev[...]
        s_ref[...] = s_prev[...]


def step2_kernel(p_in, q_in, sum_ref, rhs_ref, d_ref, l_ref, q_prev, s_prev, a_ref, q_ref, s_ref):
    active, beside = at(MAKER[2]), at(BESIDE)

    @pl.when(active)
    def _():
        lower_dot(q_ref, d_ref, p_in)
        a_ref[...] = q_ref[...]
        s_ref[...] = low(dot(l_ref[...], q_ref[...]))

    @pl.when(beside)
    def _():
        q_ref[...] = q_in[...]
        s = dot(l_ref[...], q_in[...]) + sum_ref[...].astype(jnp.float32)
        s_ref[...] = low(s)
        a_ref[...] = low(rhs_ref[0] - s)

    @pl.when(jnp.logical_not(active | beside))
    def _():
        q_ref[...] = q_prev[...]
        s_ref[...] = s_prev[...]


def step3_kernel(takers, sum_ref, a_ref, *refs):
    came, (d_ref, q_prev, q_ref, p_v) = refs[:-4], refs[-4:]
    active = at(MAKER[3])

    @pl.when(active)
    def _():
        p_v[...] = low(a_ref[...].astype(jnp.float32) - sum_ref[...].astype(jnp.float32))
        lower_dot(q_ref, d_ref, p_v)

    for devices, source in zip(takers, (a_ref, *came)):

        @pl.when(any_of(devices))
        def _():
            q_ref[...] = source[...]

    @pl.when(jnp.logical_not(active | any_of([d for devices in takers for d in devices])))
    def _():
        q_ref[...] = q_prev[...]


def update_kernel(takers, rows_ref, counts_ref, s_ref, l_ref, q_prev, *refs):
    got, q_ref, out_ref = refs[:-2], refs[-2], refs[-1]
    size = l_ref.shape[0]
    row, col = lax.axis_index("row"), lax.axis_index("col")
    below = row >= NC

    def take(flag, source):
        @pl.when(flag)
        def _():
            q_ref[...] = source[...]

    kept = jnp.logical_not(any_of([d for devices in takers for d in devices]))
    take(kept, q_prev)
    for devices, source in zip(takers, got):
        take(any_of(devices), source)

    @pl.when(below)
    def _():
        out_ref[pl.ds(0, size)] = low(dot(l_ref[...], q_ref[...]))

    @pl.when(jnp.logical_not(below))
    def _():
        out_ref[pl.ds(0, size)] = s_ref[...]

    listed = rows_ref[0, 0, 0, 0]
    there = below & (counts_ref[0, 0, 0] > 0)
    done = at(FIRST) | at(MAKER[1]) | at(BESIDE) | at(MAKER[2])
    first = (there & (listed == 0)) | done
    second = there & (listed == 1)
    ids = lax.broadcasted_iota(jnp.int32, (TAIL, out_ref.shape[1]), 0)
    flag = ((ids == 0) & first) | ((ids == 1) & second)
    out_ref[pl.ds(size, TAIL)] = low(jnp.where(flag, 1.0, 0.0))


def solved_kernel(q_ref, rest_ref, solved_ref):
    came = any_of(REST)

    @pl.when(came)
    def _():
        solved_ref[...] = rest_ref[...].astype(jnp.float32)

    @pl.when(jnp.logical_not(came))
    def _():
        solved_ref[...] = q_ref[...].astype(jnp.float32)


def final_kernel(rhs_ref, *refs):
    sums, out_ref = refs[:NC], refs[NC]
    size = out_ref.shape[1]
    for i in range(out_ref.shape[0]):
        acc = rhs_ref[i]
        for s in sums:
            keep = s[pl.ds(size, TAIL)].astype(jnp.float32)[i : i + 1] > 0.5
            acc = acc - jnp.where(keep, s[pl.ds(0, size)].astype(jnp.float32), 0.0)
        out_ref[i] = acc


def on_device_8x4(rhs, diag_inv, blocks, block_rows, counts):
    size, width = rhs.shape[2:]
    part = size // NR
    rhs = rhs[:, 0]
    block = blocks[0, 0, 0, 0]
    bf16 = jnp.bfloat16
    vec = jax.ShapeDtypeStruct((size, width), bf16)
    dma = pltpu.SemaphoreType.DMA

    wides = [pair_width(m, part) for m in range(NR // 2)]
    cuts = call(
        cut_kernel, [jax.ShapeDtypeStruct((part, w), bf16) for w in wides], [diag_inv], [HBM], [ANY] * len(wides), [dma]
    )
    at_piece = {r: (0, c) for c, rows in enumerate(PIECES) for r in rows}
    parts = []
    for m, cut in enumerate(cuts):
        pairs = []
        for r in range(1, NR):
            for c, k in enumerate(SENDS[r]):
                if k == 0 and max(r // 2, 1) == m:
                    pairs.append(((r, c), at_piece[r]))
                if k and MAKER[k][0] != r and r // 2 == m:
                    pairs.append(((r, c), MAKER[k] if r % 2 else PARTNER[k]))
        parts.append(send_only(cut, pairs))
    q = call(
        first_kernel,
        jax.ShapeDtypeStruct((2 * part, width), bf16),
        [rhs, diag_inv, *parts[1:]],
        [HBM, HBM] + [ANY] * (len(wides) - 1),
        VMEM,
        [
            pltpu.VMEM((size, width), jnp.float32),
            pltpu.VMEM((2, part, size), bf16),
            dma,
            pltpu.SemaphoreType.DMA((2,)),
        ],
    )
    takers = (FIRST, (2, 0), (3, 0))
    got = [send(q, [((0, c), takers[(c + j) % 4]) for c in range(4) if (c + j) % 4 < 3]) for j in range(4)]
    even = call(
        pack_kernel,
        jax.ShapeDtypeStruct((part, sum(wides[1:])), bf16),
        parts[1:],
        [ANY] * (len(wides) - 1),
        VMEM,
        [pltpu.SemaphoreType.DMA((len(wides) - 1,))],
    )
    even = send(even, [(PARTNER[k], MAKER[k]) for k in range(1, NC)])
    top, _ = lax.optimization_barrier((cuts[0], q))
    top = send(top, [((0, k), MAKER[k]) for k in range(1, NC)])
    diag = call(
        whole_kernel,
        jax.ShapeDtypeStruct((size, size), bf16),
        [diag_inv, top, even, *parts],
        [HBM] + [ANY] * (2 + len(wides)),
        VMEM,
        [pltpu.SemaphoreType.DMA((NR,))],
    )

    p, q, s = call(step0_kernel, [vec] * 3, [*got, rhs, block], [VMEM] * 6, [VMEM] * 3)
    p_in = send(p, [(FIRST, MAKER[1])])
    sums = send(s, [((2, 0), MAKER[1]), ((3, 0), BESIDE)])
    p, q, s = call(step1_kernel, [vec] * 3, [p_in, sums, rhs, diag, block, q, s], [VMEM] * 7, [VMEM] * 3)
    p_in = send(p, [(MAKER[1], MAKER[2])])
    q_in = send(q, [(MAKER[1], BESIDE)])

    came = send(q, [((2, 0), (4, 0)), ((3, 0), (5, 0)), ((1, 0), (0, 0)), ((2, 1), (4, 1))])
    took = [(4, 0), (5, 0), (0, 0), (4, 1)]
    p_in, came = lax.optimization_barrier((p_in, came))

    a, q, s = call(step2_kernel, [vec] * 3, [p_in, q_in, sums, rhs, diag, block, q, s], [VMEM] * 8, [VMEM] * 3)
    sums = send(s, [(MAKER[2], MAKER[3])])
    q_2 = a
    a = send_only(a, [(BESIDE, MAKER[3]), (MAKER[2], (2, 2))])
    q_2 = send_only(q_2, [(MAKER[2], (7, 2))])
    q = call(
        functools.partial(step3_kernel, [[(2, 2)], [(7, 2)], took]),
        vec,
        [sums, a, q_2, came, diag, q],
        [VMEM] * 6,
        VMEM,
        [pltpu.VMEM((size, width), bf16)],
    )

    sends = [[(MAKER[3], (r, 3))] for r in (6, 7, 4)]
    got = [send(q, pairs) for pairs in sends]
    sends += [
        [
            (MAKER[3], (3, 3)), ((2, 2), (6, 2)), (MAKER[2], (5, 2)),
            ((4, 0), (6, 0)), ((5, 0), (7, 0)), ((4, 1), (6, 1)), ((3, 1), (5, 1)), ((2, 1), (0, 1)),
        ],
        [((2, 2), (4, 2)), (MAKER[2], (1, 2)), ((4, 1), (7, 1)), ((3, 1), (1, 1))],
    ]
    got += [send_only(q, pairs) for pairs in sends[3:]]
    takers = [[b for _, b in pairs] for pairs in sends]
    q, mine = call(
        functools.partial(update_kernel, takers),
        [vec, jax.ShapeDtypeStruct((size + TAIL, width), bf16)],
        [block_rows, counts, s, block, q, *got],
        [SMEM] * 2 + [VMEM] * (3 + len(got)),
        [VMEM] * 2,
    )

    def swap(value, step):
        return send(value, [((r, c), (r, c ^ step)) for r in range(NR) for c in range(NC)])

    across = swap(mine, 2)
    rest = send_only(q, list(zip(((3, 3), (6, 3), (7, 3), (2, 2)), REST)))
    solved = call(solved_kernel, jax.ShapeDtypeStruct((size, width), jnp.float32), [q, rest], [VMEM] * 2, VMEM)
    beside, across, solved = lax.optimization_barrier((mine, across, solved))
    beside = swap(beside, 1)
    corner = swap(across, 1)
    remainder = call(
        final_kernel,
        jax.ShapeDtypeStruct(rhs.shape, jnp.float32),
        [rhs, mine, beside, across, corner],
        [VMEM] * 5,
        VMEM,
    )
    return solved[None, None], remainder[:, None]


def solution(mesh):
    in_specs = (
        P(None, "row", None, None),
        P(None, "row", None),
        P(None, "col", "row", None, None, None),
        P(None, "col", "row", None),
        P(None, "col", "row"),
    )
    out_specs = (P(None, "col", None, None), P(None, "row", None, None))
    small = mesh.shape["row"] == NR and mesh.shape["col"] == NC
    return jax.shard_map(
        on_device_8x4 if small else on_device_any,
        mesh=mesh,
        in_specs=in_specs,
        out_specs=out_specs,
        check_vma=False,
    )
```

```python
import functools

import jax
import jax.numpy as jnp
from jax import lax
from jax.experimental import pallas as pl
from jax.experimental.pallas import tpu as pltpu
from jax.sharding import PartitionSpec as P

VMEM = pl.BlockSpec(memory_space=pltpu.VMEM)
ANY = pl.BlockSpec(memory_space=pl.ANY)
HBM = pl.BlockSpec(memory_space=pltpu.HBM)
SMEM = pl.BlockSpec(memory_space=pltpu.SMEM)
TAIL = 16


def broadcast(value, axis, root):
    mine = lax.axis_index(axis) == root
    return lax.psum(jnp.where(mine, value, jnp.zeros_like(value)), axis)


def on_device_any(rhs, diag_inv, blocks, block_rows, counts):
    nrow = lax.axis_size("row")
    ncol = lax.axis_size("col")
    my_row = lax.axis_index("row")
    my_col = lax.axis_index("col")
    kc = diag_inv.shape[0]
    rb_local = rhs.shape[0]
    nz_local = blocks.shape[3]
    local_rhs = rhs[:, 0]
    partial_value = jnp.zeros(local_rhs.shape, jnp.float32)
    solved_list = [jnp.zeros(local_rhs.shape[1:], jnp.float32)]
    slot_ids = jnp.arange(nz_local, dtype=jnp.int32)
    local_ids = jnp.arange(rb_local, dtype=jnp.int32)
    for k in range(kc):
        j = k // ncol
        owner_row = k % nrow
        local_pivot = k // nrow
        mine_row = my_row == owner_row
        mine_col = my_col == k % ncol
        pivot_part = jnp.where(mine_row, partial_value[local_pivot], jnp.float32(0.0))
        summed = lax.psum(pivot_part, "col")
        updated = (local_rhs[local_pivot] - summed).astype(jnp.bfloat16)
        pivot_bf = broadcast(updated, "row", owner_row)
        row_part = jnp.dot(diag_inv[k], pivot_bf, preferred_element_type=jnp.float32)
        sol = lax.all_gather(row_part, "row", axis=0, tiled=True)
        sol_bf = sol.astype(jnp.bfloat16)
        rows = block_rows[j, 0, 0]
        glob = rows * nrow + my_row
        valid = (slot_ids < counts[j, 0, 0]) & (glob > k) & mine_col
        weights = (valid[:, None] & (rows[:, None] == local_ids[None, :])).astype(jnp.float32)
        contrib = jnp.einsum(
            "sab,bn->san", blocks[j, 0, 0], sol_bf, preferred_element_type=jnp.float32
        )
        partial_value = partial_value + jnp.einsum(
            "sl,san->lan", weights, contrib, precision=lax.Precision.HIGHEST
        )
        solved_list[j] = jnp.where(mine_col, sol, solved_list[j])
    total = lax.psum(partial_value, "col")
    remainder = (local_rhs - total)[:, None]
    solved = jnp.stack(solved_list)[:, None]
    return (solved, remainder)


NR, NC = 8, 4
MAKER = (None, (2, 1), (3, 2), (5, 3))
FIRST = (1, 0)
BESIDE = (3, 1)
PARTNER = (None, (3, 1), (3, 3), (5, 2))
PIECES = ((4, 1), (6, 3), (5, 2), (7, 0))
SENDS = (
    (0, 1, 2, 3),
    (0, 1, 2, 3),
    (3, 1, 0, 2),
    (0, 1, 3, 2),
    (0, 1, 3, 2),
    (2, 1, 3, 0),
    (0, 3, 1, 2),
    (1, 3, 0, 2),
)
REST = ((2, 3), (0, 3), (0, 2), (1, 2))


def hops(a, b):
    d = a ^ b
    if d < 2:
        return 1 if d else 10000
    return 100 + abs((a >> 3) - (b >> 3)) + ((d >> 2) & 1) + ((d >> 1) & 1)


def complete(pairs):
    to = {a * NC + b: c * NC + d for (a, b), (c, d) in pairs}
    free_from = [i for i in range(NR * NC) if i not in to]
    free_to = [i for i in range(NR * NC) if i not in to.values()]
    n = len(free_from)
    u, v, match = [0] * (n + 1), [0] * (n + 1), [0] * (n + 1)
    for i in range(1, n + 1):
        match[0], j0 = i, 0
        least, way, used = [10**9] * (n + 1), [0] * (n + 1), [False] * (n + 1)
        while True:
            used[j0] = True
            i0, delta, j1 = match[j0], 10**9, 0
            for j in range(1, n + 1):
                if not used[j]:
                    cur = hops(free_from[i0 - 1], free_to[j - 1]) - u[i0] - v[j]
                    if cur < least[j]:
                        least[j], way[j] = cur, j0
                    if least[j] < delta:
                        delta, j1 = least[j], j
            for j in range(n + 1):
                if used[j]:
                    u[match[j]] += delta
                    v[j] -= delta
                else:
                    least[j] -= delta
            j0 = j1
            if match[j0] == 0:
                break
        while j0:
            j1 = way[j0]
            match[j0] = match[j1]
            j0 = j1
    for j in range(1, n + 1):
        to[free_from[match[j] - 1]] = free_to[j - 1]
    return [(divmod(a, NC), divmod(b, NC)) for a, b in sorted(to.items())]


def send(value, pairs):
    return lax.ppermute(value, ("row", "col"), [(a * NC + b, c * NC + d) for (a, b), (c, d) in complete(pairs)])


def send_only(value, pairs):
    return lax.ppermute(value, ("row", "col"), [(a * NC + b, c * NC + d) for (a, b), (c, d) in pairs])


def dot(a, b):
    return jnp.dot(a, b, preferred_element_type=jnp.float32)


def low(a):
    return a.astype(jnp.bfloat16)


def at(device):
    return (lax.axis_index("row") == device[0]) & (lax.axis_index("col") == device[1])


def any_of(devices):
    flag = at(devices[0])
    for d in devices[1:]:
        flag = flag | at(d)
    return flag


def call(kernel, outs, ins, in_specs, out_specs, scratch=(), limit=16):
    return pl.pallas_call(
        kernel,
        out_shape=outs,
        in_specs=in_specs,
        out_specs=out_specs,
        scratch_shapes=list(scratch),
        compiler_params=pltpu.CompilerParams(vmem_limit_bytes=limit << 20),
        name=kernel.func.__name__ if isinstance(kernel, functools.partial) else kernel.__name__,
    )(*ins)


def pair_width(m, part):
    return 2 * (m + 1) * part


def cut_kernel(diag_ref, *refs):
    cuts, sem = refs[:-1], refs[-1]
    row, col = lax.axis_index("row"), lax.axis_index("col")
    part = diag_ref.shape[1]
    k = jnp.int32(0)
    for r in range(NR):
        for c in range(NC):
            k = jnp.where((row == r) & (col == c), SENDS[r][c], k)
    for m in range(NR // 2):

        @pl.when(jnp.where((row == 1) & (k == 0), 1, row // 2) == m)
        def _():
            copy = pltpu.make_async_copy(diag_ref.at[k, :, pl.ds(0, pair_width(m, part))], cuts[m], sem)
            copy.start()
            copy.wait()


def first_kernel(rhs_ref, diag_ref, *refs):
    parts, (out_ref, rhs_v, d_v, rhs_sem, d_sem) = refs[:-5], refs[-5:]
    n = out_ref.shape[0] // 2
    col = lax.axis_index("col")

    @pl.when(lax.axis_index("row") == 0)
    def _():
        rhs_copy = pltpu.make_async_copy(rhs_ref.at[0], rhs_v, rhs_sem)
        rhs_copy.start()

        def pieces(c):
            copies = []
            for i, r in enumerate(PIECES[c]):
                m = max(r // 2, 1)
                wide = pair_width(m, n)
                source = parts[m - 1] if r else diag_ref.at[0, :, pl.ds(0, wide)]
                copies.append(pltpu.make_async_copy(source, d_v.at[i, :, pl.ds(0, wide)], d_sem.at[i]))
            return copies

        for c in range(NC):

            @pl.when(col == c)
            def _():
                for copy in pieces(c):
                    copy.start()

        rhs_copy.wait()
        p = low(rhs_v[...])
        for c in range(NC):

            @pl.when(col == c)
            def _():
                for i, copy in enumerate(pieces(c)):
                    copy.wait()
                    wide = pair_width(max(PIECES[c][i] // 2, 1), n)
                    out_ref[i * n : (i + 1) * n] = low(dot(d_v[i, :, :wide], p[:wide]))


def pack_kernel(*refs):
    parts, out_ref, sem = refs[1:-2], refs[-2], refs[-1]

    @pl.when(any_of(PARTNER[1:]))
    def _():
        copies, left = [], 0
        for m, source in enumerate(parts):
            wide = source.shape[1]
            copies.append(pltpu.make_async_copy(source, out_ref.at[:, pl.ds(left, wide)], sem.at[m]))
            left += wide
        for copy in copies:
            copy.start()
        for copy in copies:
            copy.wait()


def whole_kernel(diag_ref, top_ref, even_ref, *refs):
    odd, out_ref, sem = refs[:-2], refs[-2], refs[-1]
    size = out_ref.shape[0]
    part = size // NR
    row, col = lax.axis_index("row"), lax.axis_index("col")

    @pl.when(any_of(MAKER[1:]))
    def _():
        def copy(i, source):
            wide = pair_width(i // 2, part)
            return pltpu.make_async_copy(source, out_ref.at[pl.ds(i * part, part), pl.ds(0, wide)], sem.at[i])

        left = 0
        for i in range(NR):
            wide = pair_width(i // 2, part)
            if i % 2:
                source = odd[i // 2]
            elif i:
                source = even_ref.at[:, pl.ds(left, wide)]
                left += wide
            else:
                source = top_ref

            @pl.when(row == i)
            def _():
                copy(i, diag_ref.at[col, :, pl.ds(0, wide)]).start()

            @pl.when(row != i)
            def _():
                copy(i, source).start()

        for m in range(NR // 2 - 1):
            right = pair_width(m, part)
            out_ref[pl.ds(2 * m * part, 2 * part), pl.ds(right, size - right)] = jnp.zeros(
                (2 * part, size - right), out_ref.dtype
            )
        for i in range(NR):
            copy(i, odd[i // 2]).wait()


def lower_dot(q_ref, d_ref, p_ref):
    half = d_ref.shape[0] // 2
    q_ref[:half] = low(dot(d_ref[:half, :half], p_ref[:half]))
    q_ref[half:] = low(dot(d_ref[half:], p_ref[...]))


def step0_kernel(g0, g1, g2, g3, rhs_ref, l_ref, p_ref, q_ref, s_ref):
    part = l_ref.shape[0] // NR
    row = lax.axis_index("row")

    def lookup(c, i):
        r = jnp.int32(PIECES[0][i])
        for n in range(1, NC):
            r = jnp.where(c == n, PIECES[n][i], r)
        return pl.multiple_of(r * part, part)

    @pl.when((row >= 1) & (row < 4) & (lax.axis_index("col") == 0))
    def _():
        for j, got in enumerate((g0, g1, g2, g3)):
            src = lax.rem(row + 7 - j, 4)
            q_ref[pl.ds(lookup(src, 0), part)] = got[:part]
            q_ref[pl.ds(lookup(src, 1), part)] = got[part:]
        s = dot(l_ref[...], q_ref[...])
        s_ref[...] = low(s)
        p_ref[...] = low(rhs_ref[0] - s)


def step1_kernel(p_in, d_ref, q_prev, q_ref):
    active = at(MAKER[1])

    @pl.when(active)
    def _():
        lower_dot(q_ref, d_ref, p_in)

    @pl.when(jnp.logical_not(active))
    def _():
        q_ref[...] = q_prev[...]


def step1_sum_kernel(q_in, sum_ref, rhs_ref, l_ref, s_prev, p_ref, s_ref):
    active = at(MAKER[1])

    @pl.when(active)
    def _():
        s = dot(l_ref[...], q_in[...]) + sum_ref[...].astype(jnp.float32)
        s_ref[...] = low(s)
        p_ref[...] = low(rhs_ref[0] - s)

    @pl.when(jnp.logical_not(active))
    def _():
        s_ref[...] = s_prev[...]


def step2_kernel(p_in, q_in, sum_ref, rhs_ref, d_ref, l_ref, q_prev, s_prev, a_ref, q_ref, s_ref):
    active, beside = at(MAKER[2]), at(BESIDE)

    @pl.when(active)
    def _():
        lower_dot(q_ref, d_ref, p_in)
        a_ref[...] = q_ref[...]
        s_ref[...] = low(dot(l_ref[...], q_ref[...]))

    @pl.when(beside)
    def _():
        q_ref[...] = q_in[...]
        s = dot(l_ref[...], q_in[...]) + sum_ref[...].astype(jnp.float32)
        s_ref[...] = low(s)
        a_ref[...] = low(rhs_ref[0] - s)

    @pl.when(jnp.logical_not(active | beside))
    def _():
        q_ref[...] = q_prev[...]
        s_ref[...] = s_prev[...]


def step3_kernel(takers, sum_ref, a_ref, *refs):
    came, (d_ref, q_prev, q_ref, p_v) = refs[:-4], refs[-4:]
    active = at(MAKER[3])

    @pl.when(active)
    def _():
        p_v[...] = low(a_ref[...].astype(jnp.float32) - sum_ref[...].astype(jnp.float32))
        lower_dot(q_ref, d_ref, p_v)

    for devices, source in zip(takers, (a_ref, *came)):

        @pl.when(any_of(devices))
        def _():
            q_ref[...] = source[...]

    @pl.when(jnp.logical_not(active | any_of([d for devices in takers for d in devices])))
    def _():
        q_ref[...] = q_prev[...]


def update_kernel(takers, rows_ref, counts_ref, s_ref, l_ref, q_prev, *refs):
    got, q_ref, out_ref = refs[:-2], refs[-2], refs[-1]
    size = l_ref.shape[0]
    row, col = lax.axis_index("row"), lax.axis_index("col")
    below = row >= NC

    def take(flag, source):
        @pl.when(flag)
        def _():
            q_ref[...] = source[...]

    kept = jnp.logical_not(any_of([d for devices in takers for d in devices]))
    take(kept, q_prev)
    for devices, source in zip(takers, got):
        take(any_of(devices), source)

    @pl.when(below)
    def _():
        out_ref[pl.ds(0, size)] = low(dot(l_ref[...], q_ref[...]))

    @pl.when(jnp.logical_not(below))
    def _():
        out_ref[pl.ds(0, size)] = s_ref[...]

    listed = rows_ref[0, 0, 0, 0]
    there = below & (counts_ref[0, 0, 0] > 0)
    done = at(FIRST) | at(MAKER[1]) | at(BESIDE) | at(MAKER[2])
    first = (there & (listed == 0)) | done
    second = there & (listed == 1)
    ids = lax.broadcasted_iota(jnp.int32, (TAIL, out_ref.shape[1]), 0)
    flag = ((ids == 0) & first) | ((ids == 1) & second)
    out_ref[pl.ds(size, TAIL)] = low(jnp.where(flag, 1.0, 0.0))


def solved_kernel(q_ref, rest_ref, solved_ref):
    came = any_of(REST)

    @pl.when(came)
    def _():
        solved_ref[...] = rest_ref[...].astype(jnp.float32)

    @pl.when(jnp.logical_not(came))
    def _():
        solved_ref[...] = q_ref[...].astype(jnp.float32)


def final_kernel(rhs_ref, *refs):
    sums, out_ref = refs[:NC], refs[NC]
    size = out_ref.shape[1]
    for i in range(out_ref.shape[0]):
        acc = rhs_ref[i]
        for s in sums:
            keep = s[pl.ds(size, TAIL)].astype(jnp.float32)[i : i + 1] > 0.5
            acc = acc - jnp.where(keep, s[pl.ds(0, size)].astype(jnp.float32), 0.0)
        out_ref[i] = acc


def on_device_8x4(rhs, diag_inv, blocks, block_rows, counts):
    size, width = rhs.shape[2:]
    part = size // NR
    rhs = rhs[:, 0]
    block = blocks[0, 0, 0, 0]
    bf16 = jnp.bfloat16
    vec = jax.ShapeDtypeStruct((size, width), bf16)
    dma = pltpu.SemaphoreType.DMA

    wides = [pair_width(m, part) for m in range(NR // 2)]
    cuts = call(
        cut_kernel, [jax.ShapeDtypeStruct((part, w), bf16) for w in wides], [diag_inv], [HBM], [ANY] * len(wides), [dma]
    )
    at_piece = {r: (0, c) for c, rows in enumerate(PIECES) for r in rows}
    parts = []
    for m, cut in enumerate(cuts):
        pairs = []
        for r in range(1, NR):
            for c, k in enumerate(SENDS[r]):
                if k == 0 and max(r // 2, 1) == m:
                    pairs.append(((r, c), at_piece[r]))
                if k and MAKER[k][0] != r and r // 2 == m:
                    pairs.append(((r, c), MAKER[k] if r % 2 else PARTNER[k]))
        parts.append(send_only(cut, pairs))
    q = call(
        first_kernel,
        jax.ShapeDtypeStruct((2 * part, width), bf16),
        [rhs, diag_inv, *parts[1:]],
        [HBM, HBM] + [ANY] * (len(wides) - 1),
        VMEM,
        [
            pltpu.VMEM((size, width), jnp.float32),
            pltpu.VMEM((2, part, size), bf16),
            dma,
            pltpu.SemaphoreType.DMA((2,)),
        ],
    )
    takers = (FIRST, (2, 0), (3, 0))
    got = [send(q, [((0, c), takers[(c + j) % 4]) for c in range(4) if (c + j) % 4 < 3]) for j in range(4)]
    even = call(
        pack_kernel,
        jax.ShapeDtypeStruct((part, sum(wides[1:])), bf16),
        parts,
        [ANY] * len(wides),
        VMEM,
        [pltpu.SemaphoreType.DMA((len(wides) - 1,))],
    )
    even = send(even, [(PARTNER[k], MAKER[k]) for k in range(1, NC)])
    top, _ = lax.optimization_barrier((cuts[0], q))
    top = send(top, [((0, k), MAKER[k]) for k in range(1, NC)])
    diag = call(
        whole_kernel,
        jax.ShapeDtypeStruct((size, size), bf16),
        [diag_inv, top, even, *parts],
        [HBM] + [ANY] * (2 + len(wides)),
        VMEM,
        [pltpu.SemaphoreType.DMA((NR,))],
    )

    p, q, s = call(step0_kernel, [vec] * 3, [*got, rhs, block], [VMEM] * 6, [VMEM] * 3)
    p_in = send(p, [(FIRST, MAKER[1])])
    sums = send(s, [((2, 0), MAKER[1]), ((3, 0), BESIDE)])
    q = call(step1_kernel, vec, [p_in, diag, q], [VMEM] * 3, VMEM)
    p, s = call(step1_sum_kernel, [vec] * 2, [q, sums, rhs, block, s], [VMEM] * 5, [VMEM] * 2)
    p_in = send(p, [(MAKER[1], MAKER[2])])
    q_in = send(q, [(MAKER[1], BESIDE)])

    came = send(q, [((2, 0), (4, 0)), ((3, 0), (5, 0)), ((1, 0), (0, 0)), ((2, 1), (4, 1))])
    took = [(4, 0), (5, 0), (0, 0), (4, 1)]
    p_in, came = lax.optimization_barrier((p_in, came))

    a, q, s = call(step2_kernel, [vec] * 3, [p_in, q_in, sums, rhs, diag, block, q, s], [VMEM] * 8, [VMEM] * 3)
    sums = send(s, [(MAKER[2], MAKER[3])])
    a = send_only(a, [(BESIDE, MAKER[3]), (MAKER[2], (2, 2))])
    q = call(
        functools.partial(step3_kernel, [[(2, 2)], took]),
        vec,
        [sums, a, came, diag, q],
        [VMEM] * 5,
        VMEM,
        [pltpu.VMEM((size, width), bf16)],
    )

    sends = [[(MAKER[3], (r, 3))] for r in (6, 7, 4)]
    got = [send(q, pairs) for pairs in sends]
    sends += [
        [
            (MAKER[3], (3, 3)), ((2, 2), (6, 2)), (MAKER[2], (7, 2)),
            ((4, 0), (6, 0)), ((5, 0), (7, 0)), ((4, 1), (6, 1)), ((3, 1), (5, 1)), ((2, 1), (0, 1)),
        ],
        [(MAKER[3], (1, 3)), ((2, 2), (4, 2)), (MAKER[2], (5, 2)), ((4, 1), (7, 1)), ((3, 1), (1, 1))],
    ]
    got += [send_only(q, pairs) for pairs in sends[3:]]
    takers = [[b for _, b in pairs] for pairs in sends]
    q, mine = call(
        functools.partial(update_kernel, takers),
        [vec, jax.ShapeDtypeStruct((size + TAIL, width), bf16)],
        [block_rows, counts, s, block, q, *got],
        [SMEM] * 2 + [VMEM] * (3 + len(got)),
        [VMEM] * 2,
    )

    def swap(value, step):
        return send(value, [((r, c), (r, c ^ step)) for r in range(NR) for c in range(NC)])

    across = swap(mine, 2)
    rest = send_only(q, list(zip(((3, 3), (1, 3), (2, 2), MAKER[2]), REST)))
    solved = call(solved_kernel, jax.ShapeDtypeStruct((size, width), jnp.float32), [q, rest], [VMEM] * 2, VMEM)
    beside, across, solved = lax.optimization_barrier((mine, across, solved))
    beside = swap(beside, 1)
    corner = swap(across, 1)
    remainder = call(
        final_kernel,
        jax.ShapeDtypeStruct(rhs.shape, jnp.float32),
        [rhs, mine, beside, across, corner],
        [VMEM] * 5,
        VMEM,
    )
    return solved[None, None], remainder[:, None]


def solution(mesh):
    in_specs = (
        P(None, "row", None, None),
        P(None, "row", None),
        P(None, "col", "row", None, None, None),
        P(None, "col", "row", None),
        P(None, "col", "row"),
    )
    out_specs = (P(None, "col", None, None), P(None, "row", None, None))
    small = mesh.shape["row"] == NR and mesh.shape["col"] == NC
    return jax.shard_map(
        on_device_8x4 if small else on_device_any,
        mesh=mesh,
        in_specs=in_specs,
        out_specs=out_specs,
        check_vma=False,
    )
```

```python
import functools

import jax
import jax.numpy as jnp
from jax import lax
from jax.experimental import pallas as pl
from jax.experimental.pallas import tpu as pltpu
from jax.sharding import PartitionSpec as P

VMEM = pl.BlockSpec(memory_space=pltpu.VMEM)
ANY = pl.BlockSpec(memory_space=pl.ANY)
HBM = pl.BlockSpec(memory_space=pltpu.HBM)
SMEM = pl.BlockSpec(memory_space=pltpu.SMEM)
TAIL = 16


def broadcast(value, axis, root):
    mine = lax.axis_index(axis) == root
    return lax.psum(jnp.where(mine, value, jnp.zeros_like(value)), axis)


def on_device_any(rhs, diag_inv, blocks, block_rows, counts):
    nrow = lax.axis_size("row")
    ncol = lax.axis_size("col")
    my_row = lax.axis_index("row")
    my_col = lax.axis_index("col")
    kc = diag_inv.shape[0]
    rb_local = rhs.shape[0]
    nz_local = blocks.shape[3]
    local_rhs = rhs[:, 0]
    partial_value = jnp.zeros(local_rhs.shape, jnp.float32)
    solved_list = [jnp.zeros(local_rhs.shape[1:], jnp.float32)]
    slot_ids = jnp.arange(nz_local, dtype=jnp.int32)
    local_ids = jnp.arange(rb_local, dtype=jnp.int32)
    for k in range(kc):
        j = k // ncol
        owner_row = k % nrow
        local_pivot = k // nrow
        mine_row = my_row == owner_row
        mine_col = my_col == k % ncol
        pivot_part = jnp.where(mine_row, partial_value[local_pivot], jnp.float32(0.0))
        summed = lax.psum(pivot_part, "col")
        updated = (local_rhs[local_pivot] - summed).astype(jnp.bfloat16)
        pivot_bf = broadcast(updated, "row", owner_row)
        row_part = jnp.dot(diag_inv[k], pivot_bf, preferred_element_type=jnp.float32)
        sol = lax.all_gather(row_part, "row", axis=0, tiled=True)
        sol_bf = sol.astype(jnp.bfloat16)
        rows = block_rows[j, 0, 0]
        glob = rows * nrow + my_row
        valid = (slot_ids < counts[j, 0, 0]) & (glob > k) & mine_col
        weights = (valid[:, None] & (rows[:, None] == local_ids[None, :])).astype(jnp.float32)
        contrib = jnp.einsum(
            "sab,bn->san", blocks[j, 0, 0], sol_bf, preferred_element_type=jnp.float32
        )
        partial_value = partial_value + jnp.einsum(
            "sl,san->lan", weights, contrib, precision=lax.Precision.HIGHEST
        )
        solved_list[j] = jnp.where(mine_col, sol, solved_list[j])
    total = lax.psum(partial_value, "col")
    remainder = (local_rhs - total)[:, None]
    solved = jnp.stack(solved_list)[:, None]
    return (solved, remainder)


NR, NC = 8, 4
MAKER = (None, (2, 1), (3, 2), (5, 3))
FIRST = (1, 0)
BESIDE = (3, 1)
PARTNER = (None, (3, 1), (3, 3), (5, 2))
PIECES = ((4, 1), (6, 3), (5, 2), (7, 0))
SENDS = (
    (0, 1, 2, 3),
    (0, 1, 2, 3),
    (3, 1, 0, 2),
    (0, 1, 3, 2),
    (0, 1, 3, 2),
    (2, 1, 3, 0),
    (0, 3, 1, 2),
    (1, 3, 0, 2),
)
REST = ((2, 3), (0, 3), (1, 3), (0, 2))


def hops(a, b):
    d = a ^ b
    if d < 2:
        return 1 if d else 10000
    return 100 + abs((a >> 3) - (b >> 3)) + ((d >> 2) & 1) + ((d >> 1) & 1)


def complete(pairs):
    to = {a * NC + b: c * NC + d for (a, b), (c, d) in pairs}
    free_from = [i for i in range(NR * NC) if i not in to]
    free_to = [i for i in range(NR * NC) if i not in to.values()]
    n = len(free_from)
    u, v, match = [0] * (n + 1), [0] * (n + 1), [0] * (n + 1)
    for i in range(1, n + 1):
        match[0], j0 = i, 0
        least, way, used = [10**9] * (n + 1), [0] * (n + 1), [False] * (n + 1)
        while True:
            used[j0] = True
            i0, delta, j1 = match[j0], 10**9, 0
            for j in range(1, n + 1):
                if not used[j]:
                    cur = hops(free_from[i0 - 1], free_to[j - 1]) - u[i0] - v[j]
                    if cur < least[j]:
                        least[j], way[j] = cur, j0
                    if least[j] < delta:
                        delta, j1 = least[j], j
            for j in range(n + 1):
                if used[j]:
                    u[match[j]] += delta
                    v[j] -= delta
                else:
                    least[j] -= delta
            j0 = j1
            if match[j0] == 0:
                break
        while j0:
            j1 = way[j0]
            match[j0] = match[j1]
            j0 = j1
    for j in range(1, n + 1):
        to[free_from[match[j] - 1]] = free_to[j - 1]
    return [(divmod(a, NC), divmod(b, NC)) for a, b in sorted(to.items())]


def send(value, pairs):
    return lax.ppermute(value, ("row", "col"), [(a * NC + b, c * NC + d) for (a, b), (c, d) in complete(pairs)])


def send_only(value, pairs):
    return lax.ppermute(value, ("row", "col"), [(a * NC + b, c * NC + d) for (a, b), (c, d) in pairs])


def dot(a, b):
    return jnp.dot(a, b, preferred_element_type=jnp.float32)


def low(a):
    return a.astype(jnp.bfloat16)


def at(device):
    return (lax.axis_index("row") == device[0]) & (lax.axis_index("col") == device[1])


def any_of(devices):
    flag = at(devices[0])
    for d in devices[1:]:
        flag = flag | at(d)
    return flag


def call(kernel, outs, ins, in_specs, out_specs, scratch=(), limit=16):
    return pl.pallas_call(
        kernel,
        out_shape=outs,
        in_specs=in_specs,
        out_specs=out_specs,
        scratch_shapes=list(scratch),
        compiler_params=pltpu.CompilerParams(vmem_limit_bytes=limit << 20),
        name=kernel.func.__name__ if isinstance(kernel, functools.partial) else kernel.__name__,
    )(*ins)


def pair_width(m, part):
    return 2 * (m + 1) * part


def cut_kernel(diag_ref, *refs):
    cuts, sem = refs[:-1], refs[-1]
    row, col = lax.axis_index("row"), lax.axis_index("col")
    part = diag_ref.shape[1]
    k = jnp.int32(0)
    for r in range(NR):
        for c in range(NC):
            k = jnp.where((row == r) & (col == c), SENDS[r][c], k)
    for m in range(NR // 2):

        @pl.when(jnp.where((row == 1) & (k == 0), 1, row // 2) == m)
        def _():
            copy = pltpu.make_async_copy(diag_ref.at[k, :, pl.ds(0, pair_width(m, part))], cuts[m], sem)
            copy.start()
            copy.wait()


def first_kernel(rhs_ref, diag_ref, *refs):
    parts, (out_ref, rhs_v, d_v, rhs_sem, d_sem) = refs[:-5], refs[-5:]
    n = out_ref.shape[0] // 2
    col = lax.axis_index("col")

    @pl.when(lax.axis_index("row") == 0)
    def _():
        rhs_copy = pltpu.make_async_copy(rhs_ref.at[0], rhs_v, rhs_sem)
        rhs_copy.start()

        def pieces(c):
            copies = []
            for i, r in enumerate(PIECES[c]):
                m = max(r // 2, 1)
                wide = pair_width(m, n)
                source = parts[m - 1] if r else diag_ref.at[0, :, pl.ds(0, wide)]
                copies.append(pltpu.make_async_copy(source, d_v.at[i, :, pl.ds(0, wide)], d_sem.at[i]))
            return copies

        for c in range(NC):

            @pl.when(col == c)
            def _():
                for copy in pieces(c):
                    copy.start()

        rhs_copy.wait()
        p = low(rhs_v[...])
        for c in range(NC):

            @pl.when(col == c)
            def _():
                for i, copy in enumerate(pieces(c)):
                    copy.wait()
                    wide = pair_width(max(PIECES[c][i] // 2, 1), n)
                    out_ref[i * n : (i + 1) * n] = low(dot(d_v[i, :, :wide], p[:wide]))


def pack_kernel(*refs):
    parts, out_ref, sem = refs[:-2], refs[-2], refs[-1]

    @pl.when(any_of(PARTNER[1:]))
    def _():
        copies, left = [], 0
        for m, source in enumerate(parts):
            wide = source.shape[1]
            copies.append(pltpu.make_async_copy(source, out_ref.at[:, pl.ds(left, wide)], sem.at[m]))
            left += wide
        for copy in copies:
            copy.start()
        for copy in copies:
            copy.wait()


def whole_kernel(diag_ref, even_ref, *refs):
    odd, out_ref, sem = refs[:-2], refs[-2], refs[-1]
    size = out_ref.shape[0]
    part = size // NR
    row, col = lax.axis_index("row"), lax.axis_index("col")

    @pl.when(any_of(MAKER[1:]))
    def _():
        def copy(i, source):
            wide = pair_width(i // 2, part)
            return pltpu.make_async_copy(source, out_ref.at[pl.ds(i * part, part), pl.ds(0, wide)], sem.at[i])

        left = 0
        for i in range(NR):
            wide = pair_width(i // 2, part)
            if i % 2:
                source = odd[i // 2]
            else:
                source = even_ref.at[:, pl.ds(left, wide)]
                left += wide

            @pl.when(row == i)
            def _():
                copy(i, diag_ref.at[col, :, pl.ds(0, wide)]).start()

            @pl.when(row != i)
            def _():
                copy(i, source).start()

        for m in range(NR // 2 - 1):
            right = pair_width(m, part)
            out_ref[pl.ds(2 * m * part, 2 * part), pl.ds(right, size - right)] = jnp.zeros(
                (2 * part, size - right), out_ref.dtype
            )
        for i in range(NR):
            copy(i, odd[i // 2]).wait()


def lower_dot(q_ref, d_ref, p_ref):
    half = d_ref.shape[0] // 2
    q_ref[:half] = low(dot(d_ref[:half, :half], p_ref[:half]))
    q_ref[half:] = low(dot(d_ref[half:], p_ref[...]))


def step0_kernel(g0, g1, g2, g3, rhs_ref, l_ref, p_ref, q_ref, s_ref):
    part = l_ref.shape[0] // NR
    row = lax.axis_index("row")

    def lookup(c, i):
        r = jnp.int32(PIECES[0][i])
        for n in range(1, NC):
            r = jnp.where(c == n, PIECES[n][i], r)
        return pl.multiple_of(r * part, part)

    @pl.when((row >= 1) & (row < 4) & (lax.axis_index("col") == 0))
    def _():
        for j, got in enumerate((g0, g1, g2, g3)):
            src = lax.rem(row + 7 - j, 4)
            q_ref[pl.ds(lookup(src, 0), part)] = got[:part]
            q_ref[pl.ds(lookup(src, 1), part)] = got[part:]
        s = dot(l_ref[...], q_ref[...])
        s_ref[...] = low(s)
        p_ref[...] = low(rhs_ref[0] - s)


def step1_kernel(p_in, d_ref, q_prev, q_ref):
    active = at(MAKER[1])

    @pl.when(active)
    def _():
        lower_dot(q_ref, d_ref, p_in)

    @pl.when(jnp.logical_not(active))
    def _():
        q_ref[...] = q_prev[...]


def step1_sum_kernel(q_in, sum_ref, rhs_ref, l_ref, s_prev, p_ref, s_ref):
    active = at(MAKER[1])

    @pl.when(active)
    def _():
        s = dot(l_ref[...], q_in[...]) + sum_ref[...].astype(jnp.float32)
        s_ref[...] = low(s)
        p_ref[...] = low(rhs_ref[0] - s)

    @pl.when(jnp.logical_not(active))
    def _():
        s_ref[...] = s_prev[...]


def step2_kernel(p_in, q_in, sum_ref, rhs_ref, d_ref, l_ref, q_prev, s_prev, a_ref, q_ref, s_ref):
    active, beside = at(MAKER[2]), at(BESIDE)

    @pl.when(active)
    def _():
        lower_dot(q_ref, d_ref, p_in)
        a_ref[...] = q_ref[...]
        s_ref[...] = low(dot(l_ref[...], q_ref[...]))

    @pl.when(beside)
    def _():
        q_ref[...] = q_in[...]
        s = dot(l_ref[...], q_in[...]) + sum_ref[...].astype(jnp.float32)
        s_ref[...] = low(s)
        a_ref[...] = low(rhs_ref[0] - s)

    @pl.when(jnp.logical_not(active | beside))
    def _():
        q_ref[...] = q_prev[...]
        s_ref[...] = s_prev[...]


def step3_kernel(takers, a_ref, sum_ref, *refs):
    came, (d_ref, q_prev, q_ref, p_v) = refs[:-4], refs[-4:]
    active = at(MAKER[3])

    @pl.when(active)
    def _():
        p_v[...] = low(a_ref[...].astype(jnp.float32) - sum_ref[...].astype(jnp.float32))
        lower_dot(q_ref, d_ref, p_v)

    for devices, source in zip(takers, came):

        @pl.when(any_of(devices))
        def _():
            q_ref[...] = source[...]

    @pl.when(jnp.logical_not(active | any_of([d for devices in takers for d in devices])))
    def _():
        q_ref[...] = q_prev[...]


def update_kernel(takers, rows_ref, counts_ref, s_ref, l_ref, q_prev, *refs):
    got, q_ref, out_ref = refs[:-2], refs[-2], refs[-1]
    size = l_ref.shape[0]
    row, col = lax.axis_index("row"), lax.axis_index("col")
    below = row >= NC

    def take(flag, source):
        @pl.when(flag)
        def _():
            q_ref[...] = source[...]

    kept = jnp.logical_not(any_of([d for devices in takers for d in devices]))
    take(kept, q_prev)
    for devices, source in zip(takers, got):
        take(any_of(devices), source)

    @pl.when(below)
    def _():
        out_ref[pl.ds(0, size)] = low(dot(l_ref[...], q_ref[...]))

    @pl.when(jnp.logical_not(below))
    def _():
        out_ref[pl.ds(0, size)] = s_ref[...]

    listed = rows_ref[0, 0, 0, 0]
    there = below & (counts_ref[0, 0, 0] > 0)
    done = at(FIRST) | at(MAKER[1]) | at(BESIDE) | at(MAKER[2])
    first = (there & (listed == 0)) | done
    second = there & (listed == 1)
    ids = lax.broadcasted_iota(jnp.int32, (TAIL, out_ref.shape[1]), 0)
    flag = ((ids == 0) & first) | ((ids == 1) & second)
    out_ref[pl.ds(size, TAIL)] = low(jnp.where(flag, 1.0, 0.0))


def solved_kernel(q_ref, rest_ref, solved_ref):
    came = any_of(REST)

    @pl.when(came)
    def _():
        solved_ref[...] = rest_ref[...].astype(jnp.float32)

    @pl.when(jnp.logical_not(came))
    def _():
        solved_ref[...] = q_ref[...].astype(jnp.float32)


def final_kernel(rhs_ref, *refs):
    sums, out_ref = refs[:NC], refs[NC]
    size = out_ref.shape[1]
    for i in range(out_ref.shape[0]):
        acc = rhs_ref[i]
        for s in sums:
            keep = s[pl.ds(size, TAIL)].astype(jnp.float32)[i : i + 1] > 0.5
            acc = acc - jnp.where(keep, s[pl.ds(0, size)].astype(jnp.float32), 0.0)
        out_ref[i] = acc


def on_device_8x4(rhs, diag_inv, blocks, block_rows, counts):
    size, width = rhs.shape[2:]
    part = size // NR
    rhs = rhs[:, 0]
    block = blocks[0, 0, 0, 0]
    bf16 = jnp.bfloat16
    vec = jax.ShapeDtypeStruct((size, width), bf16)
    dma = pltpu.SemaphoreType.DMA

    wides = [pair_width(m, part) for m in range(NR // 2)]
    cuts = call(
        cut_kernel, [jax.ShapeDtypeStruct((part, w), bf16) for w in wides], [diag_inv], [HBM], [ANY] * len(wides), [dma]
    )
    at_piece = {r: (0, c) for c, rows in enumerate(PIECES) for r in rows}
    parts = []
    for m, cut in enumerate(cuts):
        pairs = []
        for r in range(NR):
            for c, k in enumerate(SENDS[r]):
                if k == 0 and r and max(r // 2, 1) == m:
                    pairs.append(((r, c), at_piece[r]))
                if k and MAKER[k][0] != r and r // 2 == m:
                    pairs.append(((r, c), MAKER[k] if r % 2 else PARTNER[k]))
        parts.append(send_only(cut, pairs))
    q = call(
        first_kernel,
        jax.ShapeDtypeStruct((2 * part, width), bf16),
        [rhs, diag_inv, *parts[1:]],
        [HBM, HBM] + [ANY] * (len(wides) - 1),
        VMEM,
        [
            pltpu.VMEM((size, width), jnp.float32),
            pltpu.VMEM((2, part, size), bf16),
            dma,
            pltpu.SemaphoreType.DMA((2,)),
        ],
    )
    takers = (FIRST, (2, 0), (3, 0))
    got = [send(q, [((0, c), takers[(c + j) % 4]) for c in range(4) if (c + j) % 4 < 3]) for j in range(4)]
    even = call(
        pack_kernel,
        jax.ShapeDtypeStruct((part, sum(wides)), bf16),
        parts,
        [ANY] * len(wides),
        VMEM,
        [pltpu.SemaphoreType.DMA((len(wides),))],
    )
    even = send(even, [(PARTNER[k], MAKER[k]) for k in range(1, NC)])
    diag = call(
        whole_kernel,
        jax.ShapeDtypeStruct((size, size), bf16),
        [diag_inv, even, *parts],
        [HBM] + [ANY] * (1 + len(wides)),
        VMEM,
        [pltpu.SemaphoreType.DMA((NR,))],
    )

    p, q, s = call(step0_kernel, [vec] * 3, [*got, rhs, block], [VMEM] * 6, [VMEM] * 3)
    p_in = send(p, [(FIRST, MAKER[1])])
    sums = send(s, [((2, 0), MAKER[1]), ((3, 0), BESIDE)])
    q = call(step1_kernel, vec, [p_in, diag, q], [VMEM] * 3, VMEM)
    p, s = call(step1_sum_kernel, [vec] * 2, [q, sums, rhs, block, s], [VMEM] * 5, [VMEM] * 2)
    p_in = send(p, [(MAKER[1], MAKER[2])])
    q_in = send(q, [(MAKER[1], BESIDE)])

    came = send(q, [((2, 0), (4, 0)), ((3, 0), (5, 0)), ((1, 0), (0, 0)), ((2, 1), (4, 1))])
    took = [(4, 0), (5, 0), (0, 0), (4, 1)]
    p_in, came = lax.optimization_barrier((p_in, came))

    a, q, s = call(step2_kernel, [vec] * 3, [p_in, q_in, sums, rhs, diag, block, q, s], [VMEM] * 8, [VMEM] * 3)
    from_c = a
    a = send(a, [(BESIDE, MAKER[3])])
    sums = send(s, [(MAKER[2], MAKER[3])])
    early = ((2, 2), (7, 2), (5, 2))
    got = [send_only(from_c, [(MAKER[2], d)]) for d in early]
    q = call(
        functools.partial(step3_kernel, [[d] for d in early] + [took]),
        vec,
        [a, sums, *got, came, diag, q],
        [VMEM] * 8,
        VMEM,
        [pltpu.VMEM((size, width), bf16)],
    )

    sends = [
        [
            (MAKER[3], (6, 3)), ((2, 2), (6, 2)),
            ((4, 0), (6, 0)), ((5, 0), (7, 0)), ((4, 1), (6, 1)), ((3, 1), (5, 1)), ((2, 1), (0, 1)),
        ],
        [(MAKER[3], (7, 3)), ((2, 2), (4, 2)), ((4, 1), (7, 1)), ((3, 1), (1, 1))],
        [(MAKER[3], (4, 3))],
        [(MAKER[3], (3, 3)), (MAKER[2], (1, 2))],
    ]
    got = [send_only(q, pairs) for pairs in sends]
    takers = [[b for _, b in pairs] for pairs in sends]
    q, mine = call(
        functools.partial(update_kernel, takers),
        [vec, jax.ShapeDtypeStruct((size + TAIL, width), bf16)],
        [block_rows, counts, s, block, q, *got],
        [SMEM] * 2 + [VMEM] * (3 + len(got)),
        [VMEM] * 2,
    )

    def swap(value, step):
        return send(value, [((r, c), (r, c ^ step)) for r in range(NR) for c in range(NC)])

    across = swap(mine, 2)
    rest = send_only(q, list(zip(((3, 3), (6, 3), (7, 3), (2, 2)), REST)))
    solved = call(solved_kernel, jax.ShapeDtypeStruct((size, width), jnp.float32), [q, rest], [VMEM] * 2, VMEM)
    beside, across, solved = lax.optimization_barrier((mine, across, solved))
    beside = swap(beside, 1)
    corner = swap(across, 1)
    remainder = call(
        final_kernel,
        jax.ShapeDtypeStruct(rhs.shape, jnp.float32),
        [rhs, mine, beside, across, corner],
        [VMEM] * 5,
        VMEM,
    )
    return solved[None, None], remainder[:, None]


def solution(mesh):
    in_specs = (
        P(None, "row", None, None),
        P(None, "row", None),
        P(None, "col", "row", None, None, None),
        P(None, "col", "row", None),
        P(None, "col", "row"),
    )
    out_specs = (P(None, "col", None, None), P(None, "row", None, None))
    small = mesh.shape["row"] == NR and mesh.shape["col"] == NC
    return jax.shard_map(
        on_device_8x4 if small else on_device_any,
        mesh=mesh,
        in_specs=in_specs,
        out_specs=out_specs,
        check_vma=False,
    )
```

```python
import functools

import jax
import jax.numpy as jnp
from jax import lax
from jax.experimental import pallas as pl
from jax.experimental.pallas import tpu as pltpu
from jax.sharding import PartitionSpec as P

VMEM = pl.BlockSpec(memory_space=pltpu.VMEM)
ANY = pl.BlockSpec(memory_space=pl.ANY)
HBM = pl.BlockSpec(memory_space=pltpu.HBM)
SMEM = pl.BlockSpec(memory_space=pltpu.SMEM)
TAIL = 16


def broadcast(value, axis, root):
    mine = lax.axis_index(axis) == root
    return lax.psum(jnp.where(mine, value, jnp.zeros_like(value)), axis)


def on_device_any(rhs, diag_inv, blocks, block_rows, counts):
    nrow = lax.axis_size("row")
    ncol = lax.axis_size("col")
    my_row = lax.axis_index("row")
    my_col = lax.axis_index("col")
    kc = diag_inv.shape[0]
    rb_local = rhs.shape[0]
    nz_local = blocks.shape[3]
    local_rhs = rhs[:, 0]
    partial_value = jnp.zeros(local_rhs.shape, jnp.float32)
    solved_list = [jnp.zeros(local_rhs.shape[1:], jnp.float32)]
    slot_ids = jnp.arange(nz_local, dtype=jnp.int32)
    local_ids = jnp.arange(rb_local, dtype=jnp.int32)
    for k in range(kc):
        j = k // ncol
        owner_row = k % nrow
        local_pivot = k // nrow
        mine_row = my_row == owner_row
        mine_col = my_col == k % ncol
        pivot_part = jnp.where(mine_row, partial_value[local_pivot], jnp.float32(0.0))
        summed = lax.psum(pivot_part, "col")
        updated = (local_rhs[local_pivot] - summed).astype(jnp.bfloat16)
        pivot_bf = broadcast(updated, "row", owner_row)
        row_part = jnp.dot(diag_inv[k], pivot_bf, preferred_element_type=jnp.float32)
        sol = lax.all_gather(row_part, "row", axis=0, tiled=True)
        sol_bf = sol.astype(jnp.bfloat16)
        rows = block_rows[j, 0, 0]
        glob = rows * nrow + my_row
        valid = (slot_ids < counts[j, 0, 0]) & (glob > k) & mine_col
        weights = (valid[:, None] & (rows[:, None] == local_ids[None, :])).astype(jnp.float32)
        contrib = jnp.einsum(
            "sab,bn->san", blocks[j, 0, 0], sol_bf, preferred_element_type=jnp.float32
        )
        partial_value = partial_value + jnp.einsum(
            "sl,san->lan", weights, contrib, precision=lax.Precision.HIGHEST
        )
        solved_list[j] = jnp.where(mine_col, sol, solved_list[j])
    total = lax.psum(partial_value, "col")
    remainder = (local_rhs - total)[:, None]
    solved = jnp.stack(solved_list)[:, None]
    return (solved, remainder)


NR, NC = 8, 4
MAKER = (None, (2, 1), (3, 2), (5, 3))
FIRST = (1, 0)
BESIDE = (3, 1)
PARTNER = (None, (3, 1), (3, 3), (5, 2))
PIECES = ((6, 3), (7, 0), (4, 2), (5, 1))
SENDS = (
    (0, 1, 2, 3),
    (2, 1, 0, 3),
    (3, 1, 0, 2),
    (0, 1, 3, 2),
    (1, 3, 0, 2),
    (2, 1, 3, 0),
    (0, 1, 2, 3),
    (1, 0, 2, 3),
)
REST = ((3, 3), (0, 3), (1, 3))


def hops(a, b):
    d = a ^ b
    if d < 2:
        return 1 if d else 10000
    return 100 + abs((a >> 3) - (b >> 3)) + ((d >> 2) & 1) + ((d >> 1) & 1)


def complete(pairs):
    to = {a * NC + b: c * NC + d for (a, b), (c, d) in pairs}
    free_from = [i for i in range(NR * NC) if i not in to]
    free_to = [i for i in range(NR * NC) if i not in to.values()]
    n = len(free_from)
    u, v, match = [0] * (n + 1), [0] * (n + 1), [0] * (n + 1)
    for i in range(1, n + 1):
        match[0], j0 = i, 0
        least, way, used = [10**9] * (n + 1), [0] * (n + 1), [False] * (n + 1)
        while True:
            used[j0] = True
            i0, delta, j1 = match[j0], 10**9, 0
            for j in range(1, n + 1):
                if not used[j]:
                    cur = hops(free_from[i0 - 1], free_to[j - 1]) - u[i0] - v[j]
                    if cur < least[j]:
                        least[j], way[j] = cur, j0
                    if least[j] < delta:
                        delta, j1 = least[j], j
            for j in range(n + 1):
                if used[j]:
                    u[match[j]] += delta
                    v[j] -= delta
                else:
                    least[j] -= delta
            j0 = j1
            if match[j0] == 0:
                break
        while j0:
            j1 = way[j0]
            match[j0] = match[j1]
            j0 = j1
    for j in range(1, n + 1):
        to[free_from[match[j] - 1]] = free_to[j - 1]
    return [(divmod(a, NC), divmod(b, NC)) for a, b in sorted(to.items())]


def send(value, pairs):
    return lax.ppermute(value, ("row", "col"), [(a * NC + b, c * NC + d) for (a, b), (c, d) in complete(pairs)])


def send_only(value, pairs):
    return lax.ppermute(value, ("row", "col"), [(a * NC + b, c * NC + d) for (a, b), (c, d) in pairs])


def dot(a, b):
    return jnp.dot(a, b, preferred_element_type=jnp.float32)


def low(a):
    return a.astype(jnp.bfloat16)


def at(device):
    return (lax.axis_index("row") == device[0]) & (lax.axis_index("col") == device[1])


def any_of(devices):
    flag = at(devices[0])
    for d in devices[1:]:
        flag = flag | at(d)
    return flag


def call(kernel, outs, ins, in_specs, out_specs, scratch=(), limit=16):
    return pl.pallas_call(
        kernel,
        out_shape=outs,
        in_specs=in_specs,
        out_specs=out_specs,
        scratch_shapes=list(scratch),
        compiler_params=pltpu.CompilerParams(vmem_limit_bytes=limit << 20),
        name=kernel.func.__name__ if isinstance(kernel, functools.partial) else kernel.__name__,
    )(*ins)


def pair_width(m, part):
    return 2 * (m + 1) * part


def cut_kernel(diag_ref, *refs):
    cuts, sem = refs[:-1], refs[-1]
    row, col = lax.axis_index("row"), lax.axis_index("col")
    k = jnp.int32(0)
    for r in range(NR):
        for c in range(NC):
            k = jnp.where((row == r) & (col == c), SENDS[r][c], k)
    place = jnp.where(k > 0, row // 2, jnp.where(row < 4, 1, len(cuts) - 1))
    for m, out in enumerate(cuts):

        @pl.when(place == m)
        def _():
            copy = pltpu.make_async_copy(diag_ref.at[k, :, pl.ds(0, out.shape[1])], out, sem)
            copy.start()
            copy.wait()


def first_kernel(rhs_ref, diag_ref, hi_ref, lo_ref, out_ref, rhs_v, lo_v, rhs_sem, lo_sem):
    n, half = lo_ref.shape

    @pl.when(lax.axis_index("row") == 0)
    def _():
        copy = pltpu.make_async_copy(rhs_ref.at[0], rhs_v, rhs_sem)
        copy.start()
        own = pltpu.make_async_copy(diag_ref.at[0, :, pl.ds(0, half)], lo_v, lo_sem)
        has_own = lax.axis_index("col") == [lo for _, lo in PIECES].index(0)

        @pl.when(has_own)
        def _():
            own.start()
            own.wait()

        @pl.when(jnp.logical_not(has_own))
        def _():
            lo_v[...] = lo_ref[...]

        copy.wait()
        p = low(rhs_v[...])
        out_ref[:n] = low(dot(hi_ref[...], p))
        out_ref[n:] = low(dot(lo_v[...], p[:half]))


def pack_kernel(*refs):
    parts, out_ref, sem = refs[: NR // 2], refs[-2], refs[-1]
    part = out_ref.shape[0]

    @pl.when(any_of(PARTNER[1:]))
    def _():
        copies, left = [], 0
        for m in range(NR // 2):
            wide = pair_width(m, part)
            (source,) = [p for p in parts if p.shape[1] == wide]
            copies.append(pltpu.make_async_copy(source, out_ref.at[:, pl.ds(left, wide)], sem.at[m]))
            left += wide
        for copy in copies:
            copy.start()
        for copy in copies:
            copy.wait()


def whole_kernel(diag_ref, even_ref, *refs):
    odd, out_ref, sem = refs[:-2], refs[-2], refs[-1]
    size = out_ref.shape[0]
    part = size // NR
    row, col = lax.axis_index("row"), lax.axis_index("col")

    @pl.when(any_of(MAKER[1:]))
    def _():
        def copy(i, source):
            wide = pair_width(i // 2, part)
            return pltpu.make_async_copy(source, out_ref.at[pl.ds(i * part, part), pl.ds(0, wide)], sem.at[i])

        left = 0
        for i in range(NR):
            wide = pair_width(i // 2, part)
            if i % 2:
                source = odd[i // 2]
            else:
                source = even_ref.at[:, pl.ds(left, wide)]
                left += wide

            @pl.when(row == i)
            def _():
                copy(i, diag_ref.at[col, :, pl.ds(0, wide)]).start()

            @pl.when(row != i)
            def _():
                copy(i, source).start()

        for m in range(NR // 2 - 1):
            right = pair_width(m, part)
            out_ref[pl.ds(2 * m * part, 2 * part), pl.ds(right, size - right)] = jnp.zeros(
                (2 * part, size - right), out_ref.dtype
            )
        for i in range(NR):
            copy(i, odd[i // 2]).wait()


def lower_dot(q_ref, d_ref, p_ref):
    half = d_ref.shape[0] // 2
    q_ref[:half] = low(dot(d_ref[:half, :half], p_ref[:half]))
    q_ref[half:] = low(dot(d_ref[half:], p_ref[...]))


def step0_kernel(g0, g1, g2, g3, rhs_ref, l_ref, p_ref, q_ref, s_ref):
    part = l_ref.shape[0] // NR
    row = lax.axis_index("row")

    def lookup(c, i):
        r = jnp.int32(PIECES[0][i])
        for n in range(1, NC):
            r = jnp.where(c == n, PIECES[n][i], r)
        return pl.multiple_of(r * part, part)

    @pl.when((row >= 1) & (row < 4) & (lax.axis_index("col") == 0))
    def _():
        for j, got in enumerate((g0, g1, g2, g3)):
            src = lax.rem(row + 7 - j, 4)
            q_ref[pl.ds(lookup(src, 0), part)] = got[:part]
            q_ref[pl.ds(lookup(src, 1), part)] = got[part:]
        s = dot(l_ref[...], q_ref[...])
        s_ref[...] = low(s)
        p_ref[...] = low(rhs_ref[0] - s)


def step1_kernel(p_in, d_ref, q_prev, q_ref):
    active = at(MAKER[1])

    @pl.when(active)
    def _():
        lower_dot(q_ref, d_ref, p_in)

    @pl.when(jnp.logical_not(active))
    def _():
        q_ref[...] = q_prev[...]


def step1_sum_kernel(q_in, sum_ref, rhs_ref, l_ref, s_prev, p_ref, s_ref):
    active = at(MAKER[1])

    @pl.when(active)
    def _():
        s = dot(l_ref[...], q_in[...]) + sum_ref[...].astype(jnp.float32)
        s_ref[...] = low(s)
        p_ref[...] = low(rhs_ref[0] - s)

    @pl.when(jnp.logical_not(active))
    def _():
        s_ref[...] = s_prev[...]


def step2_kernel(p_in, q_in, sum_ref, rhs_ref, d_ref, l_ref, q_prev, s_prev, a_ref, q_ref, s_ref):
    active, beside = at(MAKER[2]), at(BESIDE)

    @pl.when(active)
    def _():
        lower_dot(q_ref, d_ref, p_in)
        a_ref[...] = q_ref[...]
        s_ref[...] = low(dot(l_ref[...], q_ref[...]))

    @pl.when(beside)
    def _():
        q_ref[...] = q_in[...]
        s = dot(l_ref[...], q_in[...]) + sum_ref[...].astype(jnp.float32)
        s_ref[...] = low(s)
        a_ref[...] = low(rhs_ref[0] - s)

    @pl.when(jnp.logical_not(active | beside))
    def _():
        q_ref[...] = q_prev[...]
        s_ref[...] = s_prev[...]


def step3_kernel(takers, a_ref, sum_ref, *refs):
    came, (d_ref, q_prev, q_ref, p_v) = refs[:-4], refs[-4:]
    active = at(MAKER[3])

    @pl.when(active)
    def _():
        p_v[...] = low(a_ref[...].astype(jnp.float32) - sum_ref[...].astype(jnp.float32))
        lower_dot(q_ref, d_ref, p_v)

    for devices, source in zip(takers, came):

        @pl.when(any_of(devices))
        def _():
            q_ref[...] = source[...]

    @pl.when(jnp.logical_not(active | any_of([d for devices in takers for d in devices])))
    def _():
        q_ref[...] = q_prev[...]


def update_kernel(takers, rows_ref, counts_ref, s_ref, l_ref, q_prev, *refs):
    got, q_ref, out_ref = refs[:-2], refs[-2], refs[-1]
    size = l_ref.shape[0]
    row, col = lax.axis_index("row"), lax.axis_index("col")
    below = row >= NC

    def take(flag, source):
        @pl.when(flag)
        def _():
            q_ref[...] = source[...]

    kept = jnp.logical_not(any_of([d for devices in takers for d in devices]))
    take(kept, q_prev)
    for devices, source in zip(takers, got):
        take(any_of(devices), source)

    @pl.when(below)
    def _():
        out_ref[pl.ds(0, size)] = low(dot(l_ref[...], q_ref[...]))

    @pl.when(jnp.logical_not(below))
    def _():
        out_ref[pl.ds(0, size)] = s_ref[...]

    listed = rows_ref[0, 0, 0, 0]
    there = below & (counts_ref[0, 0, 0] > 0)
    done = at(FIRST) | at(MAKER[1]) | at(BESIDE) | at(MAKER[2])
    first = (there & (listed == 0)) | done
    second = there & (listed == 1)
    ids = lax.broadcasted_iota(jnp.int32, (TAIL, out_ref.shape[1]), 0)
    flag = ((ids == 0) & first) | ((ids == 1) & second)
    out_ref[pl.ds(size, TAIL)] = low(jnp.where(flag, 1.0, 0.0))


def final_kernel(q_ref, rest_ref, rhs_ref, *refs):
    sums, (solved_ref, out_ref) = refs[:NC], refs[NC:]
    size = out_ref.shape[1]
    came = any_of(REST)

    @pl.when(came)
    def _():
        solved_ref[...] = rest_ref[...].astype(jnp.float32)

    @pl.when(jnp.logical_not(came))
    def _():
        solved_ref[...] = q_ref[...].astype(jnp.float32)

    for i in range(out_ref.shape[0]):
        acc = rhs_ref[i]
        for s in sums:
            keep = s[pl.ds(size, TAIL)].astype(jnp.float32)[i : i + 1] > 0.5
            acc = acc - jnp.where(keep, s[pl.ds(0, size)].astype(jnp.float32), 0.0)
        out_ref[i] = acc


def on_device_8x4(rhs, diag_inv, blocks, block_rows, counts):
    size, width = rhs.shape[2:]
    part = size // NR
    rhs = rhs[:, 0]
    block = blocks[0, 0, 0, 0]
    bf16 = jnp.bfloat16
    vec = jax.ShapeDtypeStruct((size, width), bf16)
    dma = pltpu.SemaphoreType.DMA

    wides = [pair_width(m, part) for m in range(NR // 2)]
    *cuts, hi = call(
        cut_kernel,
        [jax.ShapeDtypeStruct((part, w), bf16) for w in wides + [size]],
        [diag_inv],
        [HBM],
        [ANY] * (len(wides) + 1),
        [dma],
    )
    source = {(r, k): (r, c) for r in range(NR) for c, k in enumerate(SENDS[r])}
    hi = send_only(hi, [(source[rows[0], 0], (0, c)) for c, rows in enumerate(PIECES)])
    parts = []
    for m, cut in enumerate(cuts):
        pairs = [
            (source[r, k], MAKER[k] if r % 2 else PARTNER[k])
            for r in (2 * m, 2 * m + 1)
            for k in range(1, NC)
            if MAKER[k][0] != r
        ]
        if m == 1:
            pairs += [(source[rows[1], 0], (0, c)) for c, rows in enumerate(PIECES) if rows[1]]
        parts.append(send_only(cut, pairs))
    q = call(
        first_kernel,
        jax.ShapeDtypeStruct((2 * part, width), bf16),
        [rhs, diag_inv, hi, parts[1]],
        [HBM, HBM, VMEM, VMEM],
        VMEM,
        [pltpu.VMEM((size, width), jnp.float32), pltpu.VMEM((part, size // 2), bf16), dma, dma],
    )
    takers = (FIRST, (2, 0), (3, 0))
    got = [send(q, [((0, c), takers[(c + j) % 4]) for c in range(4) if (c + j) % 4 < 3]) for j in range(4)]
    even = call(
        pack_kernel,
        jax.ShapeDtypeStruct((part, sum(wides)), bf16),
        [parts[2], parts[3], parts[1], parts[0], hi],
        [ANY] * (len(wides) + 1),
        VMEM,
        [pltpu.SemaphoreType.DMA((len(wides),))],
    )
    even = send_only(even, [(PARTNER[k], MAKER[k]) for k in range(1, NC)])
    diag = call(
        whole_kernel,
        jax.ShapeDtypeStruct((size, size), bf16),
        [diag_inv, even, *parts],
        [HBM] + [ANY] * (1 + len(wides)),
        VMEM,
        [pltpu.SemaphoreType.DMA((NR,))],
    )

    p, q, s = call(step0_kernel, [vec] * 3, [*got, rhs, block], [VMEM] * 6, [VMEM] * 3)
    p_in = send(p, [(FIRST, MAKER[1])])
    sums = send(s, [((2, 0), MAKER[1]), ((3, 0), BESIDE)])
    q = call(step1_kernel, vec, [p_in, diag, q], [VMEM] * 3, VMEM)
    p, s = call(step1_sum_kernel, [vec] * 2, [q, sums, rhs, block, s], [VMEM] * 5, [VMEM] * 2)
    p_in = send(p, [(MAKER[1], MAKER[2])])
    q_in = send(q, [(MAKER[1], BESIDE)])

    came = send(q, [((2, 0), (4, 0)), ((3, 0), (5, 0)), ((1, 0), (0, 0)), ((2, 1), (4, 1))])
    took = [(4, 0), (5, 0), (0, 0), (4, 1)]
    p_in, came = lax.optimization_barrier((p_in, came))

    a, q, s = call(step2_kernel, [vec] * 3, [p_in, q_in, sums, rhs, diag, block, q, s], [VMEM] * 8, [VMEM] * 3)
    from_c = a
    a = send(a, [(BESIDE, MAKER[3])])
    sums = send(s, [(MAKER[2], MAKER[3])])
    early = ((2, 2), (7, 2), (5, 2))
    got = [send_only(from_c, [(MAKER[2], d)]) for d in early]
    q = call(
        functools.partial(step3_kernel, [[d] for d in early] + [took]),
        vec,
        [a, sums, *got, came, diag, q],
        [VMEM] * 8,
        VMEM,
        [pltpu.VMEM((size, width), bf16)],
    )

    sends = [
        [
            (MAKER[3], (6, 3)), ((2, 2), (6, 2)),
            ((4, 0), (6, 0)), ((5, 0), (7, 0)), ((4, 1), (6, 1)), ((3, 1), (5, 1)), ((2, 1), (0, 1)),
        ],
        [(MAKER[3], (7, 3)), ((2, 2), (4, 2)), ((4, 1), (7, 1)), ((3, 1), (1, 1))],
        [(MAKER[3], (4, 3)), ((2, 2), (0, 2)), (MAKER[2], (1, 2))],
        [(MAKER[3], (2, 3))],
    ]
    got = [send_only(q, pairs) for pairs in sends]
    takers = [[b for _, b in pairs] for pairs in sends]
    q, mine = call(
        functools.partial(update_kernel, takers),
        [vec, jax.ShapeDtypeStruct((size + TAIL, width), bf16)],
        [block_rows, counts, s, block, q, *got],
        [SMEM] * 2 + [VMEM] * (3 + len(got)),
        [VMEM] * 2,
    )

    def swap(value, step):
        return send(value, [((r, c), (r, c ^ step)) for r in range(NR) for c in range(NC)])

    across = swap(mine, 2)
    rest = send_only(q, list(zip(((2, 3), (6, 3), (7, 3)), REST)))
    beside, across, rest = lax.optimization_barrier((mine, across, rest))
    beside = swap(beside, 1)
    corner = swap(across, 1)
    solved, remainder = call(
        final_kernel,
        [jax.ShapeDtypeStruct((size, width), jnp.float32), jax.ShapeDtypeStruct(rhs.shape, jnp.float32)],
        [q, rest, rhs, mine, beside, across, corner],
        [VMEM] * 7,
        [VMEM] * 2,
    )
    return solved[None, None], remainder[:, None]


def solution(mesh):
    in_specs = (
        P(None, "row", None, None),
        P(None, "row", None),
        P(None, "col", "row", None, None, None),
        P(None, "col", "row", None),
        P(None, "col", "row"),
    )
    out_specs = (P(None, "col", None, None), P(None, "row", None, None))
    small = mesh.shape["row"] == NR and mesh.shape["col"] == NC
    return jax.shard_map(
        on_device_8x4 if small else on_device_any,
        mesh=mesh,
        in_specs=in_specs,
        out_specs=out_specs,
        check_vma=False,
    )
```

```python
import functools

import jax
import jax.numpy as jnp
from jax import lax
from jax.experimental import pallas as pl
from jax.experimental.pallas import tpu as pltpu
from jax.sharding import PartitionSpec as P

VMEM = pl.BlockSpec(memory_space=pltpu.VMEM)
ANY = pl.BlockSpec(memory_space=pl.ANY)
HBM = pl.BlockSpec(memory_space=pltpu.HBM)
SMEM = pl.BlockSpec(memory_space=pltpu.SMEM)
TAIL = 16


def broadcast(value, axis, root):
    mine = lax.axis_index(axis) == root
    return lax.psum(jnp.where(mine, value, jnp.zeros_like(value)), axis)


def on_device_any(rhs, diag_inv, blocks, block_rows, counts):
    nrow = lax.axis_size("row")
    ncol = lax.axis_size("col")
    my_row = lax.axis_index("row")
    my_col = lax.axis_index("col")
    kc = diag_inv.shape[0]
    rb_local = rhs.shape[0]
    nz_local = blocks.shape[3]
    local_rhs = rhs[:, 0]
    partial_value = jnp.zeros(local_rhs.shape, jnp.float32)
    solved_list = [jnp.zeros(local_rhs.shape[1:], jnp.float32)]
    slot_ids = jnp.arange(nz_local, dtype=jnp.int32)
    local_ids = jnp.arange(rb_local, dtype=jnp.int32)
    for k in range(kc):
        j = k // ncol
        owner_row = k % nrow
        local_pivot = k // nrow
        mine_row = my_row == owner_row
        mine_col = my_col == k % ncol
        pivot_part = jnp.where(mine_row, partial_value[local_pivot], jnp.float32(0.0))
        summed = lax.psum(pivot_part, "col")
        updated = (local_rhs[local_pivot] - summed).astype(jnp.bfloat16)
        pivot_bf = broadcast(updated, "row", owner_row)
        row_part = jnp.dot(diag_inv[k], pivot_bf, preferred_element_type=jnp.float32)
        sol = lax.all_gather(row_part, "row", axis=0, tiled=True)
        sol_bf = sol.astype(jnp.bfloat16)
        rows = block_rows[j, 0, 0]
        glob = rows * nrow + my_row
        valid = (slot_ids < counts[j, 0, 0]) & (glob > k) & mine_col
        weights = (valid[:, None] & (rows[:, None] == local_ids[None, :])).astype(jnp.float32)
        contrib = jnp.einsum(
            "sab,bn->san", blocks[j, 0, 0], sol_bf, preferred_element_type=jnp.float32
        )
        partial_value = partial_value + jnp.einsum(
            "sl,san->lan", weights, contrib, precision=lax.Precision.HIGHEST
        )
        solved_list[j] = jnp.where(mine_col, sol, solved_list[j])
    total = lax.psum(partial_value, "col")
    remainder = (local_rhs - total)[:, None]
    solved = jnp.stack(solved_list)[:, None]
    return (solved, remainder)


NR, NC = 8, 4
MAKER = (None, (2, 1), (3, 2), (5, 3))
FIRST = (1, 0)
BESIDE = (3, 1)
PARTNER = (None, (3, 1), (3, 3), (5, 2))
PIECES = ((4, 1), (6, 3), (5, 2), (7, 0))
SENDS = (
    (0, 1, 2, 3),
    (0, 1, 2, 3),
    (3, 1, 0, 2),
    (0, 1, 3, 2),
    (0, 1, 3, 2),
    (2, 1, 3, 0),
    (0, 3, 1, 2),
    (1, 3, 0, 2),
)
REST = ((3, 3), (0, 3), (1, 3))


def hops(a, b):
    d = a ^ b
    if d < 2:
        return 1 if d else 10000
    return 100 + abs((a >> 3) - (b >> 3)) + ((d >> 2) & 1) + ((d >> 1) & 1)


def complete(pairs):
    to = {a * NC + b: c * NC + d for (a, b), (c, d) in pairs}
    free_from = [i for i in range(NR * NC) if i not in to]
    free_to = [i for i in range(NR * NC) if i not in to.values()]
    n = len(free_from)
    u, v, match = [0] * (n + 1), [0] * (n + 1), [0] * (n + 1)
    for i in range(1, n + 1):
        match[0], j0 = i, 0
        least, way, used = [10**9] * (n + 1), [0] * (n + 1), [False] * (n + 1)
        while True:
            used[j0] = True
            i0, delta, j1 = match[j0], 10**9, 0
            for j in range(1, n + 1):
                if not used[j]:
                    cur = hops(free_from[i0 - 1], free_to[j - 1]) - u[i0] - v[j]
                    if cur < least[j]:
                        least[j], way[j] = cur, j0
                    if least[j] < delta:
                        delta, j1 = least[j], j
            for j in range(n + 1):
                if used[j]:
                    u[match[j]] += delta
                    v[j] -= delta
                else:
                    least[j] -= delta
            j0 = j1
            if match[j0] == 0:
                break
        while j0:
            j1 = way[j0]
            match[j0] = match[j1]
            j0 = j1
    for j in range(1, n + 1):
        to[free_from[match[j] - 1]] = free_to[j - 1]
    return [(divmod(a, NC), divmod(b, NC)) for a, b in sorted(to.items())]


def send(value, pairs):
    return lax.ppermute(value, ("row", "col"), [(a * NC + b, c * NC + d) for (a, b), (c, d) in complete(pairs)])


def send_only(value, pairs):
    return lax.ppermute(value, ("row", "col"), [(a * NC + b, c * NC + d) for (a, b), (c, d) in pairs])


def dot(a, b):
    return jnp.dot(a, b, preferred_element_type=jnp.float32)


def low(a):
    return a.astype(jnp.bfloat16)


def at(device):
    return (lax.axis_index("row") == device[0]) & (lax.axis_index("col") == device[1])


def any_of(devices):
    flag = at(devices[0])
    for d in devices[1:]:
        flag = flag | at(d)
    return flag


def call(kernel, outs, ins, in_specs, out_specs, scratch=(), limit=16):
    return pl.pallas_call(
        kernel,
        out_shape=outs,
        in_specs=in_specs,
        out_specs=out_specs,
        scratch_shapes=list(scratch),
        compiler_params=pltpu.CompilerParams(vmem_limit_bytes=limit << 20),
        name=kernel.func.__name__ if isinstance(kernel, functools.partial) else kernel.__name__,
    )(*ins)


def pair_width(m, part):
    return 2 * (m + 1) * part


def cut_kernel(diag_ref, *refs):
    cuts, sem = refs[:-1], refs[-1]
    row, col = lax.axis_index("row"), lax.axis_index("col")
    part = diag_ref.shape[1]
    k = jnp.int32(0)
    for r in range(NR):
        for c in range(NC):
            k = jnp.where((row == r) & (col == c), SENDS[r][c], k)
    for m in range(NR // 2):

        @pl.when(jnp.where((row == 1) & (k == 0), 1, row // 2) == m)
        def _():
            copy = pltpu.make_async_copy(diag_ref.at[k, :, pl.ds(0, pair_width(m, part))], cuts[m], sem)
            copy.start()
            copy.wait()


def first_kernel(rhs_ref, diag_ref, *refs):
    parts, (out_ref, rhs_v, d_v, rhs_sem, d_sem) = refs[:-5], refs[-5:]
    n = out_ref.shape[0] // 2
    col = lax.axis_index("col")

    @pl.when(lax.axis_index("row") == 0)
    def _():
        rhs_copy = pltpu.make_async_copy(rhs_ref.at[0], rhs_v, rhs_sem)
        rhs_copy.start()

        def pieces(c):
            copies = []
            for i, r in enumerate(PIECES[c]):
                m = max(r // 2, 1)
                wide = pair_width(m, n)
                source = parts[m - 1] if r else diag_ref.at[0, :, pl.ds(0, wide)]
                copies.append(pltpu.make_async_copy(source, d_v.at[i, :, pl.ds(0, wide)], d_sem.at[i]))
            return copies

        for c in range(NC):

            @pl.when(col == c)
            def _():
                for copy in pieces(c):
                    copy.start()

        rhs_copy.wait()
        p = low(rhs_v[...])
        for c in range(NC):

            @pl.when(col == c)
            def _():
                for i, copy in enumerate(pieces(c)):
                    copy.wait()
                    wide = pair_width(max(PIECES[c][i] // 2, 1), n)
                    out_ref[i * n : (i + 1) * n] = low(dot(d_v[i, :, :wide], p[:wide]))


def pack_kernel(*refs):
    parts, out_ref, sem = refs[:-2], refs[-2], refs[-1]

    @pl.when(any_of(PARTNER[1:]))
    def _():
        copies, left = [], 0
        for m, source in enumerate(parts):
            wide = source.shape[1]
            copies.append(pltpu.make_async_copy(source, out_ref.at[:, pl.ds(left, wide)], sem.at[m]))
            left += wide
        for copy in copies:
            copy.start()
        for copy in copies:
            copy.wait()


def whole_kernel(diag_ref, even_ref, *refs):
    odd, out_ref, sem = refs[:-2], refs[-2], refs[-1]
    size = out_ref.shape[0]
    part = size // NR
    row, col = lax.axis_index("row"), lax.axis_index("col")

    @pl.when(any_of(MAKER[1:]))
    def _():
        def copy(i, source):
            wide = pair_width(i // 2, part)
            return pltpu.make_async_copy(source, out_ref.at[pl.ds(i * part, part), pl.ds(0, wide)], sem.at[i])

        left = 0
        for i in range(NR):
            wide = pair_width(i // 2, part)
            if i % 2:
                source = odd[i // 2]
            else:
                source = even_ref.at[:, pl.ds(left, wide)]
                left += wide

            @pl.when(row == i)
            def _():
                copy(i, diag_ref.at[col, :, pl.ds(0, wide)]).start()

            @pl.when(row != i)
            def _():
                copy(i, source).start()

        for m in range(NR // 2 - 1):
            right = pair_width(m, part)
            out_ref[pl.ds(2 * m * part, 2 * part), pl.ds(right, size - right)] = jnp.zeros(
                (2 * part, size - right), out_ref.dtype
            )
        for i in range(NR):
            copy(i, odd[i // 2]).wait()


def lower_dot(q_ref, d_ref, p_ref):
    half = d_ref.shape[0] // 2
    q_ref[:half] = low(dot(d_ref[:half, :half], p_ref[:half]))
    q_ref[half:] = low(dot(d_ref[half:], p_ref[...]))


def step0_kernel(g0, g1, g2, g3, rhs_ref, l_ref, p_ref, q_ref, s_ref):
    part = l_ref.shape[0] // NR
    row = lax.axis_index("row")

    def lookup(c, i):
        r = jnp.int32(PIECES[0][i])
        for n in range(1, NC):
            r = jnp.where(c == n, PIECES[n][i], r)
        return pl.multiple_of(r * part, part)

    @pl.when((row >= 1) & (row < 4) & (lax.axis_index("col") == 0))
    def _():
        for j, got in enumerate((g0, g1, g2, g3)):
            src = lax.rem(row + 7 - j, 4)
            q_ref[pl.ds(lookup(src, 0), part)] = got[:part]
            q_ref[pl.ds(lookup(src, 1), part)] = got[part:]
        s = dot(l_ref[...], q_ref[...])
        s_ref[...] = low(s)
        p_ref[...] = low(rhs_ref[0] - s)


def step1_kernel(p_in, d_ref, q_prev, q_ref):
    active = at(MAKER[1])

    @pl.when(active)
    def _():
        lower_dot(q_ref, d_ref, p_in)

    @pl.when(jnp.logical_not(active))
    def _():
        q_ref[...] = q_prev[...]


def step1_sum_kernel(q_in, sum_ref, rhs_ref, l_ref, s_prev, p_ref, s_ref):
    active = at(MAKER[1])

    @pl.when(active)
    def _():
        s = dot(l_ref[...], q_in[...]) + sum_ref[...].astype(jnp.float32)
        s_ref[...] = low(s)
        p_ref[...] = low(rhs_ref[0] - s)

    @pl.when(jnp.logical_not(active))
    def _():
        s_ref[...] = s_prev[...]


def step2_kernel(p_in, q_in, sum_ref, rhs_ref, d_ref, l_ref, q_prev, s_prev, a_ref, q_ref, s_ref):
    active, beside = at(MAKER[2]), at(BESIDE)

    @pl.when(active)
    def _():
        lower_dot(q_ref, d_ref, p_in)
        a_ref[...] = q_ref[...]
        s_ref[...] = low(dot(l_ref[...], q_ref[...]))

    @pl.when(beside)
    def _():
        q_ref[...] = q_in[...]
        s = dot(l_ref[...], q_in[...]) + sum_ref[...].astype(jnp.float32)
        s_ref[...] = low(s)
        a_ref[...] = low(rhs_ref[0] - s)

    @pl.when(jnp.logical_not(active | beside))
    def _():
        q_ref[...] = q_prev[...]
        s_ref[...] = s_prev[...]


def step3_kernel(takers, a_ref, sum_ref, *refs):
    came, (d_ref, q_prev, q_ref, p_v) = refs[:-4], refs[-4:]
    active = at(MAKER[3])

    @pl.when(active)
    def _():
        p_v[...] = low(a_ref[...].astype(jnp.float32) - sum_ref[...].astype(jnp.float32))
        lower_dot(q_ref, d_ref, p_v)

    for devices, source in zip(takers, came):

        @pl.when(any_of(devices))
        def _():
            q_ref[...] = source[...]

    @pl.when(jnp.logical_not(active | any_of([d for devices in takers for d in devices])))
    def _():
        q_ref[...] = q_prev[...]


def update_kernel(takers, rows_ref, counts_ref, s_ref, l_ref, q_prev, *refs):
    got, q_ref, out_ref = refs[:-2], refs[-2], refs[-1]
    size = l_ref.shape[0]
    row, col = lax.axis_index("row"), lax.axis_index("col")
    below = row >= NC

    def take(flag, source):
        @pl.when(flag)
        def _():
            q_ref[...] = source[...]

    kept = jnp.logical_not(any_of([d for devices in takers for d in devices]))
    take(kept, q_prev)
    for devices, source in zip(takers, got):
        take(any_of(devices), source)

    @pl.when(below)
    def _():
        out_ref[pl.ds(0, size)] = low(dot(l_ref[...], q_ref[...]))

    @pl.when(jnp.logical_not(below))
    def _():
        out_ref[pl.ds(0, size)] = s_ref[...]

    listed = rows_ref[0, 0, 0, 0]
    there = below & (counts_ref[0, 0, 0] > 0)
    done = at(FIRST) | at(MAKER[1]) | at(BESIDE) | at(MAKER[2])
    first = (there & (listed == 0)) | done
    second = there & (listed == 1)
    ids = lax.broadcasted_iota(jnp.int32, (TAIL, out_ref.shape[1]), 0)
    flag = ((ids == 0) & first) | ((ids == 1) & second)
    out_ref[pl.ds(size, TAIL)] = low(jnp.where(flag, 1.0, 0.0))


def final_kernel(q_ref, rest_ref, rhs_ref, *refs):
    sums, (solved_ref, out_ref) = refs[:NC], refs[NC:]
    size = out_ref.shape[1]
    came = any_of(REST)

    @pl.when(came)
    def _():
        solved_ref[...] = rest_ref[...].astype(jnp.float32)

    @pl.when(jnp.logical_not(came))
    def _():
        solved_ref[...] = q_ref[...].astype(jnp.float32)

    for i in range(out_ref.shape[0]):
        acc = rhs_ref[i]
        for s in sums:
            keep = s[pl.ds(size, TAIL)].astype(jnp.float32)[i : i + 1] > 0.5
            acc = acc - jnp.where(keep, s[pl.ds(0, size)].astype(jnp.float32), 0.0)
        out_ref[i] = acc


def on_device_8x4(rhs, diag_inv, blocks, block_rows, counts):
    size, width = rhs.shape[2:]
    part = size // NR
    rhs = rhs[:, 0]
    block = blocks[0, 0, 0, 0]
    bf16 = jnp.bfloat16
    vec = jax.ShapeDtypeStruct((size, width), bf16)
    dma = pltpu.SemaphoreType.DMA

    wides = [pair_width(m, part) for m in range(NR // 2)]
    cuts = call(
        cut_kernel, [jax.ShapeDtypeStruct((part, w), bf16) for w in wides], [diag_inv], [HBM], [ANY] * len(wides), [dma]
    )
    at_piece = {r: (0, c) for c, rows in enumerate(PIECES) for r in rows}
    parts = []
    for m, cut in enumerate(cuts):
        pairs = []
        for r in range(NR):
            for c, k in enumerate(SENDS[r]):
                if k == 0 and r and max(r // 2, 1) == m:
                    pairs.append(((r, c), at_piece[r]))
                if k and MAKER[k][0] != r and r // 2 == m:
                    pairs.append(((r, c), MAKER[k] if r % 2 else PARTNER[k]))
        parts.append(send_only(cut, pairs))
    q = call(
        first_kernel,
        jax.ShapeDtypeStruct((2 * part, width), bf16),
        [rhs, diag_inv, *parts[1:]],
        [HBM, HBM] + [ANY] * (len(wides) - 1),
        VMEM,
        [
            pltpu.VMEM((size, width), jnp.float32),
            pltpu.VMEM((2, part, size), bf16),
            dma,
            pltpu.SemaphoreType.DMA((2,)),
        ],
    )
    takers = (FIRST, (2, 0), (3, 0))
    got = [send(q, [((0, c), takers[(c + j) % 4]) for c in range(4) if (c + j) % 4 < 3]) for j in range(4)]
    even = call(
        pack_kernel,
        jax.ShapeDtypeStruct((part, sum(wides)), bf16),
        parts,
        [ANY] * len(wides),
        VMEM,
        [pltpu.SemaphoreType.DMA((len(wides),))],
    )
    even = send(even, [(PARTNER[k], MAKER[k]) for k in range(1, NC)])
    diag = call(
        whole_kernel,
        jax.ShapeDtypeStruct((size, size), bf16),
        [diag_inv, even, *parts],
        [HBM] + [ANY] * (1 + len(wides)),
        VMEM,
        [pltpu.SemaphoreType.DMA((NR,))],
    )

    p, q, s = call(step0_kernel, [vec] * 3, [*got, rhs, block], [VMEM] * 6, [VMEM] * 3)
    p_in = send(p, [(FIRST, MAKER[1])])
    sums = send(s, [((2, 0), MAKER[1]), ((3, 0), BESIDE)])
    q = call(step1_kernel, vec, [p_in, diag, q], [VMEM] * 3, VMEM)
    p, s = call(step1_sum_kernel, [vec] * 2, [q, sums, rhs, block, s], [VMEM] * 5, [VMEM] * 2)
    p_in = send(p, [(MAKER[1], MAKER[2])])
    q_in = send(q, [(MAKER[1], BESIDE)])

    came = send(q, [((2, 0), (4, 0)), ((3, 0), (5, 0)), ((1, 0), (0, 0)), ((2, 1), (4, 1))])
    took = [(4, 0), (5, 0), (0, 0), (4, 1)]
    p_in, came = lax.optimization_barrier((p_in, came))

    a, q, s = call(step2_kernel, [vec] * 3, [p_in, q_in, sums, rhs, diag, block, q, s], [VMEM] * 8, [VMEM] * 3)
    from_c = a
    a = send(a, [(BESIDE, MAKER[3])])
    sums = send(s, [(MAKER[2], MAKER[3])])
    early = ((2, 2), (7, 2), (4, 2))
    got = [send_only(from_c, [(MAKER[2], d)]) for d in early]
    q = call(
        functools.partial(step3_kernel, [[d] for d in early] + [took]),
        vec,
        [a, sums, *got, came, diag, q],
        [VMEM] * 8,
        VMEM,
        [pltpu.VMEM((size, width), bf16)],
    )

    sends = [
        [
            (MAKER[3], (6, 3)), ((2, 2), (6, 2)), ((4, 2), (5, 2)),
            ((4, 0), (6, 0)), ((5, 0), (7, 0)), ((4, 1), (6, 1)), ((3, 1), (5, 1)), ((2, 1), (0, 1)),
        ],
        [(MAKER[3], (7, 3)), ((2, 2), (0, 2)), (MAKER[2], (1, 2)), ((4, 1), (7, 1)), ((3, 1), (1, 1))],
        [(MAKER[3], (4, 3))],
        [(MAKER[3], (2, 3))],
    ]
    got = [send_only(q, pairs) for pairs in sends]
    takers = [[b for _, b in pairs] for pairs in sends]
    q, mine = call(
        functools.partial(update_kernel, takers),
        [vec, jax.ShapeDtypeStruct((size + TAIL, width), bf16)],
        [block_rows, counts, s, block, q, *got],
        [SMEM] * 2 + [VMEM] * (3 + len(got)),
        [VMEM] * 2,
    )

    def swap(value, step):
        return send(value, [((r, c), (r, c ^ step)) for r in range(NR) for c in range(NC)])

    across = swap(mine, 2)
    rest = send_only(q, list(zip(((2, 3), (6, 3), (7, 3)), REST)))
    beside, across, rest = lax.optimization_barrier((mine, across, rest))
    beside = swap(beside, 1)
    corner = swap(across, 1)
    solved, remainder = call(
        final_kernel,
        [jax.ShapeDtypeStruct((size, width), jnp.float32), jax.ShapeDtypeStruct(rhs.shape, jnp.float32)],
        [q, rest, rhs, mine, beside, across, corner],
        [VMEM] * 7,
        [VMEM] * 2,
    )
    return solved[None, None], remainder[:, None]


def solution(mesh):
    in_specs = (
        P(None, "row", None, None),
        P(None, "row", None),
        P(None, "col", "row", None, None, None),
        P(None, "col", "row", None),
        P(None, "col", "row"),
    )
    out_specs = (P(None, "col", None, None), P(None, "row", None, None))
    small = mesh.shape["row"] == NR and mesh.shape["col"] == NC
    return jax.shard_map(
        on_device_8x4 if small else on_device_any,
        mesh=mesh,
        in_specs=in_specs,
        out_specs=out_specs,
        check_vma=False,
    )
```

```python
import functools

import jax
import jax.numpy as jnp
from jax import lax
from jax.experimental import pallas as pl
from jax.experimental.pallas import tpu as pltpu
from jax.sharding import PartitionSpec as P

VMEM = pl.BlockSpec(memory_space=pltpu.VMEM)
ANY = pl.BlockSpec(memory_space=pl.ANY)
HBM = pl.BlockSpec(memory_space=pltpu.HBM)
SMEM = pl.BlockSpec(memory_space=pltpu.SMEM)
TAIL = 16


def broadcast(value, axis, root):
    mine = lax.axis_index(axis) == root
    return lax.psum(jnp.where(mine, value, jnp.zeros_like(value)), axis)


def on_device_any(rhs, diag_inv, blocks, block_rows, counts):
    nrow = lax.axis_size("row")
    ncol = lax.axis_size("col")
    my_row = lax.axis_index("row")
    my_col = lax.axis_index("col")
    kc = diag_inv.shape[0]
    rb_local = rhs.shape[0]
    nz_local = blocks.shape[3]
    local_rhs = rhs[:, 0]
    partial_value = jnp.zeros(local_rhs.shape, jnp.float32)
    solved_list = [jnp.zeros(local_rhs.shape[1:], jnp.float32)]
    slot_ids = jnp.arange(nz_local, dtype=jnp.int32)
    local_ids = jnp.arange(rb_local, dtype=jnp.int32)
    for k in range(kc):
        j = k // ncol
        owner_row = k % nrow
        local_pivot = k // nrow
        mine_row = my_row == owner_row
        mine_col = my_col == k % ncol
        pivot_part = jnp.where(mine_row, partial_value[local_pivot], jnp.float32(0.0))
        summed = lax.psum(pivot_part, "col")
        updated = (local_rhs[local_pivot] - summed).astype(jnp.bfloat16)
        pivot_bf = broadcast(updated, "row", owner_row)
        row_part = jnp.dot(diag_inv[k], pivot_bf, preferred_element_type=jnp.float32)
        sol = lax.all_gather(row_part, "row", axis=0, tiled=True)
        sol_bf = sol.astype(jnp.bfloat16)
        rows = block_rows[j, 0, 0]
        glob = rows * nrow + my_row
        valid = (slot_ids < counts[j, 0, 0]) & (glob > k) & mine_col
        weights = (valid[:, None] & (rows[:, None] == local_ids[None, :])).astype(jnp.float32)
        contrib = jnp.einsum(
            "sab,bn->san", blocks[j, 0, 0], sol_bf, preferred_element_type=jnp.float32
        )
        partial_value = partial_value + jnp.einsum(
            "sl,san->lan", weights, contrib, precision=lax.Precision.HIGHEST
        )
        solved_list[j] = jnp.where(mine_col, sol, solved_list[j])
    total = lax.psum(partial_value, "col")
    remainder = (local_rhs - total)[:, None]
    solved = jnp.stack(solved_list)[:, None]
    return (solved, remainder)


NR, NC = 8, 4
MAKER = (None, (2, 1), (3, 2), (5, 3))
FIRST = (1, 0)
BESIDE = (3, 1)
PARTNER = (None, (3, 1), (3, 3), (5, 2))
PIECES = ((4, 1), (6, 3), (5, 2), (7, 0))
SENDS = (
    (0, 1, 2, 3),
    (0, 1, 2, 3),
    (3, 1, 0, 2),
    (0, 1, 3, 2),
    (0, 1, 3, 2),
    (2, 1, 3, 0),
    (0, 3, 1, 2),
    (1, 3, 0, 2),
)
REST = ((3, 3), (0, 3), (1, 3))


def hops(a, b):
    d = a ^ b
    if d < 2:
        return 1 if d else 10000
    return 100 + abs((a >> 3) - (b >> 3)) + ((d >> 2) & 1) + ((d >> 1) & 1)


def complete(pairs):
    to = {a * NC + b: c * NC + d for (a, b), (c, d) in pairs}
    free_from = [i for i in range(NR * NC) if i not in to]
    free_to = [i for i in range(NR * NC) if i not in to.values()]
    n = len(free_from)
    u, v, match = [0] * (n + 1), [0] * (n + 1), [0] * (n + 1)
    for i in range(1, n + 1):
        match[0], j0 = i, 0
        least, way, used = [10**9] * (n + 1), [0] * (n + 1), [False] * (n + 1)
        while True:
            used[j0] = True
            i0, delta, j1 = match[j0], 10**9, 0
            for j in range(1, n + 1):
                if not used[j]:
                    cur = hops(free_from[i0 - 1], free_to[j - 1]) - u[i0] - v[j]
                    if cur < least[j]:
                        least[j], way[j] = cur, j0
                    if least[j] < delta:
                        delta, j1 = least[j], j
            for j in range(n + 1):
                if used[j]:
                    u[match[j]] += delta
                    v[j] -= delta
                else:
                    least[j] -= delta
            j0 = j1
            if match[j0] == 0:
                break
        while j0:
            j1 = way[j0]
            match[j0] = match[j1]
            j0 = j1
    for j in range(1, n + 1):
        to[free_from[match[j] - 1]] = free_to[j - 1]
    return [(divmod(a, NC), divmod(b, NC)) for a, b in sorted(to.items())]


def send(value, pairs):
    return lax.ppermute(value, ("row", "col"), [(a * NC + b, c * NC + d) for (a, b), (c, d) in complete(pairs)])


def send_only(value, pairs):
    return lax.ppermute(value, ("row", "col"), [(a * NC + b, c * NC + d) for (a, b), (c, d) in pairs])


def dot(a, b):
    return jnp.dot(a, b, preferred_element_type=jnp.float32)


def low(a):
    return a.astype(jnp.bfloat16)


def at(device):
    return (lax.axis_index("row") == device[0]) & (lax.axis_index("col") == device[1])


def any_of(devices):
    flag = at(devices[0])
    for d in devices[1:]:
        flag = flag | at(d)
    return flag


def call(kernel, outs, ins, in_specs, out_specs, scratch=(), limit=16):
    return pl.pallas_call(
        kernel,
        out_shape=outs,
        in_specs=in_specs,
        out_specs=out_specs,
        scratch_shapes=list(scratch),
        compiler_params=pltpu.CompilerParams(vmem_limit_bytes=limit << 20),
        name=kernel.func.__name__ if isinstance(kernel, functools.partial) else kernel.__name__,
    )(*ins)


def pair_width(m, part):
    return 2 * (m + 1) * part


def cut_kernel(diag_ref, *refs):
    cuts, sem = refs[:-1], refs[-1]
    row, col = lax.axis_index("row"), lax.axis_index("col")
    part = diag_ref.shape[1]
    k = jnp.int32(0)
    for r in range(NR):
        for c in range(NC):
            k = jnp.where((row == r) & (col == c), SENDS[r][c], k)
    for m in range(NR // 2):

        @pl.when(jnp.where((row == 1) & (k == 0), 1, row // 2) == m)
        def _():
            copy = pltpu.make_async_copy(diag_ref.at[k, :, pl.ds(0, pair_width(m, part))], cuts[m], sem)
            copy.start()
            copy.wait()


def first_kernel(rhs_ref, diag_ref, *refs):
    parts, (out_ref, rhs_v, d_v, rhs_sem, d_sem) = refs[:-5], refs[-5:]
    n = out_ref.shape[0] // 2
    col = lax.axis_index("col")

    @pl.when(lax.axis_index("row") == 0)
    def _():
        rhs_copy = pltpu.make_async_copy(rhs_ref.at[0], rhs_v, rhs_sem)
        rhs_copy.start()

        def pieces(c):
            copies = []
            for i, r in enumerate(PIECES[c]):
                m = max(r // 2, 1)
                wide = pair_width(m, n)
                source = parts[m - 1] if r else diag_ref.at[0, :, pl.ds(0, wide)]
                copies.append(pltpu.make_async_copy(source, d_v.at[i, :, pl.ds(0, wide)], d_sem.at[i]))
            return copies

        for c in range(NC):

            @pl.when(col == c)
            def _():
                for copy in pieces(c):
                    copy.start()

        rhs_copy.wait()
        p = low(rhs_v[...])
        for c in range(NC):

            @pl.when(col == c)
            def _():
                for i, copy in enumerate(pieces(c)):
                    copy.wait()
                    wide = pair_width(max(PIECES[c][i] // 2, 1), n)
                    out_ref[i * n : (i + 1) * n] = low(dot(d_v[i, :, :wide], p[:wide]))


def pack_kernel(*refs):
    parts, out_ref, sem = refs[:-2], refs[-2], refs[-1]

    @pl.when(any_of(PARTNER[1:]))
    def _():
        copies, left = [], 0
        for m, source in enumerate(parts):
            wide = source.shape[1]
            copies.append(pltpu.make_async_copy(source, out_ref.at[:, pl.ds(left, wide)], sem.at[m]))
            left += wide
        for copy in copies:
            copy.start()
        for copy in copies:
            copy.wait()


def whole_kernel(diag_ref, even_ref, *refs):
    odd, out_ref, sem = refs[:-2], refs[-2], refs[-1]
    size = out_ref.shape[0]
    part = size // NR
    row, col = lax.axis_index("row"), lax.axis_index("col")

    @pl.when(any_of(MAKER[1:]))
    def _():
        def copy(i, source):
            wide = pair_width(i // 2, part)
            return pltpu.make_async_copy(source, out_ref.at[pl.ds(i * part, part), pl.ds(0, wide)], sem.at[i])

        left = 0
        for i in range(NR):
            wide = pair_width(i // 2, part)
            if i % 2:
                source = odd[i // 2]
            else:
                source = even_ref.at[:, pl.ds(left, wide)]
                left += wide

            @pl.when(row == i)
            def _():
                copy(i, diag_ref.at[col, :, pl.ds(0, wide)]).start()

            @pl.when(row != i)
            def _():
                copy(i, source).start()

        for m in range(NR // 2 - 1):
            right = pair_width(m, part)
            out_ref[pl.ds(2 * m * part, 2 * part), pl.ds(right, size - right)] = jnp.zeros(
                (2 * part, size - right), out_ref.dtype
            )
        for i in range(NR):
            copy(i, odd[i // 2]).wait()


def lower_dot(q_ref, d_ref, p_ref):
    half = d_ref.shape[0] // 2
    q_ref[:half] = low(dot(d_ref[:half, :half], p_ref[:half]))
    q_ref[half:] = low(dot(d_ref[half:], p_ref[...]))


def step0_kernel(g0, g1, g2, g3, rhs_ref, l_ref, p_ref, q_ref, s_ref):
    part = l_ref.shape[0] // NR
    row = lax.axis_index("row")

    def lookup(c, i):
        r = jnp.int32(PIECES[0][i])
        for n in range(1, NC):
            r = jnp.where(c == n, PIECES[n][i], r)
        return pl.multiple_of(r * part, part)

    @pl.when((row >= 1) & (row < 4) & (lax.axis_index("col") == 0))
    def _():
        for j, got in enumerate((g0, g1, g2, g3)):
            src = lax.rem(row + 7 - j, 4)
            q_ref[pl.ds(lookup(src, 0), part)] = got[:part]
            q_ref[pl.ds(lookup(src, 1), part)] = got[part:]
        s = dot(l_ref[...], q_ref[...])
        s_ref[...] = low(s)
        p_ref[...] = low(rhs_ref[0] - s)


def step1_kernel(p_in, d_ref, q_prev, q_ref):
    active = at(MAKER[1])

    @pl.when(active)
    def _():
        lower_dot(q_ref, d_ref, p_in)

    @pl.when(jnp.logical_not(active))
    def _():
        q_ref[...] = q_prev[...]


def step1_sum_kernel(q_in, sum_ref, rhs_ref, l_ref, s_prev, p_ref, s_ref):
    active = at(MAKER[1])

    @pl.when(active)
    def _():
        s = dot(l_ref[...], q_in[...]) + sum_ref[...].astype(jnp.float32)
        s_ref[...] = low(s)
        p_ref[...] = low(rhs_ref[0] - s)

    @pl.when(jnp.logical_not(active))
    def _():
        s_ref[...] = s_prev[...]


def step2_kernel(p_in, q_in, sum_ref, rhs_ref, d_ref, l_ref, q_prev, s_prev, a_ref, q_ref, s_ref):
    active, beside = at(MAKER[2]), at(BESIDE)

    @pl.when(active)
    def _():
        lower_dot(q_ref, d_ref, p_in)
        a_ref[...] = q_ref[...]
        s_ref[...] = low(dot(l_ref[...], q_ref[...]))

    @pl.when(beside)
    def _():
        q_ref[...] = q_in[...]
        s = dot(l_ref[...], q_in[...]) + sum_ref[...].astype(jnp.float32)
        s_ref[...] = low(s)
        a_ref[...] = low(rhs_ref[0] - s)

    @pl.when(jnp.logical_not(active | beside))
    def _():
        q_ref[...] = q_prev[...]
        s_ref[...] = s_prev[...]


def step3_kernel(takers, a_ref, sum_ref, *refs):
    came, (d_ref, q_prev, q_ref, p_v) = refs[:-4], refs[-4:]
    active = at(MAKER[3])

    @pl.when(active)
    def _():
        p_v[...] = low(a_ref[...].astype(jnp.float32) - sum_ref[...].astype(jnp.float32))
        lower_dot(q_ref, d_ref, p_v)

    for devices, source in zip(takers, came):

        @pl.when(any_of(devices))
        def _():
            q_ref[...] = source[...]

    @pl.when(jnp.logical_not(active | any_of([d for devices in takers for d in devices])))
    def _():
        q_ref[...] = q_prev[...]


def update_kernel(takers, rows_ref, counts_ref, s_ref, l_ref, q_prev, *refs):
    got, q_ref, out_ref = refs[:-2], refs[-2], refs[-1]
    size = l_ref.shape[0]
    row, col = lax.axis_index("row"), lax.axis_index("col")
    below = row >= NC

    def take(flag, source):
        @pl.when(flag)
        def _():
            q_ref[...] = source[...]

    kept = jnp.logical_not(any_of([d for devices in takers for d in devices]))
    take(kept, q_prev)
    for devices, source in zip(takers, got):
        take(any_of(devices), source)

    @pl.when(below)
    def _():
        out_ref[pl.ds(0, size)] = low(dot(l_ref[...], q_ref[...]))

    @pl.when(jnp.logical_not(below))
    def _():
        out_ref[pl.ds(0, size)] = s_ref[...]

    listed = rows_ref[0, 0, 0, 0]
    there = below & (counts_ref[0, 0, 0] > 0)
    done = at(FIRST) | at(MAKER[1]) | at(BESIDE) | at(MAKER[2])
    first = (there & (listed == 0)) | done
    second = there & (listed == 1)
    ids = lax.broadcasted_iota(jnp.int32, (TAIL, out_ref.shape[1]), 0)
    flag = ((ids == 0) & first) | ((ids == 1) & second)
    out_ref[pl.ds(size, TAIL)] = low(jnp.where(flag, 1.0, 0.0))


def minus(acc, sums, i):
    size = acc.shape[0]
    for s in sums:
        keep = s[pl.ds(size, TAIL)].astype(jnp.float32)[i : i + 1] > 0.5
        acc = acc - jnp.where(keep, s[pl.ds(0, size)].astype(jnp.float32), 0.0)
    return acc


def half_kernel(q_ref, rest_ref, rhs_ref, mine_ref, across_ref, solved_ref, out_ref):
    came = any_of(REST)

    @pl.when(came)
    def _():
        solved_ref[...] = rest_ref[...].astype(jnp.float32)

    @pl.when(jnp.logical_not(came))
    def _():
        solved_ref[...] = q_ref[...].astype(jnp.float32)

    for i in range(out_ref.shape[0]):
        out_ref[i] = minus(rhs_ref[i], (mine_ref, across_ref), i)


def final_kernel(half_ref, beside_ref, corner_ref, out_ref):
    for i in range(out_ref.shape[0]):
        out_ref[i] = minus(half_ref[i], (beside_ref, corner_ref), i)


def on_device_8x4(rhs, diag_inv, blocks, block_rows, counts):
    size, width = rhs.shape[2:]
    part = size // NR
    rhs = rhs[:, 0]
    block = blocks[0, 0, 0, 0]
    bf16 = jnp.bfloat16
    vec = jax.ShapeDtypeStruct((size, width), bf16)
    dma = pltpu.SemaphoreType.DMA

    wides = [pair_width(m, part) for m in range(NR // 2)]
    cuts = call(
        cut_kernel, [jax.ShapeDtypeStruct((part, w), bf16) for w in wides], [diag_inv], [HBM], [ANY] * len(wides), [dma]
    )
    at_piece = {r: (0, c) for c, rows in enumerate(PIECES) for r in rows}
    parts = []
    for m, cut in enumerate(cuts):
        pairs = []
        for r in range(NR):
            for c, k in enumerate(SENDS[r]):
                if k == 0 and r and max(r // 2, 1) == m:
                    pairs.append(((r, c), at_piece[r]))
                if k and MAKER[k][0] != r and r // 2 == m:
                    pairs.append(((r, c), MAKER[k] if r % 2 else PARTNER[k]))
        parts.append(send_only(cut, pairs))
    q = call(
        first_kernel,
        jax.ShapeDtypeStruct((2 * part, width), bf16),
        [rhs, diag_inv, *parts[1:]],
        [HBM, HBM] + [ANY] * (len(wides) - 1),
        VMEM,
        [
            pltpu.VMEM((size, width), jnp.float32),
            pltpu.VMEM((2, part, size), bf16),
            dma,
            pltpu.SemaphoreType.DMA((2,)),
        ],
    )
    takers = (FIRST, (2, 0), (3, 0))
    got = [send(q, [((0, c), takers[(c + j) % 4]) for c in range(4) if (c + j) % 4 < 3]) for j in range(4)]
    even = call(
        pack_kernel,
        jax.ShapeDtypeStruct((part, sum(wides)), bf16),
        parts,
        [ANY] * len(wides),
        VMEM,
        [pltpu.SemaphoreType.DMA((len(wides),))],
    )
    even = send(even, [(PARTNER[k], MAKER[k]) for k in range(1, NC)])
    diag = call(
        whole_kernel,
        jax.ShapeDtypeStruct((size, size), bf16),
        [diag_inv, even, *parts],
        [HBM] + [ANY] * (1 + len(wides)),
        VMEM,
        [pltpu.SemaphoreType.DMA((NR,))],
    )

    p, q, s = call(step0_kernel, [vec] * 3, [*got, rhs, block], [VMEM] * 6, [VMEM] * 3)
    p_in = send(p, [(FIRST, MAKER[1])])
    sums = send(s, [((2, 0), MAKER[1]), ((3, 0), BESIDE)])
    q = call(step1_kernel, vec, [p_in, diag, q], [VMEM] * 3, VMEM)
    p, s = call(step1_sum_kernel, [vec] * 2, [q, sums, rhs, block, s], [VMEM] * 5, [VMEM] * 2)
    p_in = send(p, [(MAKER[1], MAKER[2])])
    q_in = send(q, [(MAKER[1], BESIDE)])

    came = send(q, [((2, 0), (4, 0)), ((3, 0), (5, 0)), ((1, 0), (0, 0)), ((2, 1), (4, 1))])
    took = [(4, 0), (5, 0), (0, 0), (4, 1)]
    p_in, came = lax.optimization_barrier((p_in, came))

    a, q, s = call(step2_kernel, [vec] * 3, [p_in, q_in, sums, rhs, diag, block, q, s], [VMEM] * 8, [VMEM] * 3)
    from_c = a
    a = send(a, [(BESIDE, MAKER[3])])
    sums = send(s, [(MAKER[2], MAKER[3])])
    early = ((2, 2), (7, 2), (4, 2))
    got = [send_only(from_c, [(MAKER[2], d)]) for d in early]
    q = call(
        functools.partial(step3_kernel, [[d] for d in early] + [took]),
        vec,
        [a, sums, *got, came, diag, q],
        [VMEM] * 8,
        VMEM,
        [pltpu.VMEM((size, width), bf16)],
    )

    sends = [
        [
            (MAKER[3], (6, 3)), ((2, 2), (6, 2)), ((7, 2), (5, 2)),
            ((4, 0), (6, 0)), ((5, 0), (7, 0)), ((4, 1), (6, 1)), ((3, 1), (5, 1)), ((2, 1), (0, 1)),
        ],
        [(MAKER[3], (7, 3)), ((2, 2), (0, 2)), (MAKER[2], (1, 2)), ((4, 1), (7, 1)), ((3, 1), (1, 1))],
        [(MAKER[3], (4, 3))],
        [(MAKER[3], (2, 3))],
    ]
    got = [send_only(q, pairs) for pairs in sends]
    takers = [[b for _, b in pairs] for pairs in sends]
    q, mine = call(
        functools.partial(update_kernel, takers),
        [vec, jax.ShapeDtypeStruct((size + TAIL, width), bf16)],
        [block_rows, counts, s, block, q, *got],
        [SMEM] * 2 + [VMEM] * (3 + len(got)),
        [VMEM] * 2,
    )

    def swap(value, step):
        return send(value, [((r, c), (r, c ^ step)) for r in range(NR) for c in range(NC)])

    across = swap(mine, 2)
    rest = send_only(q, list(zip(((2, 3), (6, 3), (7, 3)), REST)))
    beside = swap(mine, 1)
    across, rest = lax.optimization_barrier((across, rest))
    corner = swap(across, 1)
    whole_rhs = jax.ShapeDtypeStruct(rhs.shape, jnp.float32)
    solved, half = call(
        half_kernel,
        [jax.ShapeDtypeStruct((size, width), jnp.float32), whole_rhs],
        [q, rest, rhs, mine, across],
        [VMEM] * 5,
        [VMEM] * 2,
    )
    remainder = call(final_kernel, whole_rhs, [half, beside, corner], [VMEM] * 3, VMEM)
    return solved[None, None], remainder[:, None]


def solution(mesh):
    in_specs = (
        P(None, "row", None, None),
        P(None, "row", None),
        P(None, "col", "row", None, None, None),
        P(None, "col", "row", None),
        P(None, "col", "row"),
    )
    out_specs = (P(None, "col", None, None), P(None, "row", None, None))
    small = mesh.shape["row"] == NR and mesh.shape["col"] == NC
    return jax.shard_map(
        on_device_8x4 if small else on_device_any,
        mesh=mesh,
        in_specs=in_specs,
        out_specs=out_specs,
        check_vma=False,
    )
```

```python
import functools

import jax
import jax.numpy as jnp
from jax import lax
from jax.experimental import pallas as pl
from jax.experimental.pallas import tpu as pltpu
from jax.sharding import PartitionSpec as P

VMEM = pl.BlockSpec(memory_space=pltpu.VMEM)
ANY = pl.BlockSpec(memory_space=pl.ANY)
HBM = pl.BlockSpec(memory_space=pltpu.HBM)
SMEM = pl.BlockSpec(memory_space=pltpu.SMEM)
TAIL = 16


def broadcast(value, axis, root):
    mine = lax.axis_index(axis) == root
    return lax.psum(jnp.where(mine, value, jnp.zeros_like(value)), axis)


def on_device_any(rhs, diag_inv, blocks, block_rows, counts):
    nrow = lax.axis_size("row")
    ncol = lax.axis_size("col")
    my_row = lax.axis_index("row")
    my_col = lax.axis_index("col")
    kc = diag_inv.shape[0]
    rb_local = rhs.shape[0]
    nz_local = blocks.shape[3]
    local_rhs = rhs[:, 0]
    partial_value = jnp.zeros(local_rhs.shape, jnp.float32)
    solved_list = [jnp.zeros(local_rhs.shape[1:], jnp.float32)]
    slot_ids = jnp.arange(nz_local, dtype=jnp.int32)
    local_ids = jnp.arange(rb_local, dtype=jnp.int32)
    for k in range(kc):
        j = k // ncol
        owner_row = k % nrow
        local_pivot = k // nrow
        mine_row = my_row == owner_row
        mine_col = my_col == k % ncol
        pivot_part = jnp.where(mine_row, partial_value[local_pivot], jnp.float32(0.0))
        summed = lax.psum(pivot_part, "col")
        updated = (local_rhs[local_pivot] - summed).astype(jnp.bfloat16)
        pivot_bf = broadcast(updated, "row", owner_row)
        row_part = jnp.dot(diag_inv[k], pivot_bf, preferred_element_type=jnp.float32)
        sol = lax.all_gather(row_part, "row", axis=0, tiled=True)
        sol_bf = sol.astype(jnp.bfloat16)
        rows = block_rows[j, 0, 0]
        glob = rows * nrow + my_row
        valid = (slot_ids < counts[j, 0, 0]) & (glob > k) & mine_col
        weights = (valid[:, None] & (rows[:, None] == local_ids[None, :])).astype(jnp.float32)
        contrib = jnp.einsum(
            "sab,bn->san", blocks[j, 0, 0], sol_bf, preferred_element_type=jnp.float32
        )
        partial_value = partial_value + jnp.einsum(
            "sl,san->lan", weights, contrib, precision=lax.Precision.HIGHEST
        )
        solved_list[j] = jnp.where(mine_col, sol, solved_list[j])
    total = lax.psum(partial_value, "col")
    remainder = (local_rhs - total)[:, None]
    solved = jnp.stack(solved_list)[:, None]
    return (solved, remainder)


NR, NC = 8, 4
MAKER = (None, (2, 1), (3, 2), (5, 3))
FIRST = (1, 0)
BESIDE = (3, 1)
PARTNER = (None, (3, 1), (3, 3), (5, 2))
PIECES = ((4, 1), (6, 3), (5, 2), (7, 0))
SENDS = (
    (0, 1, 2, 3),
    (0, 1, 2, 3),
    (3, 1, 0, 2),
    (0, 1, 3, 2),
    (0, 1, 3, 2),
    (2, 1, 3, 0),
    (0, 3, 1, 2),
    (1, 3, 0, 2),
)
REST = ((2, 3), (3, 3), (0, 3), (1, 3), (0, 2), (1, 2))


def hops(a, b):
    d = a ^ b
    if d < 2:
        return 1 if d else 10000
    return 100 + abs((a >> 3) - (b >> 3)) + ((d >> 2) & 1) + ((d >> 1) & 1)


def complete(pairs):
    to = {a * NC + b: c * NC + d for (a, b), (c, d) in pairs}
    free_from = [i for i in range(NR * NC) if i not in to]
    free_to = [i for i in range(NR * NC) if i not in to.values()]
    n = len(free_from)
    u, v, match = [0] * (n + 1), [0] * (n + 1), [0] * (n + 1)
    for i in range(1, n + 1):
        match[0], j0 = i, 0
        least, way, used = [10**9] * (n + 1), [0] * (n + 1), [False] * (n + 1)
        while True:
            used[j0] = True
            i0, delta, j1 = match[j0], 10**9, 0
            for j in range(1, n + 1):
                if not used[j]:
                    cur = hops(free_from[i0 - 1], free_to[j - 1]) - u[i0] - v[j]
                    if cur < least[j]:
                        least[j], way[j] = cur, j0
                    if least[j] < delta:
                        delta, j1 = least[j], j
            for j in range(n + 1):
                if used[j]:
                    u[match[j]] += delta
                    v[j] -= delta
                else:
                    least[j] -= delta
            j0 = j1
            if match[j0] == 0:
                break
        while j0:
            j1 = way[j0]
            match[j0] = match[j1]
            j0 = j1
    for j in range(1, n + 1):
        to[free_from[match[j] - 1]] = free_to[j - 1]
    return [(divmod(a, NC), divmod(b, NC)) for a, b in sorted(to.items())]


def send(value, pairs):
    return lax.ppermute(value, ("row", "col"), [(a * NC + b, c * NC + d) for (a, b), (c, d) in complete(pairs)])


def send_only(value, pairs):
    return lax.ppermute(value, ("row", "col"), [(a * NC + b, c * NC + d) for (a, b), (c, d) in pairs])


def dot(a, b):
    return jnp.dot(a, b, preferred_element_type=jnp.float32)


def low(a):
    return a.astype(jnp.bfloat16)


def at(device):
    return (lax.axis_index("row") == device[0]) & (lax.axis_index("col") == device[1])


def any_of(devices):
    flag = at(devices[0])
    for d in devices[1:]:
        flag = flag | at(d)
    return flag


def call(kernel, outs, ins, in_specs, out_specs, scratch=(), limit=16):
    return pl.pallas_call(
        kernel,
        out_shape=outs,
        in_specs=in_specs,
        out_specs=out_specs,
        scratch_shapes=list(scratch),
        compiler_params=pltpu.CompilerParams(vmem_limit_bytes=limit << 20),
        name=kernel.func.__name__ if isinstance(kernel, functools.partial) else kernel.__name__,
    )(*ins)


def pair_width(m, part):
    return 2 * (m + 1) * part


def cut_kernel(diag_ref, *refs):
    cuts, sem = refs[:-1], refs[-1]
    row, col = lax.axis_index("row"), lax.axis_index("col")
    part = diag_ref.shape[1]
    k = jnp.int32(0)
    for r in range(NR):
        for c in range(NC):
            k = jnp.where((row == r) & (col == c), SENDS[r][c], k)
    for m in range(NR // 2):

        @pl.when(jnp.where((row == 1) & (k == 0), 1, row // 2) == m)
        def _():
            copy = pltpu.make_async_copy(diag_ref.at[k, :, pl.ds(0, pair_width(m, part))], cuts[m], sem)
            copy.start()
            copy.wait()


def first_kernel(rhs_ref, diag_ref, *refs):
    parts, (out_ref, rhs_v, d_v, rhs_sem, d_sem) = refs[:-5], refs[-5:]
    n = out_ref.shape[0] // 2
    col = lax.axis_index("col")

    @pl.when(lax.axis_index("row") == 0)
    def _():
        rhs_copy = pltpu.make_async_copy(rhs_ref.at[0], rhs_v, rhs_sem)
        rhs_copy.start()

        def pieces(c):
            copies = []
            for i, r in enumerate(PIECES[c]):
                m = max(r // 2, 1)
                wide = pair_width(m, n)
                source = parts[m - 1] if r else diag_ref.at[0, :, pl.ds(0, wide)]
                copies.append(pltpu.make_async_copy(source, d_v.at[i, :, pl.ds(0, wide)], d_sem.at[i]))
            return copies

        for c in range(NC):

            @pl.when(col == c)
            def _():
                for copy in pieces(c):
                    copy.start()

        rhs_copy.wait()
        p = low(rhs_v[...])
        for c in range(NC):

            @pl.when(col == c)
            def _():
                for i, copy in enumerate(pieces(c)):
                    copy.wait()
                    wide = pair_width(max(PIECES[c][i] // 2, 1), n)
                    out_ref[i * n : (i + 1) * n] = low(dot(d_v[i, :, :wide], p[:wide]))


def pack_kernel(*refs):
    parts, out_ref, sem = refs[:-2], refs[-2], refs[-1]

    @pl.when(any_of(PARTNER[1:]))
    def _():
        copies, left = [], 0
        for m, source in enumerate(parts):
            wide = source.shape[1]
            copies.append(pltpu.make_async_copy(source, out_ref.at[:, pl.ds(left, wide)], sem.at[m]))
            left += wide
        for copy in copies:
            copy.start()
        for copy in copies:
            copy.wait()


def whole_kernel(rows_ref, counts_ref, diag_ref, even_ref, *refs):
    odd, (out_ref, tail_ref, sem) = refs[:-3], refs[-3:]
    size = out_ref.shape[0]
    part = size // NR
    row, col = lax.axis_index("row"), lax.axis_index("col")
    listed = rows_ref[0, 0, 0, 0]
    there = (row >= NC) & (counts_ref[0, 0, 0] > 0)
    done = at(FIRST) | at(MAKER[1]) | at(BESIDE) | at(MAKER[2])
    first = (there & (listed == 0)) | done
    second = there & (listed == 1)
    ids = lax.broadcasted_iota(jnp.int32, tail_ref.shape, 0)
    flag = ((ids == 0) & first) | ((ids == 1) & second)
    tail_ref[...] = low(jnp.where(flag, 1.0, 0.0))

    @pl.when(any_of(MAKER[1:]))
    def _():
        def copy(i, source):
            wide = pair_width(i // 2, part)
            return pltpu.make_async_copy(source, out_ref.at[pl.ds(i * part, part), pl.ds(0, wide)], sem.at[i])

        left = 0
        for i in range(NR):
            wide = pair_width(i // 2, part)
            if i % 2:
                source = odd[i // 2]
            else:
                source = even_ref.at[:, pl.ds(left, wide)]
                left += wide

            @pl.when(row == i)
            def _():
                copy(i, diag_ref.at[col, :, pl.ds(0, wide)]).start()

            @pl.when(row != i)
            def _():
                copy(i, source).start()

        for m in range(NR // 2 - 1):
            right = pair_width(m, part)
            out_ref[pl.ds(2 * m * part, 2 * part), pl.ds(right, size - right)] = jnp.zeros(
                (2 * part, size - right), out_ref.dtype
            )
        for i in range(NR):
            copy(i, odd[i // 2]).wait()


def lower_dot(q_ref, d_ref, p_ref):
    half = d_ref.shape[0] // 2
    q_ref[:half] = low(dot(d_ref[:half, :half], p_ref[:half]))
    q_ref[half:] = low(dot(d_ref[half:], p_ref[...]))


def step0_kernel(g0, g1, g2, g3, rhs_ref, l_ref, p_ref, q_ref, s_ref):
    part = l_ref.shape[0] // NR
    row = lax.axis_index("row")

    def lookup(c, i):
        r = jnp.int32(PIECES[0][i])
        for n in range(1, NC):
            r = jnp.where(c == n, PIECES[n][i], r)
        return pl.multiple_of(r * part, part)

    @pl.when((row >= 1) & (row < 4) & (lax.axis_index("col") == 0))
    def _():
        for j, got in enumerate((g0, g1, g2, g3)):
            src = lax.rem(row + 7 - j, 4)
            q_ref[pl.ds(lookup(src, 0), part)] = got[:part]
            q_ref[pl.ds(lookup(src, 1), part)] = got[part:]
        s = dot(l_ref[...], q_ref[...])
        s_ref[...] = low(s)
        p_ref[...] = low(rhs_ref[0] - s)


def step1_kernel(p_in, d_ref, q_prev, q_ref):
    active = at(MAKER[1])

    @pl.when(active)
    def _():
        lower_dot(q_ref, d_ref, p_in)

    @pl.when(jnp.logical_not(active))
    def _():
        q_ref[...] = q_prev[...]


def step1_sum_kernel(q_in, sum_ref, rhs_ref, l_ref, s_prev, p_ref, s_ref):
    active = at(MAKER[1])

    @pl.when(active)
    def _():
        s = dot(l_ref[...], q_in[...]) + sum_ref[...].astype(jnp.float32)
        s_ref[...] = low(s)
        p_ref[...] = low(rhs_ref[0] - s)

    @pl.when(jnp.logical_not(active))
    def _():
        s_ref[...] = s_prev[...]


def step2_kernel(p_in, q_in, sum_ref, rhs_ref, d_ref, l_ref, q_prev, s_prev, a_ref, q_ref, s_ref):
    active, beside = at(MAKER[2]), at(BESIDE)

    @pl.when(active)
    def _():
        lower_dot(q_ref, d_ref, p_in)
        a_ref[...] = q_ref[...]
        s_ref[...] = low(dot(l_ref[...], q_ref[...]))

    @pl.when(beside)
    def _():
        q_ref[...] = q_in[...]
        s = dot(l_ref[...], q_in[...]) + sum_ref[...].astype(jnp.float32)
        s_ref[...] = low(s)
        a_ref[...] = low(rhs_ref[0] - s)

    @pl.when(jnp.logical_not(active | beside))
    def _():
        q_ref[...] = q_prev[...]
        s_ref[...] = s_prev[...]


def step3_kernel(takers, a_ref, sum_ref, *refs):
    came, (d_ref, q_prev, q_ref, p_v) = refs[:-4], refs[-4:]
    active = at(MAKER[3])

    @pl.when(active)
    def _():
        p_v[...] = low(a_ref[...].astype(jnp.float32) - sum_ref[...].astype(jnp.float32))
        lower_dot(q_ref, d_ref, p_v)

    for devices, source in zip(takers, came):

        @pl.when(any_of(devices))
        def _():
            q_ref[...] = source[...]

    @pl.when(jnp.logical_not(active | any_of([d for devices in takers for d in devices])))
    def _():
        q_ref[...] = q_prev[...]


def update_kernel(takers, tail_ref, s_ref, l_ref, q_prev, *refs):
    got, q_ref, out_ref = refs[:-2], refs[-2], refs[-1]
    size = l_ref.shape[0]
    row, col = lax.axis_index("row"), lax.axis_index("col")
    below = row >= NC

    def take(flag, source):
        @pl.when(flag)
        def _():
            q_ref[...] = source[...]

    kept = jnp.logical_not(any_of([d for devices in takers for d in devices]))
    take(kept, q_prev)
    for devices, source in zip(takers, got):
        take(any_of(devices), source)

    @pl.when(below)
    def _():
        out_ref[pl.ds(0, size)] = low(dot(l_ref[...], q_ref[...]))

    @pl.when(jnp.logical_not(below))
    def _():
        out_ref[pl.ds(0, size)] = s_ref[...]

    out_ref[pl.ds(size, TAIL)] = tail_ref[...]


def minus(acc, sums, i):
    size = acc.shape[0]
    for s in sums:
        keep = s[pl.ds(size, TAIL)].astype(jnp.float32)[i : i + 1] > 0.5
        acc = acc - jnp.where(keep, s[pl.ds(0, size)].astype(jnp.float32), 0.0)
    return acc


def half_kernel(q_ref, rest_ref, rhs_ref, mine_ref, across_ref, solved_ref, out_ref):
    came = any_of(REST)

    @pl.when(came)
    def _():
        solved_ref[...] = rest_ref[...].astype(jnp.float32)

    @pl.when(jnp.logical_not(came))
    def _():
        solved_ref[...] = q_ref[...].astype(jnp.float32)

    for i in range(out_ref.shape[0]):
        out_ref[i] = minus(rhs_ref[i], (mine_ref, across_ref), i)


def final_kernel(half_ref, beside_ref, corner_ref, out_ref):
    for i in range(out_ref.shape[0]):
        out_ref[i] = minus(half_ref[i], (beside_ref, corner_ref), i)


def on_device_8x4(rhs, diag_inv, blocks, block_rows, counts):
    size, width = rhs.shape[2:]
    part = size // NR
    rhs = rhs[:, 0]
    block = blocks[0, 0, 0, 0]
    bf16 = jnp.bfloat16
    vec = jax.ShapeDtypeStruct((size, width), bf16)
    dma = pltpu.SemaphoreType.DMA

    wides = [pair_width(m, part) for m in range(NR // 2)]
    cuts = call(
        cut_kernel, [jax.ShapeDtypeStruct((part, w), bf16) for w in wides], [diag_inv], [HBM], [ANY] * len(wides), [dma]
    )
    at_piece = {r: (0, c) for c, rows in enumerate(PIECES) for r in rows}
    parts = []
    for m, cut in enumerate(cuts):
        pairs = []
        for r in range(NR):
            for c, k in enumerate(SENDS[r]):
                if k == 0 and r and max(r // 2, 1) == m:
                    pairs.append(((r, c), at_piece[r]))
                if k and MAKER[k][0] != r and r // 2 == m:
                    pairs.append(((r, c), MAKER[k] if r % 2 else PARTNER[k]))
        parts.append(send_only(cut, pairs))
    q = call(
        first_kernel,
        jax.ShapeDtypeStruct((2 * part, width), bf16),
        [rhs, diag_inv, *parts[1:]],
        [HBM, HBM] + [ANY] * (len(wides) - 1),
        VMEM,
        [
            pltpu.VMEM((size, width), jnp.float32),
            pltpu.VMEM((2, part, size), bf16),
            dma,
            pltpu.SemaphoreType.DMA((2,)),
        ],
    )
    takers = (FIRST, (2, 0), (3, 0))
    got = [send(q, [((0, c), takers[(c + j) % 4]) for c in range(4) if (c + j) % 4 < 3]) for j in range(4)]
    even = call(
        pack_kernel,
        jax.ShapeDtypeStruct((part, sum(wides)), bf16),
        parts,
        [ANY] * len(wides),
        VMEM,
        [pltpu.SemaphoreType.DMA((len(wides),))],
    )
    even = send(even, [(PARTNER[k], MAKER[k]) for k in range(1, NC)])
    diag, tail = call(
        whole_kernel,
        [jax.ShapeDtypeStruct((size, size), bf16), jax.ShapeDtypeStruct((TAIL, width), bf16)],
        [block_rows, counts, diag_inv, even, *parts],
        [SMEM, SMEM, HBM] + [ANY] * (1 + len(wides)),
        [VMEM, VMEM],
        [pltpu.SemaphoreType.DMA((NR,))],
    )

    p, q, s = call(step0_kernel, [vec] * 3, [*got, rhs, block], [VMEM] * 6, [VMEM] * 3)
    p_in = send(p, [(FIRST, MAKER[1])])
    sums = send(s, [((2, 0), MAKER[1]), ((3, 0), BESIDE)])
    q = call(step1_kernel, vec, [p_in, diag, q], [VMEM] * 3, VMEM)
    p, s = call(step1_sum_kernel, [vec] * 2, [q, sums, rhs, block, s], [VMEM] * 5, [VMEM] * 2)
    p_in = send(p, [(MAKER[1], MAKER[2])])
    q_in = send(q, [(MAKER[1], BESIDE)])

    came = send(q, [((2, 0), (4, 0)), ((3, 0), (5, 0)), ((1, 0), (0, 0)), ((2, 1), (4, 1))])
    took = [(4, 0), (5, 0), (0, 0), (4, 1)]
    p_in, came = lax.optimization_barrier((p_in, came))

    a, q, s = call(step2_kernel, [vec] * 3, [p_in, q_in, sums, rhs, diag, block, q, s], [VMEM] * 8, [VMEM] * 3)
    a = send(a, [(BESIDE, MAKER[3])])
    sums = send(s, [(MAKER[2], MAKER[3])])
    early = ((2, 2), (7, 2), (5, 2))
    got = [send_only(q, [(MAKER[2], d)]) for d in early]
    q = call(
        functools.partial(step3_kernel, [[d] for d in early] + [took]),
        vec,
        [a, sums, *got, came, diag, q],
        [VMEM] * 8,
        VMEM,
        [pltpu.VMEM((size, width), bf16)],
    )

    sends = [
        [
            (MAKER[3], (6, 3)), ((2, 2), (4, 2)),
            ((4, 0), (6, 0)), ((5, 0), (7, 0)), ((4, 1), (6, 1)), ((3, 1), (5, 1)), ((2, 1), (0, 1)),
        ],
        [(MAKER[3], (7, 3)), ((2, 2), (6, 2)), ((4, 1), (7, 1)), ((3, 1), (1, 1))],
        [(MAKER[3], (4, 3))],
    ]
    got = [send_only(q, pairs) for pairs in sends]
    takers = [[b for _, b in pairs] for pairs in sends]
    q, mine = call(
        functools.partial(update_kernel, takers),
        [vec, jax.ShapeDtypeStruct((size + TAIL, width), bf16)],
        [tail, s, block, q, *got],
        [VMEM] * (4 + len(got)),
        [VMEM] * 2,
    )

    def swap(value, step):
        return send(value, [((r, c), (r, c ^ step)) for r in range(NR) for c in range(NC)])

    across = swap(mine, 2)
    rest = send_only(q, list(zip(((4, 3), (5, 3), (6, 3), (7, 3), (2, 2), MAKER[2]), REST)))
    beside = swap(mine, 1)
    across, rest = lax.optimization_barrier((across, rest))
    corner = swap(across, 1)
    whole_rhs = jax.ShapeDtypeStruct(rhs.shape, jnp.float32)
    solved, half = call(
        half_kernel,
        [jax.ShapeDtypeStruct((size, width), jnp.float32), whole_rhs],
        [q, rest, rhs, mine, across],
        [VMEM] * 5,
        [VMEM] * 2,
    )
    remainder = call(final_kernel, whole_rhs, [half, beside, corner], [VMEM] * 3, VMEM)
    return solved[None, None], remainder[:, None]


def solution(mesh):
    in_specs = (
        P(None, "row", None, None),
        P(None, "row", None),
        P(None, "col", "row", None, None, None),
        P(None, "col", "row", None),
        P(None, "col", "row"),
    )
    out_specs = (P(None, "col", None, None), P(None, "row", None, None))
    small = mesh.shape["row"] == NR and mesh.shape["col"] == NC
    return jax.shard_map(
        on_device_8x4 if small else on_device_any,
        mesh=mesh,
        in_specs=in_specs,
        out_specs=out_specs,
        check_vma=False,
    )
```

```python
import functools

import jax
import jax.numpy as jnp
from jax import lax
from jax.experimental import pallas as pl
from jax.experimental.pallas import tpu as pltpu
from jax.sharding import PartitionSpec as P

VMEM = pl.BlockSpec(memory_space=pltpu.VMEM)
ANY = pl.BlockSpec(memory_space=pl.ANY)
HBM = pl.BlockSpec(memory_space=pltpu.HBM)
SMEM = pl.BlockSpec(memory_space=pltpu.SMEM)
TAIL = 16


def broadcast(value, axis, root):
    mine = lax.axis_index(axis) == root
    return lax.psum(jnp.where(mine, value, jnp.zeros_like(value)), axis)


def on_device_any(rhs, diag_inv, blocks, block_rows, counts):
    nrow = lax.axis_size("row")
    ncol = lax.axis_size("col")
    my_row = lax.axis_index("row")
    my_col = lax.axis_index("col")
    kc = diag_inv.shape[0]
    rb_local = rhs.shape[0]
    nz_local = blocks.shape[3]
    local_rhs = rhs[:, 0]
    partial_value = jnp.zeros(local_rhs.shape, jnp.float32)
    solved_list = [jnp.zeros(local_rhs.shape[1:], jnp.float32)]
    slot_ids = jnp.arange(nz_local, dtype=jnp.int32)
    local_ids = jnp.arange(rb_local, dtype=jnp.int32)
    for k in range(kc):
        j = k // ncol
        owner_row = k % nrow
        local_pivot = k // nrow
        mine_row = my_row == owner_row
        mine_col = my_col == k % ncol
        pivot_part = jnp.where(mine_row, partial_value[local_pivot], jnp.float32(0.0))
        summed = lax.psum(pivot_part, "col")
        updated = (local_rhs[local_pivot] - summed).astype(jnp.bfloat16)
        pivot_bf = broadcast(updated, "row", owner_row)
        row_part = jnp.dot(diag_inv[k], pivot_bf, preferred_element_type=jnp.float32)
        sol = lax.all_gather(row_part, "row", axis=0, tiled=True)
        sol_bf = sol.astype(jnp.bfloat16)
        rows = block_rows[j, 0, 0]
        glob = rows * nrow + my_row
        valid = (slot_ids < counts[j, 0, 0]) & (glob > k) & mine_col
        weights = (valid[:, None] & (rows[:, None] == local_ids[None, :])).astype(jnp.float32)
        contrib = jnp.einsum(
            "sab,bn->san", blocks[j, 0, 0], sol_bf, preferred_element_type=jnp.float32
        )
        partial_value = partial_value + jnp.einsum(
            "sl,san->lan", weights, contrib, precision=lax.Precision.HIGHEST
        )
        solved_list[j] = jnp.where(mine_col, sol, solved_list[j])
    total = lax.psum(partial_value, "col")
    remainder = (local_rhs - total)[:, None]
    solved = jnp.stack(solved_list)[:, None]
    return (solved, remainder)


NR, NC = 8, 4
MAKER = (None, (2, 1), (3, 2), (5, 3))
FIRST = (1, 0)
BESIDE = (3, 1)
PARTNER = (None, (3, 1), (3, 3), (5, 2))
PIECES = ((4, 1), (6, 3), (5, 2), (7, 0))
SENDS = (
    (0, 1, 2, 3),
    (0, 1, 2, 3),
    (3, 1, 0, 2),
    (0, 1, 3, 2),
    (0, 1, 3, 2),
    (2, 1, 3, 0),
    (0, 3, 1, 2),
    (1, 3, 0, 2),
)
REST = ((2, 3), (3, 3), (0, 3), (1, 3), (0, 2), (1, 2))


def hops(a, b):
    d = a ^ b
    if d < 2:
        return 1 if d else 10000
    return 100 + abs((a >> 3) - (b >> 3)) + ((d >> 2) & 1) + ((d >> 1) & 1)


def complete(pairs):
    to = {a * NC + b: c * NC + d for (a, b), (c, d) in pairs}
    free_from = [i for i in range(NR * NC) if i not in to]
    free_to = [i for i in range(NR * NC) if i not in to.values()]
    n = len(free_from)
    u, v, match = [0] * (n + 1), [0] * (n + 1), [0] * (n + 1)
    for i in range(1, n + 1):
        match[0], j0 = i, 0
        least, way, used = [10**9] * (n + 1), [0] * (n + 1), [False] * (n + 1)
        while True:
            used[j0] = True
            i0, delta, j1 = match[j0], 10**9, 0
            for j in range(1, n + 1):
                if not used[j]:
                    cur = hops(free_from[i0 - 1], free_to[j - 1]) - u[i0] - v[j]
                    if cur < least[j]:
                        least[j], way[j] = cur, j0
                    if least[j] < delta:
                        delta, j1 = least[j], j
            for j in range(n + 1):
                if used[j]:
                    u[match[j]] += delta
                    v[j] -= delta
                else:
                    least[j] -= delta
            j0 = j1
            if match[j0] == 0:
                break
        while j0:
            j1 = way[j0]
            match[j0] = match[j1]
            j0 = j1
    for j in range(1, n + 1):
        to[free_from[match[j] - 1]] = free_to[j - 1]
    return [(divmod(a, NC), divmod(b, NC)) for a, b in sorted(to.items())]


def send(value, pairs):
    return lax.ppermute(value, ("row", "col"), [(a * NC + b, c * NC + d) for (a, b), (c, d) in complete(pairs)])


def send_only(value, pairs):
    return lax.ppermute(value, ("row", "col"), [(a * NC + b, c * NC + d) for (a, b), (c, d) in pairs])


def dot(a, b):
    return jnp.dot(a, b, preferred_element_type=jnp.float32)


def low(a):
    return a.astype(jnp.bfloat16)


def at(device):
    return (lax.axis_index("row") == device[0]) & (lax.axis_index("col") == device[1])


def any_of(devices):
    flag = at(devices[0])
    for d in devices[1:]:
        flag = flag | at(d)
    return flag


def call(kernel, outs, ins, in_specs, out_specs, scratch=(), limit=16):
    return pl.pallas_call(
        kernel,
        out_shape=outs,
        in_specs=in_specs,
        out_specs=out_specs,
        scratch_shapes=list(scratch),
        compiler_params=pltpu.CompilerParams(vmem_limit_bytes=limit << 20),
        name=kernel.func.__name__ if isinstance(kernel, functools.partial) else kernel.__name__,
    )(*ins)


def pair_width(m, part):
    return 2 * (m + 1) * part


def cut_kernel(diag_ref, *refs):
    cuts, sem = refs[:-1], refs[-1]
    row, col = lax.axis_index("row"), lax.axis_index("col")
    part = diag_ref.shape[1]
    k = jnp.int32(0)
    for r in range(NR):
        for c in range(NC):
            k = jnp.where((row == r) & (col == c), SENDS[r][c], k)
    for m in range(NR // 2):

        @pl.when(jnp.where((row == 1) & (k == 0), 1, row // 2) == m)
        def _():
            copy = pltpu.make_async_copy(diag_ref.at[k, :, pl.ds(0, pair_width(m, part))], cuts[m], sem)
            copy.start()
            copy.wait()


def first_kernel(rhs_ref, diag_ref, *refs):
    parts, (out_ref, rhs_v, d_v, rhs_sem, d_sem) = refs[:-5], refs[-5:]
    n = out_ref.shape[0] // 2
    col = lax.axis_index("col")

    @pl.when(lax.axis_index("row") == 0)
    def _():
        rhs_copy = pltpu.make_async_copy(rhs_ref.at[0], rhs_v, rhs_sem)
        rhs_copy.start()

        def pieces(c):
            copies = []
            for i, r in enumerate(PIECES[c]):
                m = max(r // 2, 1)
                wide = pair_width(m, n)
                source = parts[m - 1] if r else diag_ref.at[0, :, pl.ds(0, wide)]
                copies.append(pltpu.make_async_copy(source, d_v.at[i, :, pl.ds(0, wide)], d_sem.at[i]))
            return copies

        for c in range(NC):

            @pl.when(col == c)
            def _():
                for copy in pieces(c):
                    copy.start()

        rhs_copy.wait()
        p = low(rhs_v[...])
        for c in range(NC):

            @pl.when(col == c)
            def _():
                for i, copy in enumerate(pieces(c)):
                    copy.wait()
                    wide = pair_width(max(PIECES[c][i] // 2, 1), n)
                    out_ref[i * n : (i + 1) * n] = low(dot(d_v[i, :, :wide], p[:wide]))


def pack_kernel(*refs):
    parts, out_ref, sem = refs[:-2], refs[-2], refs[-1]

    @pl.when(any_of(PARTNER[1:]))
    def _():
        copies, left = [], 0
        for m, source in enumerate(parts):
            wide = source.shape[1]
            copies.append(pltpu.make_async_copy(source, out_ref.at[:, pl.ds(left, wide)], sem.at[m]))
            left += wide
        for copy in copies:
            copy.start()
        for copy in copies:
            copy.wait()


def whole_kernel(rows_ref, counts_ref, diag_ref, even_ref, *refs):
    odd, (out_ref, tail_ref, sem) = refs[:-3], refs[-3:]
    size = out_ref.shape[0]
    part = size // NR
    row, col = lax.axis_index("row"), lax.axis_index("col")
    listed = rows_ref[0, 0, 0, 0]
    there = (row >= NC) & (counts_ref[0, 0, 0] > 0)
    done = at(FIRST) | at(MAKER[1]) | at(BESIDE) | at(MAKER[2])
    first = (there & (listed == 0)) | done
    second = there & (listed == 1)
    ids = lax.broadcasted_iota(jnp.int32, tail_ref.shape, 0)
    flag = ((ids == 0) & first) | ((ids == 1) & second)
    tail_ref[...] = low(jnp.where(flag, 1.0, 0.0))

    @pl.when(any_of(MAKER[1:]))
    def _():
        def copy(i, source):
            wide = pair_width(i // 2, part)
            return pltpu.make_async_copy(source, out_ref.at[pl.ds(i * part, part), pl.ds(0, wide)], sem.at[i])

        left = 0
        for i in range(NR):
            wide = pair_width(i // 2, part)
            if i % 2:
                source = odd[i // 2]
            else:
                source = even_ref.at[:, pl.ds(left, wide)]
                left += wide

            @pl.when(row == i)
            def _():
                copy(i, diag_ref.at[col, :, pl.ds(0, wide)]).start()

            @pl.when(row != i)
            def _():
                copy(i, source).start()

        for m in range(NR // 2 - 1):
            right = pair_width(m, part)
            out_ref[pl.ds(2 * m * part, 2 * part), pl.ds(right, size - right)] = jnp.zeros(
                (2 * part, size - right), out_ref.dtype
            )
        for i in range(NR):
            copy(i, odd[i // 2]).wait()


def lower_dot(q_ref, d_ref, p_ref):
    half = d_ref.shape[0] // 2
    q_ref[:half] = low(dot(d_ref[:half, :half], p_ref[:half]))
    q_ref[half:] = low(dot(d_ref[half:], p_ref[...]))


def step0_kernel(g0, g1, g2, g3, rhs_ref, l_ref, p_ref, q_ref, s_ref):
    part = l_ref.shape[0] // NR
    row = lax.axis_index("row")

    def lookup(c, i):
        r = jnp.int32(PIECES[0][i])
        for n in range(1, NC):
            r = jnp.where(c == n, PIECES[n][i], r)
        return pl.multiple_of(r * part, part)

    @pl.when((row >= 1) & (row < 4) & (lax.axis_index("col") == 0))
    def _():
        for j, got in enumerate((g0, g1, g2, g3)):
            src = lax.rem(row + 7 - j, 4)
            q_ref[pl.ds(lookup(src, 0), part)] = got[:part]
            q_ref[pl.ds(lookup(src, 1), part)] = got[part:]
        s = dot(l_ref[...], q_ref[...])
        s_ref[...] = low(s)
        p_ref[...] = low(rhs_ref[0] - s)


def step1_kernel(p_in, d_ref, q_prev, q_ref):
    active = at(MAKER[1])

    @pl.when(active)
    def _():
        lower_dot(q_ref, d_ref, p_in)

    @pl.when(jnp.logical_not(active))
    def _():
        q_ref[...] = q_prev[...]


def step1_sum_kernel(q_in, sum_ref, rhs_ref, l_ref, s_prev, p_ref, s_ref):
    active = at(MAKER[1])

    @pl.when(active)
    def _():
        s = dot(l_ref[...], q_in[...]) + sum_ref[...].astype(jnp.float32)
        s_ref[...] = low(s)
        p_ref[...] = low(rhs_ref[0] - s)

    @pl.when(jnp.logical_not(active))
    def _():
        s_ref[...] = s_prev[...]


def step2_kernel(takers, p_in, q_in, came_ref, sum_ref, rhs_ref, d_ref, l_ref, q_prev, s_prev, a_ref, q_ref, s_ref):
    active, beside, taken = at(MAKER[2]), at(BESIDE), any_of(takers)

    @pl.when(active)
    def _():
        lower_dot(q_ref, d_ref, p_in)
        s_ref[...] = low(dot(l_ref[...], q_ref[...]))

    @pl.when(beside)
    def _():
        q_ref[...] = q_in[...]
        s = dot(l_ref[...], q_in[...]) + sum_ref[...].astype(jnp.float32)
        s_ref[...] = low(s)
        a_ref[...] = low(rhs_ref[0] - s)

    @pl.when(jnp.logical_not(active | beside))
    def _():
        s_ref[...] = s_prev[...]

    @pl.when(taken)
    def _():
        q_ref[...] = came_ref[...]

    @pl.when(jnp.logical_not(active | beside | taken))
    def _():
        q_ref[...] = q_prev[...]


def step3_kernel(takers, a_ref, sum_ref, *refs):
    came, (d_ref, q_prev, q_ref, p_v) = refs[:-4], refs[-4:]
    active = at(MAKER[3])

    @pl.when(active)
    def _():
        p_v[...] = low(a_ref[...].astype(jnp.float32) - sum_ref[...].astype(jnp.float32))
        lower_dot(q_ref, d_ref, p_v)

    for devices, source in zip(takers, came):

        @pl.when(any_of(devices))
        def _():
            q_ref[...] = source[...]

    @pl.when(jnp.logical_not(active | any_of([d for devices in takers for d in devices])))
    def _():
        q_ref[...] = q_prev[...]


def update_kernel(takers, tail_ref, s_ref, l_ref, q_prev, *refs):
    got, q_ref, out_ref = refs[:-2], refs[-2], refs[-1]
    size = l_ref.shape[0]
    row, col = lax.axis_index("row"), lax.axis_index("col")
    below = row >= NC

    def take(flag, source):
        @pl.when(flag)
        def _():
            q_ref[...] = source[...]

    kept = jnp.logical_not(any_of([d for devices in takers for d in devices]))
    take(kept, q_prev)
    for devices, source in zip(takers, got):
        take(any_of(devices), source)

    @pl.when(below)
    def _():
        out_ref[pl.ds(0, size)] = low(dot(l_ref[...], q_ref[...]))

    @pl.when(jnp.logical_not(below))
    def _():
        out_ref[pl.ds(0, size)] = s_ref[...]

    out_ref[pl.ds(size, TAIL)] = tail_ref[...]


def minus(acc, sums, i):
    size = acc.shape[0]
    for s in sums:
        keep = s[pl.ds(size, TAIL)].astype(jnp.float32)[i : i + 1] > 0.5
        acc = acc - jnp.where(keep, s[pl.ds(0, size)].astype(jnp.float32), 0.0)
    return acc


def half_kernel(q_ref, rest_ref, rhs_ref, mine_ref, across_ref, solved_ref, out_ref):
    came = any_of(REST)

    @pl.when(came)
    def _():
        solved_ref[...] = rest_ref[...].astype(jnp.float32)

    @pl.when(jnp.logical_not(came))
    def _():
        solved_ref[...] = q_ref[...].astype(jnp.float32)

    for i in range(out_ref.shape[0]):
        out_ref[i] = minus(rhs_ref[i], (mine_ref, across_ref), i)


def final_kernel(half_ref, beside_ref, corner_ref, out_ref):
    for i in range(out_ref.shape[0]):
        out_ref[i] = minus(half_ref[i], (beside_ref, corner_ref), i)


def on_device_8x4(rhs, diag_inv, blocks, block_rows, counts):
    size, width = rhs.shape[2:]
    part = size // NR
    rhs = rhs[:, 0]
    block = blocks[0, 0, 0, 0]
    bf16 = jnp.bfloat16
    vec = jax.ShapeDtypeStruct((size, width), bf16)
    dma = pltpu.SemaphoreType.DMA

    wides = [pair_width(m, part) for m in range(NR // 2)]
    cuts = call(
        cut_kernel, [jax.ShapeDtypeStruct((part, w), bf16) for w in wides], [diag_inv], [HBM], [ANY] * len(wides), [dma]
    )
    at_piece = {r: (0, c) for c, rows in enumerate(PIECES) for r in rows}
    parts = []
    for m, cut in enumerate(cuts):
        pairs = []
        for r in range(NR):
            for c, k in enumerate(SENDS[r]):
                if k == 0 and r and max(r // 2, 1) == m:
                    pairs.append(((r, c), at_piece[r]))
                if k and MAKER[k][0] != r and r // 2 == m:
                    pairs.append(((r, c), MAKER[k] if r % 2 else PARTNER[k]))
        parts.append(send_only(cut, pairs))
    q = call(
        first_kernel,
        jax.ShapeDtypeStruct((2 * part, width), bf16),
        [rhs, diag_inv, *parts[1:]],
        [HBM, HBM] + [ANY] * (len(wides) - 1),
        VMEM,
        [
            pltpu.VMEM((size, width), jnp.float32),
            pltpu.VMEM((2, part, size), bf16),
            dma,
            pltpu.SemaphoreType.DMA((2,)),
        ],
    )
    takers = (FIRST, (2, 0), (3, 0))
    got = [send(q, [((0, c), takers[(c + j) % 4]) for c in range(4) if (c + j) % 4 < 3]) for j in range(4)]
    even = call(
        pack_kernel,
        jax.ShapeDtypeStruct((part, sum(wides)), bf16),
        parts,
        [ANY] * len(wides),
        VMEM,
        [pltpu.SemaphoreType.DMA((len(wides),))],
    )
    even = send(even, [(PARTNER[k], MAKER[k]) for k in range(1, NC)])
    diag, tail = call(
        whole_kernel,
        [jax.ShapeDtypeStruct((size, size), bf16), jax.ShapeDtypeStruct((TAIL, width), bf16)],
        [block_rows, counts, diag_inv, even, *parts],
        [SMEM, SMEM, HBM] + [ANY] * (1 + len(wides)),
        [VMEM, VMEM],
        [pltpu.SemaphoreType.DMA((NR,))],
    )

    p, q, s = call(step0_kernel, [vec] * 3, [*got, rhs, block], [VMEM] * 6, [VMEM] * 3)
    p_in = send(p, [(FIRST, MAKER[1])])
    sums = send(s, [((2, 0), MAKER[1]), ((3, 0), BESIDE)])
    q = call(step1_kernel, vec, [p_in, diag, q], [VMEM] * 3, VMEM)
    p, s = call(step1_sum_kernel, [vec] * 2, [q, sums, rhs, block, s], [VMEM] * 5, [VMEM] * 2)
    p_in = send(p, [(MAKER[1], MAKER[2])])
    q_in = send(q, [(MAKER[1], BESIDE)])

    came = send(q, [((2, 0), (4, 0)), ((3, 0), (5, 0)), ((1, 0), (0, 0)), ((2, 1), (4, 1))])
    took = [(4, 0), (5, 0), (0, 0), (4, 1)]
    a, q, s = call(
        functools.partial(step2_kernel, took),
        [vec] * 3,
        [p_in, q_in, came, sums, rhs, diag, block, q, s],
        [VMEM] * 9,
        [VMEM] * 3,
    )
    a = send(a, [(BESIDE, MAKER[3])])
    sums = send(s, [(MAKER[2], MAKER[3])])
    sends = [
        [(MAKER[2], (2, 2))],
        [(MAKER[2], (7, 2)), ((4, 0), (6, 0)), ((5, 0), (7, 0)), ((4, 1), (6, 1)), ((3, 1), (5, 1)), ((2, 1), (0, 1))],
        [(MAKER[2], (5, 2)), ((4, 1), (7, 1)), ((3, 1), (1, 1))],
    ]
    got = [send(q, sends[0])] + [send_only(q, pairs) for pairs in sends[1:]]
    q = call(
        functools.partial(step3_kernel, [[b for _, b in pairs] for pairs in sends]),
        vec,
        [a, sums, *got, diag, q],
        [VMEM] * 7,
        VMEM,
        [pltpu.VMEM((size, width), bf16)],
    )

    sends = [
        [(MAKER[3], (6, 3)), ((2, 2), (6, 2))],
        [(MAKER[3], (7, 3)), ((2, 2), (4, 2))],
        [(MAKER[3], (4, 3))],
    ]
    got = [send_only(q, pairs) for pairs in sends]
    takers = [[b for _, b in pairs] for pairs in sends]
    q, mine = call(
        functools.partial(update_kernel, takers),
        [vec, jax.ShapeDtypeStruct((size + TAIL, width), bf16)],
        [tail, s, block, q, *got],
        [VMEM] * (4 + len(got)),
        [VMEM] * 2,
    )

    def swap(value, step):
        return send(value, [((r, c), (r, c ^ step)) for r in range(NR) for c in range(NC)])

    across = swap(mine, 2)
    rest = send_only(q, list(zip(((4, 3), (5, 3), (6, 3), (7, 3), (2, 2), MAKER[2]), REST)))
    beside = swap(mine, 1)
    across, rest = lax.optimization_barrier((across, rest))
    corner = swap(across, 1)
    whole_rhs = jax.ShapeDtypeStruct(rhs.shape, jnp.float32)
    solved, half = call(
        half_kernel,
        [jax.ShapeDtypeStruct((size, width), jnp.float32), whole_rhs],
        [q, rest, rhs, mine, across],
        [VMEM] * 5,
        [VMEM] * 2,
    )
    remainder = call(final_kernel, whole_rhs, [half, beside, corner], [VMEM] * 3, VMEM)
    return solved[None, None], remainder[:, None]


def solution(mesh):
    in_specs = (
        P(None, "row", None, None),
        P(None, "row", None),
        P(None, "col", "row", None, None, None),
        P(None, "col", "row", None),
        P(None, "col", "row"),
    )
    out_specs = (P(None, "col", None, None), P(None, "row", None, None))
    small = mesh.shape["row"] == NR and mesh.shape["col"] == NC
    return jax.shard_map(
        on_device_8x4 if small else on_device_any,
        mesh=mesh,
        in_specs=in_specs,
        out_specs=out_specs,
        check_vma=False,
    )
```

```python
import functools

import jax
import jax.numpy as jnp
from jax import lax
from jax.experimental import pallas as pl
from jax.experimental.pallas import tpu as pltpu
from jax.sharding import PartitionSpec as P

VMEM = pl.BlockSpec(memory_space=pltpu.VMEM)
ANY = pl.BlockSpec(memory_space=pl.ANY)
HBM = pl.BlockSpec(memory_space=pltpu.HBM)
SMEM = pl.BlockSpec(memory_space=pltpu.SMEM)
TAIL = 16


def broadcast(value, axis, root):
    mine = lax.axis_index(axis) == root
    return lax.psum(jnp.where(mine, value, jnp.zeros_like(value)), axis)


def on_device_any(rhs, diag_inv, blocks, block_rows, counts):
    nrow = lax.axis_size("row")
    ncol = lax.axis_size("col")
    my_row = lax.axis_index("row")
    my_col = lax.axis_index("col")
    kc = diag_inv.shape[0]
    rb_local = rhs.shape[0]
    nz_local = blocks.shape[3]
    local_rhs = rhs[:, 0]
    partial_value = jnp.zeros(local_rhs.shape, jnp.float32)
    solved_list = [jnp.zeros(local_rhs.shape[1:], jnp.float32)]
    slot_ids = jnp.arange(nz_local, dtype=jnp.int32)
    local_ids = jnp.arange(rb_local, dtype=jnp.int32)
    for k in range(kc):
        j = k // ncol
        owner_row = k % nrow
        local_pivot = k // nrow
        mine_row = my_row == owner_row
        mine_col = my_col == k % ncol
        pivot_part = jnp.where(mine_row, partial_value[local_pivot], jnp.float32(0.0))
        summed = lax.psum(pivot_part, "col")
        updated = (local_rhs[local_pivot] - summed).astype(jnp.bfloat16)
        pivot_bf = broadcast(updated, "row", owner_row)
        row_part = jnp.dot(diag_inv[k], pivot_bf, preferred_element_type=jnp.float32)
        sol = lax.all_gather(row_part, "row", axis=0, tiled=True)
        sol_bf = sol.astype(jnp.bfloat16)
        rows = block_rows[j, 0, 0]
        glob = rows * nrow + my_row
        valid = (slot_ids < counts[j, 0, 0]) & (glob > k) & mine_col
        weights = (valid[:, None] & (rows[:, None] == local_ids[None, :])).astype(jnp.float32)
        contrib = jnp.einsum(
            "sab,bn->san", blocks[j, 0, 0], sol_bf, preferred_element_type=jnp.float32
        )
        partial_value = partial_value + jnp.einsum(
            "sl,san->lan", weights, contrib, precision=lax.Precision.HIGHEST
        )
        solved_list[j] = jnp.where(mine_col, sol, solved_list[j])
    total = lax.psum(partial_value, "col")
    remainder = (local_rhs - total)[:, None]
    solved = jnp.stack(solved_list)[:, None]
    return (solved, remainder)


NR, NC = 8, 4
MAKER = (None, (2, 1), (3, 2), (5, 3))
FIRST = (1, 0)
BESIDE = (3, 1)
PARTNER = (None, (3, 1), (3, 3), (5, 2))
PIECES = ((4, 1), (6, 3), (5, 2), (7, 0))
SENDS = (
    (0, 1, 2, 3),
    (0, 1, 2, 3),
    (3, 1, 0, 2),
    (0, 1, 3, 2),
    (0, 1, 3, 2),
    (2, 1, 3, 0),
    (0, 3, 1, 2),
    (1, 3, 0, 2),
)
REST = ((2, 3), (1, 3), (0, 3), (1, 2))


def hops(a, b):
    d = a ^ b
    if d < 2:
        return 1 if d else 10000
    return 100 + abs((a >> 3) - (b >> 3)) + ((d >> 2) & 1) + ((d >> 1) & 1)


def complete(pairs):
    to = {a * NC + b: c * NC + d for (a, b), (c, d) in pairs}
    free_from = [i for i in range(NR * NC) if i not in to]
    free_to = [i for i in range(NR * NC) if i not in to.values()]
    n = len(free_from)
    u, v, match = [0] * (n + 1), [0] * (n + 1), [0] * (n + 1)
    for i in range(1, n + 1):
        match[0], j0 = i, 0
        least, way, used = [10**9] * (n + 1), [0] * (n + 1), [False] * (n + 1)
        while True:
            used[j0] = True
            i0, delta, j1 = match[j0], 10**9, 0
            for j in range(1, n + 1):
                if not used[j]:
                    cur = hops(free_from[i0 - 1], free_to[j - 1]) - u[i0] - v[j]
                    if cur < least[j]:
                        least[j], way[j] = cur, j0
                    if least[j] < delta:
                        delta, j1 = least[j], j
            for j in range(n + 1):
                if used[j]:
                    u[match[j]] += delta
                    v[j] -= delta
                else:
                    least[j] -= delta
            j0 = j1
            if match[j0] == 0:
                break
        while j0:
            j1 = way[j0]
            match[j0] = match[j1]
            j0 = j1
    for j in range(1, n + 1):
        to[free_from[match[j] - 1]] = free_to[j - 1]
    return [(divmod(a, NC), divmod(b, NC)) for a, b in sorted(to.items())]


def send(value, pairs):
    return lax.ppermute(value, ("row", "col"), [(a * NC + b, c * NC + d) for (a, b), (c, d) in complete(pairs)])


def send_only(value, pairs):
    return lax.ppermute(value, ("row", "col"), [(a * NC + b, c * NC + d) for (a, b), (c, d) in pairs])


def dot(a, b):
    return jnp.dot(a, b, preferred_element_type=jnp.float32)


def low(a):
    return a.astype(jnp.bfloat16)


def at(device):
    return (lax.axis_index("row") == device[0]) & (lax.axis_index("col") == device[1])


def any_of(devices):
    flag = at(devices[0])
    for d in devices[1:]:
        flag = flag | at(d)
    return flag


def call(kernel, outs, ins, in_specs, out_specs, scratch=(), limit=16):
    return pl.pallas_call(
        kernel,
        out_shape=outs,
        in_specs=in_specs,
        out_specs=out_specs,
        scratch_shapes=list(scratch),
        compiler_params=pltpu.CompilerParams(vmem_limit_bytes=limit << 20),
        name=kernel.func.__name__ if isinstance(kernel, functools.partial) else kernel.__name__,
    )(*ins)


def pair_width(m, part):
    return 2 * (m + 1) * part


def cut_kernel(diag_ref, *refs):
    cuts, sem = refs[:-1], refs[-1]
    row, col = lax.axis_index("row"), lax.axis_index("col")
    part = diag_ref.shape[1]
    k = jnp.int32(0)
    for r in range(NR):
        for c in range(NC):
            k = jnp.where((row == r) & (col == c), SENDS[r][c], k)
    for m in range(NR // 2):

        @pl.when(jnp.where((row == 1) & (k == 0), 1, row // 2) == m)
        def _():
            copy = pltpu.make_async_copy(diag_ref.at[k, :, pl.ds(0, pair_width(m, part))], cuts[m], sem)
            copy.start()
            copy.wait()


def first_kernel(rhs_ref, diag_ref, *refs):
    parts, (out_ref, rhs_v, d_v, rhs_sem, d_sem) = refs[:-5], refs[-5:]
    n = out_ref.shape[0] // 2
    col = lax.axis_index("col")

    @pl.when(lax.axis_index("row") == 0)
    def _():
        rhs_copy = pltpu.make_async_copy(rhs_ref.at[0], rhs_v, rhs_sem)
        rhs_copy.start()

        def pieces(c):
            copies = []
            for i, r in enumerate(PIECES[c]):
                m = max(r // 2, 1)
                wide = pair_width(m, n)
                source = parts[m - 1] if r else diag_ref.at[0, :, pl.ds(0, wide)]
                copies.append(pltpu.make_async_copy(source, d_v.at[i, :, pl.ds(0, wide)], d_sem.at[i]))
            return copies

        for c in range(NC):

            @pl.when(col == c)
            def _():
                for copy in pieces(c):
                    copy.start()

        rhs_copy.wait()
        p = low(rhs_v[...])
        for c in range(NC):

            @pl.when(col == c)
            def _():
                for i, copy in enumerate(pieces(c)):
                    copy.wait()
                    wide = pair_width(max(PIECES[c][i] // 2, 1), n)
                    out_ref[i * n : (i + 1) * n] = low(dot(d_v[i, :, :wide], p[:wide]))


def pack_kernel(*refs):
    parts, out_ref, sem = refs[:-2], refs[-2], refs[-1]

    @pl.when(any_of(PARTNER[1:]))
    def _():
        copies, left = [], 0
        for m, source in enumerate(parts):
            wide = source.shape[1]
            copies.append(pltpu.make_async_copy(source, out_ref.at[:, pl.ds(left, wide)], sem.at[m]))
            left += wide
        for copy in copies:
            copy.start()
        for copy in copies:
            copy.wait()


def whole_kernel(rows_ref, counts_ref, diag_ref, even_ref, *refs):
    odd, (out_ref, tail_ref, sem) = refs[:-3], refs[-3:]
    size = out_ref.shape[0]
    part = size // NR
    row, col = lax.axis_index("row"), lax.axis_index("col")
    listed = rows_ref[0, 0, 0, 0]
    there = (row >= NC) & (counts_ref[0, 0, 0] > 0)
    done = at(FIRST) | at(MAKER[1]) | at(BESIDE) | at(MAKER[2])
    first = (there & (listed == 0)) | done
    second = there & (listed == 1)
    ids = lax.broadcasted_iota(jnp.int32, tail_ref.shape, 0)
    flag = ((ids == 0) & first) | ((ids == 1) & second)
    tail_ref[...] = low(jnp.where(flag, 1.0, 0.0))

    @pl.when(any_of(MAKER[1:]))
    def _():
        def copy(i, source):
            wide = pair_width(i // 2, part)
            return pltpu.make_async_copy(source, out_ref.at[pl.ds(i * part, part), pl.ds(0, wide)], sem.at[i])

        left = 0
        for i in range(NR):
            wide = pair_width(i // 2, part)
            if i % 2:
                source = odd[i // 2]
            else:
                source = even_ref.at[:, pl.ds(left, wide)]
                left += wide

            @pl.when(row == i)
            def _():
                copy(i, diag_ref.at[col, :, pl.ds(0, wide)]).start()

            @pl.when(row != i)
            def _():
                copy(i, source).start()

        for m in range(NR // 2 - 1):
            right = pair_width(m, part)
            out_ref[pl.ds(2 * m * part, 2 * part), pl.ds(right, size - right)] = jnp.zeros(
                (2 * part, size - right), out_ref.dtype
            )
        for i in range(NR):
            copy(i, odd[i // 2]).wait()


def lower_dot(q_ref, d_ref, p_ref):
    half = d_ref.shape[0] // 2
    q_ref[:half] = low(dot(d_ref[:half, :half], p_ref[:half]))
    q_ref[half:] = low(dot(d_ref[half:], p_ref[...]))


def step0_kernel(g0, g1, g2, g3, rhs_ref, l_ref, p_ref, q_ref, s_ref):
    part = l_ref.shape[0] // NR
    row = lax.axis_index("row")

    def lookup(c, i):
        r = jnp.int32(PIECES[0][i])
        for n in range(1, NC):
            r = jnp.where(c == n, PIECES[n][i], r)
        return pl.multiple_of(r * part, part)

    @pl.when((row >= 1) & (row < 4) & (lax.axis_index("col") == 0))
    def _():
        for j, got in enumerate((g0, g1, g2, g3)):
            src = lax.rem(row + 7 - j, 4)
            q_ref[pl.ds(lookup(src, 0), part)] = got[:part]
            q_ref[pl.ds(lookup(src, 1), part)] = got[part:]
        s = dot(l_ref[...], q_ref[...])
        s_ref[...] = low(s)
        p_ref[...] = low(rhs_ref[0] - s)


def step1_kernel(p_in, d_ref, q_prev, q_ref):
    active = at(MAKER[1])

    @pl.when(active)
    def _():
        lower_dot(q_ref, d_ref, p_in)

    @pl.when(jnp.logical_not(active))
    def _():
        q_ref[...] = q_prev[...]


def step1_sum_kernel(q_in, sum_ref, rhs_ref, l_ref, s_prev, p_ref, s_ref):
    active = at(MAKER[1])

    @pl.when(active)
    def _():
        s = dot(l_ref[...], q_in[...]) + sum_ref[...].astype(jnp.float32)
        s_ref[...] = low(s)
        p_ref[...] = low(rhs_ref[0] - s)

    @pl.when(jnp.logical_not(active))
    def _():
        s_ref[...] = s_prev[...]


def step2_kernel(takers, p_in, q_in, came_ref, sum_ref, rhs_ref, d_ref, l_ref, q_prev, s_prev, a_ref, q_ref, s_ref):
    active, beside, taken = at(MAKER[2]), at(BESIDE), any_of(takers)

    @pl.when(active)
    def _():
        lower_dot(q_ref, d_ref, p_in)
        s_ref[...] = low(dot(l_ref[...], q_ref[...]))

    @pl.when(beside)
    def _():
        q_ref[...] = q_in[...]
        s = dot(l_ref[...], q_in[...]) + sum_ref[...].astype(jnp.float32)
        s_ref[...] = low(s)
        a_ref[...] = low(rhs_ref[0] - s)

    @pl.when(jnp.logical_not(active | beside))
    def _():
        s_ref[...] = s_prev[...]

    @pl.when(taken)
    def _():
        q_ref[...] = came_ref[...]

    @pl.when(jnp.logical_not(active | beside | taken))
    def _():
        q_ref[...] = q_prev[...]


def step3_kernel(takers, a_ref, sum_ref, *refs):
    came, (d_ref, q_prev, q_ref, p_v) = refs[:-4], refs[-4:]
    active = at(MAKER[3])

    @pl.when(active)
    def _():
        p_v[...] = low(a_ref[...].astype(jnp.float32) - sum_ref[...].astype(jnp.float32))
        lower_dot(q_ref, d_ref, p_v)

    for devices, source in zip(takers, came):

        @pl.when(any_of(devices))
        def _():
            q_ref[...] = source[...]

    @pl.when(jnp.logical_not(active | any_of([d for devices in takers for d in devices])))
    def _():
        q_ref[...] = q_prev[...]


def update_kernel(takers, tail_ref, s_ref, l_ref, q_prev, *refs):
    got, q_ref, out_ref = refs[:-2], refs[-2], refs[-1]
    size = l_ref.shape[0]
    row, col = lax.axis_index("row"), lax.axis_index("col")
    below = row >= NC

    def take(flag, source):
        @pl.when(flag)
        def _():
            q_ref[...] = source[...]

    kept = jnp.logical_not(any_of([d for devices in takers for d in devices]))
    take(kept, q_prev)
    for devices, source in zip(takers, got):
        take(any_of(devices), source)

    @pl.when(below)
    def _():
        out_ref[pl.ds(0, size)] = low(dot(l_ref[...], q_ref[...]))

    @pl.when(jnp.logical_not(below))
    def _():
        out_ref[pl.ds(0, size)] = s_ref[...]

    out_ref[pl.ds(size, TAIL)] = tail_ref[...]


def minus(acc, sums, i):
    size = acc.shape[0]
    for s in sums:
        keep = s[pl.ds(size, TAIL)].astype(jnp.float32)[i : i + 1] > 0.5
        acc = acc - jnp.where(keep, s[pl.ds(0, size)].astype(jnp.float32), 0.0)
    return acc


def half_kernel(q_ref, rest_ref, rhs_ref, mine_ref, across_ref, solved_ref, out_ref):
    came = any_of(REST)

    @pl.when(came)
    def _():
        solved_ref[...] = rest_ref[...].astype(jnp.float32)

    @pl.when(jnp.logical_not(came))
    def _():
        solved_ref[...] = q_ref[...].astype(jnp.float32)

    for i in range(out_ref.shape[0]):
        out_ref[i] = minus(rhs_ref[i], (mine_ref, across_ref), i)


def final_kernel(half_ref, beside_ref, corner_ref, out_ref):
    for i in range(out_ref.shape[0]):
        out_ref[i] = minus(half_ref[i], (beside_ref, corner_ref), i)


def on_device_8x4(rhs, diag_inv, blocks, block_rows, counts):
    size, width = rhs.shape[2:]
    part = size // NR
    rhs = rhs[:, 0]
    block = blocks[0, 0, 0, 0]
    bf16 = jnp.bfloat16
    vec = jax.ShapeDtypeStruct((size, width), bf16)
    dma = pltpu.SemaphoreType.DMA

    wides = [pair_width(m, part) for m in range(NR // 2)]
    cuts = call(
        cut_kernel, [jax.ShapeDtypeStruct((part, w), bf16) for w in wides], [diag_inv], [HBM], [ANY] * len(wides), [dma]
    )
    at_piece = {r: (0, c) for c, rows in enumerate(PIECES) for r in rows}
    parts = []
    for m, cut in enumerate(cuts):
        pairs = []
        for r in range(NR):
            for c, k in enumerate(SENDS[r]):
                if k == 0 and r and max(r // 2, 1) == m:
                    pairs.append(((r, c), at_piece[r]))
                if k and MAKER[k][0] != r and r // 2 == m:
                    pairs.append(((r, c), MAKER[k] if r % 2 else PARTNER[k]))
        parts.append(send_only(cut, pairs))
    q = call(
        first_kernel,
        jax.ShapeDtypeStruct((2 * part, width), bf16),
        [rhs, diag_inv, *parts[1:]],
        [HBM, HBM] + [ANY] * (len(wides) - 1),
        VMEM,
        [
            pltpu.VMEM((size, width), jnp.float32),
            pltpu.VMEM((2, part, size), bf16),
            dma,
            pltpu.SemaphoreType.DMA((2,)),
        ],
    )
    takers = (FIRST, (2, 0), (3, 0))
    got = [send(q, [((0, c), takers[(c + j) % 4]) for c in range(4) if (c + j) % 4 < 3]) for j in range(4)]
    even = call(
        pack_kernel,
        jax.ShapeDtypeStruct((part, sum(wides)), bf16),
        parts,
        [ANY] * len(wides),
        VMEM,
        [pltpu.SemaphoreType.DMA((len(wides),))],
    )
    even = send(even, [(PARTNER[k], MAKER[k]) for k in range(1, NC)])
    diag, tail = call(
        whole_kernel,
        [jax.ShapeDtypeStruct((size, size), bf16), jax.ShapeDtypeStruct((TAIL, width), bf16)],
        [block_rows, counts, diag_inv, even, *parts],
        [SMEM, SMEM, HBM] + [ANY] * (1 + len(wides)),
        [VMEM, VMEM],
        [pltpu.SemaphoreType.DMA((NR,))],
    )

    p, q, s = call(step0_kernel, [vec] * 3, [*got, rhs, block], [VMEM] * 6, [VMEM] * 3)
    p_in = send(p, [(FIRST, MAKER[1])])
    sums = send(s, [((2, 0), MAKER[1]), ((3, 0), BESIDE)])
    q = call(step1_kernel, vec, [p_in, diag, q], [VMEM] * 3, VMEM)
    p, s = call(step1_sum_kernel, [vec] * 2, [q, sums, rhs, block, s], [VMEM] * 5, [VMEM] * 2)
    p_in = send(p, [(MAKER[1], MAKER[2])])
    q_in = send(q, [(MAKER[1], BESIDE)])

    came = send(q, [((2, 0), (4, 0)), ((3, 0), (5, 0)), ((1, 0), (0, 0)), ((2, 1), (4, 1))])
    took = [(4, 0), (5, 0), (0, 0), (4, 1)]
    a, q, s = call(
        functools.partial(step2_kernel, took),
        [vec] * 3,
        [p_in, q_in, came, sums, rhs, diag, block, q, s],
        [VMEM] * 9,
        [VMEM] * 3,
    )
    a = send(a, [(BESIDE, MAKER[3])])
    sums = send(s, [(MAKER[2], MAKER[3])])
    sends = [
        [(MAKER[2], (2, 2))],
        [(MAKER[2], (7, 2)), ((4, 0), (6, 0)), ((5, 0), (7, 0)), ((4, 1), (6, 1)), ((3, 1), (5, 1)), ((2, 1), (0, 1))],
        [(MAKER[2], (5, 2)), ((3, 1), (7, 1)), ((2, 1), (1, 1))],
    ]
    got = [send(q, sends[0])] + [send_only(q, pairs) for pairs in sends[1:]]
    q = call(
        functools.partial(step3_kernel, [[b for _, b in pairs] for pairs in sends]),
        vec,
        [a, sums, *got, diag, q],
        [VMEM] * 7,
        VMEM,
        [pltpu.VMEM((size, width), bf16)],
    )

    sends = [
        [(MAKER[3], (6, 3)), ((2, 2), (4, 2))],
        [(MAKER[3], (7, 3)), ((2, 2), (6, 2))],
        [(MAKER[3], (4, 3)), ((2, 2), (0, 2))],
        [(MAKER[3], (3, 3))],
    ]
    got = [send_only(q, pairs) for pairs in sends]
    takers = [[b for _, b in pairs] for pairs in sends]
    q, mine = call(
        functools.partial(update_kernel, takers),
        [vec, jax.ShapeDtypeStruct((size + TAIL, width), bf16)],
        [tail, s, block, q, *got],
        [VMEM] * (4 + len(got)),
        [VMEM] * 2,
    )

    def swap(value, step):
        return send(value, [((r, c), (r, c ^ step)) for r in range(NR) for c in range(NC)])

    across = swap(mine, 2)
    rest = send_only(q, list(zip(((3, 3), MAKER[3], (6, 3), MAKER[2]), REST)))
    beside = swap(mine, 1)
    across, rest = lax.optimization_barrier((across, rest))
    corner = swap(across, 1)
    whole_rhs = jax.ShapeDtypeStruct(rhs.shape, jnp.float32)
    solved, half = call(
        half_kernel,
        [jax.ShapeDtypeStruct((size, width), jnp.float32), whole_rhs],
        [q, rest, rhs, mine, across],
        [VMEM] * 5,
        [VMEM] * 2,
    )
    remainder = call(final_kernel, whole_rhs, [half, beside, corner], [VMEM] * 3, VMEM)
    return solved[None, None], remainder[:, None]


def solution(mesh):
    in_specs = (
        P(None, "row", None, None),
        P(None, "row", None),
        P(None, "col", "row", None, None, None),
        P(None, "col", "row", None),
        P(None, "col", "row"),
    )
    out_specs = (P(None, "col", None, None), P(None, "row", None, None))
    small = mesh.shape["row"] == NR and mesh.shape["col"] == NC
    return jax.shard_map(
        on_device_8x4 if small else on_device_any,
        mesh=mesh,
        in_specs=in_specs,
        out_specs=out_specs,
        check_vma=False,
    )
```

```python
import functools

import jax
import jax.numpy as jnp
from jax import lax
from jax.experimental import pallas as pl
from jax.experimental.pallas import tpu as pltpu
from jax.sharding import PartitionSpec as P

VMEM = pl.BlockSpec(memory_space=pltpu.VMEM)
ANY = pl.BlockSpec(memory_space=pl.ANY)
HBM = pl.BlockSpec(memory_space=pltpu.HBM)
SMEM = pl.BlockSpec(memory_space=pltpu.SMEM)
TAIL = 16


def broadcast(value, axis, root):
    mine = lax.axis_index(axis) == root
    return lax.psum(jnp.where(mine, value, jnp.zeros_like(value)), axis)


def on_device_any(rhs, diag_inv, blocks, block_rows, counts):
    nrow = lax.axis_size("row")
    ncol = lax.axis_size("col")
    my_row = lax.axis_index("row")
    my_col = lax.axis_index("col")
    kc = diag_inv.shape[0]
    rb_local = rhs.shape[0]
    nz_local = blocks.shape[3]
    local_rhs = rhs[:, 0]
    partial_value = jnp.zeros(local_rhs.shape, jnp.float32)
    solved_list = [jnp.zeros(local_rhs.shape[1:], jnp.float32)]
    slot_ids = jnp.arange(nz_local, dtype=jnp.int32)
    local_ids = jnp.arange(rb_local, dtype=jnp.int32)
    for k in range(kc):
        j = k // ncol
        owner_row = k % nrow
        local_pivot = k // nrow
        mine_row = my_row == owner_row
        mine_col = my_col == k % ncol
        pivot_part = jnp.where(mine_row, partial_value[local_pivot], jnp.float32(0.0))
        summed = lax.psum(pivot_part, "col")
        updated = (local_rhs[local_pivot] - summed).astype(jnp.bfloat16)
        pivot_bf = broadcast(updated, "row", owner_row)
        row_part = jnp.dot(diag_inv[k], pivot_bf, preferred_element_type=jnp.float32)
        sol = lax.all_gather(row_part, "row", axis=0, tiled=True)
        sol_bf = sol.astype(jnp.bfloat16)
        rows = block_rows[j, 0, 0]
        glob = rows * nrow + my_row
        valid = (slot_ids < counts[j, 0, 0]) & (glob > k) & mine_col
        weights = (valid[:, None] & (rows[:, None] == local_ids[None, :])).astype(jnp.float32)
        contrib = jnp.einsum(
            "sab,bn->san", blocks[j, 0, 0], sol_bf, preferred_element_type=jnp.float32
        )
        partial_value = partial_value + jnp.einsum(
            "sl,san->lan", weights, contrib, precision=lax.Precision.HIGHEST
        )
        solved_list[j] = jnp.where(mine_col, sol, solved_list[j])
    total = lax.psum(partial_value, "col")
    remainder = (local_rhs - total)[:, None]
    solved = jnp.stack(solved_list)[:, None]
    return (solved, remainder)


NR, NC = 8, 4
MAKER = (None, (2, 1), (3, 2), (5, 3))
FIRST = (1, 0)
BESIDE = (3, 1)
PARTNER = (None, (3, 1), (3, 3), (5, 2))
PIECES = ((4, 1), (6, 3), (5, 2), (7, 0))
SENDS = (
    (0, 1, 2, 3),
    (0, 1, 2, 3),
    (3, 1, 0, 2),
    (0, 1, 3, 2),
    (0, 1, 3, 2),
    (2, 1, 3, 0),
    (0, 3, 1, 2),
    (1, 3, 0, 2),
)
REST = ((2, 3), (3, 3), (0, 3), (1, 3), (1, 2))


def hops(a, b):
    d = a ^ b
    if d < 2:
        return 1 if d else 10000
    return 100 + abs((a >> 3) - (b >> 3)) + ((d >> 2) & 1) + ((d >> 1) & 1)


def complete(pairs):
    to = {a * NC + b: c * NC + d for (a, b), (c, d) in pairs}
    free_from = [i for i in range(NR * NC) if i not in to]
    free_to = [i for i in range(NR * NC) if i not in to.values()]
    n = len(free_from)
    u, v, match = [0] * (n + 1), [0] * (n + 1), [0] * (n + 1)
    for i in range(1, n + 1):
        match[0], j0 = i, 0
        least, way, used = [10**9] * (n + 1), [0] * (n + 1), [False] * (n + 1)
        while True:
            used[j0] = True
            i0, delta, j1 = match[j0], 10**9, 0
            for j in range(1, n + 1):
                if not used[j]:
                    cur = hops(free_from[i0 - 1], free_to[j - 1]) - u[i0] - v[j]
                    if cur < least[j]:
                        least[j], way[j] = cur, j0
                    if least[j] < delta:
                        delta, j1 = least[j], j
            for j in range(n + 1):
                if used[j]:
                    u[match[j]] += delta
                    v[j] -= delta
                else:
                    least[j] -= delta
            j0 = j1
            if match[j0] == 0:
                break
        while j0:
            j1 = way[j0]
            match[j0] = match[j1]
            j0 = j1
    for j in range(1, n + 1):
        to[free_from[match[j] - 1]] = free_to[j - 1]
    return [(divmod(a, NC), divmod(b, NC)) for a, b in sorted(to.items())]


def send(value, pairs):
    return lax.ppermute(value, ("row", "col"), [(a * NC + b, c * NC + d) for (a, b), (c, d) in complete(pairs)])


def send_only(value, pairs):
    return lax.ppermute(value, ("row", "col"), [(a * NC + b, c * NC + d) for (a, b), (c, d) in pairs])


def dot(a, b):
    return jnp.dot(a, b, preferred_element_type=jnp.float32)


def low(a):
    return a.astype(jnp.bfloat16)


def at(device):
    return (lax.axis_index("row") == device[0]) & (lax.axis_index("col") == device[1])


def any_of(devices):
    flag = at(devices[0])
    for d in devices[1:]:
        flag = flag | at(d)
    return flag


def call(kernel, outs, ins, in_specs, out_specs, scratch=(), limit=16):
    return pl.pallas_call(
        kernel,
        out_shape=outs,
        in_specs=in_specs,
        out_specs=out_specs,
        scratch_shapes=list(scratch),
        compiler_params=pltpu.CompilerParams(vmem_limit_bytes=limit << 20),
        name=kernel.func.__name__ if isinstance(kernel, functools.partial) else kernel.__name__,
    )(*ins)


def pair_width(m, part):
    return 2 * (m + 1) * part


def cut_kernel(diag_ref, *refs):
    cuts, sem = refs[:-1], refs[-1]
    row, col = lax.axis_index("row"), lax.axis_index("col")
    part = diag_ref.shape[1]
    k = jnp.int32(0)
    for r in range(NR):
        for c in range(NC):
            k = jnp.where((row == r) & (col == c), SENDS[r][c], k)
    for m in range(NR // 2):

        @pl.when(jnp.where((row == 1) & (k == 0), 1, row // 2) == m)
        def _():
            copy = pltpu.make_async_copy(diag_ref.at[k, :, pl.ds(0, pair_width(m, part))], cuts[m], sem)
            copy.start()
            copy.wait()


def first_kernel(rhs_ref, diag_ref, *refs):
    parts, (out_ref, rhs_v, d_v, rhs_sem, d_sem) = refs[:-5], refs[-5:]
    n = out_ref.shape[0] // 2
    col = lax.axis_index("col")

    @pl.when(lax.axis_index("row") == 0)
    def _():
        rhs_copy = pltpu.make_async_copy(rhs_ref.at[0], rhs_v, rhs_sem)
        rhs_copy.start()

        def pieces(c):
            copies = []
            for i, r in enumerate(PIECES[c]):
                m = max(r // 2, 1)
                wide = pair_width(m, n)
                source = parts[m - 1] if r else diag_ref.at[0, :, pl.ds(0, wide)]
                copies.append(pltpu.make_async_copy(source, d_v.at[i, :, pl.ds(0, wide)], d_sem.at[i]))
            return copies

        for c in range(NC):

            @pl.when(col == c)
            def _():
                for copy in pieces(c):
                    copy.start()

        rhs_copy.wait()
        p = low(rhs_v[...])
        for c in range(NC):

            @pl.when(col == c)
            def _():
                for i, copy in enumerate(pieces(c)):
                    copy.wait()
                    wide = pair_width(max(PIECES[c][i] // 2, 1), n)
                    out_ref[i * n : (i + 1) * n] = low(dot(d_v[i, :, :wide], p[:wide]))


def pack_kernel(*refs):
    parts, out_ref, sem = refs[:-2], refs[-2], refs[-1]

    @pl.when(any_of(PARTNER[1:]))
    def _():
        copies, left = [], 0
        for m, source in enumerate(parts):
            wide = source.shape[1]
            copies.append(pltpu.make_async_copy(source, out_ref.at[:, pl.ds(left, wide)], sem.at[m]))
            left += wide
        for copy in copies:
            copy.start()
        for copy in copies:
            copy.wait()


def whole_kernel(rows_ref, counts_ref, diag_ref, even_ref, *refs):
    odd, (out_ref, tail_ref, sem) = refs[:-3], refs[-3:]
    size = out_ref.shape[0]
    part = size // NR
    row, col = lax.axis_index("row"), lax.axis_index("col")
    listed = rows_ref[0, 0, 0, 0]
    there = (row >= NC) & (counts_ref[0, 0, 0] > 0)
    done = at(FIRST) | at(MAKER[1]) | at(BESIDE) | at(MAKER[2])
    first = (there & (listed == 0)) | done
    second = there & (listed == 1)
    ids = lax.broadcasted_iota(jnp.int32, tail_ref.shape, 0)
    flag = ((ids == 0) & first) | ((ids == 1) & second)
    tail_ref[...] = low(jnp.where(flag, 1.0, 0.0))

    @pl.when(any_of(MAKER[1:]))
    def _():
        def copy(i, source):
            wide = pair_width(i // 2, part)
            return pltpu.make_async_copy(source, out_ref.at[pl.ds(i * part, part), pl.ds(0, wide)], sem.at[i])

        left = 0
        for i in range(NR):
            wide = pair_width(i // 2, part)
            if i % 2:
                source = odd[i // 2]
            else:
                source = even_ref.at[:, pl.ds(left, wide)]
                left += wide

            @pl.when(row == i)
            def _():
                copy(i, diag_ref.at[col, :, pl.ds(0, wide)]).start()

            @pl.when(row != i)
            def _():
                copy(i, source).start()

        for m in range(NR // 2 - 1):
            right = pair_width(m, part)
            out_ref[pl.ds(2 * m * part, 2 * part), pl.ds(right, size - right)] = jnp.zeros(
                (2 * part, size - right), out_ref.dtype
            )
        for i in range(NR):
            copy(i, odd[i // 2]).wait()


def lower_dot(q_ref, d_ref, p_ref):
    half = d_ref.shape[0] // 2
    q_ref[:half] = low(dot(d_ref[:half, :half], p_ref[:half]))
    q_ref[half:] = low(dot(d_ref[half:], p_ref[...]))


def step0_kernel(g0, g1, g2, g3, rhs_ref, l_ref, p_ref, q_ref, s_ref):
    part = l_ref.shape[0] // NR
    row = lax.axis_index("row")

    def lookup(c, i):
        r = jnp.int32(PIECES[0][i])
        for n in range(1, NC):
            r = jnp.where(c == n, PIECES[n][i], r)
        return pl.multiple_of(r * part, part)

    @pl.when((row >= 1) & (row < 4) & (lax.axis_index("col") == 0))
    def _():
        for j, got in enumerate((g0, g1, g2, g3)):
            src = lax.rem(row + 7 - j, 4)
            q_ref[pl.ds(lookup(src, 0), part)] = got[:part]
            q_ref[pl.ds(lookup(src, 1), part)] = got[part:]
        s = dot(l_ref[...], q_ref[...])
        s_ref[...] = low(s)
        p_ref[...] = low(rhs_ref[0] - s)


def step1_kernel(p_in, d_ref, q_prev, q_ref):
    active = at(MAKER[1])

    @pl.when(active)
    def _():
        lower_dot(q_ref, d_ref, p_in)

    @pl.when(jnp.logical_not(active))
    def _():
        q_ref[...] = q_prev[...]


def step1_sum_kernel(q_in, sum_ref, rhs_ref, l_ref, s_prev, p_ref, s_ref):
    active = at(MAKER[1])

    @pl.when(active)
    def _():
        s = dot(l_ref[...], q_in[...]) + sum_ref[...].astype(jnp.float32)
        s_ref[...] = low(s)
        p_ref[...] = low(rhs_ref[0] - s)

    @pl.when(jnp.logical_not(active))
    def _():
        s_ref[...] = s_prev[...]


def step2_kernel(takers, p_in, q_in, came_ref, sum_ref, rhs_ref, d_ref, l_ref, q_prev, s_prev, a_ref, q_ref, s_ref):
    active, beside, taken = at(MAKER[2]), at(BESIDE), any_of(takers)

    @pl.when(active)
    def _():
        lower_dot(q_ref, d_ref, p_in)
        s_ref[...] = low(dot(l_ref[...], q_ref[...]))

    @pl.when(beside)
    def _():
        q_ref[...] = q_in[...]
        s = dot(l_ref[...], q_in[...]) + sum_ref[...].astype(jnp.float32)
        s_ref[...] = low(s)
        a_ref[...] = low(rhs_ref[0] - s)

    @pl.when(jnp.logical_not(active | beside))
    def _():
        s_ref[...] = s_prev[...]

    @pl.when(taken)
    def _():
        q_ref[...] = came_ref[...]

    @pl.when(jnp.logical_not(active | beside | taken))
    def _():
        q_ref[...] = q_prev[...]


def step3_kernel(takers, a_ref, sum_ref, *refs):
    came, (d_ref, q_prev, q_ref, p_v) = refs[:-4], refs[-4:]
    active = at(MAKER[3])

    @pl.when(active)
    def _():
        p_v[...] = low(a_ref[...].astype(jnp.float32) - sum_ref[...].astype(jnp.float32))
        lower_dot(q_ref, d_ref, p_v)

    for devices, source in zip(takers, came):

        @pl.when(any_of(devices))
        def _():
            q_ref[...] = source[...]

    @pl.when(jnp.logical_not(active | any_of([d for devices in takers for d in devices])))
    def _():
        q_ref[...] = q_prev[...]


def update_kernel(takers, tail_ref, s_ref, l_ref, q_prev, *refs):
    got, q_ref, out_ref = refs[:-2], refs[-2], refs[-1]
    size = l_ref.shape[0]
    row, col = lax.axis_index("row"), lax.axis_index("col")
    below = row >= NC

    def take(flag, source):
        @pl.when(flag)
        def _():
            q_ref[...] = source[...]

    kept = jnp.logical_not(any_of([d for devices in takers for d in devices]))
    take(kept, q_prev)
    for devices, source in zip(takers, got):
        take(any_of(devices), source)

    @pl.when(below)
    def _():
        out_ref[pl.ds(0, size)] = low(dot(l_ref[...], q_ref[...]))

    @pl.when(jnp.logical_not(below))
    def _():
        out_ref[pl.ds(0, size)] = s_ref[...]

    out_ref[pl.ds(size, TAIL)] = tail_ref[...]


def minus(acc, sums, i):
    size = acc.shape[0]
    for s in sums:
        keep = s[pl.ds(size, TAIL)].astype(jnp.float32)[i : i + 1] > 0.5
        acc = acc - jnp.where(keep, s[pl.ds(0, size)].astype(jnp.float32), 0.0)
    return acc


def half_kernel(q_ref, rest_ref, rhs_ref, mine_ref, across_ref, solved_ref, out_ref):
    came = any_of(REST)

    @pl.when(came)
    def _():
        solved_ref[...] = rest_ref[...].astype(jnp.float32)

    @pl.when(jnp.logical_not(came))
    def _():
        solved_ref[...] = q_ref[...].astype(jnp.float32)

    for i in range(out_ref.shape[0]):
        out_ref[i] = minus(rhs_ref[i], (mine_ref, across_ref), i)


def final_kernel(half_ref, beside_ref, corner_ref, out_ref):
    for i in range(out_ref.shape[0]):
        out_ref[i] = minus(half_ref[i], (beside_ref, corner_ref), i)


def on_device_8x4(rhs, diag_inv, blocks, block_rows, counts):
    size, width = rhs.shape[2:]
    part = size // NR
    rhs = rhs[:, 0]
    block = blocks[0, 0, 0, 0]
    bf16 = jnp.bfloat16
    vec = jax.ShapeDtypeStruct((size, width), bf16)
    dma = pltpu.SemaphoreType.DMA

    wides = [pair_width(m, part) for m in range(NR // 2)]
    cuts = call(
        cut_kernel, [jax.ShapeDtypeStruct((part, w), bf16) for w in wides], [diag_inv], [HBM], [ANY] * len(wides), [dma]
    )
    at_piece = {r: (0, c) for c, rows in enumerate(PIECES) for r in rows}
    parts = []
    for m, cut in enumerate(cuts):
        pairs = []
        for r in range(NR):
            for c, k in enumerate(SENDS[r]):
                if k == 0 and r and max(r // 2, 1) == m:
                    pairs.append(((r, c), at_piece[r]))
                if k and MAKER[k][0] != r and r // 2 == m:
                    pairs.append(((r, c), MAKER[k] if r % 2 else PARTNER[k]))
        parts.append(send_only(cut, pairs))
    q = call(
        first_kernel,
        jax.ShapeDtypeStruct((2 * part, width), bf16),
        [rhs, diag_inv, *parts[1:]],
        [HBM, HBM] + [ANY] * (len(wides) - 1),
        VMEM,
        [
            pltpu.VMEM((size, width), jnp.float32),
            pltpu.VMEM((2, part, size), bf16),
            dma,
            pltpu.SemaphoreType.DMA((2,)),
        ],
    )
    takers = (FIRST, (2, 0), (3, 0))
    got = [send(q, [((0, c), takers[(c + j) % 4]) for c in range(4) if (c + j) % 4 < 3]) for j in range(4)]
    even = call(
        pack_kernel,
        jax.ShapeDtypeStruct((part, sum(wides)), bf16),
        parts,
        [ANY] * len(wides),
        VMEM,
        [pltpu.SemaphoreType.DMA((len(wides),))],
    )
    even = send(even, [(PARTNER[k], MAKER[k]) for k in range(1, NC)])
    diag, tail = call(
        whole_kernel,
        [jax.ShapeDtypeStruct((size, size), bf16), jax.ShapeDtypeStruct((TAIL, width), bf16)],
        [block_rows, counts, diag_inv, even, *parts],
        [SMEM, SMEM, HBM] + [ANY] * (1 + len(wides)),
        [VMEM, VMEM],
        [pltpu.SemaphoreType.DMA((NR,))],
    )

    p, q, s = call(step0_kernel, [vec] * 3, [*got, rhs, block], [VMEM] * 6, [VMEM] * 3)
    p_in = send(p, [(FIRST, MAKER[1])])
    sums = send(s, [((2, 0), MAKER[1]), ((3, 0), BESIDE)])
    q = call(step1_kernel, vec, [p_in, diag, q], [VMEM] * 3, VMEM)
    p, s = call(step1_sum_kernel, [vec] * 2, [q, sums, rhs, block, s], [VMEM] * 5, [VMEM] * 2)
    p_in = send(p, [(MAKER[1], MAKER[2])])
    q_in = send(q, [(MAKER[1], BESIDE)])

    came = send(q, [((2, 0), (4, 0)), ((3, 0), (5, 0)), ((1, 0), (0, 0)), ((2, 1), (4, 1))])
    took = [(4, 0), (5, 0), (0, 0), (4, 1)]
    a, q, s = call(
        functools.partial(step2_kernel, took),
        [vec] * 3,
        [p_in, q_in, came, sums, rhs, diag, block, q, s],
        [VMEM] * 9,
        [VMEM] * 3,
    )
    a = send(a, [(BESIDE, MAKER[3])])
    sums = send(s, [(MAKER[2], MAKER[3])])
    sends = [
        [(MAKER[2], (2, 2))],
        [(MAKER[2], (7, 2)), ((4, 0), (6, 0)), ((5, 0), (7, 0)), ((4, 1), (6, 1)), ((3, 1), (5, 1)), ((2, 1), (0, 1))],
        [(MAKER[2], (5, 2)), ((3, 1), (7, 1)), ((2, 1), (1, 1))],
    ]
    got = [send(q, sends[0])] + [send_only(q, pairs) for pairs in sends[1:]]
    q = call(
        functools.partial(step3_kernel, [[b for _, b in pairs] for pairs in sends]),
        vec,
        [a, sums, *got, diag, q],
        [VMEM] * 7,
        VMEM,
        [pltpu.VMEM((size, width), bf16)],
    )

    sends = [
        [(MAKER[3], (6, 3)), ((2, 2), (4, 2))],
        [(MAKER[3], (7, 3)), ((2, 2), (6, 2))],
        [(MAKER[3], (4, 3)), ((2, 2), (0, 2))],
    ]
    got = [send_only(q, pairs) for pairs in sends]
    takers = [[b for _, b in pairs] for pairs in sends]
    q, mine = call(
        functools.partial(update_kernel, takers),
        [vec, jax.ShapeDtypeStruct((size + TAIL, width), bf16)],
        [tail, s, block, q, *got],
        [VMEM] * (4 + len(got)),
        [VMEM] * 2,
    )

    def swap(value, step):
        return send(value, [((r, c), (r, c ^ step)) for r in range(NR) for c in range(NC)])

    across = swap(mine, 2)
    rest = send_only(q, list(zip(((4, 3), (5, 3), (6, 3), (7, 3), MAKER[2]), REST)))
    beside = swap(mine, 1)
    across, rest = lax.optimization_barrier((across, rest))
    corner = swap(across, 1)
    whole_rhs = jax.ShapeDtypeStruct(rhs.shape, jnp.float32)
    solved, half = call(
        half_kernel,
        [jax.ShapeDtypeStruct((size, width), jnp.float32), whole_rhs],
        [q, rest, rhs, mine, across],
        [VMEM] * 5,
        [VMEM] * 2,
    )
    remainder = call(final_kernel, whole_rhs, [half, beside, corner], [VMEM] * 3, VMEM)
    return solved[None, None], remainder[:, None]


def solution(mesh):
    in_specs = (
        P(None, "row", None, None),
        P(None, "row", None),
        P(None, "col", "row", None, None, None),
        P(None, "col", "row", None),
        P(None, "col", "row"),
    )
    out_specs = (P(None, "col", None, None), P(None, "row", None, None))
    small = mesh.shape["row"] == NR and mesh.shape["col"] == NC
    return jax.shard_map(
        on_device_8x4 if small else on_device_any,
        mesh=mesh,
        in_specs=in_specs,
        out_specs=out_specs,
        check_vma=False,
    )
```

```python
import functools

import jax
import jax.numpy as jnp
from jax import lax
from jax.experimental import pallas as pl
from jax.experimental.pallas import tpu as pltpu
from jax.sharding import PartitionSpec as P

VMEM = pl.BlockSpec(memory_space=pltpu.VMEM)
ANY = pl.BlockSpec(memory_space=pl.ANY)
HBM = pl.BlockSpec(memory_space=pltpu.HBM)
SMEM = pl.BlockSpec(memory_space=pltpu.SMEM)
TAIL = 16


def broadcast(value, axis, root):
    mine = lax.axis_index(axis) == root
    return lax.psum(jnp.where(mine, value, jnp.zeros_like(value)), axis)


def on_device_any(rhs, diag_inv, blocks, block_rows, counts):
    nrow = lax.axis_size("row")
    ncol = lax.axis_size("col")
    my_row = lax.axis_index("row")
    my_col = lax.axis_index("col")
    kc = diag_inv.shape[0]
    rb_local = rhs.shape[0]
    nz_local = blocks.shape[3]
    local_rhs = rhs[:, 0]
    partial_value = jnp.zeros(local_rhs.shape, jnp.float32)
    solved_list = [jnp.zeros(local_rhs.shape[1:], jnp.float32)]
    slot_ids = jnp.arange(nz_local, dtype=jnp.int32)
    local_ids = jnp.arange(rb_local, dtype=jnp.int32)
    for k in range(kc):
        j = k // ncol
        owner_row = k % nrow
        local_pivot = k // nrow
        mine_row = my_row == owner_row
        mine_col = my_col == k % ncol
        pivot_part = jnp.where(mine_row, partial_value[local_pivot], jnp.float32(0.0))
        summed = lax.psum(pivot_part, "col")
        updated = (local_rhs[local_pivot] - summed).astype(jnp.bfloat16)
        pivot_bf = broadcast(updated, "row", owner_row)
        row_part = jnp.dot(diag_inv[k], pivot_bf, preferred_element_type=jnp.float32)
        sol = lax.all_gather(row_part, "row", axis=0, tiled=True)
        sol_bf = sol.astype(jnp.bfloat16)
        rows = block_rows[j, 0, 0]
        glob = rows * nrow + my_row
        valid = (slot_ids < counts[j, 0, 0]) & (glob > k) & mine_col
        weights = (valid[:, None] & (rows[:, None] == local_ids[None, :])).astype(jnp.float32)
        contrib = jnp.einsum(
            "sab,bn->san", blocks[j, 0, 0], sol_bf, preferred_element_type=jnp.float32
        )
        partial_value = partial_value + jnp.einsum(
            "sl,san->lan", weights, contrib, precision=lax.Precision.HIGHEST
        )
        solved_list[j] = jnp.where(mine_col, sol, solved_list[j])
    total = lax.psum(partial_value, "col")
    remainder = (local_rhs - total)[:, None]
    solved = jnp.stack(solved_list)[:, None]
    return (solved, remainder)


NR, NC = 8, 4
MAKER = (None, (2, 1), (3, 2), (5, 3))
FIRST = (1, 0)
BESIDE = (3, 1)
PARTNER = (None, (3, 1), (3, 3), (5, 2))
PIECES = ((4, 1), (6, 3), (5, 2), (7, 0))
SENDS = (
    (0, 1, 2, 3),
    (0, 1, 2, 3),
    (3, 1, 0, 2),
    (0, 1, 3, 2),
    (0, 1, 3, 2),
    (2, 1, 3, 0),
    (0, 3, 1, 2),
    (1, 3, 0, 2),
)
REST = ((2, 3), (3, 3), (0, 3), (1, 3), (1, 2))


def hops(a, b):
    d = a ^ b
    if d < 2:
        return 1 if d else 10000
    return 100 + abs((a >> 3) - (b >> 3)) + ((d >> 2) & 1) + ((d >> 1) & 1)


def complete(pairs):
    to = {a * NC + b: c * NC + d for (a, b), (c, d) in pairs}
    free_from = [i for i in range(NR * NC) if i not in to]
    free_to = [i for i in range(NR * NC) if i not in to.values()]
    n = len(free_from)
    u, v, match = [0] * (n + 1), [0] * (n + 1), [0] * (n + 1)
    for i in range(1, n + 1):
        match[0], j0 = i, 0
        least, way, used = [10**9] * (n + 1), [0] * (n + 1), [False] * (n + 1)
        while True:
            used[j0] = True
            i0, delta, j1 = match[j0], 10**9, 0
            for j in range(1, n + 1):
                if not used[j]:
                    cur = hops(free_from[i0 - 1], free_to[j - 1]) - u[i0] - v[j]
                    if cur < least[j]:
                        least[j], way[j] = cur, j0
                    if least[j] < delta:
                        delta, j1 = least[j], j
            for j in range(n + 1):
                if used[j]:
                    u[match[j]] += delta
                    v[j] -= delta
                else:
                    least[j] -= delta
            j0 = j1
            if match[j0] == 0:
                break
        while j0:
            j1 = way[j0]
            match[j0] = match[j1]
            j0 = j1
    for j in range(1, n + 1):
        to[free_from[match[j] - 1]] = free_to[j - 1]
    return [(divmod(a, NC), divmod(b, NC)) for a, b in sorted(to.items())]


def send(value, pairs):
    return lax.ppermute(value, ("row", "col"), [(a * NC + b, c * NC + d) for (a, b), (c, d) in complete(pairs)])


def send_only(value, pairs):
    return lax.ppermute(value, ("row", "col"), [(a * NC + b, c * NC + d) for (a, b), (c, d) in pairs])


def dot(a, b):
    return jnp.dot(a, b, preferred_element_type=jnp.float32)


def low(a):
    return a.astype(jnp.bfloat16)


def at(device):
    return (lax.axis_index("row") == device[0]) & (lax.axis_index("col") == device[1])


def any_of(devices):
    flag = at(devices[0])
    for d in devices[1:]:
        flag = flag | at(d)
    return flag


def call(kernel, outs, ins, in_specs, out_specs, scratch=(), limit=16):
    return pl.pallas_call(
        kernel,
        out_shape=outs,
        in_specs=in_specs,
        out_specs=out_specs,
        scratch_shapes=list(scratch),
        compiler_params=pltpu.CompilerParams(vmem_limit_bytes=limit << 20),
        name=kernel.func.__name__ if isinstance(kernel, functools.partial) else kernel.__name__,
    )(*ins)


def pair_width(m, part):
    return 2 * (m + 1) * part


def cut_kernel(diag_ref, *refs):
    cuts, sem = refs[:-1], refs[-1]
    row, col = lax.axis_index("row"), lax.axis_index("col")
    part = diag_ref.shape[1]
    k = jnp.int32(0)
    for r in range(NR):
        for c in range(NC):
            k = jnp.where((row == r) & (col == c), SENDS[r][c], k)
    for m in range(NR // 2):

        @pl.when(jnp.where((row == 1) & (k == 0), 1, row // 2) == m)
        def _():
            copy = pltpu.make_async_copy(diag_ref.at[k, :, pl.ds(0, pair_width(m, part))], cuts[m], sem)
            copy.start()
            copy.wait()


def first_kernel(rhs_ref, diag_ref, *refs):
    parts, (out_ref, rhs_v, d_v, rhs_sem, d_sem) = refs[:-5], refs[-5:]
    n = out_ref.shape[0] // 2
    col = lax.axis_index("col")

    @pl.when(lax.axis_index("row") == 0)
    def _():
        rhs_copy = pltpu.make_async_copy(rhs_ref.at[0], rhs_v, rhs_sem)
        rhs_copy.start()

        def pieces(c):
            copies = []
            for i, r in enumerate(PIECES[c]):
                m = max(r // 2, 1)
                wide = pair_width(m, n)
                source = parts[m - 1] if r else diag_ref.at[0, :, pl.ds(0, wide)]
                copies.append(pltpu.make_async_copy(source, d_v.at[i, :, pl.ds(0, wide)], d_sem.at[i]))
            return copies

        for c in range(NC):

            @pl.when(col == c)
            def _():
                for copy in pieces(c):
                    copy.start()

        rhs_copy.wait()
        p = low(rhs_v[...])
        for c in range(NC):

            @pl.when(col == c)
            def _():
                for i, copy in enumerate(pieces(c)):
                    copy.wait()
                    wide = pair_width(max(PIECES[c][i] // 2, 1), n)
                    out_ref[i * n : (i + 1) * n] = low(dot(d_v[i, :, :wide], p[:wide]))


def pack_kernel(*refs):
    parts, out_ref, sem = refs[:-2], refs[-2], refs[-1]

    @pl.when(any_of(PARTNER[1:]))
    def _():
        copies, left = [], 0
        for m, source in enumerate(parts):
            wide = source.shape[1]
            copies.append(pltpu.make_async_copy(source, out_ref.at[:, pl.ds(left, wide)], sem.at[m]))
            left += wide
        for copy in copies:
            copy.start()
        for copy in copies:
            copy.wait()


def whole_kernel(rows_ref, counts_ref, diag_ref, even_ref, *refs):
    odd, (out_ref, tail_ref, sem) = refs[:-3], refs[-3:]
    size = out_ref.shape[0]
    part = size // NR
    row, col = lax.axis_index("row"), lax.axis_index("col")
    listed = rows_ref[0, 0, 0, 0]
    there = (row >= NC) & (counts_ref[0, 0, 0] > 0)
    done = at(FIRST) | at(MAKER[1]) | at(BESIDE) | at(MAKER[2])
    first = (there & (listed == 0)) | done
    second = there & (listed == 1)
    ids = lax.broadcasted_iota(jnp.int32, tail_ref.shape, 0)
    flag = ((ids == 0) & first) | ((ids == 1) & second)
    tail_ref[...] = low(jnp.where(flag, 1.0, 0.0))

    @pl.when(any_of(MAKER[1:]))
    def _():
        def copy(i, source):
            wide = pair_width(i // 2, part)
            return pltpu.make_async_copy(source, out_ref.at[pl.ds(i * part, part), pl.ds(0, wide)], sem.at[i])

        left = 0
        for i in range(NR):
            wide = pair_width(i // 2, part)
            if i % 2:
                source = odd[i // 2]
            else:
                source = even_ref.at[:, pl.ds(left, wide)]
                left += wide

            @pl.when(row == i)
            def _():
                copy(i, diag_ref.at[col, :, pl.ds(0, wide)]).start()

            @pl.when(row != i)
            def _():
                copy(i, source).start()

        for m in range(NR // 2 - 1):
            right = pair_width(m, part)
            out_ref[pl.ds(2 * m * part, 2 * part), pl.ds(right, size - right)] = jnp.zeros(
                (2 * part, size - right), out_ref.dtype
            )
        for i in range(NR):
            copy(i, odd[i // 2]).wait()


def lower_dot(q_ref, d_ref, p_ref):
    half = d_ref.shape[0] // 2
    q_ref[:half] = low(dot(d_ref[:half, :half], p_ref[:half]))
    q_ref[half:] = low(dot(d_ref[half:], p_ref[...]))


def step0_kernel(g0, g1, g2, g3, rhs_ref, l_ref, p_ref, q_ref, s_ref):
    part = l_ref.shape[0] // NR
    row = lax.axis_index("row")

    def lookup(c, i):
        r = jnp.int32(PIECES[0][i])
        for n in range(1, NC):
            r = jnp.where(c == n, PIECES[n][i], r)
        return pl.multiple_of(r * part, part)

    @pl.when((row >= 1) & (row < 4) & (lax.axis_index("col") == 0))
    def _():
        for j, got in enumerate((g0, g1, g2, g3)):
            src = lax.rem(row + 7 - j, 4)
            q_ref[pl.ds(lookup(src, 0), part)] = got[:part]
            q_ref[pl.ds(lookup(src, 1), part)] = got[part:]
        s = dot(l_ref[...], q_ref[...])
        s_ref[...] = low(s)
        p_ref[...] = low(rhs_ref[0] - s)


def step1_kernel(p_in, d_ref, q_prev, q_ref):
    active = at(MAKER[1])

    @pl.when(active)
    def _():
        lower_dot(q_ref, d_ref, p_in)

    @pl.when(jnp.logical_not(active))
    def _():
        q_ref[...] = q_prev[...]


def step1_sum_kernel(q_in, sum_ref, rhs_ref, l_ref, s_prev, p_ref, s_ref):
    active = at(MAKER[1])

    @pl.when(active)
    def _():
        s = dot(l_ref[...], q_in[...]) + sum_ref[...].astype(jnp.float32)
        s_ref[...] = low(s)
        p_ref[...] = low(rhs_ref[0] - s)

    @pl.when(jnp.logical_not(active))
    def _():
        s_ref[...] = s_prev[...]


def step2_kernel(takers, p_in, q_in, came_ref, sum_ref, rhs_ref, d_ref, l_ref, q_prev, s_prev, a_ref, q_ref, s_ref):
    active, beside, taken = at(MAKER[2]), at(BESIDE), any_of(takers)

    @pl.when(active)
    def _():
        lower_dot(q_ref, d_ref, p_in)
        s_ref[...] = low(dot(l_ref[...], q_ref[...]))

    @pl.when(beside)
    def _():
        q_ref[...] = q_in[...]
        s = dot(l_ref[...], q_in[...]) + sum_ref[...].astype(jnp.float32)
        s_ref[...] = low(s)
        a_ref[...] = low(rhs_ref[0] - s)

    @pl.when(jnp.logical_not(active | beside))
    def _():
        s_ref[...] = s_prev[...]

    @pl.when(taken)
    def _():
        q_ref[...] = came_ref[...]

    @pl.when(jnp.logical_not(active | beside | taken))
    def _():
        q_ref[...] = q_prev[...]


def step3_kernel(takers, a_ref, sum_ref, *refs):
    came, (d_ref, q_prev, q_ref, p_v) = refs[:-4], refs[-4:]
    active = at(MAKER[3])

    @pl.when(active)
    def _():
        p_v[...] = low(a_ref[...].astype(jnp.float32) - sum_ref[...].astype(jnp.float32))
        lower_dot(q_ref, d_ref, p_v)

    for devices, source in zip(takers, came):

        @pl.when(any_of(devices))
        def _():
            q_ref[...] = source[...]

    @pl.when(jnp.logical_not(active | any_of([d for devices in takers for d in devices])))
    def _():
        q_ref[...] = q_prev[...]


def update_kernel(takers, tail_ref, s_ref, l_ref, q_prev, *refs):
    got, q_ref, out_ref = refs[:-2], refs[-2], refs[-1]
    size = l_ref.shape[0]
    row, col = lax.axis_index("row"), lax.axis_index("col")
    below = row >= NC

    def take(flag, source):
        @pl.when(flag)
        def _():
            q_ref[...] = source[...]

    kept = jnp.logical_not(any_of([d for devices in takers for d in devices]))
    take(kept, q_prev)
    for devices, source in zip(takers, got):
        take(any_of(devices), source)

    @pl.when(below)
    def _():
        out_ref[pl.ds(0, size)] = low(dot(l_ref[...], q_ref[...]))

    @pl.when(jnp.logical_not(below))
    def _():
        out_ref[pl.ds(0, size)] = s_ref[...]

    out_ref[pl.ds(size, TAIL)] = tail_ref[...]


def minus(acc, sums, i):
    size = acc.shape[0]
    for s in sums:
        keep = s[pl.ds(size, TAIL)].astype(jnp.float32)[i : i + 1] > 0.5
        acc = acc - jnp.where(keep, s[pl.ds(0, size)].astype(jnp.float32), 0.0)
    return acc


def half_kernel(q_ref, rest_ref, rhs_ref, mine_ref, across_ref, solved_ref, out_ref):
    came = any_of(REST)

    @pl.when(came)
    def _():
        solved_ref[...] = rest_ref[...].astype(jnp.float32)

    @pl.when(jnp.logical_not(came))
    def _():
        solved_ref[...] = q_ref[...].astype(jnp.float32)

    for i in range(out_ref.shape[0]):
        out_ref[i] = minus(rhs_ref[i], (mine_ref, across_ref), i)


def final_kernel(half_ref, beside_ref, corner_ref, out_ref):
    for i in range(out_ref.shape[0]):
        out_ref[i] = minus(half_ref[i], (beside_ref, corner_ref), i)


def on_device_8x4(rhs, diag_inv, blocks, block_rows, counts):
    size, width = rhs.shape[2:]
    part = size // NR
    rhs = rhs[:, 0]
    block = blocks[0, 0, 0, 0]
    bf16 = jnp.bfloat16
    vec = jax.ShapeDtypeStruct((size, width), bf16)
    dma = pltpu.SemaphoreType.DMA

    wides = [pair_width(m, part) for m in range(NR // 2)]
    cuts = call(
        cut_kernel, [jax.ShapeDtypeStruct((part, w), bf16) for w in wides], [diag_inv], [HBM], [ANY] * len(wides), [dma]
    )
    at_piece = {r: (0, c) for c, rows in enumerate(PIECES) for r in rows}
    parts = []
    for m, cut in enumerate(cuts):
        pairs = []
        for r in range(NR):
            for c, k in enumerate(SENDS[r]):
                if k == 0 and r and max(r // 2, 1) == m:
                    pairs.append(((r, c), at_piece[r]))
                if k and MAKER[k][0] != r and r // 2 == m:
                    pairs.append(((r, c), MAKER[k] if r % 2 else PARTNER[k]))
        parts.append(send_only(cut, pairs))
    q = call(
        first_kernel,
        jax.ShapeDtypeStruct((2 * part, width), bf16),
        [rhs, diag_inv, *parts[1:]],
        [HBM, HBM] + [ANY] * (len(wides) - 1),
        VMEM,
        [
            pltpu.VMEM((size, width), jnp.float32),
            pltpu.VMEM((2, part, size), bf16),
            dma,
            pltpu.SemaphoreType.DMA((2,)),
        ],
    )
    takers = (FIRST, (2, 0), (3, 0))
    got = [send(q, [((0, c), takers[(c + j) % 4]) for c in range(4) if (c + j) % 4 < 3]) for j in range(4)]
    even = call(
        pack_kernel,
        jax.ShapeDtypeStruct((part, sum(wides)), bf16),
        parts,
        [ANY] * len(wides),
        VMEM,
        [pltpu.SemaphoreType.DMA((len(wides),))],
    )
    even = send(even, [(PARTNER[k], MAKER[k]) for k in range(1, NC)])
    diag, tail = call(
        whole_kernel,
        [jax.ShapeDtypeStruct((size, size), bf16), jax.ShapeDtypeStruct((TAIL, width), bf16)],
        [block_rows, counts, diag_inv, even, *parts],
        [SMEM, SMEM, HBM] + [ANY] * (1 + len(wides)),
        [VMEM, VMEM],
        [pltpu.SemaphoreType.DMA((NR,))],
    )

    p, q, s = call(step0_kernel, [vec] * 3, [*got, rhs, block], [VMEM] * 6, [VMEM] * 3)
    p_in = send(p, [(FIRST, MAKER[1])])
    sums = send(s, [((2, 0), MAKER[1]), ((3, 0), BESIDE)])
    q = call(step1_kernel, vec, [p_in, diag, q], [VMEM] * 3, VMEM)
    p, s = call(step1_sum_kernel, [vec] * 2, [q, sums, rhs, block, s], [VMEM] * 5, [VMEM] * 2)
    p_in = send(p, [(MAKER[1], MAKER[2])])
    q_in = send(q, [(MAKER[1], BESIDE)])

    came = send(q, [((2, 0), (4, 0)), ((3, 0), (5, 0)), ((1, 0), (0, 0)), ((2, 1), (4, 1))])
    took = [(4, 0), (5, 0), (0, 0), (4, 1)]
    a, q, s = call(
        functools.partial(step2_kernel, took),
        [vec] * 3,
        [p_in, q_in, came, sums, rhs, diag, block, q, s],
        [VMEM] * 9,
        [VMEM] * 3,
    )
    a = send(a, [(BESIDE, MAKER[3])])
    sums = send(s, [(MAKER[2], MAKER[3])])
    sends = [
        [(MAKER[2], (2, 2))],
        [(MAKER[2], (7, 2)), ((4, 0), (6, 0)), ((5, 0), (7, 0)), ((4, 1), (6, 1)), ((3, 1), (1, 1)), ((2, 1), (0, 1))],
        [(MAKER[2], (5, 2)), ((3, 1), (7, 1)), ((4, 1), (5, 1))],
    ]
    got = [send(q, sends[0])] + [send_only(q, pairs) for pairs in sends[1:]]
    q = call(
        functools.partial(step3_kernel, [[b for _, b in pairs] for pairs in sends]),
        vec,
        [a, sums, *got, diag, q],
        [VMEM] * 7,
        VMEM,
        [pltpu.VMEM((size, width), bf16)],
    )

    sends = [
        [(MAKER[3], (6, 3)), ((2, 2), (4, 2)), ((7, 2), (6, 2))],
        [(MAKER[3], (4, 3)), ((2, 2), (0, 2))],
        [(MAKER[3], (7, 3))],
    ]
    got = [send_only(q, pairs) for pairs in sends]
    takers = [[b for _, b in pairs] for pairs in sends]
    q, mine = call(
        functools.partial(update_kernel, takers),
        [vec, jax.ShapeDtypeStruct((size + TAIL, width), bf16)],
        [tail, s, block, q, *got],
        [VMEM] * (4 + len(got)),
        [VMEM] * 2,
    )

    def swap(value, step):
        return send(value, [((r, c), (r, c ^ step)) for r in range(NR) for c in range(NC)])

    across = swap(mine, 2)
    rest = send_only(q, list(zip(((4, 3), (5, 3), (6, 3), (7, 3), MAKER[2]), REST)))
    beside = swap(mine, 1)
    across, rest = lax.optimization_barrier((across, rest))
    corner = swap(across, 1)
    whole_rhs = jax.ShapeDtypeStruct(rhs.shape, jnp.float32)
    solved, half = call(
        half_kernel,
        [jax.ShapeDtypeStruct((size, width), jnp.float32), whole_rhs],
        [q, rest, rhs, mine, across],
        [VMEM] * 5,
        [VMEM] * 2,
    )
    remainder = call(final_kernel, whole_rhs, [half, beside, corner], [VMEM] * 3, VMEM)
    return solved[None, None], remainder[:, None]


def solution(mesh):
    in_specs = (
        P(None, "row", None, None),
        P(None, "row", None),
        P(None, "col", "row", None, None, None),
        P(None, "col", "row", None),
        P(None, "col", "row"),
    )
    out_specs = (P(None, "col", None, None), P(None, "row", None, None))
    small = mesh.shape["row"] == NR and mesh.shape["col"] == NC
    return jax.shard_map(
        on_device_8x4 if small else on_device_any,
        mesh=mesh,
        in_specs=in_specs,
        out_specs=out_specs,
        check_vma=False,
    )
```

```python
import functools

import jax
import jax.numpy as jnp
from jax import lax
from jax.experimental import pallas as pl
from jax.experimental.pallas import tpu as pltpu
from jax.sharding import PartitionSpec as P

VMEM = pl.BlockSpec(memory_space=pltpu.VMEM)
ANY = pl.BlockSpec(memory_space=pl.ANY)
HBM = pl.BlockSpec(memory_space=pltpu.HBM)
SMEM = pl.BlockSpec(memory_space=pltpu.SMEM)
TAIL = 16


def broadcast(value, axis, root):
    mine = lax.axis_index(axis) == root
    return lax.psum(jnp.where(mine, value, jnp.zeros_like(value)), axis)


def on_device_any(rhs, diag_inv, blocks, block_rows, counts):
    nrow = lax.axis_size("row")
    ncol = lax.axis_size("col")
    my_row = lax.axis_index("row")
    my_col = lax.axis_index("col")
    kc = diag_inv.shape[0]
    rb_local = rhs.shape[0]
    nz_local = blocks.shape[3]
    local_rhs = rhs[:, 0]
    partial_value = jnp.zeros(local_rhs.shape, jnp.float32)
    solved_list = [jnp.zeros(local_rhs.shape[1:], jnp.float32)]
    slot_ids = jnp.arange(nz_local, dtype=jnp.int32)
    local_ids = jnp.arange(rb_local, dtype=jnp.int32)
    for k in range(kc):
        j = k // ncol
        owner_row = k % nrow
        local_pivot = k // nrow
        mine_row = my_row == owner_row
        mine_col = my_col == k % ncol
        pivot_part = jnp.where(mine_row, partial_value[local_pivot], jnp.float32(0.0))
        summed = lax.psum(pivot_part, "col")
        updated = (local_rhs[local_pivot] - summed).astype(jnp.bfloat16)
        pivot_bf = broadcast(updated, "row", owner_row)
        row_part = jnp.dot(diag_inv[k], pivot_bf, preferred_element_type=jnp.float32)
        sol = lax.all_gather(row_part, "row", axis=0, tiled=True)
        sol_bf = sol.astype(jnp.bfloat16)
        rows = block_rows[j, 0, 0]
        glob = rows * nrow + my_row
        valid = (slot_ids < counts[j, 0, 0]) & (glob > k) & mine_col
        weights = (valid[:, None] & (rows[:, None] == local_ids[None, :])).astype(jnp.float32)
        contrib = jnp.einsum(
            "sab,bn->san", blocks[j, 0, 0], sol_bf, preferred_element_type=jnp.float32
        )
        partial_value = partial_value + jnp.einsum(
            "sl,san->lan", weights, contrib, precision=lax.Precision.HIGHEST
        )
        solved_list[j] = jnp.where(mine_col, sol, solved_list[j])
    total = lax.psum(partial_value, "col")
    remainder = (local_rhs - total)[:, None]
    solved = jnp.stack(solved_list)[:, None]
    return (solved, remainder)


NR, NC = 8, 4
MAKER = (None, (2, 1), (3, 2), (5, 3))
FIRST = (1, 0)
BESIDE = (3, 1)
PARTNER = (None, (3, 1), (3, 3), (5, 2))
PIECES = ((4, 1), (6, 3), (5, 2), (7, 0))
SENDS = (
    (0, 1, 2, 3),
    (0, 1, 2, 3),
    (3, 1, 0, 2),
    (0, 1, 3, 2),
    (0, 1, 3, 2),
    (2, 1, 3, 0),
    (0, 3, 1, 2),
    (1, 3, 0, 2),
)
REST = ((3, 3), (0, 3), (1, 3), (1, 2))


def hops(a, b):
    d = a ^ b
    if d < 2:
        return 1 if d else 10000
    return 100 + abs((a >> 3) - (b >> 3)) + ((d >> 2) & 1) + ((d >> 1) & 1)


def complete(pairs):
    to = {a * NC + b: c * NC + d for (a, b), (c, d) in pairs}
    free_from = [i for i in range(NR * NC) if i not in to]
    free_to = [i for i in range(NR * NC) if i not in to.values()]
    n = len(free_from)
    u, v, match = [0] * (n + 1), [0] * (n + 1), [0] * (n + 1)
    for i in range(1, n + 1):
        match[0], j0 = i, 0
        least, way, used = [10**9] * (n + 1), [0] * (n + 1), [False] * (n + 1)
        while True:
            used[j0] = True
            i0, delta, j1 = match[j0], 10**9, 0
            for j in range(1, n + 1):
                if not used[j]:
                    cur = hops(free_from[i0 - 1], free_to[j - 1]) - u[i0] - v[j]
                    if cur < least[j]:
                        least[j], way[j] = cur, j0
                    if least[j] < delta:
                        delta, j1 = least[j], j
            for j in range(n + 1):
                if used[j]:
                    u[match[j]] += delta
                    v[j] -= delta
                else:
                    least[j] -= delta
            j0 = j1
            if match[j0] == 0:
                break
        while j0:
            j1 = way[j0]
            match[j0] = match[j1]
            j0 = j1
    for j in range(1, n + 1):
        to[free_from[match[j] - 1]] = free_to[j - 1]
    return [(divmod(a, NC), divmod(b, NC)) for a, b in sorted(to.items())]


def send(value, pairs):
    return lax.ppermute(value, ("row", "col"), [(a * NC + b, c * NC + d) for (a, b), (c, d) in complete(pairs)])


def send_only(value, pairs):
    return lax.ppermute(value, ("row", "col"), [(a * NC + b, c * NC + d) for (a, b), (c, d) in pairs])


def dot(a, b):
    return jnp.dot(a, b, preferred_element_type=jnp.float32)


def low(a):
    return a.astype(jnp.bfloat16)


def at(device):
    return (lax.axis_index("row") == device[0]) & (lax.axis_index("col") == device[1])


def any_of(devices):
    flag = at(devices[0])
    for d in devices[1:]:
        flag = flag | at(d)
    return flag


def call(kernel, outs, ins, in_specs, out_specs, scratch=(), limit=16, aliases=None):
    return pl.pallas_call(
        kernel,
        out_shape=outs,
        in_specs=in_specs,
        out_specs=out_specs,
        scratch_shapes=list(scratch),
        input_output_aliases=aliases or {},
        compiler_params=pltpu.CompilerParams(vmem_limit_bytes=limit << 20),
        name=kernel.func.__name__ if isinstance(kernel, functools.partial) else kernel.__name__,
    )(*ins)


def pair_width(m, part):
    return 2 * (m + 1) * part


def cut_kernel(diag_ref, *refs):
    cuts, sem = refs[:-1], refs[-1]
    row, col = lax.axis_index("row"), lax.axis_index("col")
    part = diag_ref.shape[1]
    k = jnp.int32(0)
    for r in range(NR):
        for c in range(NC):
            k = jnp.where((row == r) & (col == c), SENDS[r][c], k)
    for m in range(NR // 2):

        @pl.when(jnp.where((row == 1) & (k == 0), 1, row // 2) == m)
        def _():
            copy = pltpu.make_async_copy(diag_ref.at[k, :, pl.ds(0, pair_width(m, part))], cuts[m], sem)
            copy.start()
            copy.wait()


def first_kernel(rhs_ref, diag_ref, *refs):
    parts, (out_ref, rhs_v, d_v, rhs_sem, d_sem) = refs[:-5], refs[-5:]
    n = out_ref.shape[0] // 2
    col = lax.axis_index("col")

    @pl.when(lax.axis_index("row") == 0)
    def _():
        rhs_copy = pltpu.make_async_copy(rhs_ref.at[0], rhs_v, rhs_sem)
        rhs_copy.start()

        def pieces(c):
            copies = []
            for i, r in enumerate(PIECES[c]):
                m = max(r // 2, 1)
                wide = pair_width(m, n)
                source = parts[m - 1] if r else diag_ref.at[0, :, pl.ds(0, wide)]
                copies.append(pltpu.make_async_copy(source, d_v.at[i, :, pl.ds(0, wide)], d_sem.at[i]))
            return copies

        for c in range(NC):

            @pl.when(col == c)
            def _():
                for copy in pieces(c):
                    copy.start()

        rhs_copy.wait()
        p = low(rhs_v[...])
        for c in range(NC):

            @pl.when(col == c)
            def _():
                for i, copy in enumerate(pieces(c)):
                    copy.wait()
                    wide = pair_width(max(PIECES[c][i] // 2, 1), n)
                    out_ref[i * n : (i + 1) * n] = low(dot(d_v[i, :, :wide], p[:wide]))


def pack_kernel(*refs):
    parts, out_ref, sem = refs[:-2], refs[-2], refs[-1]

    @pl.when(any_of(PARTNER[1:]))
    def _():
        copies, left = [], 0
        for m, source in enumerate(parts):
            wide = source.shape[1]
            copies.append(pltpu.make_async_copy(source, out_ref.at[:, pl.ds(left, wide)], sem.at[m]))
            left += wide
        for copy in copies:
            copy.start()
        for copy in copies:
            copy.wait()


def whole_kernel(rows_ref, counts_ref, diag_ref, even_ref, *refs):
    odd, (out_ref, tail_ref, sem) = refs[:-3], refs[-3:]
    size = out_ref.shape[0]
    part = size // NR
    row, col = lax.axis_index("row"), lax.axis_index("col")
    listed = rows_ref[0, 0, 0, 0]
    there = (row >= NC) & (counts_ref[0, 0, 0] > 0)
    done = at(FIRST) | at(MAKER[1]) | at(BESIDE) | at(MAKER[2])
    first = (there & (listed == 0)) | done
    second = there & (listed == 1)
    ids = lax.broadcasted_iota(jnp.int32, tail_ref.shape, 0)
    flag = ((ids == 0) & first) | ((ids == 1) & second)
    tail_ref[...] = low(jnp.where(flag, 1.0, 0.0))

    @pl.when(any_of(MAKER[1:]))
    def _():
        def copy(i, source):
            wide = pair_width(i // 2, part)
            return pltpu.make_async_copy(source, out_ref.at[pl.ds(i * part, part), pl.ds(0, wide)], sem.at[i])

        left = 0
        for i in range(NR):
            wide = pair_width(i // 2, part)
            if i % 2:
                source = odd[i // 2]
            else:
                source = even_ref.at[:, pl.ds(left, wide)]
                left += wide

            @pl.when(row == i)
            def _():
                copy(i, diag_ref.at[col, :, pl.ds(0, wide)]).start()

            @pl.when(row != i)
            def _():
                copy(i, source).start()

        for m in range(NR // 2 - 1):
            right = pair_width(m, part)
            out_ref[pl.ds(2 * m * part, 2 * part), pl.ds(right, size - right)] = jnp.zeros(
                (2 * part, size - right), out_ref.dtype
            )
        for i in range(NR):
            copy(i, odd[i // 2]).wait()


def lower_dot(q_ref, d_ref, p_ref):
    half = d_ref.shape[0] // 2
    q_ref[:half] = low(dot(d_ref[:half, :half], p_ref[:half]))
    q_ref[half:] = low(dot(d_ref[half:], p_ref[...]))


def step0_kernel(g0, g1, g2, g3, rhs_ref, l_ref, p_ref, q_ref, s_ref):
    part = l_ref.shape[0] // NR
    row = lax.axis_index("row")

    def lookup(c, i):
        r = jnp.int32(PIECES[0][i])
        for n in range(1, NC):
            r = jnp.where(c == n, PIECES[n][i], r)
        return pl.multiple_of(r * part, part)

    @pl.when((row >= 1) & (row < 4) & (lax.axis_index("col") == 0))
    def _():
        for j, got in enumerate((g0, g1, g2, g3)):
            src = lax.rem(row + 7 - j, 4)
            q_ref[pl.ds(lookup(src, 0), part)] = got[:part]
            q_ref[pl.ds(lookup(src, 1), part)] = got[part:]
        s = dot(l_ref[...], q_ref[...])
        s_ref[...] = low(s)
        p_ref[...] = low(rhs_ref[0] - s)


def step1_kernel(p_in, d_ref, q_prev, q_ref):
    active = at(MAKER[1])

    @pl.when(active)
    def _():
        lower_dot(q_ref, d_ref, p_in)

    @pl.when(jnp.logical_not(active))
    def _():
        q_ref[...] = q_prev[...]


def step1_sum_kernel(q_in, sum_ref, rhs_ref, l_ref, s_prev, p_ref, s_ref):
    active = at(MAKER[1])

    @pl.when(active)
    def _():
        s = dot(l_ref[...], q_in[...]) + sum_ref[...].astype(jnp.float32)
        s_ref[...] = low(s)
        p_ref[...] = low(rhs_ref[0] - s)

    @pl.when(jnp.logical_not(active))
    def _():
        s_ref[...] = s_prev[...]


def step2_kernel(takers, p_in, q_in, came_ref, sum_ref, rhs_ref, d_ref, l_ref, q_prev, s_prev, a_ref, q_ref, s_ref):
    active, beside, taken = at(MAKER[2]), at(BESIDE), any_of(takers)

    @pl.when(active)
    def _():
        lower_dot(q_ref, d_ref, p_in)
        s_ref[...] = low(dot(l_ref[...], q_ref[...]))

    @pl.when(beside)
    def _():
        q_ref[...] = q_in[...]
        s = dot(l_ref[...], q_in[...]) + sum_ref[...].astype(jnp.float32)
        s_ref[...] = low(s)
        a_ref[...] = low(rhs_ref[0] - s)

    @pl.when(jnp.logical_not(active | beside))
    def _():
        s_ref[...] = s_prev[...]

    @pl.when(taken)
    def _():
        q_ref[...] = came_ref[...]

    @pl.when(jnp.logical_not(active | beside | taken))
    def _():
        q_ref[...] = q_prev[...]


def step3_kernel(takers, a_ref, sum_ref, *refs):
    came, (d_ref, q_prev, q_ref, p_v) = refs[:-4], refs[-4:]
    active = at(MAKER[3])

    @pl.when(active)
    def _():
        p_v[...] = low(a_ref[...].astype(jnp.float32) - sum_ref[...].astype(jnp.float32))
        lower_dot(q_ref, d_ref, p_v)

    for devices, source in zip(takers, came):

        @pl.when(any_of(devices))
        def _():
            q_ref[...] = source[...]

    @pl.when(jnp.logical_not(active | any_of([d for devices in takers for d in devices])))
    def _():
        q_ref[...] = q_prev[...]


def update_kernel(takers, tail_ref, s_ref, l_ref, q_prev, *refs):
    got, q_ref, out_ref = refs[:-2], refs[-2], refs[-1]
    size = l_ref.shape[0]
    row, col = lax.axis_index("row"), lax.axis_index("col")
    below = row >= NC

    def take(flag, source):
        @pl.when(flag)
        def _():
            q_ref[...] = source[...]

    kept = jnp.logical_not(any_of([d for devices in takers for d in devices]))
    take(kept, q_prev)
    for devices, source in zip(takers, got):
        take(any_of(devices), source)

    @pl.when(below)
    def _():
        out_ref[pl.ds(0, size)] = low(dot(l_ref[...], q_ref[...]))

    @pl.when(jnp.logical_not(below))
    def _():
        out_ref[pl.ds(0, size)] = s_ref[...]

    out_ref[pl.ds(size, TAIL)] = tail_ref[...]


def minus(acc, sums, i):
    size = acc.shape[0]
    for s in sums:
        keep = s[pl.ds(size, TAIL)].astype(jnp.float32)[i : i + 1] > 0.5
        acc = acc - jnp.where(keep, s[pl.ds(0, size)].astype(jnp.float32), 0.0)
    return acc


def half_kernel(q_ref, rest_ref, rhs_ref, mine_ref, across_ref, beside_ref, solved_ref, out_ref, acc_ref):
    came = any_of(REST)

    @pl.when(came)
    def _():
        solved_ref[...] = rest_ref[...].astype(jnp.float32)

    @pl.when(jnp.logical_not(came))
    def _():
        solved_ref[...] = q_ref[...].astype(jnp.float32)

    for i in range(out_ref.shape[0]):
        acc_ref[i] = minus(rhs_ref[i], (mine_ref, across_ref, beside_ref), i)
        out_ref[i] = acc_ref[i]


def final_kernel(whole_ref, acc_ref, corner_ref, out_ref, new_v, sem):
    size = new_v.shape[0]
    tail = corner_ref[pl.ds(size, TAIL)].astype(jnp.float32)
    for i in range(acc_ref.shape[0]):

        @pl.when(jnp.max(tail[i : i + 1]) > 0.5)
        def _():
            new_v[...] = acc_ref[i] - corner_ref[pl.ds(0, size)].astype(jnp.float32)
            copy = pltpu.make_async_copy(new_v, out_ref.at[i], sem)
            copy.start()
            copy.wait()


def on_device_8x4(rhs, diag_inv, blocks, block_rows, counts):
    size, width = rhs.shape[2:]
    part = size // NR
    rhs = rhs[:, 0]
    block = blocks[0, 0, 0, 0]
    bf16 = jnp.bfloat16
    vec = jax.ShapeDtypeStruct((size, width), bf16)
    dma = pltpu.SemaphoreType.DMA

    wides = [pair_width(m, part) for m in range(NR // 2)]
    cuts = call(
        cut_kernel, [jax.ShapeDtypeStruct((part, w), bf16) for w in wides], [diag_inv], [HBM], [ANY] * len(wides), [dma]
    )
    at_piece = {r: (0, c) for c, rows in enumerate(PIECES) for r in rows}
    parts = []
    for m, cut in enumerate(cuts):
        pairs = []
        for r in range(NR):
            for c, k in enumerate(SENDS[r]):
                if k == 0 and r and max(r // 2, 1) == m:
                    pairs.append(((r, c), at_piece[r]))
                if k and MAKER[k][0] != r and r // 2 == m:
                    pairs.append(((r, c), MAKER[k] if r % 2 else PARTNER[k]))
        parts.append(send_only(cut, pairs))
    q = call(
        first_kernel,
        jax.ShapeDtypeStruct((2 * part, width), bf16),
        [rhs, diag_inv, *parts[1:]],
        [HBM, HBM] + [ANY] * (len(wides) - 1),
        VMEM,
        [
            pltpu.VMEM((size, width), jnp.float32),
            pltpu.VMEM((2, part, size), bf16),
            dma,
            pltpu.SemaphoreType.DMA((2,)),
        ],
    )
    takers = (FIRST, (2, 0), (3, 0))
    got = [send(q, [((0, c), takers[(c + j) % 4]) for c in range(4) if (c + j) % 4 < 3]) for j in range(4)]
    even = call(
        pack_kernel,
        jax.ShapeDtypeStruct((part, sum(wides)), bf16),
        parts,
        [ANY] * len(wides),
        VMEM,
        [pltpu.SemaphoreType.DMA((len(wides),))],
    )
    even = send(even, [(PARTNER[k], MAKER[k]) for k in range(1, NC)])
    diag, tail = call(
        whole_kernel,
        [jax.ShapeDtypeStruct((size, size), bf16), jax.ShapeDtypeStruct((TAIL, width), bf16)],
        [block_rows, counts, diag_inv, even, *parts],
        [SMEM, SMEM, HBM] + [ANY] * (1 + len(wides)),
        [VMEM, VMEM],
        [pltpu.SemaphoreType.DMA((NR,))],
    )

    p, q, s = call(step0_kernel, [vec] * 3, [*got, rhs, block], [VMEM] * 6, [VMEM] * 3)
    p_in = send(p, [(FIRST, MAKER[1])])
    sums = send(s, [((2, 0), MAKER[1]), ((3, 0), BESIDE)])
    q = call(step1_kernel, vec, [p_in, diag, q], [VMEM] * 3, VMEM)
    p, s = call(step1_sum_kernel, [vec] * 2, [q, sums, rhs, block, s], [VMEM] * 5, [VMEM] * 2)
    p_in = send(p, [(MAKER[1], MAKER[2])])
    q_in = send(q, [(MAKER[1], BESIDE)])

    came = send(q, [((2, 0), (4, 0)), ((3, 0), (5, 0)), ((1, 0), (0, 0)), ((2, 1), (4, 1))])
    took = [(4, 0), (5, 0), (0, 0), (4, 1)]
    a, q, s = call(
        functools.partial(step2_kernel, took),
        [vec] * 3,
        [p_in, q_in, came, sums, rhs, diag, block, q, s],
        [VMEM] * 9,
        [VMEM] * 3,
    )
    a = send(a, [(BESIDE, MAKER[3])])
    sums = send(s, [(MAKER[2], MAKER[3])])
    sends = [
        [(MAKER[2], (2, 2))],
        [(MAKER[2], (7, 2)), ((4, 0), (6, 0)), ((5, 0), (7, 0)), ((4, 1), (6, 1)), ((3, 1), (1, 1)), ((2, 1), (0, 1))],
        [(MAKER[2], (5, 2)), ((3, 1), (7, 1)), ((4, 1), (5, 1))],
    ]
    got = [send(q, sends[0])] + [send_only(q, pairs) for pairs in sends[1:]]
    q = call(
        functools.partial(step3_kernel, [[b for _, b in pairs] for pairs in sends]),
        vec,
        [a, sums, *got, diag, q],
        [VMEM] * 7,
        VMEM,
        [pltpu.VMEM((size, width), bf16)],
    )

    sends = [
        [(MAKER[3], (6, 3)), ((2, 2), (4, 2)), ((7, 2), (6, 2))],
        [(MAKER[3], (4, 3)), ((2, 2), (0, 2))],
        [(MAKER[3], (7, 3))],
        [(MAKER[3], (2, 3))],
    ]
    got = [send_only(q, pairs) for pairs in sends]
    takers = [[b for _, b in pairs] for pairs in sends]
    q, mine = call(
        functools.partial(update_kernel, takers),
        [vec, jax.ShapeDtypeStruct((size + TAIL, width), bf16)],
        [tail, s, block, q, *got],
        [VMEM] * (4 + len(got)),
        [VMEM] * 2,
    )

    def swap(value, step):
        return send(value, [((r, c), (r, c ^ step)) for r in range(NR) for c in range(NC)])

    across = swap(mine, 2)
    rest = send_only(q, list(zip(((2, 3), (6, 3), (7, 3), MAKER[2]), REST)))
    beside = swap(mine, 1)
    across, rest = lax.optimization_barrier((across, rest))
    corner = swap(across, 1)
    whole_rhs = jax.ShapeDtypeStruct(rhs.shape, jnp.float32)
    solved, half, acc = call(
        half_kernel,
        [jax.ShapeDtypeStruct((size, width), jnp.float32), whole_rhs, whole_rhs],
        [q, rest, rhs, mine, across, beside],
        [VMEM] * 6,
        [VMEM] * 3,
    )
    remainder = call(
        final_kernel,
        whole_rhs,
        [half, acc, corner],
        [ANY, VMEM, VMEM],
        ANY,
        [pltpu.VMEM((size, width), jnp.float32), dma],
        aliases={0: 0},
    )
    return solved[None, None], remainder[:, None]


def solution(mesh):
    in_specs = (
        P(None, "row", None, None),
        P(None, "row", None),
        P(None, "col", "row", None, None, None),
        P(None, "col", "row", None),
        P(None, "col", "row"),
    )
    out_specs = (P(None, "col", None, None), P(None, "row", None, None))
    small = mesh.shape["row"] == NR and mesh.shape["col"] == NC
    return jax.shard_map(
        on_device_8x4 if small else on_device_any,
        mesh=mesh,
        in_specs=in_specs,
        out_specs=out_specs,
        check_vma=False,
    )
```

```python
import functools

import jax
import jax.numpy as jnp
from jax import lax
from jax.experimental import pallas as pl
from jax.experimental.pallas import tpu as pltpu
from jax.sharding import PartitionSpec as P

VMEM = pl.BlockSpec(memory_space=pltpu.VMEM)
ANY = pl.BlockSpec(memory_space=pl.ANY)
HBM = pl.BlockSpec(memory_space=pltpu.HBM)
SMEM = pl.BlockSpec(memory_space=pltpu.SMEM)
TAIL = 16


def broadcast(value, axis, root):
    mine = lax.axis_index(axis) == root
    return lax.psum(jnp.where(mine, value, jnp.zeros_like(value)), axis)


def on_device_any(rhs, diag_inv, blocks, block_rows, counts):
    nrow = lax.axis_size("row")
    ncol = lax.axis_size("col")
    my_row = lax.axis_index("row")
    my_col = lax.axis_index("col")
    kc = diag_inv.shape[0]
    rb_local = rhs.shape[0]
    nz_local = blocks.shape[3]
    local_rhs = rhs[:, 0]
    partial_value = jnp.zeros(local_rhs.shape, jnp.float32)
    solved_list = [jnp.zeros(local_rhs.shape[1:], jnp.float32)]
    slot_ids = jnp.arange(nz_local, dtype=jnp.int32)
    local_ids = jnp.arange(rb_local, dtype=jnp.int32)
    for k in range(kc):
        j = k // ncol
        owner_row = k % nrow
        local_pivot = k // nrow
        mine_row = my_row == owner_row
        mine_col = my_col == k % ncol
        pivot_part = jnp.where(mine_row, partial_value[local_pivot], jnp.float32(0.0))
        summed = lax.psum(pivot_part, "col")
        updated = (local_rhs[local_pivot] - summed).astype(jnp.bfloat16)
        pivot_bf = broadcast(updated, "row", owner_row)
        row_part = jnp.dot(diag_inv[k], pivot_bf, preferred_element_type=jnp.float32)
        sol = lax.all_gather(row_part, "row", axis=0, tiled=True)
        sol_bf = sol.astype(jnp.bfloat16)
        rows = block_rows[j, 0, 0]
        glob = rows * nrow + my_row
        valid = (slot_ids < counts[j, 0, 0]) & (glob > k) & mine_col
        weights = (valid[:, None] & (rows[:, None] == local_ids[None, :])).astype(jnp.float32)
        contrib = jnp.einsum(
            "sab,bn->san", blocks[j, 0, 0], sol_bf, preferred_element_type=jnp.float32
        )
        partial_value = partial_value + jnp.einsum(
            "sl,san->lan", weights, contrib, precision=lax.Precision.HIGHEST
        )
        solved_list[j] = jnp.where(mine_col, sol, solved_list[j])
    total = lax.psum(partial_value, "col")
    remainder = (local_rhs - total)[:, None]
    solved = jnp.stack(solved_list)[:, None]
    return (solved, remainder)


NR, NC = 8, 4
MAKER = (None, (2, 1), (3, 2), (5, 3))
FIRST = (1, 0)
BESIDE = (3, 1)
PARTNER = (None, (3, 1), (3, 3), (5, 2))
PIECES = ((4, 1), (6, 3), (5, 2), (7, 0))
SENDS = (
    (0, 1, 2, 3),
    (0, 1, 2, 3),
    (3, 1, 0, 2),
    (0, 1, 3, 2),
    (0, 1, 3, 2),
    (2, 1, 3, 0),
    (0, 3, 1, 2),
    (1, 3, 0, 2),
)
REST = ((3, 3), (0, 3), (1, 3), (1, 2))


def hops(a, b):
    d = a ^ b
    if d < 2:
        return 1 if d else 10000
    return 100 + abs((a >> 3) - (b >> 3)) + ((d >> 2) & 1) + ((d >> 1) & 1)


def complete(pairs):
    to = {a * NC + b: c * NC + d for (a, b), (c, d) in pairs}
    free_from = [i for i in range(NR * NC) if i not in to]
    free_to = [i for i in range(NR * NC) if i not in to.values()]
    n = len(free_from)
    u, v, match = [0] * (n + 1), [0] * (n + 1), [0] * (n + 1)
    for i in range(1, n + 1):
        match[0], j0 = i, 0
        least, way, used = [10**9] * (n + 1), [0] * (n + 1), [False] * (n + 1)
        while True:
            used[j0] = True
            i0, delta, j1 = match[j0], 10**9, 0
            for j in range(1, n + 1):
                if not used[j]:
                    cur = hops(free_from[i0 - 1], free_to[j - 1]) - u[i0] - v[j]
                    if cur < least[j]:
                        least[j], way[j] = cur, j0
                    if least[j] < delta:
                        delta, j1 = least[j], j
            for j in range(n + 1):
                if used[j]:
                    u[match[j]] += delta
                    v[j] -= delta
                else:
                    least[j] -= delta
            j0 = j1
            if match[j0] == 0:
                break
        while j0:
            j1 = way[j0]
            match[j0] = match[j1]
            j0 = j1
    for j in range(1, n + 1):
        to[free_from[match[j] - 1]] = free_to[j - 1]
    return [(divmod(a, NC), divmod(b, NC)) for a, b in sorted(to.items())]


def send(value, pairs):
    return lax.ppermute(value, ("row", "col"), [(a * NC + b, c * NC + d) for (a, b), (c, d) in complete(pairs)])


def send_only(value, pairs):
    return lax.ppermute(value, ("row", "col"), [(a * NC + b, c * NC + d) for (a, b), (c, d) in pairs])


def dot(a, b):
    return jnp.dot(a, b, preferred_element_type=jnp.float32)


def low(a):
    return a.astype(jnp.bfloat16)


def at(device):
    return (lax.axis_index("row") == device[0]) & (lax.axis_index("col") == device[1])


def any_of(devices):
    flag = at(devices[0])
    for d in devices[1:]:
        flag = flag | at(d)
    return flag


def call(kernel, outs, ins, in_specs, out_specs, scratch=(), limit=16):
    return pl.pallas_call(
        kernel,
        out_shape=outs,
        in_specs=in_specs,
        out_specs=out_specs,
        scratch_shapes=list(scratch),
        compiler_params=pltpu.CompilerParams(vmem_limit_bytes=limit << 20),
        name=kernel.func.__name__ if isinstance(kernel, functools.partial) else kernel.__name__,
    )(*ins)


def pair_width(m, part):
    return 2 * (m + 1) * part


def cut_kernel(diag_ref, *refs):
    cuts, sem = refs[:-1], refs[-1]
    row, col = lax.axis_index("row"), lax.axis_index("col")
    part = diag_ref.shape[1]
    k = jnp.int32(0)
    for r in range(NR):
        for c in range(NC):
            k = jnp.where((row == r) & (col == c), SENDS[r][c], k)
    for m in range(NR // 2):

        @pl.when(jnp.where((row == 1) & (k == 0), 1, row // 2) == m)
        def _():
            copy = pltpu.make_async_copy(diag_ref.at[k, :, pl.ds(0, pair_width(m, part))], cuts[m], sem)
            copy.start()
            copy.wait()


def first_kernel(rhs_ref, diag_ref, *refs):
    parts, (out_ref, rhs_v, d_v, rhs_sem, d_sem) = refs[:-5], refs[-5:]
    n = out_ref.shape[0] // 2
    col = lax.axis_index("col")

    @pl.when(lax.axis_index("row") == 0)
    def _():
        rhs_copy = pltpu.make_async_copy(rhs_ref.at[0], rhs_v, rhs_sem)
        rhs_copy.start()

        def pieces(c):
            copies = []
            for i, r in enumerate(PIECES[c]):
                m = max(r // 2, 1)
                wide = pair_width(m, n)
                source = parts[m - 1] if r else diag_ref.at[0, :, pl.ds(0, wide)]
                copies.append(pltpu.make_async_copy(source, d_v.at[i, :, pl.ds(0, wide)], d_sem.at[i]))
            return copies

        for c in range(NC):

            @pl.when(col == c)
            def _():
                for copy in pieces(c):
                    copy.start()

        rhs_copy.wait()
        p = low(rhs_v[...])
        for c in range(NC):

            @pl.when(col == c)
            def _():
                for i, copy in enumerate(pieces(c)):
                    copy.wait()
                    wide = pair_width(max(PIECES[c][i] // 2, 1), n)
                    out_ref[i * n : (i + 1) * n] = low(dot(d_v[i, :, :wide], p[:wide]))


def pack_kernel(*refs):
    parts, out_ref, sem = refs[:-2], refs[-2], refs[-1]

    @pl.when(any_of(PARTNER[1:]))
    def _():
        copies, left = [], 0
        for m, source in enumerate(parts):
            wide = source.shape[1]
            copies.append(pltpu.make_async_copy(source, out_ref.at[:, pl.ds(left, wide)], sem.at[m]))
            left += wide
        for copy in copies:
            copy.start()
        for copy in copies:
            copy.wait()


def whole_kernel(rows_ref, counts_ref, diag_ref, even_ref, *refs):
    odd, (out_ref, tail_ref, sem) = refs[:-3], refs[-3:]
    size = out_ref.shape[0]
    part = size // NR
    row, col = lax.axis_index("row"), lax.axis_index("col")
    listed = rows_ref[0, 0, 0, 0]
    there = (row >= NC) & (counts_ref[0, 0, 0] > 0)
    done = at(FIRST) | at(MAKER[1]) | at(BESIDE) | at(MAKER[2])
    first = (there & (listed == 0)) | done
    second = there & (listed == 1)
    ids = lax.broadcasted_iota(jnp.int32, tail_ref.shape, 0)
    flag = ((ids == 0) & first) | ((ids == 1) & second)
    tail_ref[...] = low(jnp.where(flag, 1.0, 0.0))

    @pl.when(any_of(MAKER[1:]))
    def _():
        def copy(i, source):
            wide = pair_width(i // 2, part)
            return pltpu.make_async_copy(source, out_ref.at[pl.ds(i * part, part), pl.ds(0, wide)], sem.at[i])

        left = 0
        for i in range(NR):
            wide = pair_width(i // 2, part)
            if i % 2:
                source = odd[i // 2]
            else:
                source = even_ref.at[:, pl.ds(left, wide)]
                left += wide

            @pl.when(row == i)
            def _():
                copy(i, diag_ref.at[col, :, pl.ds(0, wide)]).start()

            @pl.when(row != i)
            def _():
                copy(i, source).start()

        for m in range(NR // 2 - 1):
            right = pair_width(m, part)
            out_ref[pl.ds(2 * m * part, 2 * part), pl.ds(right, size - right)] = jnp.zeros(
                (2 * part, size - right), out_ref.dtype
            )
        for i in range(NR):
            copy(i, odd[i // 2]).wait()


def lower_dot(q_ref, d_ref, p_ref):
    half = d_ref.shape[0] // 2
    q_ref[:half] = low(dot(d_ref[:half, :half], p_ref[:half]))
    q_ref[half:] = low(dot(d_ref[half:], p_ref[...]))


def step0_kernel(g0, g1, g2, g3, rhs_ref, l_ref, p_ref, q_ref, s_ref):
    part = l_ref.shape[0] // NR
    row = lax.axis_index("row")

    def lookup(c, i):
        r = jnp.int32(PIECES[0][i])
        for n in range(1, NC):
            r = jnp.where(c == n, PIECES[n][i], r)
        return pl.multiple_of(r * part, part)

    @pl.when((row >= 1) & (row < 4) & (lax.axis_index("col") == 0))
    def _():
        for j, got in enumerate((g0, g1, g2, g3)):
            src = lax.rem(row + 7 - j, 4)
            q_ref[pl.ds(lookup(src, 0), part)] = got[:part]
            q_ref[pl.ds(lookup(src, 1), part)] = got[part:]
        s = dot(l_ref[...], q_ref[...])
        s_ref[...] = low(s)
        p_ref[...] = low(rhs_ref[0] - s)


def step1_kernel(p_in, d_ref, q_prev, q_ref):
    active = at(MAKER[1])

    @pl.when(active)
    def _():
        lower_dot(q_ref, d_ref, p_in)

    @pl.when(jnp.logical_not(active))
    def _():
        q_ref[...] = q_prev[...]


def step1_sum_kernel(q_in, sum_ref, rhs_ref, l_ref, s_prev, p_ref, s_ref):
    active = at(MAKER[1])

    @pl.when(active)
    def _():
        s = dot(l_ref[...], q_in[...]) + sum_ref[...].astype(jnp.float32)
        s_ref[...] = low(s)
        p_ref[...] = low(rhs_ref[0] - s)

    @pl.when(jnp.logical_not(active))
    def _():
        s_ref[...] = s_prev[...]


def step2_kernel(takers, p_in, q_in, came_ref, sum_ref, rhs_ref, d_ref, l_ref, q_prev, s_prev, a_ref, q_ref, s_ref):
    active, beside, taken = at(MAKER[2]), at(BESIDE), any_of(takers)

    @pl.when(active)
    def _():
        lower_dot(q_ref, d_ref, p_in)
        s_ref[...] = low(dot(l_ref[...], q_ref[...]))

    @pl.when(beside)
    def _():
        q_ref[...] = q_in[...]
        s = dot(l_ref[...], q_in[...]) + sum_ref[...].astype(jnp.float32)
        s_ref[...] = low(s)
        a_ref[...] = low(rhs_ref[0] - s)

    @pl.when(jnp.logical_not(active | beside))
    def _():
        s_ref[...] = s_prev[...]

    @pl.when(taken)
    def _():
        q_ref[...] = came_ref[...]

    @pl.when(jnp.logical_not(active | beside | taken))
    def _():
        q_ref[...] = q_prev[...]


def step3_kernel(takers, a_ref, sum_ref, *refs):
    came, (d_ref, q_prev, q_ref, p_v) = refs[:-4], refs[-4:]
    active = at(MAKER[3])

    @pl.when(active)
    def _():
        p_v[...] = low(a_ref[...].astype(jnp.float32) - sum_ref[...].astype(jnp.float32))
        lower_dot(q_ref, d_ref, p_v)

    for devices, source in zip(takers, came):

        @pl.when(any_of(devices))
        def _():
            q_ref[...] = source[...]

    @pl.when(jnp.logical_not(active | any_of([d for devices in takers for d in devices])))
    def _():
        q_ref[...] = q_prev[...]


def relay_kernel(takers, q_ref, got_ref, out_ref):
    taken = any_of(takers)

    @pl.when(taken)
    def _():
        out_ref[...] = got_ref[...]

    @pl.when(jnp.logical_not(taken))
    def _():
        out_ref[...] = q_ref[...]


def update_kernel(takers, tail_ref, s_ref, l_ref, q_prev, *refs):
    got, q_ref, out_ref = refs[:-2], refs[-2], refs[-1]
    size = l_ref.shape[0]
    row, col = lax.axis_index("row"), lax.axis_index("col")
    below = row >= NC

    def take(flag, source):
        @pl.when(flag)
        def _():
            q_ref[...] = source[...]

    kept = jnp.logical_not(any_of([d for devices in takers for d in devices]))
    take(kept, q_prev)
    for devices, source in zip(takers, got):
        take(any_of(devices), source)

    @pl.when(below)
    def _():
        out_ref[pl.ds(0, size)] = low(dot(l_ref[...], q_ref[...]))

    @pl.when(jnp.logical_not(below))
    def _():
        out_ref[pl.ds(0, size)] = s_ref[...]

    out_ref[pl.ds(size, TAIL)] = tail_ref[...]


def minus(acc, sums, i):
    size = acc.shape[0]
    for s in sums:
        keep = s[pl.ds(size, TAIL)].astype(jnp.float32)[i : i + 1] > 0.5
        acc = acc - jnp.where(keep, s[pl.ds(0, size)].astype(jnp.float32), 0.0)
    return acc


def half_kernel(q_ref, rest_ref, rhs_ref, mine_ref, across_ref, beside_ref, solved_ref, out_ref):
    came = any_of(REST)

    @pl.when(came)
    def _():
        solved_ref[...] = rest_ref[...].astype(jnp.float32)

    @pl.when(jnp.logical_not(came))
    def _():
        solved_ref[...] = q_ref[...].astype(jnp.float32)

    for i in range(out_ref.shape[0]):
        out_ref[i] = minus(rhs_ref[i], (mine_ref, across_ref, beside_ref), i)


def final_kernel(half_ref, corner_ref, out_ref):
    for i in range(out_ref.shape[0]):
        out_ref[i] = minus(half_ref[i], (corner_ref,), i)


def on_device_8x4(rhs, diag_inv, blocks, block_rows, counts):
    size, width = rhs.shape[2:]
    part = size // NR
    rhs = rhs[:, 0]
    block = blocks[0, 0, 0, 0]
    bf16 = jnp.bfloat16
    vec = jax.ShapeDtypeStruct((size, width), bf16)
    dma = pltpu.SemaphoreType.DMA

    wides = [pair_width(m, part) for m in range(NR // 2)]
    cuts = call(
        cut_kernel, [jax.ShapeDtypeStruct((part, w), bf16) for w in wides], [diag_inv], [HBM], [ANY] * len(wides), [dma]
    )
    at_piece = {r: (0, c) for c, rows in enumerate(PIECES) for r in rows}
    parts = []
    for m, cut in enumerate(cuts):
        pairs = []
        for r in range(NR):
            for c, k in enumerate(SENDS[r]):
                if k == 0 and r and max(r // 2, 1) == m:
                    pairs.append(((r, c), at_piece[r]))
                if k and MAKER[k][0] != r and r // 2 == m:
                    pairs.append(((r, c), MAKER[k] if r % 2 else PARTNER[k]))
        parts.append(send_only(cut, pairs))
    q = call(
        first_kernel,
        jax.ShapeDtypeStruct((2 * part, width), bf16),
        [rhs, diag_inv, *parts[1:]],
        [HBM, HBM] + [ANY] * (len(wides) - 1),
        VMEM,
        [
            pltpu.VMEM((size, width), jnp.float32),
            pltpu.VMEM((2, part, size), bf16),
            dma,
            pltpu.SemaphoreType.DMA((2,)),
        ],
    )
    takers = (FIRST, (2, 0), (3, 0))
    got = [send(q, [((0, c), takers[(c + j) % 4]) for c in range(4) if (c + j) % 4 < 3]) for j in range(4)]
    even = call(
        pack_kernel,
        jax.ShapeDtypeStruct((part, sum(wides)), bf16),
        parts,
        [ANY] * len(wides),
        VMEM,
        [pltpu.SemaphoreType.DMA((len(wides),))],
    )
    even = send(even, [(PARTNER[k], MAKER[k]) for k in range(1, NC)])
    diag, tail = call(
        whole_kernel,
        [jax.ShapeDtypeStruct((size, size), bf16), jax.ShapeDtypeStruct((TAIL, width), bf16)],
        [block_rows, counts, diag_inv, even, *parts],
        [SMEM, SMEM, HBM] + [ANY] * (1 + len(wides)),
        [VMEM, VMEM],
        [pltpu.SemaphoreType.DMA((NR,))],
    )

    p, q, s = call(step0_kernel, [vec] * 3, [*got, rhs, block], [VMEM] * 6, [VMEM] * 3)
    p_in = send(p, [(FIRST, MAKER[1])])
    sums = send(s, [((2, 0), MAKER[1]), ((3, 0), BESIDE)])
    q = call(step1_kernel, vec, [p_in, diag, q], [VMEM] * 3, VMEM)
    p, s = call(step1_sum_kernel, [vec] * 2, [q, sums, rhs, block, s], [VMEM] * 5, [VMEM] * 2)
    p_in = send(p, [(MAKER[1], MAKER[2])])
    q_in = send(q, [(MAKER[1], BESIDE)])

    came = send(q, [((2, 0), (4, 0)), ((3, 0), (5, 0)), ((1, 0), (0, 0)), ((2, 1), (4, 1))])
    took = [(4, 0), (5, 0), (0, 0), (4, 1)]
    a, q, s = call(
        functools.partial(step2_kernel, took),
        [vec] * 3,
        [p_in, q_in, came, sums, rhs, diag, block, q, s],
        [VMEM] * 9,
        [VMEM] * 3,
    )
    a = send(a, [(BESIDE, MAKER[3])])
    sums = send(s, [(MAKER[2], MAKER[3])])
    sends = [
        [(MAKER[2], (2, 2))],
        [(MAKER[2], (7, 2)), ((4, 0), (6, 0)), ((5, 0), (7, 0)), ((4, 1), (6, 1)), ((3, 1), (1, 1)), ((2, 1), (0, 1))],
        [(MAKER[2], (5, 2)), ((3, 1), (7, 1)), ((4, 1), (5, 1))],
    ]
    got = [send(q, sends[0])] + [send_only(q, pairs) for pairs in sends[1:]]
    q = call(
        functools.partial(step3_kernel, [[b for _, b in pairs] for pairs in sends]),
        vec,
        [a, sums, *got, diag, q],
        [VMEM] * 7,
        VMEM,
        [pltpu.VMEM((size, width), bf16)],
    )

    sends = [
        [(MAKER[3], (6, 3)), ((2, 2), (4, 2)), ((7, 2), (6, 2))],
        [(MAKER[3], (4, 3)), ((2, 2), (0, 2))],
        [(MAKER[3], (7, 3))],
    ]
    got = [send_only(q, pairs) for pairs in sends]
    above = [(2, 3)]
    came = send_only(q, [(MAKER[3], d) for d in above])
    takers = [[b for _, b in pairs] for pairs in sends]
    q, mine = call(
        functools.partial(update_kernel, takers),
        [vec, jax.ShapeDtypeStruct((size + TAIL, width), bf16)],
        [tail, s, block, q, *got],
        [VMEM] * (4 + len(got)),
        [VMEM] * 2,
    )

    def swap(value, step):
        return send(value, [((r, c), (r, c ^ step)) for r in range(NR) for c in range(NC)])

    across = swap(mine, 2)
    q = call(functools.partial(relay_kernel, above), vec, [q, came], [VMEM] * 2, VMEM)
    rest = send_only(q, list(zip(((2, 3), (6, 3), (7, 3), MAKER[2]), REST)))
    beside = swap(mine, 1)
    across, rest = lax.optimization_barrier((across, rest))
    corner = swap(across, 1)
    whole_rhs = jax.ShapeDtypeStruct(rhs.shape, jnp.float32)
    solved, half = call(
        half_kernel,
        [jax.ShapeDtypeStruct((size, width), jnp.float32), whole_rhs],
        [q, rest, rhs, mine, across, beside],
        [VMEM] * 6,
        [VMEM] * 2,
    )
    remainder = call(final_kernel, whole_rhs, [half, corner], [VMEM] * 2, VMEM)
    return solved[None, None], remainder[:, None]


def solution(mesh):
    in_specs = (
        P(None, "row", None, None),
        P(None, "row", None),
        P(None, "col", "row", None, None, None),
        P(None, "col", "row", None),
        P(None, "col", "row"),
    )
    out_specs = (P(None, "col", None, None), P(None, "row", None, None))
    small = mesh.shape["row"] == NR and mesh.shape["col"] == NC
    return jax.shard_map(
        on_device_8x4 if small else on_device_any,
        mesh=mesh,
        in_specs=in_specs,
        out_specs=out_specs,
        check_vma=False,
    )
```

```python
import functools

import jax
import jax.numpy as jnp
from jax import lax
from jax.experimental import pallas as pl
from jax.experimental.pallas import tpu as pltpu
from jax.sharding import PartitionSpec as P

VMEM = pl.BlockSpec(memory_space=pltpu.VMEM)
ANY = pl.BlockSpec(memory_space=pl.ANY)
HBM = pl.BlockSpec(memory_space=pltpu.HBM)
SMEM = pl.BlockSpec(memory_space=pltpu.SMEM)
TAIL = 16


def broadcast(value, axis, root):
    mine = lax.axis_index(axis) == root
    return lax.psum(jnp.where(mine, value, jnp.zeros_like(value)), axis)


def on_device_any(rhs, diag_inv, blocks, block_rows, counts):
    nrow = lax.axis_size("row")
    ncol = lax.axis_size("col")
    my_row = lax.axis_index("row")
    my_col = lax.axis_index("col")
    kc = diag_inv.shape[0]
    rb_local = rhs.shape[0]
    nz_local = blocks.shape[3]
    local_rhs = rhs[:, 0]
    partial_value = jnp.zeros(local_rhs.shape, jnp.float32)
    solved_list = [jnp.zeros(local_rhs.shape[1:], jnp.float32)]
    slot_ids = jnp.arange(nz_local, dtype=jnp.int32)
    local_ids = jnp.arange(rb_local, dtype=jnp.int32)
    for k in range(kc):
        j = k // ncol
        owner_row = k % nrow
        local_pivot = k // nrow
        mine_row = my_row == owner_row
        mine_col = my_col == k % ncol
        pivot_part = jnp.where(mine_row, partial_value[local_pivot], jnp.float32(0.0))
        summed = lax.psum(pivot_part, "col")
        updated = (local_rhs[local_pivot] - summed).astype(jnp.bfloat16)
        pivot_bf = broadcast(updated, "row", owner_row)
        row_part = jnp.dot(diag_inv[k], pivot_bf, preferred_element_type=jnp.float32)
        sol = lax.all_gather(row_part, "row", axis=0, tiled=True)
        sol_bf = sol.astype(jnp.bfloat16)
        rows = block_rows[j, 0, 0]
        glob = rows * nrow + my_row
        valid = (slot_ids < counts[j, 0, 0]) & (glob > k) & mine_col
        weights = (valid[:, None] & (rows[:, None] == local_ids[None, :])).astype(jnp.float32)
        contrib = jnp.einsum(
            "sab,bn->san", blocks[j, 0, 0], sol_bf, preferred_element_type=jnp.float32
        )
        partial_value = partial_value + jnp.einsum(
            "sl,san->lan", weights, contrib, precision=lax.Precision.HIGHEST
        )
        solved_list[j] = jnp.where(mine_col, sol, solved_list[j])
    total = lax.psum(partial_value, "col")
    remainder = (local_rhs - total)[:, None]
    solved = jnp.stack(solved_list)[:, None]
    return (solved, remainder)


NR, NC = 8, 4
MAKER = (None, (2, 1), (3, 2), (5, 3))
FIRST = (1, 0)
BESIDE = (3, 1)
PARTNER = (None, (3, 1), (3, 3), (5, 2))
PIECES = ((4, 1), (6, 3), (5, 2), (7, 0))
SENDS = (
    (0, 1, 2, 3),
    (0, 1, 2, 3),
    (3, 1, 0, 2),
    (0, 1, 3, 2),
    (0, 1, 3, 2),
    (2, 1, 3, 0),
    (0, 3, 1, 2),
    (1, 3, 0, 2),
)
REST = ((3, 3), (0, 3), (1, 3), (1, 2))


def hops(a, b):
    d = a ^ b
    if d < 2:
        return 1 if d else 10000
    return 100 + abs((a >> 3) - (b >> 3)) + ((d >> 2) & 1) + ((d >> 1) & 1)


def complete(pairs):
    to = {a * NC + b: c * NC + d for (a, b), (c, d) in pairs}
    free_from = [i for i in range(NR * NC) if i not in to]
    free_to = [i for i in range(NR * NC) if i not in to.values()]
    n = len(free_from)
    u, v, match = [0] * (n + 1), [0] * (n + 1), [0] * (n + 1)
    for i in range(1, n + 1):
        match[0], j0 = i, 0
        least, way, used = [10**9] * (n + 1), [0] * (n + 1), [False] * (n + 1)
        while True:
            used[j0] = True
            i0, delta, j1 = match[j0], 10**9, 0
            for j in range(1, n + 1):
                if not used[j]:
                    cur = hops(free_from[i0 - 1], free_to[j - 1]) - u[i0] - v[j]
                    if cur < least[j]:
                        least[j], way[j] = cur, j0
                    if least[j] < delta:
                        delta, j1 = least[j], j
            for j in range(n + 1):
                if used[j]:
                    u[match[j]] += delta
                    v[j] -= delta
                else:
                    least[j] -= delta
            j0 = j1
            if match[j0] == 0:
                break
        while j0:
            j1 = way[j0]
            match[j0] = match[j1]
            j0 = j1
    for j in range(1, n + 1):
        to[free_from[match[j] - 1]] = free_to[j - 1]
    return [(divmod(a, NC), divmod(b, NC)) for a, b in sorted(to.items())]


def send(value, pairs):
    return lax.ppermute(value, ("row", "col"), [(a * NC + b, c * NC + d) for (a, b), (c, d) in complete(pairs)])


def send_only(value, pairs):
    return lax.ppermute(value, ("row", "col"), [(a * NC + b, c * NC + d) for (a, b), (c, d) in pairs])


def dot(a, b):
    return jnp.dot(a, b, preferred_element_type=jnp.float32)


def low(a):
    return a.astype(jnp.bfloat16)


def at(device):
    return (lax.axis_index("row") == device[0]) & (lax.axis_index("col") == device[1])


def any_of(devices):
    flag = at(devices[0])
    for d in devices[1:]:
        flag = flag | at(d)
    return flag


def call(kernel, outs, ins, in_specs, out_specs, scratch=(), limit=16):
    return pl.pallas_call(
        kernel,
        out_shape=outs,
        in_specs=in_specs,
        out_specs=out_specs,
        scratch_shapes=list(scratch),
        compiler_params=pltpu.CompilerParams(vmem_limit_bytes=limit << 20),
        name=kernel.func.__name__ if isinstance(kernel, functools.partial) else kernel.__name__,
    )(*ins)


def pair_width(m, part):
    return 2 * (m + 1) * part


def cut_kernel(diag_ref, *refs):
    cuts, sem = refs[:-1], refs[-1]
    row, col = lax.axis_index("row"), lax.axis_index("col")
    part = diag_ref.shape[1]
    k = jnp.int32(0)
    for r in range(NR):
        for c in range(NC):
            k = jnp.where((row == r) & (col == c), SENDS[r][c], k)
    for m in range(NR // 2):

        @pl.when(jnp.where((row == 1) & (k == 0), 1, row // 2) == m)
        def _():
            copy = pltpu.make_async_copy(diag_ref.at[k, :, pl.ds(0, pair_width(m, part))], cuts[m], sem)
            copy.start()
            copy.wait()


def first_kernel(rhs_ref, diag_ref, *refs):
    parts, (out_ref, rhs_v, d_v, rhs_sem, d_sem) = refs[:-5], refs[-5:]
    n = out_ref.shape[0] // 2
    col = lax.axis_index("col")

    @pl.when(lax.axis_index("row") == 0)
    def _():
        rhs_copy = pltpu.make_async_copy(rhs_ref.at[0], rhs_v, rhs_sem)
        rhs_copy.start()

        def pieces(c):
            copies = []
            for i, r in enumerate(PIECES[c]):
                m = max(r // 2, 1)
                wide = pair_width(m, n)
                source = parts[m - 1] if r else diag_ref.at[0, :, pl.ds(0, wide)]
                copies.append(pltpu.make_async_copy(source, d_v.at[i, :, pl.ds(0, wide)], d_sem.at[i]))
            return copies

        for c in range(NC):

            @pl.when(col == c)
            def _():
                for copy in pieces(c):
                    copy.start()

        rhs_copy.wait()
        p = low(rhs_v[...])
        for c in range(NC):

            @pl.when(col == c)
            def _():
                for i, copy in enumerate(pieces(c)):
                    copy.wait()
                    wide = pair_width(max(PIECES[c][i] // 2, 1), n)
                    out_ref[i * n : (i + 1) * n] = low(dot(d_v[i, :, :wide], p[:wide]))


def pack_kernel(*refs):
    parts, out_ref, sem = refs[:-2], refs[-2], refs[-1]

    @pl.when(any_of(PARTNER[1:]))
    def _():
        copies, left = [], 0
        for m, source in enumerate(parts):
            wide = source.shape[1]
            copies.append(pltpu.make_async_copy(source, out_ref.at[:, pl.ds(left, wide)], sem.at[m]))
            left += wide
        for copy in copies:
            copy.start()
        for copy in copies:
            copy.wait()


def whole_kernel(rows_ref, counts_ref, diag_ref, even_ref, *refs):
    odd, (out_ref, tail_ref, sem) = refs[:-3], refs[-3:]
    size = out_ref.shape[0]
    part = size // NR
    row, col = lax.axis_index("row"), lax.axis_index("col")
    listed = rows_ref[0, 0, 0, 0]
    there = (row >= NC) & (counts_ref[0, 0, 0] > 0)
    done = at(FIRST) | at(MAKER[1]) | at(BESIDE) | at(MAKER[2])
    first = (there & (listed == 0)) | done
    second = there & (listed == 1)
    ids = lax.broadcasted_iota(jnp.int32, tail_ref.shape, 0)
    flag = ((ids == 0) & first) | ((ids == 1) & second)
    tail_ref[...] = low(jnp.where(flag, 1.0, 0.0))

    @pl.when(any_of(MAKER[1:]))
    def _():
        def copy(i, source):
            wide = pair_width(i // 2, part)
            return pltpu.make_async_copy(source, out_ref.at[pl.ds(i * part, part), pl.ds(0, wide)], sem.at[i])

        left = 0
        for i in range(NR):
            wide = pair_width(i // 2, part)
            if i % 2:
                source = odd[i // 2]
            else:
                source = even_ref.at[:, pl.ds(left, wide)]
                left += wide

            @pl.when(row == i)
            def _():
                copy(i, diag_ref.at[col, :, pl.ds(0, wide)]).start()

            @pl.when(row != i)
            def _():
                copy(i, source).start()

        for m in range(NR // 2 - 1):
            right = pair_width(m, part)
            out_ref[pl.ds(2 * m * part, 2 * part), pl.ds(right, size - right)] = jnp.zeros(
                (2 * part, size - right), out_ref.dtype
            )
        for i in range(NR):
            copy(i, odd[i // 2]).wait()


def lower_dot(q_ref, d_ref, p_ref):
    half = d_ref.shape[0] // 2
    q_ref[:half] = low(dot(d_ref[:half, :half], p_ref[:half]))
    q_ref[half:] = low(dot(d_ref[half:], p_ref[...]))


def step0_kernel(g0, g1, g2, g3, rhs_ref, l_ref, p_ref, q_ref, s_ref):
    part = l_ref.shape[0] // NR
    row = lax.axis_index("row")

    def lookup(c, i):
        r = jnp.int32(PIECES[0][i])
        for n in range(1, NC):
            r = jnp.where(c == n, PIECES[n][i], r)
        return pl.multiple_of(r * part, part)

    @pl.when((row >= 1) & (row < 4) & (lax.axis_index("col") == 0))
    def _():
        for j, got in enumerate((g0, g1, g2, g3)):
            src = lax.rem(row + 7 - j, 4)
            q_ref[pl.ds(lookup(src, 0), part)] = got[:part]
            q_ref[pl.ds(lookup(src, 1), part)] = got[part:]
        s = dot(l_ref[...], q_ref[...])
        s_ref[...] = low(s)
        p_ref[...] = low(rhs_ref[0] - s)


def step1_kernel(p_in, d_ref, q_prev, q_ref):
    active = at(MAKER[1])

    @pl.when(active)
    def _():
        lower_dot(q_ref, d_ref, p_in)

    @pl.when(jnp.logical_not(active))
    def _():
        q_ref[...] = q_prev[...]


def step1_sum_kernel(q_in, sum_ref, rhs_ref, l_ref, s_prev, p_ref, s_ref):
    active = at(MAKER[1])

    @pl.when(active)
    def _():
        s = dot(l_ref[...], q_in[...]) + sum_ref[...].astype(jnp.float32)
        s_ref[...] = low(s)
        p_ref[...] = low(rhs_ref[0] - s)

    @pl.when(jnp.logical_not(active))
    def _():
        s_ref[...] = s_prev[...]


def step2_kernel(takers, p_in, q_in, came_ref, sum_ref, rhs_ref, d_ref, l_ref, q_prev, s_prev, a_ref, q_ref, s_ref):
    active, beside, taken = at(MAKER[2]), at(BESIDE), any_of(takers)

    @pl.when(active)
    def _():
        lower_dot(q_ref, d_ref, p_in)
        s_ref[...] = low(dot(l_ref[...], q_ref[...]))

    @pl.when(beside)
    def _():
        q_ref[...] = q_in[...]
        s = dot(l_ref[...], q_in[...]) + sum_ref[...].astype(jnp.float32)
        s_ref[...] = low(s)
        a_ref[...] = low(rhs_ref[0] - s)

    @pl.when(jnp.logical_not(active | beside))
    def _():
        s_ref[...] = s_prev[...]

    @pl.when(taken)
    def _():
        q_ref[...] = came_ref[...]

    @pl.when(jnp.logical_not(active | beside | taken))
    def _():
        q_ref[...] = q_prev[...]


def step3_kernel(takers, a_ref, sum_ref, *refs):
    came, (d_ref, q_prev, q_ref, p_v) = refs[:-4], refs[-4:]
    active = at(MAKER[3])

    @pl.when(active)
    def _():
        p_v[...] = low(a_ref[...].astype(jnp.float32) - sum_ref[...].astype(jnp.float32))
        lower_dot(q_ref, d_ref, p_v)

    for devices, source in zip(takers, came):

        @pl.when(any_of(devices))
        def _():
            q_ref[...] = source[...]

    @pl.when(jnp.logical_not(active | any_of([d for devices in takers for d in devices])))
    def _():
        q_ref[...] = q_prev[...]


def relay_kernel(takers, q_ref, got_ref, out_ref):
    taken = any_of(takers)

    @pl.when(taken)
    def _():
        out_ref[...] = got_ref[...]

    @pl.when(jnp.logical_not(taken))
    def _():
        out_ref[...] = q_ref[...]


def update_kernel(takers, tail_ref, s_ref, l_ref, q_prev, *refs):
    got, q_ref, out_ref = refs[:-2], refs[-2], refs[-1]
    size = l_ref.shape[0]
    row, col = lax.axis_index("row"), lax.axis_index("col")
    below = row >= NC

    def take(flag, source):
        @pl.when(flag)
        def _():
            q_ref[...] = source[...]

    kept = jnp.logical_not(any_of([d for devices in takers for d in devices]))
    take(kept, q_prev)
    for devices, source in zip(takers, got):
        take(any_of(devices), source)

    @pl.when(below)
    def _():
        out_ref[pl.ds(0, size)] = low(dot(l_ref[...], q_ref[...]))

    @pl.when(jnp.logical_not(below))
    def _():
        out_ref[pl.ds(0, size)] = s_ref[...]

    out_ref[pl.ds(size, TAIL)] = tail_ref[...]


def minus(acc, sums, i):
    size = acc.shape[0]
    for s in sums:
        keep = s[pl.ds(size, TAIL)].astype(jnp.float32)[i : i + 1] > 0.5
        acc = acc - jnp.where(keep, s[pl.ds(0, size)].astype(jnp.float32), 0.0)
    return acc


def half_kernel(q_ref, rest_ref, rhs_ref, mine_ref, across_ref, beside_ref, solved_ref, out_ref):
    came = any_of(REST)

    @pl.when(came)
    def _():
        solved_ref[...] = rest_ref[...].astype(jnp.float32)

    @pl.when(jnp.logical_not(came))
    def _():
        solved_ref[...] = q_ref[...].astype(jnp.float32)

    for i in range(out_ref.shape[0]):
        out_ref[i] = minus(rhs_ref[i], (mine_ref, across_ref, beside_ref), i)


def final_kernel(half_ref, corner_ref, out_ref):
    for i in range(out_ref.shape[0]):
        out_ref[i] = minus(half_ref[i], (corner_ref,), i)


def on_device_8x4(rhs, diag_inv, blocks, block_rows, counts):
    size, width = rhs.shape[2:]
    part = size // NR
    rhs = rhs[:, 0]
    block = blocks[0, 0, 0, 0]
    bf16 = jnp.bfloat16
    vec = jax.ShapeDtypeStruct((size, width), bf16)
    dma = pltpu.SemaphoreType.DMA

    wides = [pair_width(m, part) for m in range(NR // 2)]
    cuts = call(
        cut_kernel, [jax.ShapeDtypeStruct((part, w), bf16) for w in wides], [diag_inv], [HBM], [ANY] * len(wides), [dma]
    )
    at_piece = {r: (0, c) for c, rows in enumerate(PIECES) for r in rows}
    parts = []
    for m, cut in enumerate(cuts):
        pairs = []
        for r in range(NR):
            for c, k in enumerate(SENDS[r]):
                if k == 0 and r and max(r // 2, 1) == m:
                    pairs.append(((r, c), at_piece[r]))
                if k and MAKER[k][0] != r and r // 2 == m:
                    pairs.append(((r, c), MAKER[k] if r % 2 else PARTNER[k]))
        parts.append(send_only(cut, pairs))
    q = call(
        first_kernel,
        jax.ShapeDtypeStruct((2 * part, width), bf16),
        [rhs, diag_inv, *parts[1:]],
        [HBM, HBM] + [ANY] * (len(wides) - 1),
        VMEM,
        [
            pltpu.VMEM((size, width), jnp.float32),
            pltpu.VMEM((2, part, size), bf16),
            dma,
            pltpu.SemaphoreType.DMA((2,)),
        ],
    )
    takers = (FIRST, (2, 0), (3, 0))
    got = [send(q, [((0, c), takers[(c + j) % 4]) for c in range(4) if (c + j) % 4 < 3]) for j in range(4)]
    even = call(
        pack_kernel,
        jax.ShapeDtypeStruct((part, sum(wides)), bf16),
        parts,
        [ANY] * len(wides),
        VMEM,
        [pltpu.SemaphoreType.DMA((len(wides),))],
    )
    even = send(even, [(PARTNER[k], MAKER[k]) for k in range(1, NC)])
    diag, tail = call(
        whole_kernel,
        [jax.ShapeDtypeStruct((size, size), bf16), jax.ShapeDtypeStruct((TAIL, width), bf16)],
        [block_rows, counts, diag_inv, even, *parts],
        [SMEM, SMEM, HBM] + [ANY] * (1 + len(wides)),
        [VMEM, VMEM],
        [pltpu.SemaphoreType.DMA((NR,))],
    )

    p, q, s = call(step0_kernel, [vec] * 3, [*got, rhs, block], [VMEM] * 6, [VMEM] * 3)
    p_in = send(p, [(FIRST, MAKER[1])])
    sums = send(s, [((2, 0), MAKER[1]), ((3, 0), BESIDE)])
    q = call(step1_kernel, vec, [p_in, diag, q], [VMEM] * 3, VMEM)
    p, s = call(step1_sum_kernel, [vec] * 2, [q, sums, rhs, block, s], [VMEM] * 5, [VMEM] * 2)
    p_in = send(p, [(MAKER[1], MAKER[2])])
    q_in = send(q, [(MAKER[1], BESIDE)])

    came = send(q, [((2, 0), (4, 0)), ((3, 0), (5, 0)), ((1, 0), (0, 0)), ((2, 1), (4, 1))])
    took = [(4, 0), (5, 0), (0, 0), (4, 1)]
    a, q, s = call(
        functools.partial(step2_kernel, took),
        [vec] * 3,
        [p_in, q_in, came, sums, rhs, diag, block, q, s],
        [VMEM] * 9,
        [VMEM] * 3,
    )
    a = send(a, [(BESIDE, MAKER[3])])
    sums = send(s, [(MAKER[2], MAKER[3])])
    sends = [
        [(MAKER[2], (2, 2))],
        [(MAKER[2], (7, 2)), ((4, 0), (6, 0)), ((5, 0), (7, 0)), ((4, 1), (6, 1)), ((3, 1), (1, 1)), ((2, 1), (0, 1))],
        [(MAKER[2], (5, 2)), ((3, 1), (7, 1)), ((4, 1), (5, 1))],
    ]
    got = [send(q, sends[0])] + [send_only(q, pairs) for pairs in sends[1:]]
    q = call(
        functools.partial(step3_kernel, [[b for _, b in pairs] for pairs in sends]),
        vec,
        [a, sums, *got, diag, q],
        [VMEM] * 7,
        VMEM,
        [pltpu.VMEM((size, width), bf16)],
    )

    sends = [
        [(MAKER[3], (6, 3)), ((2, 2), (4, 2))],
        [(MAKER[3], (4, 3)), ((2, 2), (6, 2))],
        [(MAKER[3], (7, 3))],
    ]
    got = [send_only(q, pairs) for pairs in sends]
    above = [(2, 3), (0, 2)]
    came = send_only(q, list(zip((MAKER[3], (2, 2)), above)))
    takers = [[b for _, b in pairs] for pairs in sends]
    q, mine = call(
        functools.partial(update_kernel, takers),
        [vec, jax.ShapeDtypeStruct((size + TAIL, width), bf16)],
        [tail, s, block, q, *got],
        [VMEM] * (4 + len(got)),
        [VMEM] * 2,
    )

    def swap(value, step):
        return send(value, [((r, c), (r, c ^ step)) for r in range(NR) for c in range(NC)])

    across = swap(mine, 2)
    q = call(functools.partial(relay_kernel, above), vec, [q, came], [VMEM] * 2, VMEM)
    rest = send_only(q, list(zip(((2, 3), (6, 3), (7, 3), MAKER[2]), REST)))
    beside = swap(mine, 1)
    across, rest = lax.optimization_barrier((across, rest))
    corner = swap(across, 1)
    whole_rhs = jax.ShapeDtypeStruct(rhs.shape, jnp.float32)
    solved, half = call(
        half_kernel,
        [jax.ShapeDtypeStruct((size, width), jnp.float32), whole_rhs],
        [q, rest, rhs, mine, across, beside],
        [VMEM] * 6,
        [VMEM] * 2,
    )
    remainder = call(final_kernel, whole_rhs, [half, corner], [VMEM] * 2, VMEM)
    return solved[None, None], remainder[:, None]


def solution(mesh):
    in_specs = (
        P(None, "row", None, None),
        P(None, "row", None),
        P(None, "col", "row", None, None, None),
        P(None, "col", "row", None),
        P(None, "col", "row"),
    )
    out_specs = (P(None, "col", None, None), P(None, "row", None, None))
    small = mesh.shape["row"] == NR and mesh.shape["col"] == NC
    return jax.shard_map(
        on_device_8x4 if small else on_device_any,
        mesh=mesh,
        in_specs=in_specs,
        out_specs=out_specs,
        check_vma=False,
    )
```

```python
import functools

import jax
import jax.numpy as jnp
from jax import lax
from jax.experimental import pallas as pl
from jax.experimental.pallas import tpu as pltpu
from jax.sharding import PartitionSpec as P

VMEM = pl.BlockSpec(memory_space=pltpu.VMEM)
ANY = pl.BlockSpec(memory_space=pl.ANY)
HBM = pl.BlockSpec(memory_space=pltpu.HBM)
SMEM = pl.BlockSpec(memory_space=pltpu.SMEM)
TAIL = 16


def broadcast(value, axis, root):
    mine = lax.axis_index(axis) == root
    return lax.psum(jnp.where(mine, value, jnp.zeros_like(value)), axis)


def on_device_any(rhs, diag_inv, blocks, block_rows, counts):
    nrow = lax.axis_size("row")
    ncol = lax.axis_size("col")
    my_row = lax.axis_index("row")
    my_col = lax.axis_index("col")
    kc = diag_inv.shape[0]
    rb_local = rhs.shape[0]
    nz_local = blocks.shape[3]
    local_rhs = rhs[:, 0]
    partial_value = jnp.zeros(local_rhs.shape, jnp.float32)
    solved_list = [jnp.zeros(local_rhs.shape[1:], jnp.float32)]
    slot_ids = jnp.arange(nz_local, dtype=jnp.int32)
    local_ids = jnp.arange(rb_local, dtype=jnp.int32)
    for k in range(kc):
        j = k // ncol
        owner_row = k % nrow
        local_pivot = k // nrow
        mine_row = my_row == owner_row
        mine_col = my_col == k % ncol
        pivot_part = jnp.where(mine_row, partial_value[local_pivot], jnp.float32(0.0))
        summed = lax.psum(pivot_part, "col")
        updated = (local_rhs[local_pivot] - summed).astype(jnp.bfloat16)
        pivot_bf = broadcast(updated, "row", owner_row)
        row_part = jnp.dot(diag_inv[k], pivot_bf, preferred_element_type=jnp.float32)
        sol = lax.all_gather(row_part, "row", axis=0, tiled=True)
        sol_bf = sol.astype(jnp.bfloat16)
        rows = block_rows[j, 0, 0]
        glob = rows * nrow + my_row
        valid = (slot_ids < counts[j, 0, 0]) & (glob > k) & mine_col
        weights = (valid[:, None] & (rows[:, None] == local_ids[None, :])).astype(jnp.float32)
        contrib = jnp.einsum(
            "sab,bn->san", blocks[j, 0, 0], sol_bf, preferred_element_type=jnp.float32
        )
        partial_value = partial_value + jnp.einsum(
            "sl,san->lan", weights, contrib, precision=lax.Precision.HIGHEST
        )
        solved_list[j] = jnp.where(mine_col, sol, solved_list[j])
    total = lax.psum(partial_value, "col")
    remainder = (local_rhs - total)[:, None]
    solved = jnp.stack(solved_list)[:, None]
    return (solved, remainder)


NR, NC = 8, 4
MAKER = (None, (2, 1), (3, 2), (5, 3))
FIRST = (1, 0)
BESIDE = (3, 1)
PARTNER = (None, (3, 1), (3, 3), (5, 2))
PIECES = ((4, 1), (6, 3), (5, 2), (7, 0))
SENDS = (
    (0, 1, 2, 3),
    (0, 1, 2, 3),
    (3, 1, 0, 2),
    (0, 1, 3, 2),
    (0, 1, 3, 2),
    (2, 1, 3, 0),
    (0, 3, 1, 2),
    (1, 3, 0, 2),
)
REST = ((3, 3), (0, 3), (1, 3), (1, 2))


def hops(a, b):
    d = a ^ b
    if d < 2:
        return 1 if d else 10000
    return 100 + abs((a >> 3) - (b >> 3)) + ((d >> 2) & 1) + ((d >> 1) & 1)


def complete(pairs):
    to = {a * NC + b: c * NC + d for (a, b), (c, d) in pairs}
    free_from = [i for i in range(NR * NC) if i not in to]
    free_to = [i for i in range(NR * NC) if i not in to.values()]
    n = len(free_from)
    u, v, match = [0] * (n + 1), [0] * (n + 1), [0] * (n + 1)
    for i in range(1, n + 1):
        match[0], j0 = i, 0
        least, way, used = [10**9] * (n + 1), [0] * (n + 1), [False] * (n + 1)
        while True:
            used[j0] = True
            i0, delta, j1 = match[j0], 10**9, 0
            for j in range(1, n + 1):
                if not used[j]:
                    cur = hops(free_from[i0 - 1], free_to[j - 1]) - u[i0] - v[j]
                    if cur < least[j]:
                        least[j], way[j] = cur, j0
                    if least[j] < delta:
                        delta, j1 = least[j], j
            for j in range(n + 1):
                if used[j]:
                    u[match[j]] += delta
                    v[j] -= delta
                else:
                    least[j] -= delta
            j0 = j1
            if match[j0] == 0:
                break
        while j0:
            j1 = way[j0]
            match[j0] = match[j1]
            j0 = j1
    for j in range(1, n + 1):
        to[free_from[match[j] - 1]] = free_to[j - 1]
    return [(divmod(a, NC), divmod(b, NC)) for a, b in sorted(to.items())]


def send(value, pairs):
    return lax.ppermute(value, ("row", "col"), [(a * NC + b, c * NC + d) for (a, b), (c, d) in complete(pairs)])


def send_only(value, pairs):
    return lax.ppermute(value, ("row", "col"), [(a * NC + b, c * NC + d) for (a, b), (c, d) in pairs])


def dot(a, b):
    return jnp.dot(a, b, preferred_element_type=jnp.float32)


def low(a):
    return a.astype(jnp.bfloat16)


def at(device):
    return (lax.axis_index("row") == device[0]) & (lax.axis_index("col") == device[1])


def any_of(devices):
    flag = at(devices[0])
    for d in devices[1:]:
        flag = flag | at(d)
    return flag


def call(kernel, outs, ins, in_specs, out_specs, scratch=(), limit=16):
    return pl.pallas_call(
        kernel,
        out_shape=outs,
        in_specs=in_specs,
        out_specs=out_specs,
        scratch_shapes=list(scratch),
        compiler_params=pltpu.CompilerParams(vmem_limit_bytes=limit << 20),
        name=kernel.func.__name__ if isinstance(kernel, functools.partial) else kernel.__name__,
    )(*ins)


def pair_width(m, part):
    return 2 * (m + 1) * part


def cut_kernel(diag_ref, *refs):
    cuts, sem = refs[:-1], refs[-1]
    row, col = lax.axis_index("row"), lax.axis_index("col")
    part = diag_ref.shape[1]
    k = jnp.int32(0)
    for r in range(NR):
        for c in range(NC):
            k = jnp.where((row == r) & (col == c), SENDS[r][c], k)
    for m in range(NR // 2):

        @pl.when(jnp.where((row == 1) & (k == 0), 1, row // 2) == m)
        def _():
            copy = pltpu.make_async_copy(diag_ref.at[k, :, pl.ds(0, pair_width(m, part))], cuts[m], sem)
            copy.start()
            copy.wait()


def first_kernel(rhs_ref, diag_ref, *refs):
    parts, (out_ref, rhs_v, d_v, rhs_sem, d_sem) = refs[:-5], refs[-5:]
    n = out_ref.shape[0] // 2
    col = lax.axis_index("col")

    @pl.when(lax.axis_index("row") == 0)
    def _():
        rhs_copy = pltpu.make_async_copy(rhs_ref.at[0], rhs_v, rhs_sem)
        rhs_copy.start()

        def pieces(c):
            copies = []
            for i, r in enumerate(PIECES[c]):
                m = max(r // 2, 1)
                wide = pair_width(m, n)
                source = parts[m - 1] if r else diag_ref.at[0, :, pl.ds(0, wide)]
                copies.append(pltpu.make_async_copy(source, d_v.at[i, :, pl.ds(0, wide)], d_sem.at[i]))
            return copies

        for c in range(NC):

            @pl.when(col == c)
            def _():
                for copy in pieces(c):
                    copy.start()

        rhs_copy.wait()
        p = low(rhs_v[...])
        for c in range(NC):

            @pl.when(col == c)
            def _():
                for i, copy in enumerate(pieces(c)):
                    copy.wait()
                    wide = pair_width(max(PIECES[c][i] // 2, 1), n)
                    out_ref[i * n : (i + 1) * n] = low(dot(d_v[i, :, :wide], p[:wide]))


def pack_kernel(*refs):
    parts, out_ref, sem = refs[:-2], refs[-2], refs[-1]

    @pl.when(any_of(PARTNER[1:]))
    def _():
        copies, left = [], 0
        for m, source in enumerate(parts):
            wide = source.shape[1]
            copies.append(pltpu.make_async_copy(source, out_ref.at[:, pl.ds(left, wide)], sem.at[m]))
            left += wide
        for copy in copies:
            copy.start()
        for copy in copies:
            copy.wait()


def whole_kernel(rows_ref, counts_ref, diag_ref, even_ref, *refs):
    odd, (out_ref, tail_ref, sem) = refs[:-3], refs[-3:]
    size = out_ref.shape[0]
    part = size // NR
    row, col = lax.axis_index("row"), lax.axis_index("col")
    listed = rows_ref[0, 0, 0, 0]
    there = (row >= NC) & (counts_ref[0, 0, 0] > 0)
    done = at(FIRST) | at(MAKER[1]) | at(BESIDE) | at(MAKER[2])
    first = (there & (listed == 0)) | done
    second = there & (listed == 1)
    ids = lax.broadcasted_iota(jnp.int32, tail_ref.shape, 0)
    flag = ((ids == 0) & first) | ((ids == 1) & second)
    tail_ref[...] = low(jnp.where(flag, 1.0, 0.0))

    @pl.when(any_of(MAKER[1:]))
    def _():
        def copy(i, source):
            wide = pair_width(i // 2, part)
            return pltpu.make_async_copy(source, out_ref.at[pl.ds(i * part, part), pl.ds(0, wide)], sem.at[i])

        left = 0
        for i in range(NR):
            wide = pair_width(i // 2, part)
            if i % 2:
                source = odd[i // 2]
            else:
                source = even_ref.at[:, pl.ds(left, wide)]
                left += wide

            @pl.when(row == i)
            def _():
                copy(i, diag_ref.at[col, :, pl.ds(0, wide)]).start()

            @pl.when(row != i)
            def _():
                copy(i, source).start()

        for m in range(NR // 2 - 1):
            right = pair_width(m, part)
            out_ref[pl.ds(2 * m * part, 2 * part), pl.ds(right, size - right)] = jnp.zeros(
                (2 * part, size - right), out_ref.dtype
            )
        for i in range(NR):
            copy(i, odd[i // 2]).wait()


def lower_dot(q_ref, d_ref, p_ref):
    half = d_ref.shape[0] // 2
    q_ref[:half] = low(dot(d_ref[:half, :half], p_ref[:half]))
    q_ref[half:] = low(dot(d_ref[half:], p_ref[...]))


def step0_kernel(g0, g1, g2, g3, rhs_ref, l_ref, p_ref, q_ref, s_ref):
    part = l_ref.shape[0] // NR
    row = lax.axis_index("row")

    def lookup(c, i):
        r = jnp.int32(PIECES[0][i])
        for n in range(1, NC):
            r = jnp.where(c == n, PIECES[n][i], r)
        return pl.multiple_of(r * part, part)

    @pl.when((row >= 1) & (row < 4) & (lax.axis_index("col") == 0))
    def _():
        for j, got in enumerate((g0, g1, g2, g3)):
            src = lax.rem(row + 7 - j, 4)
            q_ref[pl.ds(lookup(src, 0), part)] = got[:part]
            q_ref[pl.ds(lookup(src, 1), part)] = got[part:]
        s = dot(l_ref[...], q_ref[...])
        s_ref[...] = low(s)
        p_ref[...] = low(rhs_ref[0] - s)


def step1_kernel(p_in, d_ref, q_prev, q_ref):
    active = at(MAKER[1])

    @pl.when(active)
    def _():
        lower_dot(q_ref, d_ref, p_in)

    @pl.when(jnp.logical_not(active))
    def _():
        q_ref[...] = q_prev[...]


def step1_sum_kernel(q_in, sum_ref, rhs_ref, l_ref, s_prev, p_ref, s_ref):
    active = at(MAKER[1])

    @pl.when(active)
    def _():
        s = dot(l_ref[...], q_in[...]) + sum_ref[...].astype(jnp.float32)
        s_ref[...] = low(s)
        p_ref[...] = low(rhs_ref[0] - s)

    @pl.when(jnp.logical_not(active))
    def _():
        s_ref[...] = s_prev[...]


def step2_kernel(takers, p_in, q_in, came_ref, sum_ref, rhs_ref, d_ref, l_ref, q_prev, s_prev, a_ref, q_ref, s_ref):
    active, beside, taken = at(MAKER[2]), at(BESIDE), any_of(takers)

    @pl.when(active)
    def _():
        lower_dot(q_ref, d_ref, p_in)
        s_ref[...] = low(dot(l_ref[...], q_ref[...]))

    @pl.when(beside)
    def _():
        q_ref[...] = q_in[...]
        s = dot(l_ref[...], q_in[...]) + sum_ref[...].astype(jnp.float32)
        s_ref[...] = low(s)
        a_ref[...] = low(rhs_ref[0] - s)

    @pl.when(jnp.logical_not(active | beside))
    def _():
        s_ref[...] = s_prev[...]

    @pl.when(taken)
    def _():
        q_ref[...] = came_ref[...]

    @pl.when(jnp.logical_not(active | beside | taken))
    def _():
        q_ref[...] = q_prev[...]


def step3_kernel(takers, a_ref, sum_ref, *refs):
    came, (d_ref, q_prev, q_ref, p_v) = refs[:-4], refs[-4:]
    active = at(MAKER[3])

    @pl.when(active)
    def _():
        p_v[...] = low(a_ref[...].astype(jnp.float32) - sum_ref[...].astype(jnp.float32))
        lower_dot(q_ref, d_ref, p_v)

    for devices, source in zip(takers, came):

        @pl.when(any_of(devices))
        def _():
            q_ref[...] = source[...]

    @pl.when(jnp.logical_not(active | any_of([d for devices in takers for d in devices])))
    def _():
        q_ref[...] = q_prev[...]


def relay_kernel(takers, q_ref, got_ref, out_ref):
    taken = any_of(takers)

    @pl.when(taken)
    def _():
        out_ref[...] = got_ref[...]

    @pl.when(jnp.logical_not(taken))
    def _():
        out_ref[...] = q_ref[...]


def update_kernel(takers, tail_ref, s_ref, l_ref, q_prev, *refs):
    got, q_ref, out_ref = refs[:-2], refs[-2], refs[-1]
    size = l_ref.shape[0]
    row, col = lax.axis_index("row"), lax.axis_index("col")
    below = row >= NC

    def take(flag, source):
        @pl.when(flag)
        def _():
            q_ref[...] = source[...]

    kept = jnp.logical_not(any_of([d for devices in takers for d in devices]))
    take(kept, q_prev)
    for devices, source in zip(takers, got):
        take(any_of(devices), source)

    @pl.when(below)
    def _():
        out_ref[pl.ds(0, size)] = low(dot(l_ref[...], q_ref[...]))

    @pl.when(jnp.logical_not(below))
    def _():
        out_ref[pl.ds(0, size)] = s_ref[...]

    out_ref[pl.ds(size, TAIL)] = tail_ref[...]


def minus(acc, sums, i):
    size = acc.shape[0]
    for s in sums:
        keep = s[pl.ds(size, TAIL)].astype(jnp.float32)[i : i + 1] > 0.5
        acc = acc - jnp.where(keep, s[pl.ds(0, size)].astype(jnp.float32), 0.0)
    return acc


def half_kernel(q_ref, rest_ref, rhs_ref, mine_ref, across_ref, beside_ref, solved_ref, out_ref):
    came = any_of(REST)

    @pl.when(came)
    def _():
        solved_ref[...] = rest_ref[...].astype(jnp.float32)

    @pl.when(jnp.logical_not(came))
    def _():
        solved_ref[...] = q_ref[...].astype(jnp.float32)

    for i in range(out_ref.shape[0]):
        out_ref[i] = minus(rhs_ref[i], (mine_ref, across_ref, beside_ref), i)


def final_kernel(half_ref, corner_ref, out_ref):
    for i in range(out_ref.shape[0]):
        out_ref[i] = minus(half_ref[i], (corner_ref,), i)


def on_device_8x4(rhs, diag_inv, blocks, block_rows, counts):
    size, width = rhs.shape[2:]
    part = size // NR
    rhs = rhs[:, 0]
    block = blocks[0, 0, 0, 0]
    bf16 = jnp.bfloat16
    vec = jax.ShapeDtypeStruct((size, width), bf16)
    dma = pltpu.SemaphoreType.DMA

    wides = [pair_width(m, part) for m in range(NR // 2)]
    cuts = call(
        cut_kernel, [jax.ShapeDtypeStruct((part, w), bf16) for w in wides], [diag_inv], [HBM], [ANY] * len(wides), [dma]
    )
    at_piece = {r: (0, c) for c, rows in enumerate(PIECES) for r in rows}
    parts = []
    for m, cut in enumerate(cuts):
        pairs = []
        for r in range(NR):
            for c, k in enumerate(SENDS[r]):
                if k == 0 and r and max(r // 2, 1) == m:
                    pairs.append(((r, c), at_piece[r]))
                if k and MAKER[k][0] != r and r // 2 == m:
                    pairs.append(((r, c), MAKER[k] if r % 2 else PARTNER[k]))
        parts.append(send_only(cut, pairs))
    q = call(
        first_kernel,
        jax.ShapeDtypeStruct((2 * part, width), bf16),
        [rhs, diag_inv, *parts[1:]],
        [HBM, HBM] + [ANY] * (len(wides) - 1),
        VMEM,
        [
            pltpu.VMEM((size, width), jnp.float32),
            pltpu.VMEM((2, part, size), bf16),
            dma,
            pltpu.SemaphoreType.DMA((2,)),
        ],
    )
    takers = (FIRST, (2, 0), (3, 0))
    got = [send(q, [((0, c), takers[(c + j) % 4]) for c in range(4) if (c + j) % 4 < 3]) for j in range(4)]
    even = call(
        pack_kernel,
        jax.ShapeDtypeStruct((part, sum(wides)), bf16),
        parts,
        [ANY] * len(wides),
        VMEM,
        [pltpu.SemaphoreType.DMA((len(wides),))],
    )
    even = send(even, [(PARTNER[k], MAKER[k]) for k in range(1, NC)])
    diag, tail = call(
        whole_kernel,
        [jax.ShapeDtypeStruct((size, size), bf16), jax.ShapeDtypeStruct((TAIL, width), bf16)],
        [block_rows, counts, diag_inv, even, *parts],
        [SMEM, SMEM, HBM] + [ANY] * (1 + len(wides)),
        [VMEM, VMEM],
        [pltpu.SemaphoreType.DMA((NR,))],
    )

    p, q, s = call(step0_kernel, [vec] * 3, [*got, rhs, block], [VMEM] * 6, [VMEM] * 3)
    p_in = send(p, [(FIRST, MAKER[1])])
    sums = send(s, [((2, 0), MAKER[1]), ((3, 0), BESIDE)])
    q = call(step1_kernel, vec, [p_in, diag, q], [VMEM] * 3, VMEM)
    p, s = call(step1_sum_kernel, [vec] * 2, [q, sums, rhs, block, s], [VMEM] * 5, [VMEM] * 2)
    p_in = send(p, [(MAKER[1], MAKER[2])])
    q_in = send(q, [(MAKER[1], BESIDE)])

    came = send(q, [((2, 0), (4, 0)), ((3, 0), (5, 0)), ((1, 0), (0, 0)), ((2, 1), (4, 1))])
    took = [(4, 0), (5, 0), (0, 0), (4, 1)]
    a, q, s = call(
        functools.partial(step2_kernel, took),
        [vec] * 3,
        [p_in, q_in, came, sums, rhs, diag, block, q, s],
        [VMEM] * 9,
        [VMEM] * 3,
    )
    a = send(a, [(BESIDE, MAKER[3])])
    sums = send(s, [(MAKER[2], MAKER[3])])
    sends = [
        [(MAKER[2], (2, 2))],
        [(MAKER[2], (7, 2)), ((4, 0), (6, 0)), ((5, 0), (7, 0)), ((4, 1), (6, 1)), ((3, 1), (1, 1)), ((2, 1), (0, 1))],
        [(MAKER[2], (5, 2)), ((3, 1), (7, 1)), ((4, 1), (5, 1))],
    ]
    got = [send(q, sends[0])] + [send_only(q, pairs) for pairs in sends[1:]]
    q = call(
        functools.partial(step3_kernel, [[b for _, b in pairs] for pairs in sends]),
        vec,
        [a, sums, *got, diag, q],
        [VMEM] * 7,
        VMEM,
        [pltpu.VMEM((size, width), bf16)],
    )

    sends = [
        [(MAKER[3], (6, 3)), ((2, 2), (4, 2))],
        [(MAKER[3], (4, 3)), ((2, 2), (6, 2))],
        [(MAKER[3], (7, 3))],
    ]
    got = [send_only(q, pairs) for pairs in sends]
    above = [(2, 3), (0, 2)]
    came = send_only(q, list(zip((MAKER[3], (2, 2)), above)))
    takers = [[b for _, b in pairs] for pairs in sends]
    q, mine = call(
        functools.partial(update_kernel, takers),
        [vec, jax.ShapeDtypeStruct((size + TAIL, width), bf16)],
        [tail, s, block, q, *got],
        [VMEM] * (4 + len(got)),
        [VMEM] * 2,
    )

    def swap(value, step):
        return send(value, [((r, c), (r, c ^ step)) for r in range(NR) for c in range(NC)])

    across = swap(mine, 2)
    q = call(functools.partial(relay_kernel, above), vec, [q, came], [VMEM] * 2, VMEM)
    rest = send_only(q, list(zip(((2, 3), (4, 3), MAKER[3], MAKER[2]), REST)))
    beside = swap(mine, 1)
    across, rest = lax.optimization_barrier((across, rest))
    corner = swap(across, 1)
    whole_rhs = jax.ShapeDtypeStruct(rhs.shape, jnp.float32)
    solved, half = call(
        half_kernel,
        [jax.ShapeDtypeStruct((size, width), jnp.float32), whole_rhs],
        [q, rest, rhs, mine, across, beside],
        [VMEM] * 6,
        [VMEM] * 2,
    )
    remainder = call(final_kernel, whole_rhs, [half, corner], [VMEM] * 2, VMEM)
    return solved[None, None], remainder[:, None]


def solution(mesh):
    in_specs = (
        P(None, "row", None, None),
        P(None, "row", None),
        P(None, "col", "row", None, None, None),
        P(None, "col", "row", None),
        P(None, "col", "row"),
    )
    out_specs = (P(None, "col", None, None), P(None, "row", None, None))
    small = mesh.shape["row"] == NR and mesh.shape["col"] == NC
    return jax.shard_map(
        on_device_8x4 if small else on_device_any,
        mesh=mesh,
        in_specs=in_specs,
        out_specs=out_specs,
        check_vma=False,
    )
```

```python
import functools

import jax
import jax.numpy as jnp
from jax import lax
from jax.experimental import pallas as pl
from jax.experimental.pallas import tpu as pltpu
from jax.sharding import PartitionSpec as P

VMEM = pl.BlockSpec(memory_space=pltpu.VMEM)
ANY = pl.BlockSpec(memory_space=pl.ANY)
HBM = pl.BlockSpec(memory_space=pltpu.HBM)
SMEM = pl.BlockSpec(memory_space=pltpu.SMEM)
TAIL = 16


def broadcast(value, axis, root):
    mine = lax.axis_index(axis) == root
    return lax.psum(jnp.where(mine, value, jnp.zeros_like(value)), axis)


def on_device_any(rhs, diag_inv, blocks, block_rows, counts):
    nrow = lax.axis_size("row")
    ncol = lax.axis_size("col")
    my_row = lax.axis_index("row")
    my_col = lax.axis_index("col")
    kc = diag_inv.shape[0]
    rb_local = rhs.shape[0]
    nz_local = blocks.shape[3]
    local_rhs = rhs[:, 0]
    partial_value = jnp.zeros(local_rhs.shape, jnp.float32)
    solved_list = [jnp.zeros(local_rhs.shape[1:], jnp.float32)]
    slot_ids = jnp.arange(nz_local, dtype=jnp.int32)
    local_ids = jnp.arange(rb_local, dtype=jnp.int32)
    for k in range(kc):
        j = k // ncol
        owner_row = k % nrow
        local_pivot = k // nrow
        mine_row = my_row == owner_row
        mine_col = my_col == k % ncol
        pivot_part = jnp.where(mine_row, partial_value[local_pivot], jnp.float32(0.0))
        summed = lax.psum(pivot_part, "col")
        updated = (local_rhs[local_pivot] - summed).astype(jnp.bfloat16)
        pivot_bf = broadcast(updated, "row", owner_row)
        row_part = jnp.dot(diag_inv[k], pivot_bf, preferred_element_type=jnp.float32)
        sol = lax.all_gather(row_part, "row", axis=0, tiled=True)
        sol_bf = sol.astype(jnp.bfloat16)
        rows = block_rows[j, 0, 0]
        glob = rows * nrow + my_row
        valid = (slot_ids < counts[j, 0, 0]) & (glob > k) & mine_col
        weights = (valid[:, None] & (rows[:, None] == local_ids[None, :])).astype(jnp.float32)
        contrib = jnp.einsum(
            "sab,bn->san", blocks[j, 0, 0], sol_bf, preferred_element_type=jnp.float32
        )
        partial_value = partial_value + jnp.einsum(
            "sl,san->lan", weights, contrib, precision=lax.Precision.HIGHEST
        )
        solved_list[j] = jnp.where(mine_col, sol, solved_list[j])
    total = lax.psum(partial_value, "col")
    remainder = (local_rhs - total)[:, None]
    solved = jnp.stack(solved_list)[:, None]
    return (solved, remainder)


NR, NC = 8, 4
MAKER = (None, (2, 1), (3, 2), (5, 3))
FIRST = (1, 0)
BESIDE = (3, 1)
PARTNER = (None, (3, 1), (3, 3), (5, 2))
PIECES = ((4, 1), (6, 3), (5, 2), (7, 0))
SENDS = (
    (0, 1, 2, 3),
    (0, 1, 2, 3),
    (3, 1, 0, 2),
    (0, 1, 3, 2),
    (0, 1, 3, 2),
    (2, 1, 3, 0),
    (0, 3, 1, 2),
    (1, 3, 0, 2),
)
REST = ((3, 3), (0, 3), (1, 3), (1, 2))


def hops(a, b):
    d = a ^ b
    if d < 2:
        return 1 if d else 10000
    return 100 + abs((a >> 3) - (b >> 3)) + ((d >> 2) & 1) + ((d >> 1) & 1)


def complete(pairs):
    to = {a * NC + b: c * NC + d for (a, b), (c, d) in pairs}
    free_from = [i for i in range(NR * NC) if i not in to]
    free_to = [i for i in range(NR * NC) if i not in to.values()]
    n = len(free_from)
    u, v, match = [0] * (n + 1), [0] * (n + 1), [0] * (n + 1)
    for i in range(1, n + 1):
        match[0], j0 = i, 0
        least, way, used = [10**9] * (n + 1), [0] * (n + 1), [False] * (n + 1)
        while True:
            used[j0] = True
            i0, delta, j1 = match[j0], 10**9, 0
            for j in range(1, n + 1):
                if not used[j]:
                    cur = hops(free_from[i0 - 1], free_to[j - 1]) - u[i0] - v[j]
                    if cur < least[j]:
                        least[j], way[j] = cur, j0
                    if least[j] < delta:
                        delta, j1 = least[j], j
            for j in range(n + 1):
                if used[j]:
                    u[match[j]] += delta
                    v[j] -= delta
                else:
                    least[j] -= delta
            j0 = j1
            if match[j0] == 0:
                break
        while j0:
            j1 = way[j0]
            match[j0] = match[j1]
            j0 = j1
    for j in range(1, n + 1):
        to[free_from[match[j] - 1]] = free_to[j - 1]
    return [(divmod(a, NC), divmod(b, NC)) for a, b in sorted(to.items())]


def send(value, pairs):
    return lax.ppermute(value, ("row", "col"), [(a * NC + b, c * NC + d) for (a, b), (c, d) in complete(pairs)])


def send_only(value, pairs):
    return lax.ppermute(value, ("row", "col"), [(a * NC + b, c * NC + d) for (a, b), (c, d) in pairs])


def dot(a, b):
    return jnp.dot(a, b, preferred_element_type=jnp.float32)


def low(a):
    return a.astype(jnp.bfloat16)


def at(device):
    return (lax.axis_index("row") == device[0]) & (lax.axis_index("col") == device[1])


def any_of(devices):
    flag = at(devices[0])
    for d in devices[1:]:
        flag = flag | at(d)
    return flag


def call(kernel, outs, ins, in_specs, out_specs, scratch=(), limit=16):
    return pl.pallas_call(
        kernel,
        out_shape=outs,
        in_specs=in_specs,
        out_specs=out_specs,
        scratch_shapes=list(scratch),
        compiler_params=pltpu.CompilerParams(vmem_limit_bytes=limit << 20),
        name=kernel.func.__name__ if isinstance(kernel, functools.partial) else kernel.__name__,
    )(*ins)


def pair_width(m, part):
    return 2 * (m + 1) * part


def cut_kernel(diag_ref, *refs):
    cuts, sem = refs[:-1], refs[-1]
    row, col = lax.axis_index("row"), lax.axis_index("col")
    part = diag_ref.shape[1]
    k = jnp.int32(0)
    for r in range(NR):
        for c in range(NC):
            k = jnp.where((row == r) & (col == c), SENDS[r][c], k)
    for m in range(NR // 2):

        @pl.when(jnp.where((row == 1) & (k == 0), 1, row // 2) == m)
        def _():
            copy = pltpu.make_async_copy(diag_ref.at[k, :, pl.ds(0, pair_width(m, part))], cuts[m], sem)
            copy.start()
            copy.wait()


def first_kernel(rhs_ref, diag_ref, *refs):
    parts, (out_ref, rhs_v, d_v, rhs_sem, d_sem) = refs[:-5], refs[-5:]
    n = out_ref.shape[0] // 2
    col = lax.axis_index("col")

    @pl.when(lax.axis_index("row") == 0)
    def _():
        rhs_copy = pltpu.make_async_copy(rhs_ref.at[0], rhs_v, rhs_sem)
        rhs_copy.start()

        def pieces(c):
            copies = []
            for i, r in enumerate(PIECES[c]):
                m = max(r // 2, 1)
                wide = pair_width(m, n)
                source = parts[m - 1] if r else diag_ref.at[0, :, pl.ds(0, wide)]
                copies.append(pltpu.make_async_copy(source, d_v.at[i, :, pl.ds(0, wide)], d_sem.at[i]))
            return copies

        for c in range(NC):

            @pl.when(col == c)
            def _():
                for copy in pieces(c):
                    copy.start()

        rhs_copy.wait()
        p = low(rhs_v[...])
        for c in range(NC):

            @pl.when(col == c)
            def _():
                for i, copy in enumerate(pieces(c)):
                    copy.wait()
                    wide = pair_width(max(PIECES[c][i] // 2, 1), n)
                    out_ref[i * n : (i + 1) * n] = low(dot(d_v[i, :, :wide], p[:wide]))


def pack_kernel(*refs):
    parts, out_ref, sem = refs[:-2], refs[-2], refs[-1]

    @pl.when(any_of(PARTNER[1:]))
    def _():
        copies, left = [], 0
        for m, source in enumerate(parts):
            wide = source.shape[1]
            copies.append(pltpu.make_async_copy(source, out_ref.at[:, pl.ds(left, wide)], sem.at[m]))
            left += wide
        for copy in copies:
            copy.start()
        for copy in copies:
            copy.wait()


def whole_kernel(rows_ref, counts_ref, diag_ref, even_ref, *refs):
    odd, (out_ref, tail_ref, sem) = refs[:-3], refs[-3:]
    size = out_ref.shape[0]
    part = size // NR
    row, col = lax.axis_index("row"), lax.axis_index("col")
    listed = rows_ref[0, 0, 0, 0]
    there = (row >= NC) & (counts_ref[0, 0, 0] > 0)
    done = at(FIRST) | at(MAKER[1]) | at(BESIDE) | at(MAKER[2])
    first = (there & (listed == 0)) | done
    second = there & (listed == 1)
    ids = lax.broadcasted_iota(jnp.int32, tail_ref.shape, 0)
    flag = ((ids == 0) & first) | ((ids == 1) & second)
    tail_ref[...] = low(jnp.where(flag, 1.0, 0.0))

    @pl.when(any_of(MAKER[1:]))
    def _():
        def copy(i, source):
            wide = pair_width(i // 2, part)
            return pltpu.make_async_copy(source, out_ref.at[pl.ds(i * part, part), pl.ds(0, wide)], sem.at[i])

        left = 0
        for i in range(NR):
            wide = pair_width(i // 2, part)
            if i % 2:
                source = odd[i // 2]
            else:
                source = even_ref.at[:, pl.ds(left, wide)]
                left += wide

            @pl.when(row == i)
            def _():
                copy(i, diag_ref.at[col, :, pl.ds(0, wide)]).start()

            @pl.when(row != i)
            def _():
                copy(i, source).start()

        for m in range(NR // 2 - 1):
            right = pair_width(m, part)
            out_ref[pl.ds(2 * m * part, 2 * part), pl.ds(right, size - right)] = jnp.zeros(
                (2 * part, size - right), out_ref.dtype
            )
        for i in range(NR):
            copy(i, odd[i // 2]).wait()


def lower_dot(q_ref, d_ref, p_ref):
    half = d_ref.shape[0] // 2
    q_ref[:half] = low(dot(d_ref[:half, :half], p_ref[:half]))
    q_ref[half:] = low(dot(d_ref[half:], p_ref[...]))


def step0_kernel(g0, g1, g2, g3, rhs_ref, l_ref, p_ref, q_ref, s_ref):
    part = l_ref.shape[0] // NR
    row = lax.axis_index("row")

    def lookup(c, i):
        r = jnp.int32(PIECES[0][i])
        for n in range(1, NC):
            r = jnp.where(c == n, PIECES[n][i], r)
        return pl.multiple_of(r * part, part)

    @pl.when((row >= 1) & (row < 4) & (lax.axis_index("col") == 0))
    def _():
        for j, got in enumerate((g0, g1, g2, g3)):
            src = lax.rem(row + 7 - j, 4)
            q_ref[pl.ds(lookup(src, 0), part)] = got[:part]
            q_ref[pl.ds(lookup(src, 1), part)] = got[part:]
        s = dot(l_ref[...], q_ref[...])
        s_ref[...] = low(s)
        p_ref[...] = low(rhs_ref[0] - s)


def step1_kernel(p_in, d_ref, q_prev, q_ref):
    active = at(MAKER[1])

    @pl.when(active)
    def _():
        lower_dot(q_ref, d_ref, p_in)

    @pl.when(jnp.logical_not(active))
    def _():
        q_ref[...] = q_prev[...]


def step1_sum_kernel(q_in, sum_ref, rhs_ref, l_ref, s_prev, p_ref, s_ref):
    active = at(MAKER[1])

    @pl.when(active)
    def _():
        s = dot(l_ref[...], q_in[...]) + sum_ref[...].astype(jnp.float32)
        s_ref[...] = low(s)
        p_ref[...] = low(rhs_ref[0] - s)

    @pl.when(jnp.logical_not(active))
    def _():
        s_ref[...] = s_prev[...]


def step2_kernel(takers, p_in, q_in, came_ref, sum_ref, rhs_ref, d_ref, l_ref, q_prev, s_prev, a_ref, q_ref, s_ref):
    active, beside, taken = at(MAKER[2]), at(BESIDE), any_of(takers)

    @pl.when(active)
    def _():
        lower_dot(q_ref, d_ref, p_in)
        s_ref[...] = low(dot(l_ref[...], q_ref[...]))

    @pl.when(beside)
    def _():
        q_ref[...] = q_in[...]
        s = dot(l_ref[...], q_in[...]) + sum_ref[...].astype(jnp.float32)
        s_ref[...] = low(s)
        a_ref[...] = low(rhs_ref[0] - s)

    @pl.when(jnp.logical_not(active | beside))
    def _():
        s_ref[...] = s_prev[...]

    @pl.when(taken)
    def _():
        q_ref[...] = came_ref[...]

    @pl.when(jnp.logical_not(active | beside | taken))
    def _():
        q_ref[...] = q_prev[...]


def step3_kernel(takers, a_ref, sum_ref, *refs):
    came, (d_ref, q_prev, q_ref, p_v) = refs[:-4], refs[-4:]
    active = at(MAKER[3])

    @pl.when(active)
    def _():
        p_v[...] = low(a_ref[...].astype(jnp.float32) - sum_ref[...].astype(jnp.float32))
        lower_dot(q_ref, d_ref, p_v)

    for devices, source in zip(takers, came):

        @pl.when(any_of(devices))
        def _():
            q_ref[...] = source[...]

    @pl.when(jnp.logical_not(active | any_of([d for devices in takers for d in devices])))
    def _():
        q_ref[...] = q_prev[...]


def relay_kernel(takers, q_ref, got_ref, out_ref):
    taken = any_of(takers)

    @pl.when(taken)
    def _():
        out_ref[...] = got_ref[...]

    @pl.when(jnp.logical_not(taken))
    def _():
        out_ref[...] = q_ref[...]


def update_kernel(takers, tail_ref, s_ref, l_ref, q_prev, *refs):
    got, q_ref, out_ref = refs[:-2], refs[-2], refs[-1]
    size = l_ref.shape[0]
    row, col = lax.axis_index("row"), lax.axis_index("col")
    below = row >= NC

    def take(flag, source):
        @pl.when(flag)
        def _():
            q_ref[...] = source[...]

    kept = jnp.logical_not(any_of([d for devices in takers for d in devices]))
    take(kept, q_prev)
    for devices, source in zip(takers, got):
        take(any_of(devices), source)

    @pl.when(below)
    def _():
        out_ref[pl.ds(0, size)] = low(dot(l_ref[...], q_ref[...]))

    @pl.when(jnp.logical_not(below))
    def _():
        out_ref[pl.ds(0, size)] = s_ref[...]

    out_ref[pl.ds(size, TAIL)] = tail_ref[...]


def minus(acc, sums, i):
    size = acc.shape[0]
    for s in sums:
        keep = s[pl.ds(size, TAIL)].astype(jnp.float32)[i : i + 1] > 0.5
        acc = acc - jnp.where(keep, s[pl.ds(0, size)].astype(jnp.float32), 0.0)
    return acc


def half_kernel(q_ref, rest_ref, rhs_ref, mine_ref, across_ref, beside_ref, solved_ref, out_ref):
    came = any_of(REST)

    @pl.when(came)
    def _():
        solved_ref[...] = rest_ref[...].astype(jnp.float32)

    @pl.when(jnp.logical_not(came))
    def _():
        solved_ref[...] = q_ref[...].astype(jnp.float32)

    for i in range(out_ref.shape[0]):
        out_ref[i] = minus(rhs_ref[i], (mine_ref, across_ref, beside_ref), i)


def final_kernel(half_ref, corner_ref, out_ref):
    for i in range(out_ref.shape[0]):
        out_ref[i] = minus(half_ref[i], (corner_ref,), i)


def on_device_8x4(rhs, diag_inv, blocks, block_rows, counts):
    size, width = rhs.shape[2:]
    part = size // NR
    rhs = rhs[:, 0]
    block = blocks[0, 0, 0, 0]
    bf16 = jnp.bfloat16
    vec = jax.ShapeDtypeStruct((size, width), bf16)
    dma = pltpu.SemaphoreType.DMA

    wides = [pair_width(m, part) for m in range(NR // 2)]
    cuts = call(
        cut_kernel, [jax.ShapeDtypeStruct((part, w), bf16) for w in wides], [diag_inv], [HBM], [ANY] * len(wides), [dma]
    )
    at_piece = {r: (0, c) for c, rows in enumerate(PIECES) for r in rows}
    parts = []
    for m, cut in enumerate(cuts):
        pairs = []
        for r in range(NR):
            for c, k in enumerate(SENDS[r]):
                if k == 0 and r and max(r // 2, 1) == m:
                    pairs.append(((r, c), at_piece[r]))
                if k and MAKER[k][0] != r and r // 2 == m:
                    pairs.append(((r, c), MAKER[k] if r % 2 else PARTNER[k]))
        parts.append(send_only(cut, pairs))
    q = call(
        first_kernel,
        jax.ShapeDtypeStruct((2 * part, width), bf16),
        [rhs, diag_inv, *parts[1:]],
        [HBM, HBM] + [ANY] * (len(wides) - 1),
        VMEM,
        [
            pltpu.VMEM((size, width), jnp.float32),
            pltpu.VMEM((2, part, size), bf16),
            dma,
            pltpu.SemaphoreType.DMA((2,)),
        ],
    )
    takers = (FIRST, (2, 0), (3, 0))
    got = [send(q, [((0, c), takers[(c + j) % 4]) for c in range(4) if (c + j) % 4 < 3]) for j in range(4)]
    even = call(
        pack_kernel,
        jax.ShapeDtypeStruct((part, sum(wides)), bf16),
        parts,
        [ANY] * len(wides),
        VMEM,
        [pltpu.SemaphoreType.DMA((len(wides),))],
    )
    even = send(even, [(PARTNER[k], MAKER[k]) for k in range(1, NC)])
    diag, tail = call(
        whole_kernel,
        [jax.ShapeDtypeStruct((size, size), bf16), jax.ShapeDtypeStruct((TAIL, width), bf16)],
        [block_rows, counts, diag_inv, even, *parts],
        [SMEM, SMEM, HBM] + [ANY] * (1 + len(wides)),
        [VMEM, VMEM],
        [pltpu.SemaphoreType.DMA((NR,))],
    )

    p, q, s = call(step0_kernel, [vec] * 3, [*got, rhs, block], [VMEM] * 6, [VMEM] * 3)
    p_in = send(p, [(FIRST, MAKER[1])])
    sums = send(s, [((2, 0), MAKER[1]), ((3, 0), BESIDE)])
    q = call(step1_kernel, vec, [p_in, diag, q], [VMEM] * 3, VMEM)
    p, s = call(step1_sum_kernel, [vec] * 2, [q, sums, rhs, block, s], [VMEM] * 5, [VMEM] * 2)
    p_in = send(p, [(MAKER[1], MAKER[2])])
    q_in = send(q, [(MAKER[1], BESIDE)])

    came = send(q, [((2, 0), (4, 0)), ((3, 0), (5, 0)), ((1, 0), (0, 0)), ((2, 1), (4, 1))])
    took = [(4, 0), (5, 0), (0, 0), (4, 1)]
    a, q, s = call(
        functools.partial(step2_kernel, took),
        [vec] * 3,
        [p_in, q_in, came, sums, rhs, diag, block, q, s],
        [VMEM] * 9,
        [VMEM] * 3,
    )
    a = send(a, [(BESIDE, MAKER[3])])
    sums = send(s, [(MAKER[2], MAKER[3])])
    sends = [
        [(MAKER[2], (2, 2))],
        [(MAKER[2], (7, 2)), ((4, 0), (6, 0)), ((5, 0), (7, 0)), ((4, 1), (6, 1)), ((3, 1), (1, 1)), ((2, 1), (0, 1))],
        [(MAKER[2], (5, 2)), ((3, 1), (7, 1)), ((4, 1), (5, 1))],
    ]
    got = [send(q, sends[0])] + [send_only(q, pairs) for pairs in sends[1:]]
    q = call(
        functools.partial(step3_kernel, [[b for _, b in pairs] for pairs in sends]),
        vec,
        [a, sums, *got, diag, q],
        [VMEM] * 7,
        VMEM,
        [pltpu.VMEM((size, width), bf16)],
    )

    sends = [
        [(MAKER[3], (6, 3)), ((2, 2), (4, 2))],
        [(MAKER[3], (4, 3)), ((2, 2), (6, 2))],
        [(MAKER[3], (7, 3))],
    ]
    got = [send_only(q, pairs) for pairs in sends]
    above = [(2, 3), (0, 2)]
    came = send_only(q, list(zip((MAKER[3], (2, 2)), above)))
    takers = [[b for _, b in pairs] for pairs in sends]
    q, mine = call(
        functools.partial(update_kernel, takers),
        [vec, jax.ShapeDtypeStruct((size + TAIL, width), bf16)],
        [tail, s, block, q, *got],
        [VMEM] * (4 + len(got)),
        [VMEM] * 2,
    )

    def swap(value, step):
        return send(value, [((r, c), (r, c ^ step)) for r in range(NR) for c in range(NC)])

    across = swap(mine, 2)
    q = call(functools.partial(relay_kernel, above), vec, [q, came], [VMEM] * 2, VMEM)
    rest = send_only(q, list(zip(((2, 3), (4, 3), (7, 3), MAKER[2]), REST)))
    beside = swap(mine, 1)
    across, rest = lax.optimization_barrier((across, rest))
    corner = swap(across, 1)
    whole_rhs = jax.ShapeDtypeStruct(rhs.shape, jnp.float32)
    solved, half = call(
        half_kernel,
        [jax.ShapeDtypeStruct((size, width), jnp.float32), whole_rhs],
        [q, rest, rhs, mine, across, beside],
        [VMEM] * 6,
        [VMEM] * 2,
    )
    remainder = call(final_kernel, whole_rhs, [half, corner], [VMEM] * 2, VMEM)
    return solved[None, None], remainder[:, None]


def solution(mesh):
    in_specs = (
        P(None, "row", None, None),
        P(None, "row", None),
        P(None, "col", "row", None, None, None),
        P(None, "col", "row", None),
        P(None, "col", "row"),
    )
    out_specs = (P(None, "col", None, None), P(None, "row", None, None))
    small = mesh.shape["row"] == NR and mesh.shape["col"] == NC
    return jax.shard_map(
        on_device_8x4 if small else on_device_any,
        mesh=mesh,
        in_specs=in_specs,
        out_specs=out_specs,
        check_vma=False,
    )
```

```python
import functools

import jax
import jax.numpy as jnp
from jax import lax
from jax.experimental import pallas as pl
from jax.experimental.pallas import tpu as pltpu
from jax.sharding import PartitionSpec as P

VMEM = pl.BlockSpec(memory_space=pltpu.VMEM)
ANY = pl.BlockSpec(memory_space=pl.ANY)
HBM = pl.BlockSpec(memory_space=pltpu.HBM)
SMEM = pl.BlockSpec(memory_space=pltpu.SMEM)
TAIL = 16


def broadcast(value, axis, root):
    mine = lax.axis_index(axis) == root
    return lax.psum(jnp.where(mine, value, jnp.zeros_like(value)), axis)


def on_device_any(rhs, diag_inv, blocks, block_rows, counts):
    nrow = lax.axis_size("row")
    ncol = lax.axis_size("col")
    my_row = lax.axis_index("row")
    my_col = lax.axis_index("col")
    kc = diag_inv.shape[0]
    rb_local = rhs.shape[0]
    nz_local = blocks.shape[3]
    local_rhs = rhs[:, 0]
    partial_value = jnp.zeros(local_rhs.shape, jnp.float32)
    solved_list = [jnp.zeros(local_rhs.shape[1:], jnp.float32)]
    slot_ids = jnp.arange(nz_local, dtype=jnp.int32)
    local_ids = jnp.arange(rb_local, dtype=jnp.int32)
    for k in range(kc):
        j = k // ncol
        owner_row = k % nrow
        local_pivot = k // nrow
        mine_row = my_row == owner_row
        mine_col = my_col == k % ncol
        pivot_part = jnp.where(mine_row, partial_value[local_pivot], jnp.float32(0.0))
        summed = lax.psum(pivot_part, "col")
        updated = (local_rhs[local_pivot] - summed).astype(jnp.bfloat16)
        pivot_bf = broadcast(updated, "row", owner_row)
        row_part = jnp.dot(diag_inv[k], pivot_bf, preferred_element_type=jnp.float32)
        sol = lax.all_gather(row_part, "row", axis=0, tiled=True)
        sol_bf = sol.astype(jnp.bfloat16)
        rows = block_rows[j, 0, 0]
        glob = rows * nrow + my_row
        valid = (slot_ids < counts[j, 0, 0]) & (glob > k) & mine_col
        weights = (valid[:, None] & (rows[:, None] == local_ids[None, :])).astype(jnp.float32)
        contrib = jnp.einsum(
            "sab,bn->san", blocks[j, 0, 0], sol_bf, preferred_element_type=jnp.float32
        )
        partial_value = partial_value + jnp.einsum(
            "sl,san->lan", weights, contrib, precision=lax.Precision.HIGHEST
        )
        solved_list[j] = jnp.where(mine_col, sol, solved_list[j])
    total = lax.psum(partial_value, "col")
    remainder = (local_rhs - total)[:, None]
    solved = jnp.stack(solved_list)[:, None]
    return (solved, remainder)


NR, NC = 8, 4
MAKER = (None, (2, 1), (3, 2), (5, 3))
FIRST = (1, 0)
BESIDE = (3, 1)
PARTNER = (None, (3, 1), (3, 3), (5, 2))
PIECES = ((4, 1), (6, 3), (5, 2), (7, 0))
SENDS = (
    (0, 1, 2, 3),
    (0, 1, 2, 3),
    (3, 1, 0, 2),
    (0, 1, 3, 2),
    (0, 1, 3, 2),
    (2, 1, 3, 0),
    (0, 3, 1, 2),
    (1, 3, 0, 2),
)
REST = ((3, 3), (0, 3), (1, 3), (1, 2))


def hops(a, b):
    d = a ^ b
    if d < 2:
        return 1 if d else 10000
    return 100 + abs((a >> 3) - (b >> 3)) + ((d >> 2) & 1) + ((d >> 1) & 1)


def complete(pairs):
    to = {a * NC + b: c * NC + d for (a, b), (c, d) in pairs}
    free_from = [i for i in range(NR * NC) if i not in to]
    free_to = [i for i in range(NR * NC) if i not in to.values()]
    n = len(free_from)
    u, v, match = [0] * (n + 1), [0] * (n + 1), [0] * (n + 1)
    for i in range(1, n + 1):
        match[0], j0 = i, 0
        least, way, used = [10**9] * (n + 1), [0] * (n + 1), [False] * (n + 1)
        while True:
            used[j0] = True
            i0, delta, j1 = match[j0], 10**9, 0
            for j in range(1, n + 1):
                if not used[j]:
                    cur = hops(free_from[i0 - 1], free_to[j - 1]) - u[i0] - v[j]
                    if cur < least[j]:
                        least[j], way[j] = cur, j0
                    if least[j] < delta:
                        delta, j1 = least[j], j
            for j in range(n + 1):
                if used[j]:
                    u[match[j]] += delta
                    v[j] -= delta
                else:
                    least[j] -= delta
            j0 = j1
            if match[j0] == 0:
                break
        while j0:
            j1 = way[j0]
            match[j0] = match[j1]
            j0 = j1
    for j in range(1, n + 1):
        to[free_from[match[j] - 1]] = free_to[j - 1]
    return [(divmod(a, NC), divmod(b, NC)) for a, b in sorted(to.items())]


def send(value, pairs):
    return lax.ppermute(value, ("row", "col"), [(a * NC + b, c * NC + d) for (a, b), (c, d) in complete(pairs)])


def send_only(value, pairs):
    return lax.ppermute(value, ("row", "col"), [(a * NC + b, c * NC + d) for (a, b), (c, d) in pairs])


def dot(a, b):
    return jnp.dot(a, b, preferred_element_type=jnp.float32)


def low(a):
    return a.astype(jnp.bfloat16)


def at(device):
    return (lax.axis_index("row") == device[0]) & (lax.axis_index("col") == device[1])


def any_of(devices):
    flag = at(devices[0])
    for d in devices[1:]:
        flag = flag | at(d)
    return flag


def call(kernel, outs, ins, in_specs, out_specs, scratch=(), limit=16):
    return pl.pallas_call(
        kernel,
        out_shape=outs,
        in_specs=in_specs,
        out_specs=out_specs,
        scratch_shapes=list(scratch),
        compiler_params=pltpu.CompilerParams(vmem_limit_bytes=limit << 20),
        name=kernel.func.__name__ if isinstance(kernel, functools.partial) else kernel.__name__,
    )(*ins)


def pair_width(m, part):
    return 2 * (m + 1) * part


def cut_kernel(diag_ref, *refs):
    cuts, sem = refs[:-1], refs[-1]
    row, col = lax.axis_index("row"), lax.axis_index("col")
    part = diag_ref.shape[1]
    k = jnp.int32(0)
    for r in range(NR):
        for c in range(NC):
            k = jnp.where((row == r) & (col == c), SENDS[r][c], k)
    for m in range(NR // 2):

        @pl.when(jnp.where((row == 1) & (k == 0), 1, row // 2) == m)
        def _():
            copy = pltpu.make_async_copy(diag_ref.at[k, :, pl.ds(0, pair_width(m, part))], cuts[m], sem)
            copy.start()
            copy.wait()


def first_kernel(rhs_ref, diag_ref, *refs):
    parts, (out_ref, rhs_v, d_v, rhs_sem, d_sem) = refs[:-5], refs[-5:]
    n = out_ref.shape[0] // 2
    col = lax.axis_index("col")

    @pl.when(lax.axis_index("row") == 0)
    def _():
        rhs_copy = pltpu.make_async_copy(rhs_ref.at[0], rhs_v, rhs_sem)
        rhs_copy.start()

        def pieces(c):
            copies = []
            for i, r in enumerate(PIECES[c]):
                m = max(r // 2, 1)
                wide = pair_width(m, n)
                source = parts[m - 1] if r else diag_ref.at[0, :, pl.ds(0, wide)]
                copies.append(pltpu.make_async_copy(source, d_v.at[i, :, pl.ds(0, wide)], d_sem.at[i]))
            return copies

        for c in range(NC):

            @pl.when(col == c)
            def _():
                for copy in pieces(c):
                    copy.start()

        rhs_copy.wait()
        p = low(rhs_v[...])
        for c in range(NC):

            @pl.when(col == c)
            def _():
                for i, copy in enumerate(pieces(c)):
                    copy.wait()
                    wide = pair_width(max(PIECES[c][i] // 2, 1), n)
                    out_ref[i * n : (i + 1) * n] = low(dot(d_v[i, :, :wide], p[:wide]))


def pack_kernel(*refs):
    parts, out_ref, sem = refs[:-2], refs[-2], refs[-1]

    @pl.when(any_of(PARTNER[1:]))
    def _():
        copies, left = [], 0
        for m, source in enumerate(parts):
            wide = source.shape[1]
            copies.append(pltpu.make_async_copy(source, out_ref.at[:, pl.ds(left, wide)], sem.at[m]))
            left += wide
        for copy in copies:
            copy.start()
        for copy in copies:
            copy.wait()


def whole_kernel(rows_ref, counts_ref, diag_ref, even_ref, *refs):
    odd, (out_ref, tail_ref, sem) = refs[:-3], refs[-3:]
    size = out_ref.shape[0]
    part = size // NR
    row, col = lax.axis_index("row"), lax.axis_index("col")
    listed = rows_ref[0, 0, 0, 0]
    there = (row >= NC) & (counts_ref[0, 0, 0] > 0)
    done = at(FIRST) | at(MAKER[1]) | at(BESIDE) | at(MAKER[2])
    first = (there & (listed == 0)) | done
    second = there & (listed == 1)
    ids = lax.broadcasted_iota(jnp.int32, tail_ref.shape, 0)
    flag = ((ids == 0) & first) | ((ids == 1) & second)
    tail_ref[...] = low(jnp.where(flag, 1.0, 0.0))

    @pl.when(any_of(MAKER[1:]))
    def _():
        def copy(i, source):
            wide = pair_width(i // 2, part)
            return pltpu.make_async_copy(source, out_ref.at[pl.ds(i * part, part), pl.ds(0, wide)], sem.at[i])

        left = 0
        for i in range(NR):
            wide = pair_width(i // 2, part)
            if i % 2:
                source = odd[i // 2]
            else:
                source = even_ref.at[:, pl.ds(left, wide)]
                left += wide

            @pl.when(row == i)
            def _():
                copy(i, diag_ref.at[col, :, pl.ds(0, wide)]).start()

            @pl.when(row != i)
            def _():
                copy(i, source).start()

        for m in range(NR // 2 - 1):
            right = pair_width(m, part)
            out_ref[pl.ds(2 * m * part, 2 * part), pl.ds(right, size - right)] = jnp.zeros(
                (2 * part, size - right), out_ref.dtype
            )
        for i in range(NR):
            copy(i, odd[i // 2]).wait()


def lower_dot(q_ref, d_ref, p_ref):
    half = d_ref.shape[0] // 2
    q_ref[:half] = low(dot(d_ref[:half, :half], p_ref[:half]))
    q_ref[half:] = low(dot(d_ref[half:], p_ref[...]))


def step0_kernel(g0, g1, g2, g3, rhs_ref, l_ref, p_ref, q_ref, s_ref):
    part = l_ref.shape[0] // NR
    row = lax.axis_index("row")

    def lookup(c, i):
        r = jnp.int32(PIECES[0][i])
        for n in range(1, NC):
            r = jnp.where(c == n, PIECES[n][i], r)
        return pl.multiple_of(r * part, part)

    @pl.when((row >= 1) & (row < 4) & (lax.axis_index("col") == 0))
    def _():
        for j, got in enumerate((g0, g1, g2, g3)):
            src = lax.rem(row + 7 - j, 4)
            q_ref[pl.ds(lookup(src, 0), part)] = got[:part]
            q_ref[pl.ds(lookup(src, 1), part)] = got[part:]
        s = dot(l_ref[...], q_ref[...])
        s_ref[...] = low(s)
        p_ref[...] = low(rhs_ref[0] - s)


def step1_kernel(p_in, d_ref, q_prev, q_ref):
    active = at(MAKER[1])

    @pl.when(active)
    def _():
        lower_dot(q_ref, d_ref, p_in)

    @pl.when(jnp.logical_not(active))
    def _():
        q_ref[...] = q_prev[...]


def step1_sum_kernel(q_in, sum_ref, rhs_ref, l_ref, s_prev, p_ref, s_ref):
    active = at(MAKER[1])

    @pl.when(active)
    def _():
        s = dot(l_ref[...], q_in[...]) + sum_ref[...].astype(jnp.float32)
        s_ref[...] = low(s)
        p_ref[...] = low(rhs_ref[0] - s)

    @pl.when(jnp.logical_not(active))
    def _():
        s_ref[...] = s_prev[...]


def step2_kernel(takers, p_in, q_in, came_ref, sum_ref, rhs_ref, d_ref, l_ref, q_prev, s_prev, a_ref, q_ref, s_ref):
    active, beside, taken = at(MAKER[2]), at(BESIDE), any_of(takers)

    @pl.when(active)
    def _():
        lower_dot(q_ref, d_ref, p_in)
        s_ref[...] = low(dot(l_ref[...], q_ref[...]))

    @pl.when(beside)
    def _():
        q_ref[...] = q_in[...]
        s = dot(l_ref[...], q_in[...]) + sum_ref[...].astype(jnp.float32)
        s_ref[...] = low(s)
        a_ref[...] = low(rhs_ref[0] - s)

    @pl.when(jnp.logical_not(active | beside))
    def _():
        s_ref[...] = s_prev[...]

    @pl.when(taken)
    def _():
        q_ref[...] = came_ref[...]

    @pl.when(jnp.logical_not(active | beside | taken))
    def _():
        q_ref[...] = q_prev[...]


def step3_kernel(takers, a_ref, sum_ref, *refs):
    came, (d_ref, q_prev, q_ref, p_v) = refs[:-4], refs[-4:]
    active = at(MAKER[3])

    @pl.when(active)
    def _():
        p_v[...] = low(a_ref[...].astype(jnp.float32) - sum_ref[...].astype(jnp.float32))
        lower_dot(q_ref, d_ref, p_v)

    for devices, source in zip(takers, came):

        @pl.when(any_of(devices))
        def _():
            q_ref[...] = source[...]

    @pl.when(jnp.logical_not(active | any_of([d for devices in takers for d in devices])))
    def _():
        q_ref[...] = q_prev[...]


def relay_kernel(takers, q_ref, got_ref, out_ref):
    taken = any_of(takers)

    @pl.when(taken)
    def _():
        out_ref[...] = got_ref[...]

    @pl.when(jnp.logical_not(taken))
    def _():
        out_ref[...] = q_ref[...]


def update_kernel(takers, tail_ref, s_ref, l_ref, q_prev, *refs):
    got, q_ref, out_ref = refs[:-2], refs[-2], refs[-1]
    size = l_ref.shape[0]
    row, col = lax.axis_index("row"), lax.axis_index("col")
    below = row >= NC

    def take(flag, source):
        @pl.when(flag)
        def _():
            q_ref[...] = source[...]

    kept = jnp.logical_not(any_of([d for devices in takers for d in devices]))
    take(kept, q_prev)
    for devices, source in zip(takers, got):
        take(any_of(devices), source)

    @pl.when(below)
    def _():
        out_ref[pl.ds(0, size)] = low(dot(l_ref[...], q_ref[...]))

    @pl.when(jnp.logical_not(below))
    def _():
        out_ref[pl.ds(0, size)] = s_ref[...]

    out_ref[pl.ds(size, TAIL)] = tail_ref[...]


def minus(acc, sums, i):
    size = acc.shape[0]
    for s in sums:
        keep = s[pl.ds(size, TAIL)].astype(jnp.float32)[i : i + 1] > 0.5
        acc = acc - jnp.where(keep, s[pl.ds(0, size)].astype(jnp.float32), 0.0)
    return acc


def half_kernel(q_ref, rest_ref, rhs_ref, mine_ref, across_ref, beside_ref, solved_ref, out_ref):
    came = any_of(REST)

    @pl.when(came)
    def _():
        solved_ref[...] = rest_ref[...].astype(jnp.float32)

    @pl.when(jnp.logical_not(came))
    def _():
        solved_ref[...] = q_ref[...].astype(jnp.float32)

    for i in range(out_ref.shape[0]):
        out_ref[i] = minus(rhs_ref[i], (mine_ref, across_ref, beside_ref), i)


def final_kernel(half_ref, corner_ref, out_ref):
    for i in range(out_ref.shape[0]):
        out_ref[i] = minus(half_ref[i], (corner_ref,), i)


def on_device_8x4(rhs, diag_inv, blocks, block_rows, counts):
    size, width = rhs.shape[2:]
    part = size // NR
    rhs = rhs[:, 0]
    block = blocks[0, 0, 0, 0]
    bf16 = jnp.bfloat16
    vec = jax.ShapeDtypeStruct((size, width), bf16)
    dma = pltpu.SemaphoreType.DMA

    wides = [pair_width(m, part) for m in range(NR // 2)]
    cuts = call(
        cut_kernel,
        [jax.ShapeDtypeStruct((part, w), bf16) for w in wides],
        [diag_inv],
        [HBM],
        [ANY] * len(wides),
        [dma],
        limit=60,
    )
    at_piece = {r: (0, c) for c, rows in enumerate(PIECES) for r in rows}
    parts = []
    for m, cut in enumerate(cuts):
        pairs = []
        for r in range(NR):
            for c, k in enumerate(SENDS[r]):
                if k == 0 and r and max(r // 2, 1) == m:
                    pairs.append(((r, c), at_piece[r]))
                if k and MAKER[k][0] != r and r // 2 == m:
                    pairs.append(((r, c), MAKER[k] if r % 2 else PARTNER[k]))
        parts.append(send_only(cut, pairs))
    q = call(
        first_kernel,
        jax.ShapeDtypeStruct((2 * part, width), bf16),
        [rhs, diag_inv, *parts[1:]],
        [HBM, HBM] + [ANY] * (len(wides) - 1),
        VMEM,
        [
            pltpu.VMEM((size, width), jnp.float32),
            pltpu.VMEM((2, part, size), bf16),
            dma,
            pltpu.SemaphoreType.DMA((2,)),
        ],
    )
    takers = (FIRST, (2, 0), (3, 0))
    got = [send(q, [((0, c), takers[(c + j) % 4]) for c in range(4) if (c + j) % 4 < 3]) for j in range(4)]
    even = call(
        pack_kernel,
        jax.ShapeDtypeStruct((part, sum(wides)), bf16),
        parts,
        [ANY] * len(wides),
        VMEM,
        [pltpu.SemaphoreType.DMA((len(wides),))],
    )
    even = send(even, [(PARTNER[k], MAKER[k]) for k in range(1, NC)])
    diag, tail = call(
        whole_kernel,
        [jax.ShapeDtypeStruct((size, size), bf16), jax.ShapeDtypeStruct((TAIL, width), bf16)],
        [block_rows, counts, diag_inv, even, *parts],
        [SMEM, SMEM, HBM] + [ANY] * (1 + len(wides)),
        [VMEM, VMEM],
        [pltpu.SemaphoreType.DMA((NR,))],
    )

    p, q, s = call(step0_kernel, [vec] * 3, [*got, rhs, block], [VMEM] * 6, [VMEM] * 3)
    p_in = send(p, [(FIRST, MAKER[1])])
    sums = send(s, [((2, 0), MAKER[1]), ((3, 0), BESIDE)])
    q = call(step1_kernel, vec, [p_in, diag, q], [VMEM] * 3, VMEM)
    p, s = call(step1_sum_kernel, [vec] * 2, [q, sums, rhs, block, s], [VMEM] * 5, [VMEM] * 2)
    p_in = send(p, [(MAKER[1], MAKER[2])])
    q_in = send(q, [(MAKER[1], BESIDE)])

    came = send(q, [((2, 0), (4, 0)), ((3, 0), (5, 0)), ((1, 0), (0, 0)), ((2, 1), (4, 1))])
    took = [(4, 0), (5, 0), (0, 0), (4, 1)]
    a, q, s = call(
        functools.partial(step2_kernel, took),
        [vec] * 3,
        [p_in, q_in, came, sums, rhs, diag, block, q, s],
        [VMEM] * 9,
        [VMEM] * 3,
    )
    a = send(a, [(BESIDE, MAKER[3])])
    sums = send(s, [(MAKER[2], MAKER[3])])
    sends = [
        [(MAKER[2], (2, 2))],
        [(MAKER[2], (7, 2)), ((4, 0), (6, 0)), ((5, 0), (7, 0)), ((4, 1), (6, 1)), ((3, 1), (1, 1)), ((2, 1), (0, 1))],
        [(MAKER[2], (5, 2)), ((3, 1), (7, 1)), ((4, 1), (5, 1))],
    ]
    got = [send(q, sends[0])] + [send_only(q, pairs) for pairs in sends[1:]]
    q = call(
        functools.partial(step3_kernel, [[b for _, b in pairs] for pairs in sends]),
        vec,
        [a, sums, *got, diag, q],
        [VMEM] * 7,
        VMEM,
        [pltpu.VMEM((size, width), bf16)],
    )

    sends = [
        [(MAKER[3], (6, 3)), ((2, 2), (4, 2))],
        [(MAKER[3], (4, 3)), ((2, 2), (6, 2))],
        [(MAKER[3], (7, 3))],
    ]
    got = [send_only(q, pairs) for pairs in sends]
    above = [(2, 3), (0, 2)]
    came = send_only(q, list(zip((MAKER[3], (2, 2)), above)))
    takers = [[b for _, b in pairs] for pairs in sends]
    q, mine = call(
        functools.partial(update_kernel, takers),
        [vec, jax.ShapeDtypeStruct((size + TAIL, width), bf16)],
        [tail, s, block, q, *got],
        [VMEM] * (4 + len(got)),
        [VMEM] * 2,
    )

    def swap(value, step):
        return send(value, [((r, c), (r, c ^ step)) for r in range(NR) for c in range(NC)])

    across = swap(mine, 2)
    q = call(functools.partial(relay_kernel, above), vec, [q, came], [VMEM] * 2, VMEM)
    rest = send_only(q, list(zip(((2, 3), (4, 3), (7, 3), MAKER[2]), REST)))
    beside = swap(mine, 1)
    across, rest = lax.optimization_barrier((across, rest))
    corner = swap(across, 1)
    whole_rhs = jax.ShapeDtypeStruct(rhs.shape, jnp.float32)
    solved, half = call(
        half_kernel,
        [jax.ShapeDtypeStruct((size, width), jnp.float32), whole_rhs],
        [q, rest, rhs, mine, across, beside],
        [VMEM] * 6,
        [VMEM] * 2,
    )
    remainder = call(final_kernel, whole_rhs, [half, corner], [VMEM] * 2, VMEM)
    return solved[None, None], remainder[:, None]


def solution(mesh):
    in_specs = (
        P(None, "row", None, None),
        P(None, "row", None),
        P(None, "col", "row", None, None, None),
        P(None, "col", "row", None),
        P(None, "col", "row"),
    )
    out_specs = (P(None, "col", None, None), P(None, "row", None, None))
    small = mesh.shape["row"] == NR and mesh.shape["col"] == NC
    return jax.shard_map(
        on_device_8x4 if small else on_device_any,
        mesh=mesh,
        in_specs=in_specs,
        out_specs=out_specs,
        check_vma=False,
    )
```
